32 devices in a mesh: shard: 8 (over z, y), ctx: 2 (over x), tp: 2 (over core).
Axes of the slice: x: 2, y: 2, z: 4, core: 2. Of those that a mesh axis runs over, the one named last changes fastest.
Arguments:
- inputs: bfloat16 [2, 8192, 1024], P(None, ('shard', 'ctx')), may hold values from -6 to 6
- cotangent: bfloat16 [2, 8192, 1024], P(None, ('shard', 'ctx')), may hold values from -6 to 6
- lengths: int32 [2, 8], P(None, 'shard'), may hold values from 256 to 1024, as said below
- buckets: int32 [1024, 1024], P('ctx'), may hold values from 0 to 31, as said below
- query_weight: bfloat16 [1024, 1024], P(('shard', 'ctx'), 'tp'), may hold values from -0.09375 to 0.09375
- key_weight: bfloat16 [1024, 1024], P(('shard', 'ctx'), 'tp'), may hold values from -0.09375 to 0.09375
- value_weight: bfloat16 [1024, 1024], P(('shard', 'ctx'), 'tp'), may hold values from -0.1875 to 0.1875
- projection_weight: bfloat16 [1024, 1024], P(('shard', 'ctx'), 'tp'), may hold values from -1 to 1
- gate_weight: bfloat16 [1024, 2816], P(('shard', 'ctx'), 'tp'), may hold values from -0.1875 to 0.1875
- up_weight: bfloat16 [1024, 2816], P(('shard', 'ctx'), 'tp'), may hold values from -0.1875 to 0.1875
- down_weight: bfloat16 [1024, 2816], P(('shard', 'ctx'), 'tp'), may hold values from -0.21875 to 0.21875
- attention_gain: bfloat16 [1024], P(('shard', 'ctx')), may hold values from 0.099609375 to 1.8984375
- feedforward_gain: bfloat16 [1024], P(('shard', 'ctx')), may hold values from 0.099609375 to 1.8984375
- bias_table: bfloat16 [32, 16], P(None, 'tp'), may hold values from -4 to 4
Outputs:
- output: bfloat16 [2, 8192, 1024], P(None, ('shard', 'ctx'))
- input_grad: float32 [2, 8192, 1024], P(None, ('shard', 'ctx'))
- query_grad: float32 [1024, 1024], P(('shard', 'ctx'), 'tp')
- key_grad: float32 [1024, 1024], P(('shard', 'ctx'), 'tp')
- value_grad: float32 [1024, 1024], P(('shard', 'ctx'), 'tp')
- projection_grad: float32 [1024, 1024], P(('shard', 'ctx'), 'tp')
- gate_grad: float32 [1024, 2816], P(('shard', 'ctx'), 'tp')
- up_grad: float32 [1024, 2816], P(('shard', 'ctx'), 'tp')
- down_grad: float32 [1024, 2816], P(('shard', 'ctx'), 'tp')
- attention_gain_grad: float32 [1024], P(('shard', 'ctx'))
- feedforward_gain_grad: float32 [1024], P(('shard', 'ctx'))
- table_grad: float32 [32, 16], P(None, 'tp')
The draws below stay inside these ranges and needn't reach their ends.
Inputs may be any that keep to these rules, and one draw needn't show every extreme that they name: For every sequence index s, at least one of the 2 micro-batches has lengths[m, s] = 1024. T5's bidirectional bucket (16 buckets each way, exact below a distance of 8, logarithmic up to 128) of key position minus query position, where the position ids rise by 1 or 2 from slot to slot.
All inputs are finite; a program needn't handle non-finite values.
Results may differ from the reference program's by a relative error of at most 0.017.
The reference program's roundings to bfloat16 on the way count: a program that leaves them out, or rounds other values in their place, can miss the bound.
Values may be sent and summed in bfloat16 or wider, within the bound.
A program may use at most 256 MiB of HBM per device.

```python
import jax
import jax.numpy as jnp
from jax import lax

D = 1024
HEADS = 16
HEAD_DIM = 64
FF = 2816
BUCKETS = 32
LEN = 1024
MICRO = 2
INNER = 1024
SEQS = 8
TOKENS = 8192


def draw_lengths(key, part):
    key = jax.random.fold_in(key, 11)
    base = jax.random.randint(jax.random.fold_in(key, 1), (MICRO, SEQS), LEN // 4, LEN + 1)
    chosen = jax.random.randint(jax.random.fold_in(key, 2), (SEQS,), 0, MICRO)
    full_rows = jnp.arange(MICRO, dtype=jnp.int32)[:, None] == chosen[None, :]
    return jnp.where(full_rows, LEN, base).astype(jnp.int32)


def draw_buckets(key, part):
    key = jax.random.fold_in(key, 23)
    steps = jax.random.randint(key, (LEN,), 1, 3)
    places = jnp.cumsum(steps).astype(jnp.int32)
    relative = places[None, :] - places[:, None]
    distance = jnp.abs(relative)
    level = sum(((distance >= edge).astype(jnp.int32) for edge in (8, 12, 16, 23, 32, 46, 64, 91)))
    magnitude = jnp.where(distance < 8, distance, 7 + level)
    return (magnitude + 16 * (relative > 0).astype(jnp.int32)).astype(jnp.int32)


def strengthened(values, rng, source, target, shards_of, factor):
    def block_of(axis_at):
        return (jnp.arange(values.shape[axis_at]) // (values.shape[axis_at] // shards_of)).reshape((-1,) + (1,) * (values.ndim - 1 - axis_at))

    first = jax.random.permutation(rng, shards_of)[block_of(target)]
    far = (block_of(target) + shards_of // 2) % shards_of
    return jnp.where((block_of(source) == first) | (block_of(source) == far), factor * values, values)


def level_of(rng, shape, split, least, high):
    def one(axis_at, shards_of):
        heights = jax.random.uniform(jax.random.fold_in(jax.random.fold_in(rng, 6), axis_at), (shards_of,), jnp.float32, least / len(split), high / len(split))
        return jnp.repeat(jnp.exp(heights), shape[axis_at] // shards_of).reshape((-1,) + (1,) * (len(shape) - axis_at - 1))

    gain = one(*split[0])
    for cut in split[1:]:
        gain = gain * one(*cut)
    return gain


def gaussian(rng, shape, deviation, bound, cuts=(), kind=jnp.bfloat16):
    factor_of = level_of(rng, shape, cuts, -0.22, 0.18) if cuts else 1.0
    values = jax.random.normal(rng, shape, jnp.float32) * deviation * factor_of
    return jnp.minimum(jnp.maximum(values, -bound), bound).astype(kind)


def gaussian_with(rng, extent, deviation, limit, split, heavy, kind=jnp.bfloat16):
    drawn = deviation * jax.random.normal(rng, extent, jnp.float32)
    if split:
        drawn = drawn * level_of(rng, extent, split, -0.22, 0.18)
    return jnp.clip(strengthened(drawn, jax.random.fold_in(rng, 3), *heavy), -limit, limit).astype(kind)


def setup_inputs(seed: int = 0) -> dict:
    seeds = jax.random.split(jax.random.key(seed), 15)
    inputs = gaussian(seeds[0], (MICRO, TOKENS, D), 1.0, 6.0, ((1, 16),))
    cotangent = gaussian_with(seeds[1], (MICRO, TOKENS, D), 1.0, 6.0, ((1, 16),), (1, 2, 16, 2.0))
    lengths = draw_lengths(jax.random.fold_in(seeds[14], 71), 0)
    buckets = draw_buckets(jax.random.fold_in(seeds[14], 71), 0)
    query_weight = gaussian(seeds[4], (D, INNER), (4 * D) ** -0.5, 0.09375, ((0, 16), (1, 2)))
    key_weight = gaussian(seeds[5], (D, INNER), (4 * D) ** -0.5, 0.09375, ((0, 16), (1, 2)))
    value_weight = gaussian(seeds[6], (D, INNER), D ** -0.5, 0.1875, ((0, 16), (1, 2)))
    projection_weight = gaussian(seeds[7], (D, INNER), (max(INNER // 32, 2)) ** -0.5, 1.0, ((0, 16), (1, 2)))
    gate_weight = gaussian(seeds[8], (D, FF), D ** -0.5, 0.1875, ((0, 16), (1, 2)))
    up_weight = gaussian(seeds[9], (D, FF), D ** -0.5, 0.1875, ((0, 16), (1, 2)))
    down_weight = gaussian(seeds[10], (D, FF), (max(FF // 4, 2)) ** -0.5, 0.21875, ((0, 16), (1, 2)))
    attention_gain = jnp.clip(1.0 + 0.18 * jax.random.normal(seeds[11], (D,), jnp.float32), 0.099609375, 1.8984375).astype(jnp.bfloat16)
    feedforward_gain = jnp.clip(1.0 + 0.18 * jax.random.normal(seeds[12], (D,), jnp.float32), 0.099609375, 1.8984375).astype(jnp.bfloat16)
    bias_table = gaussian(seeds[13], (BUCKETS, HEADS), 1.0, 4.0, ((1, 2),))
    return {"inputs": inputs, "cotangent": cotangent, "lengths": lengths, "buckets": buckets, "query_weight": query_weight, "key_weight": key_weight, "value_weight": value_weight, "projection_weight": projection_weight, "gate_weight": gate_weight, "up_weight": up_weight, "down_weight": down_weight, "attention_gain": attention_gain, "feedforward_gain": feedforward_gain, "bias_table": bias_table}


@jax.custom_vjp
def low(v):
    return lax.optimization_barrier(v.astype(jnp.bfloat16)).astype(jnp.float32)

@jax.custom_vjp
def low_back(v):
    return v

def low_keep(v):
    return (low(v), None)

def low_pass(kept, grad):
    return (grad,)

def back_keep(v):
    return (v, None)

def back_low(kept, grad):
    return (low(grad),)
low.defvjp(low_keep, low_pass)
low_back.defvjp(back_keep, back_low)
EPSILON = 1e-06
GELU_ROOT = 0.7978845608028654
GELU_CUBIC = 0.044715
HIGHEST = lax.Precision.HIGHEST

def gelu_tanh(activation):
    return 0.5 * activation * (1.0 + jnp.tanh(GELU_ROOT * (activation + GELU_CUBIC * activation * activation * activation)))

def normalize(tokens_in, gain_values):
    return tokens_in * lax.rsqrt(lax.optimization_barrier(jnp.mean(tokens_in * tokens_in, axis=-1, keepdims=True)) + EPSILON) * gain_values

def sequence_layer(parameters, buckets, tokens_in, length):
    query_weight, key_weight, value_weight, projection_weight, gate_weight, up_weight, down_weight, attention_gain, feedforward_gain, bias_table = parameters
    normed_one = low(normalize(tokens_in, attention_gain))
    queries = low_back(low(jnp.dot(normed_one, query_weight, precision=HIGHEST)))
    key_rows = low_back(low(jnp.dot(normed_one, key_weight, precision=HIGHEST)))
    values = low_back(low(jnp.dot(normed_one, value_weight, precision=HIGHEST)))
    split_heads = (LEN, HEADS, HEAD_DIM)
    scores = jnp.einsum('qhd,khd->hqk', queries.reshape(split_heads), key_rows.reshape(split_heads), precision=HIGHEST)
    bias_values = jnp.transpose(jnp.take(bias_table, buckets, axis=0), (2, 0, 1))
    valid_keys = jnp.arange(LEN, dtype=jnp.int32) < length
    scores = low_back(jnp.where(valid_keys[None, None, :], scores + bias_values, -1e+30))
    highest = lax.optimization_barrier(jnp.max(scores, axis=-1, keepdims=True))
    exponent = jnp.exp(scores - highest)
    attention_probs = low(exponent / lax.optimization_barrier(jnp.sum(exponent, axis=-1, keepdims=True)))
    attended = jnp.einsum('hqk,khd->qhd', attention_probs, values.reshape(split_heads), precision=HIGHEST).reshape(LEN, INNER)
    attended = low_back(low(attended))
    middle = tokens_in + low_back(jnp.dot(attended, projection_weight.T, precision=HIGHEST))
    normed_two = low(normalize(middle, feedforward_gain))
    gate_value = low_back(jnp.dot(normed_two, gate_weight, precision=HIGHEST))
    up_value = low_back(jnp.dot(normed_two, up_weight, precision=HIGHEST))
    hidden = low(gelu_tanh(gate_value) * up_value)
    return middle + low_back(jnp.dot(hidden, down_weight.T, precision=HIGHEST))

def reference(inputs, cotangent, lengths, buckets, query_weight, key_weight, value_weight, projection_weight, gate_weight, up_weight, down_weight, attention_gain, feedforward_gain, bias_table):
    parameters = tuple((weight.astype(jnp.float32) for weight in (query_weight, key_weight, value_weight, projection_weight, gate_weight, up_weight, down_weight, attention_gain, feedforward_gain, bias_table)))
    present = inputs.astype(jnp.float32)
    flat_lengths = lengths.reshape(MICRO * SEQS)
    checked_layer = jax.checkpoint(sequence_layer)

    def forward(whole, weights_all):
        sequences = whole.reshape(MICRO * SEQS, LEN, D)

        def single_sequence(packed):
            return checked_layer(weights_all, buckets, packed[0], packed[1])
        return lax.map(single_sequence, (sequences, flat_lengths)).reshape(MICRO, TOKENS, D)
    output, pullback = jax.vjp(forward, present, parameters)
    live_rows = (jnp.arange(LEN, dtype=jnp.int32)[None, None, :] < lengths[:, :, None]).astype(jnp.float32)
    masked = (cotangent.astype(jnp.float32).reshape(MICRO, SEQS, LEN, D) * live_rows[:, :, :, None]).reshape(MICRO, TOKENS, D)
    grad_input, gradients = pullback(masked)
    return (output.astype(jnp.bfloat16), grad_input, gradients[0], gradients[1], gradients[2], gradients[3], gradients[4], gradients[5], gradients[6], gradients[7], gradients[8], gradients[9])
```

```python
import functools

import jax
import jax.numpy as jnp
from jax import lax
from jax.experimental import pallas as pl
from jax.experimental.pallas import tpu as pltpu
from jax.sharding import PartitionSpec as P

EPSILON = 1e-06
GELU_ROOT = 0.7978845608028654
GELU_CUBIC = 0.044715
MESH = pl.DeviceIdType.MESH
MIB = 1024 * 1024


BAND = 3
BLOCK = 128


def lane_head(rows, width, which):
    lanes = lax.broadcasted_iota(jnp.int32, (rows, width), 1)
    half = width // 2
    return (lanes < half) if which == 0 else (lanes >= half)


def bias_kernel(band_ref, bandt_ref, table_ref, bias_ref, biast_ref):
    rows = table_ref[0]
    for part in range(band_ref.shape[1] // 8):
        piece = band_ref[0, pl.ds(8 * part, 8), :]
        for col in range(BAND):
            index = piece[:, col * BLOCK : (col + 1) * BLOCK]
            got = jnp.take_along_axis(rows, index, axis=1)
            bias_ref[0, 0, pl.ds(8 * part, 8), col * BLOCK : (col + 1) * BLOCK] = got
    for part in range(bandt_ref.shape[1] // 8):
        index = bandt_ref[0, pl.ds(8 * part, 8), :]
        biast_ref[0, 0, pl.ds(8 * part, 8), :] = jnp.take_along_axis(rows, index, axis=1)


def bias_bands(band, bandt, table_rows):
    blocks = band.shape[0]
    heads = table_rows.shape[0]
    return pl.pallas_call(
        bias_kernel,
        grid=(blocks, heads),
        in_specs=[
            pl.BlockSpec((1, BLOCK, BAND * BLOCK), lambda i, h: (i, 0, 0)),
            pl.BlockSpec((1, BAND * BLOCK, BLOCK), lambda i, h: (i, 0, 0)),
            pl.BlockSpec((1, 8, 128), lambda i, h: (h, 0, 0)),
        ],
        out_specs=[
            pl.BlockSpec((1, 1, BLOCK, BAND * BLOCK), lambda i, h: (h, i, 0, 0)),
            pl.BlockSpec((1, 1, BAND * BLOCK, BLOCK), lambda i, h: (h, i, 0, 0)),
        ],
        out_shape=[
            jax.ShapeDtypeStruct((heads, blocks, BLOCK, BAND * BLOCK), jnp.float32),
            jax.ShapeDtypeStruct((heads, blocks, BAND * BLOCK, BLOCK), jnp.float32),
        ],
        name="bias_bands",
    )(band, bandt, table_rows)


def band_start(row_block, blocks):
    return jnp.clip(row_block - 1, 0, blocks - BAND)


def forward_kernel(q_ref, k_ref, v_ref, kaux_ref, qaux_ref, bias_ref, out_ref, lse_ref, s_ref, *, blocks):
    step = pl.program_id(1)
    rows = q_ref.shape[0]
    subs = rows // BLOCK
    pair = q_ref[...]
    keys = jnp.concatenate([k_ref[...], kaux_ref[...]], axis=1)
    outs = []
    for head in range(2):
        aux = jnp.concatenate(
            [jnp.broadcast_to(qaux_ref[head, sub : sub + 1, :], (BLOCK, 128)) for sub in range(subs)], axis=0
        ).astype(jnp.bfloat16)
        masked = jnp.where(lane_head(rows, 128, head), pair, jnp.zeros_like(pair))
        left = jnp.concatenate([masked, aux], axis=1)
        s_ref[...] = lax.dot_general(
            left, keys, (((1,), (1,)), ((), ())), preferred_element_type=jnp.float32
        )
        for sub in range(subs):
            start = pl.multiple_of(band_start(step * subs + sub, blocks) * BLOCK, BLOCK)
            s_ref[sub * BLOCK : (sub + 1) * BLOCK, pl.ds(start, BAND * BLOCK)] += bias_ref[head, sub]
        scores = s_ref[...]
        highest = jnp.max(scores, axis=1, keepdims=True)
        exponent = jnp.exp(scores - highest)
        total = jnp.sum(exponent, axis=1, keepdims=True)
        outs.append(
            jnp.dot(exponent.astype(jnp.bfloat16), v_ref[...], preferred_element_type=jnp.float32)
            * (1.0 / total)
        )
        lse = jnp.broadcast_to(highest + jnp.log(total), (rows, 128))
        lse_ref[0, head : head + 1, :] = jnp.transpose(lse)[0:1, :]
    out_ref[...] = jnp.where(lane_head(rows, 128, 0), outs[0], outs[1]).astype(jnp.bfloat16)


def attention_forward(qkv, kaux, qaux, bias):
    length = qkv.shape[0]
    heads, blocks = bias.shape[:2]
    pairs = heads // 2
    rows = 256
    subs = rows // BLOCK
    return pl.pallas_call(
        functools.partial(forward_kernel, blocks=blocks),
        grid=(pairs, length // rows),
        in_specs=[
            pl.BlockSpec((rows, 128), lambda p, i: (i, p)),
            pl.BlockSpec((length, 128), lambda p, i: (0, pairs + p)),
            pl.BlockSpec((length, 128), lambda p, i: (0, 2 * pairs + p)),
            pl.BlockSpec((length, 128), lambda p, i: (0, 0)),
            pl.BlockSpec((2, None, subs, 128), lambda p, i: (p, i, 0, 0)),
            pl.BlockSpec((2, subs, BLOCK, BAND * BLOCK), lambda p, i: (p, i, 0, 0)),
        ],
        out_specs=[
            pl.BlockSpec((rows, 128), lambda p, i: (i, p)),
            pl.BlockSpec((1, 2, rows), lambda p, i: (p, 0, i)),
        ],
        out_shape=[
            jax.ShapeDtypeStruct((length, pairs * 128), jnp.bfloat16),
            jax.ShapeDtypeStruct((pairs, 2, length), jnp.float32),
        ],
        scratch_shapes=[pltpu.VMEM((rows, length), jnp.float32)],
        compiler_params=pltpu.CompilerParams(vmem_limit_bytes=40 * 1024 * 1024),
        name="attention_forward",
    )(qkv, qkv, qkv, kaux, qaux.reshape(heads, blocks // subs, subs, 128), bias)


def backward_kernel(
    q_ref, k_ref, v_ref, kaux_ref, qaux_ref, bias_ref, lse_ref, do_ref,
    dq_ref, dk_ref, dv_ref, gs_ref, sums_ref, s_ref, g_ref, dk_acc, dv_acc, *, blocks
):
    step = pl.program_id(1)
    steps = pl.num_programs(1)
    rows = q_ref.shape[0]
    subs = rows // BLOCK

    @pl.when(step == 0)
    def _():
        dk_acc[...] = jnp.zeros_like(dk_acc)
        dv_acc[...] = jnp.zeros_like(dv_acc)

    pair = q_ref[...]
    grad = do_ref[...]
    key_pair = k_ref[...]
    keys = jnp.concatenate([key_pair, kaux_ref[...]], axis=1)
    last = (((1,), (1,)), ((), ()))
    dq = None
    for head in range(2):
        here = lane_head(rows, 128, head)
        aux = jnp.concatenate(
            [jnp.broadcast_to(qaux_ref[head, sub : sub + 1, :], (BLOCK, 128)) for sub in range(subs)], axis=0
        ).astype(jnp.bfloat16)
        q_masked = jnp.where(here, pair, jnp.zeros_like(pair))
        do_masked = jnp.where(here, grad, jnp.zeros_like(grad))
        s_ref[...] = lax.dot_general(
            keys, jnp.concatenate([q_masked, aux], axis=1), last, preferred_element_type=jnp.float32
        )
        for sub in range(subs):
            start = pl.multiple_of(band_start(step * subs + sub, blocks) * BLOCK, BLOCK)
            s_ref[pl.ds(start, BAND * BLOCK), sub * BLOCK : (sub + 1) * BLOCK] += bias_ref[head, sub]
        soft = jnp.exp(s_ref[...] - lse_ref[0, head : head + 1, :])
        dv_acc[...] += jnp.dot(soft.astype(jnp.bfloat16), do_masked, preferred_element_type=jnp.float32)
        grad_probs = lax.dot_general(v_ref[...], do_masked, last, preferred_element_type=jnp.float32)
        weighted = jnp.sum(soft * grad_probs, axis=0, keepdims=True)
        grad_scores = (soft * (grad_probs - weighted)).astype(jnp.bfloat16)
        g_ref[...] = grad_scores
        dk_acc[...] += jnp.dot(grad_scores, q_masked, preferred_element_type=jnp.float32)
        k_masked = jnp.where(lane_head(key_pair.shape[0], 128, head), key_pair, jnp.zeros_like(key_pair))
        part = lax.dot_general(
            grad_scores, k_masked, (((0,), (0,)), ((), ())), preferred_element_type=jnp.float32
        )
        dq = part if dq is None else dq + part
        for sub in range(subs):
            start = pl.multiple_of(band_start(step * subs + sub, blocks) * BLOCK, BLOCK)
            gs_ref[head, sub] = g_ref[pl.ds(start, BAND * BLOCK), sub * BLOCK : (sub + 1) * BLOCK]
        for block in range(blocks):
            sums_ref[head, block : block + 1, :] = jnp.sum(
                grad_scores[block * BLOCK : (block + 1) * BLOCK, :].astype(jnp.float32), axis=0, keepdims=True
            )
    dq_ref[...] = dq.astype(jnp.bfloat16)

    @pl.when(step == steps - 1)
    def _():
        dk_ref[...] = dk_acc[...].astype(jnp.bfloat16)
        dv_ref[...] = dv_acc[...].astype(jnp.bfloat16)


def attention_backward(qkv, kaux, qaux, biast, lse, grad_attended):
    length = qkv.shape[0]
    heads, blocks = biast.shape[:2]
    pairs = heads // 2
    rows = 256
    subs = rows // BLOCK
    wide = jax.ShapeDtypeStruct((length, pairs * 128), jnp.bfloat16)
    return pl.pallas_call(
        functools.partial(backward_kernel, blocks=blocks),
        grid=(pairs, length // rows),
        in_specs=[
            pl.BlockSpec((rows, 128), lambda p, i: (i, p)),
            pl.BlockSpec((length, 128), lambda p, i: (0, pairs + p)),
            pl.BlockSpec((length, 128), lambda p, i: (0, 2 * pairs + p)),
            pl.BlockSpec((length, 128), lambda p, i: (0, 0)),
            pl.BlockSpec((2, None, subs, 128), lambda p, i: (p, i, 0, 0)),
            pl.BlockSpec((2, subs, BAND * BLOCK, BLOCK), lambda p, i: (p, i, 0, 0)),
            pl.BlockSpec((1, 2, rows), lambda p, i: (p, 0, i)),
            pl.BlockSpec((rows, 128), lambda p, i: (i, p)),
        ],
        out_specs=[
            pl.BlockSpec((rows, 128), lambda p, i: (i, p)),
            pl.BlockSpec((length, 128), lambda p, i: (0, p)),
            pl.BlockSpec((length, 128), lambda p, i: (0, p)),
            pl.BlockSpec((2, subs, BAND * BLOCK, BLOCK), lambda p, i: (p, i, 0, 0)),
            pl.BlockSpec((2, blocks, rows), lambda p, i: (p, 0, i)),
        ],
        out_shape=[
            wide,
            wide,
            wide,
            jax.ShapeDtypeStruct((heads, blocks, BAND * BLOCK, BLOCK), jnp.bfloat16),
            jax.ShapeDtypeStruct((heads, blocks, length), jnp.float32),
        ],
        scratch_shapes=[
            pltpu.VMEM((length, rows), jnp.float32),
            pltpu.VMEM((length, rows), jnp.bfloat16),
            pltpu.VMEM((length, 128), jnp.float32),
            pltpu.VMEM((length, 128), jnp.float32),
        ],
        compiler_params=pltpu.CompilerParams(vmem_limit_bytes=40 * 1024 * 1024),
        name="attention_backward",
    )(qkv, qkv, qkv, kaux, qaux.reshape(heads, blocks // subs, subs, 128), biast, lse, grad_attended)


GROUP = 16


def table_kernel(bandt_ref, gs_ref, out_ref, acc_ref, *, buckets):
    step = pl.program_id(0)

    @pl.when(step == 0)
    def _():
        acc_ref[...] = jnp.zeros_like(acc_ref)

    heads = gs_ref.shape[0]

    def one(group, carry):
        start = pl.multiple_of(group * GROUP, GROUP)
        grads = jnp.concatenate(
            [gs_ref[:, two, pl.ds(start, GROUP), :].reshape(heads * GROUP, BLOCK) for two in range(2)], axis=1
        )
        index = jnp.concatenate([bandt_ref[two, pl.ds(start, GROUP), :] for two in range(2)], axis=1)
        index = index.astype(jnp.float32)
        hot = jnp.concatenate(
            [jnp.where(index == float(b), 1.0, 0.0) for b in range(buckets)], axis=0
        ).astype(jnp.bfloat16)
        acc_ref[...] += lax.dot_general(
            hot, grads, (((1,), (1,)), ((), ())), preferred_element_type=jnp.float32
        )
        return carry

    lax.fori_loop(0, BAND * BLOCK // GROUP, one, 0)

    @pl.when(step == pl.num_programs(0) - 1)
    def _():
        row = lax.broadcasted_iota(jnp.int32, acc_ref.shape, 0) % GROUP
        col = lax.broadcasted_iota(jnp.int32, acc_ref.shape, 1) % GROUP
        out_ref[...] = jnp.where(row == col, acc_ref[...], 0.0)


def table_band(bandt, gs, buckets):
    heads, blocks = gs.shape[:2]
    out = pl.pallas_call(
        functools.partial(table_kernel, buckets=buckets),
        grid=(blocks // 2,),
        in_specs=[
            pl.BlockSpec((2, BAND * BLOCK, BLOCK), lambda i: (i, 0, 0)),
            pl.BlockSpec((heads, 2, BAND * BLOCK, BLOCK), lambda i: (0, i, 0, 0)),
        ],
        out_specs=pl.BlockSpec((buckets * GROUP, heads * GROUP), lambda i: (0, 0)),
        out_shape=jax.ShapeDtypeStruct((buckets * GROUP, heads * GROUP), jnp.float32),
        scratch_shapes=[pltpu.VMEM((buckets * GROUP, heads * GROUP), jnp.float32)],
        compiler_params=pltpu.CompilerParams(vmem_limit_bytes=40 * 1024 * 1024),
        name="table_band",
    )(bandt, gs)
    return out.reshape(buckets, GROUP, heads, GROUP).sum((1, 3))
def split_columns(start, stop, pieces):
    tiles = (stop - start) // 128
    edges = [start + 128 * (tiles * i // pieces) for i in range(pieces + 1)]
    return [(a, b) for a, b in zip(edges, edges[1:]) if b > a]


class Place:
    def __init__(self, shard_size):
        self.deep = shard_size // 2
        shard = lax.axis_index("shard")
        self.z = shard // 2
        self.y = shard % 2
        self.x = lax.axis_index("ctx")
        self.c = lax.axis_index("tp")

    def device(self, z=None, y=None, x=None, c=None):
        z = self.z if z is None else z
        y = self.y if y is None else y
        x = self.x if x is None else x
        c = self.c if c is None else c
        return (z * 2 + y, x, c)

    def line(self, distance):
        return (self.z + distance) % self.deep

    def peers(self):
        others = [self.device(z=self.line(d)) for d in range(1, self.deep)]
        return others + [self.device(y=1 - self.y), self.device(x=1 - self.x), self.device(c=1 - self.c)]


def meet(place):
    barrier = pltpu.get_barrier_semaphore()
    peers = place.peers()
    for peer in peers:
        pl.semaphore_signal(barrier, inc=1, device_id=peer, device_id_type=MESH)
    pl.semaphore_wait(barrier, len(peers))


def send(source, target, send_sem, recv_sem, device):
    return pltpu.make_async_remote_copy(
        src_ref=source, dst_ref=target, send_sem=send_sem, recv_sem=recv_sem, device_id=device, device_id_type=MESH
    )


def gather_kernel(shard_size, chunks, own_ref, full_ref, local_sem, send_line, recv_line, send_near, recv_near, send_far, recv_far):
    place = Place(shard_size)
    z, y, x, deep = place.z, place.y, place.x, place.deep
    meet(place)

    def line_copy(j, d):
        a, b, _ = chunks[j]
        return send(
            own_ref.at[:, a:b],
            full_ref.at[z, y, x, :, a:b],
            send_line.at[j, d - 1],
            recv_line.at[j, d - 1],
            place.device(z=place.line(d)),
        )

    def near_copy(j):
        a, b, kind = chunks[j]
        here = full_ref.at[:, y, x, :, a:b]
        device = place.device(y=1 - y) if kind == 0 else place.device(x=1 - x)
        return send(here, here, send_near.at[j], recv_near.at[j], device)

    def far_copy(j):
        a, b, kind = chunks[j]
        here = full_ref.at[:, :, x, :, a:b] if kind == 0 else full_ref.at[:, y, :, :, a:b]
        device = place.device(x=1 - x) if kind == 0 else place.device(y=1 - y)
        return send(here, here, send_far.at[j], recv_far.at[j], device)

    count = len(chunks)
    own = pltpu.make_async_copy(own_ref, full_ref.at[z, y, x], local_sem)
    own.start()
    for j in range(count):
        for d in range(1, deep):
            line_copy(j, d).start()
    own.wait()
    for j in range(count + 1):
        if j < count:
            for d in range(1, deep):
                line_copy(j, d).wait_recv()
            near_copy(j).start()
        if j > 0:
            near_copy(j - 1).wait_recv()
            far_copy(j - 1).start()
    for j in range(count):
        far_copy(j).wait_recv()
    for j in range(count):
        for d in range(1, deep):
            line_copy(j, d).wait_send()
        near_copy(j).wait_send()
        far_copy(j).wait_send()


def gather_weights(shard_size, own, chunks):
    rows, width = own.shape
    deep = shard_size // 2
    count = len(chunks)
    return pl.pallas_call(
        functools.partial(gather_kernel, shard_size, chunks),
        out_shape=jax.ShapeDtypeStruct((deep, 2, 2, rows, width), own.dtype),
        in_specs=[pl.BlockSpec(memory_space=pl.ANY)],
        out_specs=pl.BlockSpec(memory_space=pl.ANY),
        scratch_shapes=[
            pltpu.SemaphoreType.DMA,
            pltpu.SemaphoreType.DMA((count, deep - 1)),
            pltpu.SemaphoreType.DMA((count, deep - 1)),
            pltpu.SemaphoreType.DMA((count,)),
            pltpu.SemaphoreType.DMA((count,)),
            pltpu.SemaphoreType.DMA((count,)),
            pltpu.SemaphoreType.DMA((count,)),
        ],
        compiler_params=pltpu.CompilerParams(collective_id=1, has_side_effects=True),
        name="gather_weights",
    )(own)


def scatter_kernel(shard_size, chunks, tensors, *refs):
    grad_refs, refs = refs[:tensors], refs[tensors:]
    small_ref, refs = refs[0], refs[1:]
    out_refs, refs = refs[:tensors], refs[tensors:]
    small_out, refs = refs[0], refs[1:]
    count = len(chunks)
    first_bufs, refs = refs[:count], refs[count:]
    own_bufs, refs = refs[:count], refs[count:]
    second_bufs, refs = refs[:count], refs[count:]
    line_bufs, refs = refs[:count], refs[count:]
    (
        small_x, small_y, small_z, small_c, hold_x, hold_y, hold_z,
        own_sem, send_first, recv_first, send_second, recv_second, send_line, recv_line,
        small_send, small_recv,
    ) = refs
    place = Place(shard_size)
    z, y, x, deep = place.z, place.y, place.x, place.deep
    meet(place)

    def first_copy(j):
        t, a, b, kind = chunks[j]
        grads = grad_refs[t]
        source = grads.at[:, :, 1 - x, :, a:b] if kind == 0 else grads.at[:, 1 - y, :, :, a:b]
        device = place.device(x=1 - x) if kind == 0 else place.device(y=1 - y)
        return send(source, first_bufs[j], send_first.at[j], recv_first.at[j], device)

    def own_copy(j):
        t, a, b, kind = chunks[j]
        grads = grad_refs[t]
        source = grads.at[:, :, x, :, a:b] if kind == 0 else grads.at[:, y, :, :, a:b]
        return pltpu.make_async_copy(source, own_bufs[j], own_sem.at[j])

    def second_copy(j):
        kind = chunks[j][3]
        mine = y if kind == 0 else x
        device = place.device(y=1 - y) if kind == 0 else place.device(x=1 - x)
        return send(own_bufs[j].at[:, 1 - mine], second_bufs[j], send_second.at[j], recv_second.at[j], device)

    def line_copy(j, d):
        kind = chunks[j][3]
        mine = y if kind == 0 else x
        return send(
            own_bufs[j].at[place.line(d), mine],
            line_bufs[j].at[d - 1],
            send_line.at[j, d - 1],
            recv_line.at[j, d - 1],
            place.device(z=place.line(d)),
        )

    def small_line(d):
        return send(hold_z.at[z], hold_z.at[z], small_send.at[d + 2], small_recv.at[d + 2], place.device(z=place.line(d)))

    for j in range(count):
        first_copy(j).start()
        own_copy(j).start()

    step = send(small_ref, small_x, small_send.at[0], small_recv.at[0], place.device(x=1 - x))
    step.start()
    step.wait()
    hold_x[...] = small_ref[...] + small_x[...]
    step = send(hold_x, small_y, small_send.at[1], small_recv.at[1], place.device(y=1 - y))
    step.start()
    step.wait()
    hold_z[z] = hold_x[...] + small_y[...]
    for d in range(1, deep):
        small_line(d).start()
    for d in range(1, deep):
        small_line(d).wait()
    hold_y[...] = jnp.sum(hold_z[...], axis=0)
    step = send(hold_y, small_c, small_send.at[2], small_recv.at[2], place.device(c=1 - place.c))
    step.start()
    step.wait()
    small_out[0] = hold_y[...]
    small_out[1] = hold_y[...] + small_c[...]

    def add_first(j):
        first_copy(j).wait_recv()
        own_copy(j).wait()

        def body(i, carry):
            for k in range(2):
                own_bufs[j][i, k] = (
                    own_bufs[j][i, k].astype(jnp.float32) + first_bufs[j][i, k].astype(jnp.float32)
                ).astype(jnp.bfloat16)
            return carry

        lax.fori_loop(0, deep, body, 0)
        second_copy(j).start()

    def add_second(j):
        second_copy(j).wait_recv()
        kind = chunks[j][3]
        mine = y if kind == 0 else x

        def body(i, carry):
            own_bufs[j][i, mine] = (
                own_bufs[j][i, mine].astype(jnp.float32) + second_bufs[j][i].astype(jnp.float32)
            ).astype(jnp.bfloat16)
            return carry

        lax.fori_loop(0, deep, body, 0)
        for d in range(1, deep):
            line_copy(j, d).start()

    def add_line(j):
        t, a, b, kind = chunks[j]
        mine = y if kind == 0 else x
        total = own_bufs[j][z, mine].astype(jnp.float32)
        for d in range(1, deep):
            line_copy(j, d).wait_recv()
            total = total + line_bufs[j][d - 1].astype(jnp.float32)
        out_refs[t][:, a:b] = total

    for j in range(count + 2):
        if j < count:
            add_first(j)
        if 0 < j <= count:
            add_second(j - 1)
        if j > 1:
            add_line(j - 2)
    for j in range(count):
        first_copy(j).wait_send()
        second_copy(j).wait_send()
        for d in range(1, deep):
            line_copy(j, d).wait_send()


def scatter_gradients(shard_size, grads, small, chunks):
    deep = shard_size // 2
    rows = grads[0].shape[3]
    tensors, count = len(grads), len(chunks)
    widths = [b - a for _, a, b, _ in chunks]
    low = jnp.bfloat16
    dma = pltpu.SemaphoreType.DMA
    small_buffer = pltpu.VMEM(small.shape, jnp.float32)
    vmem = pl.BlockSpec(memory_space=pltpu.VMEM)
    return pl.pallas_call(
        functools.partial(scatter_kernel, shard_size, chunks, tensors),
        out_shape=[jax.ShapeDtypeStruct((rows, g.shape[4]), jnp.float32) for g in grads]
        + [jax.ShapeDtypeStruct((2,) + small.shape, jnp.float32)],
        in_specs=[pl.BlockSpec(memory_space=pl.ANY)] * tensors + [vmem],
        out_specs=[vmem] * (tensors + 1),
        scratch_shapes=[pltpu.VMEM((deep, 2, rows, w), low) for w in widths]
        + [pltpu.VMEM((deep, 2, rows, w), low) for w in widths]
        + [pltpu.VMEM((deep, rows, w), low) for w in widths]
        + [pltpu.VMEM((deep - 1, rows, w), low) for w in widths]
        + [small_buffer, small_buffer, pltpu.VMEM((deep,) + small.shape, jnp.float32), small_buffer]
        + [small_buffer, small_buffer, pltpu.VMEM((deep,) + small.shape, jnp.float32)]
        + [dma((count,))] * 5
        + [dma((count, deep - 1))] * 2
        + [dma((deep + 2,))] * 2,
        compiler_params=pltpu.CompilerParams(
            collective_id=2, has_side_effects=True, vmem_limit_bytes=48 * MIB
        ),
        name="scatter_gradients",
    )(*grads, small)


def gelu_parts(gate):
    tangent = jnp.tanh(GELU_ROOT * (gate + GELU_CUBIC * gate * gate * gate))
    value = 0.5 * gate * (1.0 + tangent)
    slope = 0.5 * (1.0 + tangent) + 0.5 * gate * (1.0 - tangent * tangent) * GELU_ROOT * (
        1.0 + 3.0 * GELU_CUBIC * gate * gate
    )
    return value, slope


def normalize(tokens_in):
    inverse = lax.rsqrt(jnp.mean(tokens_in * tokens_in, axis=-1, keepdims=True) + EPSILON)
    return tokens_in * inverse, inverse


def normalize_back(grad, normal, inverse, gain):
    scaled = grad * gain
    back = inverse * (scaled - normal * jnp.mean(scaled * normal, axis=-1, keepdims=True))
    axes = tuple(range(grad.ndim - 1))
    return back, jnp.sum(grad * normal, axis=axes)


def dot(a, b, left, right, kind=jnp.float32):
    return lax.dot_general(a, b, (((left,), (right,)), ((), ())), preferred_element_type=jnp.float32).astype(kind)


def swap(values, axis):
    return lax.ppermute(values, axis, [(0, 1), (1, 0)])


def ordered(mine, other, place, axis):
    first = place == 0
    return jnp.stack([jnp.where(first, mine, other), jnp.where(first, other, mine)], axis=axis)


def take(values, index, axis):
    return lax.dynamic_index_in_dim(values, index, axis, keepdims=False)


def shards(
    inputs, cotangent, lengths, buckets,
    query_weight, key_weight, value_weight, projection_weight, gate_weight, up_weight, down_weight,
    attention_gain, feedforward_gain, bias_table,
):
    low = jnp.bfloat16
    x, c = lax.axis_index("ctx"), lax.axis_index("tp")
    shard_size = lax.axis_size("shard")
    half, width = inputs.shape[1:]
    quarter = half // 2
    length = 2 * half
    blocks = length // BLOCK
    bucket_count, heads = bias_table.shape
    inner = query_weight.shape[1]
    hidden_width = gate_weight.shape[1]

    gains = jnp.pad(jnp.stack([attention_gain, feedforward_gain], axis=1), ((0, 0), (0, 126)))
    own = jnp.concatenate(
        [query_weight, key_weight, value_weight, gains, projection_weight, gate_weight, up_weight, down_weight], axis=1
    )
    at_gain = 3 * inner
    at_project = at_gain + 128
    at_gate = at_project + inner
    at_up = at_gate + hidden_width
    at_down = at_up + hidden_width
    at_end = at_down + hidden_width
    pieces = split_columns(0, at_project, 2) + split_columns(at_project, at_gate, 1) + split_columns(at_gate, at_end, 6)
    chunks = [(a, b, i % 2) for i, (a, b) in enumerate(pieces)]
    full = gather_weights(shard_size, own, chunks).reshape(width, at_end)
    qkv_full = full[:, :at_gain]
    project_full = full[:, at_project:at_gate]
    gate_full = full[:, at_gate:at_up]
    up_full = full[:, at_up:at_down]
    down_full = full[:, at_down:at_end]
    gain_one = full[:, at_gain].astype(jnp.float32)
    gain_two = full[:, at_gain + 1].astype(jnp.float32)

    sequence_length = take(lengths[:, 0], x, 0)
    both = jnp.stack([inputs, cotangent])
    away = take(both, 1 - x, 1)
    arrived = swap(lax.dynamic_slice_in_dim(away, c * quarter, quarter, 1), "ctx")
    arrived = ordered(arrived, swap(arrived, "tp"), c, 1).reshape(2, half, width)
    whole = ordered(take(both, x, 1), arrived, x, 1)
    tokens, cots = whole[0].reshape(length, width), whole[1].reshape(length, width)

    starts = [min(max(i - 1, 0), blocks - BAND) * BLOCK for i in range(blocks)]
    start_of = jnp.asarray(starts, jnp.int32)
    own_band = jnp.stack(
        [
            lax.dynamic_slice(buckets, (i * BLOCK, start_of[x * (blocks // 2) + i]), (BLOCK, BAND * BLOCK))
            for i in range(blocks // 2)
        ]
    ).astype(low)
    band = ordered(own_band, swap(own_band, "ctx"), x, 0).reshape(blocks, BLOCK, BAND * BLOCK).astype(jnp.int32)
    bandt = jnp.swapaxes(band, 1, 2)
    table = bias_table.astype(jnp.float32)
    table_rows = jnp.broadcast_to(
        jnp.pad(table.T, ((0, 0), (0, 128 - bucket_count)))[:, None, :], (heads, 8, 128)
    )
    bias, biast = bias_bands(band, bandt, table_rows)
    block_at = jnp.arange(blocks) * BLOCK
    below = (block_at[None, :] < start_of[:, None])[None]
    above = (block_at[None, :] >= start_of[:, None] + BAND * BLOCK)[None]
    far_low, far_high = bucket_count // 2 - 1, bucket_count - 1
    constant = jnp.where(below, table[far_low][:, None, None], 0.0) + jnp.where(above, table[far_high][:, None, None], 0.0)
    qaux = jnp.concatenate(
        [constant, jnp.ones((heads, blocks, 1)), jnp.zeros((heads, blocks, 127 - blocks))], axis=-1
    )
    slots = jnp.arange(length, dtype=jnp.int32)
    kaux = jnp.concatenate(
        [
            (slots[:, None] // BLOCK == jnp.arange(blocks)[None, :]).astype(jnp.float32),
            jnp.where(slots < sequence_length, 0.0, -1e30)[:, None],
            jnp.zeros((length, 127 - blocks)),
        ],
        axis=1,
    ).astype(low)

    present = tokens.astype(jnp.float32)
    normal_one, inverse_one = normalize(present)
    normed_one = (normal_one * gain_one).astype(low)
    qkv = dot(normed_one, qkv_full, 1, 0, low)
    attended, lse = attention_forward(qkv, kaux, qaux, bias)
    grid = (2, 2, quarter, width)

    def reduce_rows(partial):
        parts = partial.reshape(grid)
        return take(parts, c, 1) + swap(take(parts, 1 - c, 1).astype(low), "tp").astype(jnp.float32)

    def share_rows(mine):
        return ordered(mine, swap(mine, "tp"), c, 1).reshape(length, width)

    def own_rows(values):
        return take(values.reshape(grid), c, 1)

    middle = own_rows(present) + reduce_rows(dot(attended, project_full, 1, 1))
    normal_two, inverse_two = normalize(middle)
    normed_two = share_rows((normal_two * gain_two).astype(low))
    gate = dot(normed_two, gate_full, 1, 0)
    up = dot(normed_two, up_full, 1, 0)
    value, slope = gelu_parts(gate)
    hidden = (value * up).astype(low)
    output = (middle + reduce_rows(dot(hidden, down_full, 1, 1))).astype(low)

    live = (slots < sequence_length).astype(jnp.float32)[:, None]
    grad_out = cots.astype(jnp.float32) * live
    grad_low = grad_out.astype(low)
    grad_down = dot(grad_low, hidden, 0, 0, low)
    grad_hidden = dot(grad_low, down_full, 1, 0)
    grad_gate = (grad_hidden * up * slope).astype(low)
    grad_up = (grad_hidden * value).astype(low)
    grad_gate_weight = dot(normed_two, grad_gate, 0, 0, low)
    grad_up_weight = dot(normed_two, grad_up, 0, 0, low)
    grad_two = reduce_rows(dot(grad_gate, gate_full, 1, 1) + dot(grad_up, up_full, 1, 1))
    back_two, gain_two_part = normalize_back(grad_two, normal_two, inverse_two, gain_two)
    grad_middle = own_rows(grad_out) + back_two
    grad_branch = share_rows(grad_middle.astype(low))
    grad_project = dot(grad_branch, attended, 0, 0, low)
    grad_attended = dot(grad_branch, project_full, 1, 0, low)
    grad_q, grad_k, grad_v, band_grads, sums = attention_backward(qkv, kaux, qaux, biast, lse, grad_attended)
    table_grad = table_band(bandt, band_grads, bucket_count)
    sums = sums.reshape(heads, blocks, blocks, BLOCK).sum(-1)
    table_grad = table_grad.at[far_low].add(jnp.sum(jnp.where(jnp.swapaxes(below, 1, 2), sums, 0.0), axis=(1, 2)))
    table_grad = table_grad.at[far_high].add(jnp.sum(jnp.where(jnp.swapaxes(above, 1, 2), sums, 0.0), axis=(1, 2)))
    grad_query = dot(normed_one, grad_q, 0, 0, low)
    grad_key = dot(normed_one, grad_k, 0, 0, low)
    grad_value = dot(normed_one, grad_v, 0, 0, low)
    grad_one = reduce_rows(
        dot(grad_q, qkv_full[:, :inner], 1, 1)
        + dot(grad_k, qkv_full[:, inner : 2 * inner], 1, 1)
        + dot(grad_v, qkv_full[:, 2 * inner :], 1, 1)
    )
    back_one, gain_one_part = normalize_back(grad_one, own_rows(normal_one), take(inverse_one.reshape(2, 2, quarter, 1), c, 1), gain_one)
    input_grad = (grad_middle + back_one).astype(low)

    def to_owners(mine):
        kept, leaving = take(mine, x, 0), take(mine, 1 - x, 0)
        pair = ordered(kept, swap(leaving, "ctx"), x, 0)
        return ordered(pair, swap(pair, "tp"), c, 1).reshape(2, half, width)

    output = to_owners(output)
    input_grad = to_owners(input_grad).astype(jnp.float32)

    rows = query_weight.shape[0]
    small = jnp.concatenate(
        [gain_one_part.reshape(-1, 128), gain_two_part.reshape(-1, 128), table_grad.reshape(-1, 128)], axis=0
    )
    used = small.shape[0]
    small = jnp.pad(small, ((0, -used % 8), (0, 0)))
    grads = [
        g.reshape(shard_size // 2, 2, 2, rows, g.shape[1])
        for g in (grad_down, grad_gate_weight, grad_up_weight, grad_project, grad_query, grad_key, grad_value)
    ]
    cuts = []
    for t, g in enumerate(grads):
        cuts += [(t, a, b) for a, b in split_columns(0, g.shape[4], 2 if t < 3 else 1)]
    cuts = [(t, a, b, i % 2) for i, (t, a, b) in enumerate(cuts)]
    *sums_out, small_out = scatter_gradients(shard_size, grads, small, cuts)
    down, gate_w, up_w, project, query, key, value_w = sums_out
    lines = width // 128
    me = lax.axis_index("shard") * 2 + x

    def own_gain(part):
        return lax.dynamic_slice_in_dim(small_out[1, part * lines : (part + 1) * lines].reshape(-1), me * rows, rows)

    table_total = small_out[0, 2 * lines : used].reshape(bucket_count, heads)
    return (
        output, input_grad, query, key, value_w, project, gate_w, up_w, down,
        own_gain(0), own_gain(1), table_total,
    )


def solution(mesh):
    rows = P(None, ("shard", "ctx"), None)
    weight = P(("shard", "ctx"), "tp")
    gain = P(("shard", "ctx"))
    table = P(None, "tp")
    return jax.shard_map(
        shards,
        mesh=mesh,
        in_specs=(rows, rows, P(None, "shard"), P("ctx", None)) + (weight,) * 7 + (gain, gain, table),
        out_specs=(rows, rows) + (weight,) * 7 + (gain, gain, table),
        check_vma=False,
    )
```

```python
import functools

import jax
import jax.numpy as jnp
from jax import lax
from jax.experimental import pallas as pl
from jax.experimental.pallas import tpu as pltpu
from jax.sharding import PartitionSpec as P

EPSILON = 1e-06
GELU_ROOT = 0.7978845608028654
GELU_CUBIC = 0.044715
MESH = pl.DeviceIdType.MESH
MIB = 1024 * 1024


BAND = 3
BLOCK = 128


def lane_head(rows, width, which):
    lanes = lax.broadcasted_iota(jnp.int32, (rows, width), 1)
    half = width // 2
    return (lanes < half) if which == 0 else (lanes >= half)


def band_start(row_block, blocks):
    return jnp.clip(row_block - 1, 0, blocks - BAND)


def bias_kernel(bandt_ref, table_ref, out_ref):
    def step(i, carry):
        at = pl.multiple_of(i * 16, 16)
        index = bandt_ref[0, pl.ds(at, 16), :]
        for head in range(table_ref.shape[0]):
            got = [jnp.take_along_axis(table_ref[head], index[8 * k : 8 * k + 8], axis=1) for k in range(2)]
            out_ref[head, 0, pl.ds(at, 16), :] = jnp.concatenate(got, axis=0).astype(jnp.bfloat16)
        return carry

    lax.fori_loop(0, BAND * BLOCK // 16, step, 0)


def bias_bands(bandt, table_rows):
    blocks = bandt.shape[0]
    heads = table_rows.shape[0]
    return pl.pallas_call(
        bias_kernel,
        grid=(blocks,),
        in_specs=[
            pl.BlockSpec((1, BAND * BLOCK, BLOCK), lambda i: (i, 0, 0)),
            pl.BlockSpec((heads, 8, 128), lambda i: (0, 0, 0)),
        ],
        out_specs=pl.BlockSpec((heads, 1, BAND * BLOCK, BLOCK), lambda i: (0, i, 0, 0)),
        out_shape=jax.ShapeDtypeStruct((heads, blocks, BAND * BLOCK, BLOCK), jnp.bfloat16),
        name="bias_bands",
    )(bandt, table_rows)


def backward_kernel(
    q_ref, k_ref, v_ref, kaux_ref, qaux_ref, bias_ref, lse_ref, do_ref,
    dq_ref, dk_ref, dv_ref, gs_ref, sums_ref, s_ref, g_ref, dk_acc, dv_acc, *, blocks
):
    step = pl.program_id(1)
    steps = pl.num_programs(1)
    rows = q_ref.shape[0]
    subs = rows // BLOCK

    @pl.when(step == 0)
    def _():
        dk_acc[...] = jnp.zeros_like(dk_acc)
        dv_acc[...] = jnp.zeros_like(dv_acc)

    pair = q_ref[...]
    grad = do_ref[...]
    key_pair = k_ref[...]
    keys = jnp.concatenate([key_pair, kaux_ref[...]], axis=1)
    last = (((1,), (1,)), ((), ()))
    dq = None
    for head in range(2):
        here = lane_head(rows, 128, head)
        aux = jnp.concatenate(
            [jnp.broadcast_to(qaux_ref[head, sub : sub + 1, :], (BLOCK, 128)) for sub in range(subs)], axis=0
        ).astype(jnp.bfloat16)
        q_masked = jnp.where(here, pair, jnp.zeros_like(pair))
        do_masked = jnp.where(here, grad, jnp.zeros_like(grad))
        s_ref[...] = lax.dot_general(
            keys, jnp.concatenate([q_masked, aux], axis=1), last, preferred_element_type=jnp.float32
        )
        for sub in range(subs):
            start = pl.multiple_of(band_start(step * subs + sub, blocks) * BLOCK, BLOCK)
            s_ref[pl.ds(start, BAND * BLOCK), sub * BLOCK : (sub + 1) * BLOCK] += bias_ref[head, sub].astype(jnp.float32)
        soft = jnp.exp(s_ref[...] - lse_ref[0, 0, head : head + 1, :])
        dv_acc[...] += jnp.dot(soft.astype(jnp.bfloat16), do_masked, preferred_element_type=jnp.float32)
        grad_probs = lax.dot_general(v_ref[...], do_masked, last, preferred_element_type=jnp.float32)
        weighted = jnp.sum(soft * grad_probs, axis=0, keepdims=True)
        grad_scores = (soft * (grad_probs - weighted)).astype(jnp.bfloat16)
        g_ref[...] = grad_scores
        dk_acc[...] += jnp.dot(grad_scores, q_masked, preferred_element_type=jnp.float32)
        k_masked = jnp.where(lane_head(key_pair.shape[0], 128, head), key_pair, jnp.zeros_like(key_pair))
        part = lax.dot_general(
            grad_scores, k_masked, (((0,), (0,)), ((), ())), preferred_element_type=jnp.float32
        )
        dq = part if dq is None else dq + part
        for sub in range(subs):
            start = pl.multiple_of(band_start(step * subs + sub, blocks) * BLOCK, BLOCK)
            gs_ref[head, sub] = g_ref[pl.ds(start, BAND * BLOCK), sub * BLOCK : (sub + 1) * BLOCK]
        for block in range(blocks):
            sums_ref[head, block : block + 1, :] = jnp.sum(
                grad_scores[block * BLOCK : (block + 1) * BLOCK, :].astype(jnp.float32), axis=0, keepdims=True
            )
    dq_ref[...] = dq.astype(jnp.bfloat16)

    @pl.when(step == steps - 1)
    def _():
        dk_ref[...] = dk_acc[...].astype(jnp.bfloat16)
        dv_ref[...] = dv_acc[...].astype(jnp.bfloat16)


def attention_backward(qkv, kaux, qaux, biast, lse, grad_attended):
    length = qkv.shape[1]
    heads, blocks = biast.shape[:2]
    pairs = heads // 2
    rows = 256
    subs = rows // BLOCK
    wide = jax.ShapeDtypeStruct((length, pairs * 128), jnp.bfloat16)
    return pl.pallas_call(
        functools.partial(backward_kernel, blocks=blocks),
        grid=(pairs, length // rows),
        in_specs=[
            pl.BlockSpec((None, rows, 128), lambda p, i: (p, i, 0)),
            pl.BlockSpec((None, length, 128), lambda p, i: (pairs + p, 0, 0)),
            pl.BlockSpec((None, length, 128), lambda p, i: (2 * pairs + p, 0, 0)),
            pl.BlockSpec((length, 128), lambda p, i: (0, 0)),
            pl.BlockSpec((2, None, subs, 128), lambda p, i: (p, i, 0, 0)),
            pl.BlockSpec((2, subs, BAND * BLOCK, BLOCK), lambda p, i: (p, i, 0, 0)),
            pl.BlockSpec((1, 1, 2, rows), lambda p, i: (p, i, 0, 0)),
            pl.BlockSpec((rows, 128), lambda p, i: (i, p)),
        ],
        out_specs=[
            pl.BlockSpec((rows, 128), lambda p, i: (i, p)),
            pl.BlockSpec((length, 128), lambda p, i: (0, p)),
            pl.BlockSpec((length, 128), lambda p, i: (0, p)),
            pl.BlockSpec((2, subs, BAND * BLOCK, BLOCK), lambda p, i: (p, i, 0, 0)),
            pl.BlockSpec((2, blocks, rows), lambda p, i: (p, 0, i)),
        ],
        out_shape=[
            wide,
            wide,
            wide,
            jax.ShapeDtypeStruct((heads, blocks, BAND * BLOCK, BLOCK), jnp.bfloat16),
            jax.ShapeDtypeStruct((heads, blocks, length), jnp.float32),
        ],
        scratch_shapes=[
            pltpu.VMEM((length, rows), jnp.float32),
            pltpu.VMEM((length, rows), jnp.bfloat16),
            pltpu.VMEM((length, 128), jnp.float32),
            pltpu.VMEM((length, 128), jnp.float32),
        ],
        compiler_params=pltpu.CompilerParams(vmem_limit_bytes=40 * 1024 * 1024),
        name="attention_backward",
    )(qkv, qkv, qkv, kaux, qaux.reshape(heads, blocks // subs, subs, 128), biast, lse, grad_attended)


GROUP = 16


def table_kernel(bandt_ref, gs_ref, out_ref, acc_ref, *, buckets):
    step = pl.program_id(0)

    @pl.when(step == 0)
    def _():
        acc_ref[...] = jnp.zeros_like(acc_ref)

    heads = gs_ref.shape[0]

    def one(group, carry):
        start = pl.multiple_of(group * GROUP, GROUP)
        grads = jnp.concatenate(
            [gs_ref[:, two, pl.ds(start, GROUP), :].reshape(heads * GROUP, BLOCK) for two in range(2)], axis=1
        )
        index = jnp.concatenate([bandt_ref[two, pl.ds(start, GROUP), :] for two in range(2)], axis=1)
        index = index.astype(jnp.float32)
        hot = jnp.concatenate(
            [jnp.where(index == float(b), 1.0, 0.0) for b in range(buckets)], axis=0
        ).astype(jnp.bfloat16)
        acc_ref[...] += lax.dot_general(
            hot, grads, (((1,), (1,)), ((), ())), preferred_element_type=jnp.float32
        )
        return carry

    lax.fori_loop(0, BAND * BLOCK // GROUP, one, 0)

    @pl.when(step == pl.num_programs(0) - 1)
    def _():
        row = lax.broadcasted_iota(jnp.int32, acc_ref.shape, 0) % GROUP
        col = lax.broadcasted_iota(jnp.int32, acc_ref.shape, 1) % GROUP
        out_ref[...] = jnp.where(row == col, acc_ref[...], 0.0)


def table_band(bandt, gs, buckets):
    heads, blocks = gs.shape[:2]
    out = pl.pallas_call(
        functools.partial(table_kernel, buckets=buckets),
        grid=(blocks // 2,),
        in_specs=[
            pl.BlockSpec((2, BAND * BLOCK, BLOCK), lambda i: (i, 0, 0)),
            pl.BlockSpec((heads, 2, BAND * BLOCK, BLOCK), lambda i: (0, i, 0, 0)),
        ],
        out_specs=pl.BlockSpec((buckets * GROUP, heads * GROUP), lambda i: (0, 0)),
        out_shape=jax.ShapeDtypeStruct((buckets * GROUP, heads * GROUP), jnp.float32),
        scratch_shapes=[pltpu.VMEM((buckets * GROUP, heads * GROUP), jnp.float32)],
        compiler_params=pltpu.CompilerParams(vmem_limit_bytes=40 * 1024 * 1024),
        name="table_band",
    )(bandt, gs)
    return out.reshape(buckets, GROUP, heads, GROUP).sum((1, 3))
def split_columns(start, stop, pieces):
    tiles = (stop - start) // 128
    edges = [start + 128 * (tiles * i // pieces) for i in range(pieces + 1)]
    return [(a, b) for a, b in zip(edges, edges[1:]) if b > a]


class Place:
    def __init__(self, shard_size):
        self.deep = shard_size // 2
        shard = lax.axis_index("shard")
        self.z = shard // 2
        self.y = shard % 2
        self.x = lax.axis_index("ctx")
        self.c = lax.axis_index("tp")

    def device(self, z=None, y=None, x=None, c=None):
        z = self.z if z is None else z
        y = self.y if y is None else y
        x = self.x if x is None else x
        c = self.c if c is None else c
        return (z * 2 + y, x, c)

    def line(self, distance):
        return (self.z + distance) % self.deep

    def peers(self):
        others = [self.device(z=self.line(d)) for d in range(1, self.deep)]
        return others + [self.device(y=1 - self.y), self.device(x=1 - self.x), self.device(c=1 - self.c)]


def meet(place):
    barrier = pltpu.get_barrier_semaphore()
    peers = place.peers()
    for peer in peers:
        pl.semaphore_signal(barrier, inc=1, device_id=peer, device_id_type=MESH)
    pl.semaphore_wait(barrier, len(peers))


def send(source, target, send_sem, recv_sem, device):
    return pltpu.make_async_remote_copy(
        src_ref=source, dst_ref=target, send_sem=send_sem, recv_sem=recv_sem, device_id=device, device_id_type=MESH
    )


def gather_kernel(shard_size, chunks, own_ref, full_ref, local_sem, send_line, recv_line, send_near, recv_near, send_far, recv_far):
    place = Place(shard_size)
    z, y, x, deep = place.z, place.y, place.x, place.deep
    meet(place)

    def line_copy(j, d):
        a, b, _ = chunks[j]
        return send(
            own_ref.at[:, a:b],
            full_ref.at[z, y, x, :, a:b],
            send_line.at[j, d - 1],
            recv_line.at[j, d - 1],
            place.device(z=place.line(d)),
        )

    def near_copy(j):
        a, b, kind = chunks[j]
        here = full_ref.at[:, y, x, :, a:b]
        device = place.device(y=1 - y) if kind == 0 else place.device(x=1 - x)
        return send(here, here, send_near.at[j], recv_near.at[j], device)

    def far_copy(j):
        a, b, kind = chunks[j]
        here = full_ref.at[:, :, x, :, a:b] if kind == 0 else full_ref.at[:, y, :, :, a:b]
        device = place.device(x=1 - x) if kind == 0 else place.device(y=1 - y)
        return send(here, here, send_far.at[j], recv_far.at[j], device)

    count = len(chunks)
    own = pltpu.make_async_copy(own_ref, full_ref.at[z, y, x], local_sem)
    own.start()
    for j in range(count):
        for d in range(1, deep):
            line_copy(j, d).start()
    own.wait()
    for j in range(count + 1):
        if j < count:
            for d in range(1, deep):
                line_copy(j, d).wait_recv()
            near_copy(j).start()
        if j > 0:
            near_copy(j - 1).wait_recv()
            far_copy(j - 1).start()
    for j in range(count):
        far_copy(j).wait_recv()
    for j in range(count):
        for d in range(1, deep):
            line_copy(j, d).wait_send()
        near_copy(j).wait_send()
        far_copy(j).wait_send()


def gather_weights(shard_size, own, chunks):
    rows, width = own.shape
    deep = shard_size // 2
    count = len(chunks)
    return pl.pallas_call(
        functools.partial(gather_kernel, shard_size, chunks),
        out_shape=jax.ShapeDtypeStruct((deep, 2, 2, rows, width), own.dtype),
        in_specs=[pl.BlockSpec(memory_space=pl.ANY)],
        out_specs=pl.BlockSpec(memory_space=pl.ANY),
        scratch_shapes=[
            pltpu.SemaphoreType.DMA,
            pltpu.SemaphoreType.DMA((count, deep - 1)),
            pltpu.SemaphoreType.DMA((count, deep - 1)),
            pltpu.SemaphoreType.DMA((count,)),
            pltpu.SemaphoreType.DMA((count,)),
            pltpu.SemaphoreType.DMA((count,)),
            pltpu.SemaphoreType.DMA((count,)),
        ],
        compiler_params=pltpu.CompilerParams(collective_id=1, has_side_effects=True),
        name="gather_weights",
    )(own)


def scatter_kernel(shard_size, chunks, tensors, *refs):
    grad_refs, refs = refs[:tensors], refs[tensors:]
    small_ref, refs = refs[0], refs[1:]
    out_refs, refs = refs[:tensors], refs[tensors:]
    small_out, refs = refs[0], refs[1:]
    count = len(chunks)
    first_bufs, refs = refs[:count], refs[count:]
    own_bufs, refs = refs[:count], refs[count:]
    second_bufs, refs = refs[:count], refs[count:]
    line_bufs, refs = refs[:count], refs[count:]
    (
        small_x, small_y, small_z, small_c, hold_x, hold_y, hold_z,
        own_sem, send_first, recv_first, send_second, recv_second, send_line, recv_line,
        small_send, small_recv,
    ) = refs
    place = Place(shard_size)
    z, y, x, deep = place.z, place.y, place.x, place.deep
    meet(place)

    def first_copy(j):
        t, a, b, kind = chunks[j]
        grads = grad_refs[t]
        source = grads.at[:, :, 1 - x, :, a:b] if kind == 0 else grads.at[:, 1 - y, :, :, a:b]
        device = place.device(x=1 - x) if kind == 0 else place.device(y=1 - y)
        return send(source, first_bufs[j], send_first.at[j], recv_first.at[j], device)

    def own_copy(j):
        t, a, b, kind = chunks[j]
        grads = grad_refs[t]
        source = grads.at[:, :, x, :, a:b] if kind == 0 else grads.at[:, y, :, :, a:b]
        return pltpu.make_async_copy(source, own_bufs[j], own_sem.at[j])

    def second_copy(j):
        kind = chunks[j][3]
        mine = y if kind == 0 else x
        device = place.device(y=1 - y) if kind == 0 else place.device(x=1 - x)
        return send(own_bufs[j].at[:, 1 - mine], second_bufs[j], send_second.at[j], recv_second.at[j], device)

    def line_copy(j, d):
        kind = chunks[j][3]
        mine = y if kind == 0 else x
        return send(
            own_bufs[j].at[place.line(d), mine],
            line_bufs[j].at[d - 1],
            send_line.at[j, d - 1],
            recv_line.at[j, d - 1],
            place.device(z=place.line(d)),
        )

    def small_line(d):
        return send(hold_z.at[z], hold_z.at[z], small_send.at[d + 2], small_recv.at[d + 2], place.device(z=place.line(d)))

    for j in range(count):
        first_copy(j).start()
        own_copy(j).start()

    step = send(small_ref, small_x, small_send.at[0], small_recv.at[0], place.device(x=1 - x))
    step.start()
    step.wait()
    hold_x[...] = small_ref[...] + small_x[...]
    step = send(hold_x, small_y, small_send.at[1], small_recv.at[1], place.device(y=1 - y))
    step.start()
    step.wait()
    hold_z[z] = hold_x[...] + small_y[...]
    for d in range(1, deep):
        small_line(d).start()
    for d in range(1, deep):
        small_line(d).wait()
    hold_y[...] = jnp.sum(hold_z[...], axis=0)
    step = send(hold_y, small_c, small_send.at[2], small_recv.at[2], place.device(c=1 - place.c))
    step.start()
    step.wait()
    small_out[0] = hold_y[...]
    small_out[1] = hold_y[...] + small_c[...]

    def add_first(j):
        first_copy(j).wait_recv()
        own_copy(j).wait()

        def body(i, carry):
            for k in range(2):
                own_bufs[j][i, k] = (
                    own_bufs[j][i, k].astype(jnp.float32) + first_bufs[j][i, k].astype(jnp.float32)
                ).astype(jnp.bfloat16)
            return carry

        lax.fori_loop(0, deep, body, 0)
        second_copy(j).start()

    def add_second(j):
        second_copy(j).wait_recv()
        kind = chunks[j][3]
        mine = y if kind == 0 else x

        def body(i, carry):
            own_bufs[j][i, mine] = (
                own_bufs[j][i, mine].astype(jnp.float32) + second_bufs[j][i].astype(jnp.float32)
            ).astype(jnp.bfloat16)
            return carry

        lax.fori_loop(0, deep, body, 0)
        for d in range(1, deep):
            line_copy(j, d).start()

    def add_line(j):
        t, a, b, kind = chunks[j]
        mine = y if kind == 0 else x
        total = own_bufs[j][z, mine].astype(jnp.float32)
        for d in range(1, deep):
            line_copy(j, d).wait_recv()
            total = total + line_bufs[j][d - 1].astype(jnp.float32)
        out_refs[t][:, a:b] = total

    for j in range(count + 2):
        if j < count:
            add_first(j)
        if 0 < j <= count:
            add_second(j - 1)
        if j > 1:
            add_line(j - 2)
    for j in range(count):
        first_copy(j).wait_send()
        second_copy(j).wait_send()
        for d in range(1, deep):
            line_copy(j, d).wait_send()


def scatter_gradients(shard_size, grads, small, chunks):
    deep = shard_size // 2
    rows = grads[0].shape[3]
    tensors, count = len(grads), len(chunks)
    widths = [b - a for _, a, b, _ in chunks]
    low = jnp.bfloat16
    dma = pltpu.SemaphoreType.DMA
    small_buffer = pltpu.VMEM(small.shape, jnp.float32)
    vmem = pl.BlockSpec(memory_space=pltpu.VMEM)
    return pl.pallas_call(
        functools.partial(scatter_kernel, shard_size, chunks, tensors),
        out_shape=[jax.ShapeDtypeStruct((rows, g.shape[4]), jnp.float32) for g in grads]
        + [jax.ShapeDtypeStruct((2,) + small.shape, jnp.float32)],
        in_specs=[pl.BlockSpec(memory_space=pl.ANY)] * tensors + [vmem],
        out_specs=[vmem] * (tensors + 1),
        scratch_shapes=[pltpu.VMEM((deep, 2, rows, w), low) for w in widths]
        + [pltpu.VMEM((deep, 2, rows, w), low) for w in widths]
        + [pltpu.VMEM((deep, rows, w), low) for w in widths]
        + [pltpu.VMEM((deep - 1, rows, w), low) for w in widths]
        + [small_buffer, small_buffer, pltpu.VMEM((deep,) + small.shape, jnp.float32), small_buffer]
        + [small_buffer, small_buffer, pltpu.VMEM((deep,) + small.shape, jnp.float32)]
        + [dma((count,))] * 5
        + [dma((count, deep - 1))] * 2
        + [dma((deep + 2,))] * 2,
        compiler_params=pltpu.CompilerParams(
            collective_id=2, has_side_effects=True, vmem_limit_bytes=48 * MIB
        ),
        name="scatter_gradients",
    )(*grads, small)


LAST = (((1,), (1,)), ((), ()))
FIRST = (((0,), (0,)), ((), ()))
HIDDEN_STEP = 256


def hidden_steps(hidden):
    return [min(HIDDEN_STEP, hidden - at) for at in range(0, hidden, HIDDEN_STEP)]


class Gather:
    def __init__(self, place, pieces, own_ref, full_ref, send_sem, recv_sem):
        self.place, self.pieces, self.own, self.full = place, pieces, own_ref, full_ref
        self.send_sem, self.recv_sem = send_sem, recv_sem
        self.queue = []

    def held(self, piece, hop):
        a, b, order = self.pieces[piece]
        place, done = self.place, order[:hop]
        at = [slice(None) if name in done else getattr(place, name) for name in "zyx"]
        return self.full.at[at[0], at[1], at[2], :, a:b]

    def copies(self, piece, hop):
        place = self.place
        a, b, order = self.pieces[piece]
        target = self.held(piece, hop)
        source = self.own.at[:, a:b] if hop == 0 else target
        name = order[hop]
        if name == "z":
            peers = [place.device(z=place.line(d)) for d in range(1, place.deep)]
        elif name == "y":
            peers = [place.device(y=1 - place.y)]
        else:
            peers = [place.device(x=1 - place.x)]
        return [
            send(source, target, self.send_sem.at[piece, hop, i], self.recv_sem.at[piece, hop, i], peer)
            for i, peer in enumerate(peers)
        ]

    def start(self, piece, hop):
        for copy in self.copies(piece, hop):
            copy.start()

    def arrive(self, piece, hop):
        for copy in self.copies(piece, hop):
            copy.wait_recv()

    def sent(self):
        for piece in range(len(self.pieces)):
            for hop in range(3):
                for copy in self.copies(piece, hop):
                    copy.wait_send()

    def plan(self, window):
        count = len(self.pieces)
        self.window = window

        def second(piece):
            def act():
                self.arrive(piece, 0)
                self.start(piece, 1)
                if piece + window < count:
                    self.start(piece + window, 0)
            return act

        def third(piece):
            def act():
                self.arrive(piece, 1)
                self.start(piece, 2)
            return act

        for piece in range(count + 1):
            if piece < count:
                self.queue.append((None, second(piece)))
            if piece > 0:
                self.queue.append((piece - 1, third(piece - 1)))
        for piece in range(min(window, count)):
            self.start(piece, 0)

    def run(self, steps):
        for _ in range(min(steps, len(self.queue))):
            self.queue.pop(0)[1]()

    def take(self, steps):
        taken, self.queue = self.queue[:steps], self.queue[steps:]
        return [act for _, act in taken]

    def need(self, pieces):
        for piece in pieces:
            while any(mark == piece for mark, _ in self.queue):
                self.run(1)
        for piece in pieces:
            self.arrive(piece, 2)


def gelu_all(gate):
    square = gate * gate
    tangent = jnp.tanh(GELU_ROOT * (gate + GELU_CUBIC * square * gate))
    value = 0.5 * gate * (1.0 + tangent)
    slope = 0.5 * (1.0 + tangent) + 0.5 * gate * (1.0 - tangent * tangent) * (
        GELU_ROOT + (3.0 * GELU_CUBIC * GELU_ROOT) * square
    )
    return value, slope


def front_kernel(
    shard_size, pieces, window, sizes,
    own_ref, inputs_ref, cots_ref, band_in_ref, table_ref, qaux_ref, kaux_ref, live_ref,
    full_ref, normed_out, qkv_out, attended_out, band_out, grads_out, branch_out, tokens_own_ref,
    lse_ref, output_ref, middle_grad_ref, gain_ref,
    tok, cot, band, bias, wide, qkv, normed, scores, attended, project_w,
    normal, away, arrived, two_t, low_t, acc_out, acc_two, w_buf, g_buf, hid, ggate, gup,
    send_sem, recv_sem, near_send, near_recv, local_sem, w_sem, g_sem,
):
    inner, hidden = sizes
    length, width = tok.shape
    half, quarter = length // 2, length // 4
    heads, blocks = bias.shape[:2]
    pairs = heads // 2
    deep = shard_size // 2
    low = jnp.bfloat16
    place = Place(shard_size)
    x, c = place.x, place.c
    at_q = 128
    at_project = at_q + 3 * inner
    at_hidden = at_project + inner
    steps = hidden_steps(hidden)
    per_step = 2
    first_hidden_piece = len(pieces) - per_step * len(steps)
    project_pieces = [i for i, (a, b, _) in enumerate(pieces) if at_project <= a < at_hidden]
    qkv_pieces = [i for i, (a, b, _) in enumerate(pieces) if a < at_project]

    def own_load(i, source, target):
        return pltpu.make_async_copy(source, target, local_sem.at[i])

    own_tok = own_load(0, inputs_ref.at[x], tok.at[pl.ds(x * half, half)])
    own_cot = own_load(1, cots_ref.at[x], cot.at[pl.ds(x * half, half)])
    own_band = own_load(2, band_in_ref, band.at[pl.ds(x * (blocks // 2), blocks // 2)])
    own_full = own_load(3, own_ref, full_ref.at[place.z, place.y, x])
    for copy in (own_tok, own_cot, own_band, own_full):
        copy.start()
    meet(place)

    gather = Gather(place, pieces, own_ref, full_ref, send_sem, recv_sem)
    to_x, to_c = place.device(x=1 - x), place.device(c=1 - c)

    def x_rows(sender_x, sender_c):
        return pl.ds(sender_x * half + sender_c * quarter, quarter)

    def band_rows(sender_x, sender_c):
        return pl.ds(sender_x * (blocks // 2) + sender_c * (blocks // 4), blocks // 4)

    def near(i, source, target, device):
        return send(source, target, near_send.at[i], near_recv.at[i], device)

    band_x = near(0, band_in_ref.at[pl.ds(c * (blocks // 4), blocks // 4)], band.at[band_rows(x, c)], to_x)
    tok_x = near(1, inputs_ref.at[1 - x, pl.ds(c * quarter, quarter)], tok.at[x_rows(x, c)], to_x)
    cot_x = near(2, cots_ref.at[1 - x, pl.ds(c * quarter, quarter)], cot.at[x_rows(x, c)], to_x)
    band_c = near(3, band.at[band_rows(1 - x, c)], band.at[band_rows(1 - x, c)], to_c)
    tok_c = near(4, tok.at[x_rows(1 - x, c)], tok.at[x_rows(1 - x, c)], to_c)
    cot_c = near(5, cot.at[x_rows(1 - x, c)], cot.at[x_rows(1 - x, c)], to_c)
    band_x.start()
    tok_x.start()
    gather.plan(window)
    cot_x.start()
    own_full.wait()
    band_x.wait()
    band_c.start()
    tok_x.wait()
    tok_c.start()
    own_band.wait()
    band_c.wait()
    gather.run(2)

    def bias_step(i, carry):
        block = i // (BLOCK // 16)
        at = pl.multiple_of((i % (BLOCK // 16)) * 16, 16)
        index = band[block, pl.ds(at, 16), :].astype(jnp.float32).astype(jnp.int32)
        for col in range(BAND):
            lanes = slice(col * BLOCK, (col + 1) * BLOCK)
            for head in range(heads):
                table = table_ref[head]
                got = [jnp.take_along_axis(table, index[8 * k : 8 * k + 8, lanes], axis=1) for k in range(2)]
                bias[head, block, pl.ds(at, 16), lanes] = jnp.concatenate(got, axis=0).astype(low)
        return carry

    lax.fori_loop(0, blocks * (BLOCK // 16) // 2, bias_step, 0)
    gather.run(4)
    lax.fori_loop(blocks * (BLOCK // 16) // 2, blocks * (BLOCK // 16), bias_step, 0)
    gather.run(4)
    band_store = own_load(4, band, band_out)
    band_store.start()
    own_tok.wait()
    tok_c.wait()
    own_cot.wait()
    cot_x.wait()
    cot_c.start()
    cot_c.wait()

    def live_step(i, carry):
        rows = pl.ds(pl.multiple_of(i * BLOCK, BLOCK), BLOCK)
        masked = (cot[rows, :].astype(jnp.float32) * live_ref[rows, 0:1]).astype(low)
        cot[rows, :] = masked
        low_t[:, rows] = jnp.transpose(masked)
        return carry

    lax.fori_loop(0, blocks, live_step, 0)

    gather.need(qkv_pieces)
    load_wide = own_load(5, full_ref.at[:, :, :, :, 0:at_project], wide)
    load_wide.start()
    load_wide.wait()
    gains = jnp.transpose(wide[:, :, :, :, 0:128].reshape(width, 128).astype(jnp.float32))
    gain_one, gain_two = gains[0:1, :], gains[1:2, :]

    def norm_step(i, carry):
        rows = pl.ds(pl.multiple_of(i * BLOCK, BLOCK), BLOCK)
        present = tok[rows, :].astype(jnp.float32)
        inverse = lax.rsqrt(jnp.mean(present * present, axis=-1, keepdims=True) + EPSILON)
        normed[rows, :] = (present * inverse * gain_one).astype(low)
        return carry

    lax.fori_loop(0, blocks, norm_step, 0)
    normed_store = own_load(6, normed, normed_out)
    normed_store.start()
    gather.run(2)

    for col in range(3 * pairs // 2):
        lanes = slice(at_q + 256 * col, at_q + 256 * col + 256)

        def qkv_step(i, carry):
            rows = pl.ds(pl.multiple_of(i * 256, 256), 256)
            got = jnp.dot(
                normed[rows, :], wide[:, :, :, :, lanes].reshape(width, 256), preferred_element_type=jnp.float32
            ).astype(low)
            qkv[2 * col, rows, :] = got[:, :128]
            qkv[2 * col + 1, rows, :] = got[:, 128:]
            return carry

        lax.fori_loop(0, length // 256, qkv_step, 0)
        if col % 2:
            gather.run(1)
    qkv_store = own_load(7, qkv, qkv_out)
    qkv_store.start()

    units = pairs * (length // 256)
    acts = gather.take(min(len(gather.queue), 10))

    def unit_step(unit, carry):
        for k, act in enumerate(acts):
            @pl.when(unit == (k * units) // len(acts))
            def _(act=act):
                act()
        pair = unit // (length // 256)
        step = unit % (length // 256)
        rows = pl.ds(pl.multiple_of(step * 256, 256), 256)
        queries = qkv[pair, rows, :]
        keys = jnp.concatenate([qkv[pairs + pair], kaux_ref[...]], axis=1)
        outs = []
        for head in range(2):
            aux = jnp.concatenate(
                [jnp.broadcast_to(qaux_ref[2 * pair + head, pl.ds(2 * step + sub, 1), :], (BLOCK, 128)) for sub in range(2)],
                axis=0,
            ).astype(low)
            masked = jnp.where(lane_head(256, 128, head), queries, jnp.zeros_like(queries))
            scores[...] = lax.dot_general(
                jnp.concatenate([masked, aux], axis=1), keys, LAST, preferred_element_type=jnp.float32
            )
            for sub in range(2):
                start = pl.multiple_of(band_start(step * 2 + sub, blocks) * BLOCK, BLOCK)
                scores[sub * BLOCK : (sub + 1) * BLOCK, pl.ds(start, BAND * BLOCK)] += bias[
                    2 * pair + head, 2 * step + sub
                ].astype(jnp.float32)
            got = scores[...]
            highest = jnp.max(got, axis=1, keepdims=True)
            exponent = jnp.exp(got - highest)
            total = jnp.sum(exponent, axis=1, keepdims=True)
            outs.append(
                jnp.dot(exponent.astype(low), qkv[2 * pairs + pair], preferred_element_type=jnp.float32) * (1.0 / total)
            )
            lse = jnp.broadcast_to(highest + jnp.log(total), (256, 128))
            lse_ref[pair, step, head : head + 1, :] = jnp.transpose(lse)[0:1, :]
        attended[pair, rows, :] = jnp.where(lane_head(256, 128, 0), outs[0], outs[1]).astype(low)
        return carry

    lax.fori_loop(0, units, unit_step, 0)
    attended_store = own_load(8, attended, attended_out)
    attended_store.start()

    normed_store.wait()
    two = normed
    gather.need(project_pieces)
    load_project = own_load(9, full_ref.at[:, :, :, :, at_project:at_hidden], project_w)
    load_project.start()
    load_project.wait()

    def branch(rows):
        left = jnp.concatenate([attended[pair, rows, :] for pair in range(pairs)], axis=1)
        return lax.dot_general(left, project_w[...].reshape(width, inner), LAST, preferred_element_type=jnp.float32)

    def part_rows(part, core):
        return pl.ds(pl.multiple_of(part * half + core * quarter, quarter), quarter)

    def swap_part(i, part, slot=0):
        return near(i + part, away.at[slot + part], arrived.at[slot + part], to_c)

    for part in range(2):
        away[part] = branch(part_rows(part, 1 - c)).astype(low)
        swap_part(6, part).start()
    for part in range(2):
        normal[part] = branch(part_rows(part, c)) + tok[part_rows(part, c), :].astype(jnp.float32)

    def share(i, part, buffer):
        return near(i + part, buffer.at[part_rows(part, c)], buffer.at[part_rows(part, c)], to_c)

    tokens_store = [own_load(11 + part, tok.at[part_rows(part, c)], tokens_own_ref.at[part]) for part in range(2)]
    for copy in tokens_store:
        copy.start()
    for part in range(2):
        swap_part(6, part).wait()
        middle = normal[part] + arrived[part].astype(jnp.float32)
        normal[part] = middle
        inverse = lax.rsqrt(jnp.mean(middle * middle, axis=-1, keepdims=True) + EPSILON)
        two[part_rows(part, c), :] = (middle * inverse * gain_two).astype(low)
        share(8, part, two).start()
    gather.run(2)
    for part in range(2):
        share(8, part, two).wait()

    def turn_step(i, carry):
        rows = pl.ds(pl.multiple_of(i * BLOCK, BLOCK), BLOCK)
        two_t[:, rows] = jnp.transpose(two[rows, :])
        return carry

    lax.fori_loop(0, blocks, turn_step, 0)
    gather.run(2)

    def bounds(j):
        at = at_hidden + 3 * HIDDEN_STEP * j
        return at, at + 3 * steps[j]

    def load_step(j):
        a, b = bounds(j)
        return pltpu.make_async_copy(
            full_ref.at[:, :, :, :, a:b], w_buf.at[j % 2, :, :, :, :, 0 : b - a], w_sem.at[j % 2]
        )

    def store_step(j):
        a, b = bounds(j)
        return pltpu.make_async_copy(
            g_buf.at[j % 2, :, :, :, :, 0 : b - a],
            grads_out.at[:, :, :, :, a - at_hidden : b - at_hidden],
            g_sem.at[j % 2],
        )

    gather.need(range(first_hidden_piece, first_hidden_piece + per_step))
    load_step(0).start()
    for j, units_here in enumerate(steps):
        n = units_here
        slot = j % 2
        load_step(j).wait()

        def weight(k, slot=slot, n=n):
            return w_buf[slot, :, :, :, :, k * n : (k + 1) * n].reshape(width, n)

        def rows_step(i, carry, j=j, n=n, weight=weight):
            rows = pl.ds(pl.multiple_of(i * 256, 256), 256)
            left, grad = two[rows, :], cot[rows, :]
            gate = jnp.dot(left, weight(0), preferred_element_type=jnp.float32)
            up = jnp.dot(left, weight(1), preferred_element_type=jnp.float32)
            grad_hidden = jnp.dot(grad, weight(2), preferred_element_type=jnp.float32)
            value, slope = gelu_all(gate)
            hid[rows, 0:n] = (value * up).astype(low)
            ggate[rows, 0:n] = (grad_hidden * up * slope).astype(low)
            gup[rows, 0:n] = (grad_hidden * value).astype(low)
            out = lax.dot_general(hid[rows, 0:n], weight(2), LAST, preferred_element_type=jnp.float32)
            back = lax.dot_general(ggate[rows, 0:n], weight(0), LAST, preferred_element_type=jnp.float32)
            back = back + lax.dot_general(gup[rows, 0:n], weight(1), LAST, preferred_element_type=jnp.float32)
            if j == 0:
                acc_out[rows, :] = out
                acc_two[rows, :] = back
            else:
                acc_out[rows, :] += out
                acc_two[rows, :] += back
            return carry

        lax.fori_loop(0, length // 256, rows_step, 0)
        gather.run(2)
        if j + 1 < len(steps):
            first = first_hidden_piece + per_step * (j + 1)
            gather.need(range(first, first + per_step))
            load_step(j + 1).start()
        if j > 1:
            store_step(j - 2).wait()

        tiles = width // 256

        def grads_step(i, carry, slot=slot, n=n):
            rows = pl.ds(pl.multiple_of(i * 256, 256), 256)
            for k, (left, right) in enumerate(((two_t, ggate), (two_t, gup), (low_t, hid))):
                got = jnp.dot(left[rows, :], right[:, 0:n], preferred_element_type=jnp.float32).astype(low)
                span = deep // tiles
                g_buf[slot, pl.ds(i * span, span), :, :, :, k * n : (k + 1) * n] = got.reshape(
                    (span,) + g_buf.shape[2:5] + (n,)
                )
            return carry

        lax.fori_loop(0, tiles, grads_step, 0)
        store_step(j).start()
    gather.run(len(gather.queue))

    def share_sum(i, acc, slot):
        for part in range(2):
            away[slot + part] = acc[part_rows(part, 1 - c), :].astype(low)
            swap_part(i, part, slot).start()

    share_sum(10, acc_two, 0)
    for part in range(2):
        swap_part(10, part).wait()
        grad_two = acc_two[part_rows(part, c), :] + arrived[part].astype(jnp.float32)
        middle = normal[part]
        inverse = lax.rsqrt(jnp.mean(middle * middle, axis=-1, keepdims=True) + EPSILON)
        unit = middle * inverse
        weighted = jnp.sum((grad_two * unit).reshape(quarter // 8, 8, width), axis=0)
        gain_ref[part] = weighted
        scaled = grad_two * gain_two
        grad_middle = cot[part_rows(part, c), :].astype(jnp.float32) + inverse * (
            scaled - unit * jnp.mean(scaled * unit, axis=-1, keepdims=True)
        )
        middle_grad_ref[part] = grad_middle
        two[part_rows(part, c), :] = grad_middle.astype(low)
        share(12, part, two).start()
    share_sum(14, acc_out, 2)
    for part in range(2):
        swap_part(14, part, 2).wait()
        output_ref[part] = (normal[part] + acc_out[part_rows(part, c), :] + arrived[2 + part].astype(jnp.float32)).astype(low)
    for part in range(2):
        share(12, part, two).wait()
    branch_store = own_load(10, two, branch_out)
    branch_store.start()

    for j in range(max(0, len(steps) - 2), len(steps)):
        store_step(j).wait()
    for copy in (band_store, qkv_store, attended_store, branch_store, *tokens_store):
        copy.wait()
    gather.sent()


def front(shard_size, pieces, window, inner, hidden, own, inputs, cots, band_in, table_rows, qaux, kaux, live):
    low, f32 = jnp.bfloat16, jnp.float32
    deep = shard_size // 2
    rows, wide = own.shape
    half, width = inputs.shape[1:]
    length, quarter = 2 * half, half // 2
    heads, blocks = qaux.shape[:2]
    pairs = heads // 2
    at_project = 128 + 3 * inner
    shape = jax.ShapeDtypeStruct
    vmem, hbm = pl.BlockSpec(memory_space=pltpu.VMEM), pl.BlockSpec(memory_space=pl.ANY)
    dma = pltpu.SemaphoreType.DMA
    count = len(pieces)
    out_shape = [
        shape((deep, 2, 2, rows, wide), low),
        shape((length, width), low),
        shape((3 * pairs, length, 128), low),
        shape((pairs, length, 128), low),
        shape((blocks, BLOCK, BAND * BLOCK), low),
        shape((deep, 2, 2, rows, 3 * hidden), low),
        shape((length, width), low),
        shape((2, quarter, width), low),
        shape((pairs, length // 256, 2, 256), f32),
        shape((2, quarter, width), low),
        shape((2, quarter, width), f32),
        shape((2, 8, width), f32),
    ]
    step = HIDDEN_STEP
    scratch = [
        pltpu.VMEM((length, width), low),
        pltpu.VMEM((length, width), low),
        pltpu.VMEM((blocks, BLOCK, BAND * BLOCK), low),
        pltpu.VMEM((heads, blocks, BLOCK, BAND * BLOCK), low),
        pltpu.VMEM((deep, 2, 2, rows, at_project), low),
        pltpu.VMEM((3 * pairs, length, 128), low),
        pltpu.VMEM((length, width), low),
        pltpu.VMEM((256, length), f32),
        pltpu.VMEM((pairs, length, 128), low),
        pltpu.VMEM((deep, 2, 2, rows, inner), low),
        pltpu.VMEM((2, quarter, width), f32),
        pltpu.VMEM((4, quarter, width), low),
        pltpu.VMEM((4, quarter, width), low),
        pltpu.VMEM((width, length), low),
        pltpu.VMEM((width, length), low),
        pltpu.VMEM((length, width), f32),
        pltpu.VMEM((length, width), f32),
        pltpu.VMEM((2, deep, 2, 2, rows, 3 * step), low),
        pltpu.VMEM((2, deep, 2, 2, rows, 3 * step), low),
        pltpu.VMEM((length, step), low),
        pltpu.VMEM((length, step), low),
        pltpu.VMEM((length, step), low),
        dma((count, 3, deep - 1)),
        dma((count, 3, deep - 1)),
        dma((16,)),
        dma((16,)),
        dma((13,)),
        dma((2,)),
        dma((2,)),
    ]
    return pl.pallas_call(
        functools.partial(front_kernel, shard_size, pieces, window, (inner, hidden)),
        out_shape=out_shape,
        in_specs=[vmem, hbm, hbm, hbm, vmem, vmem, vmem, vmem],
        out_specs=[hbm] * 8 + [vmem] * 4,
        scratch_shapes=scratch,
        compiler_params=pltpu.CompilerParams(
            collective_id=1, has_side_effects=True, vmem_limit_bytes=58 * MIB
        ),
        name="front",
    )(own, inputs, cots, band_in, table_rows, qaux, kaux, live)


ORDERS = ("zyx", "zxy")
WINDOW = 6


def normalize(tokens_in):
    inverse = lax.rsqrt(jnp.mean(tokens_in * tokens_in, axis=-1, keepdims=True) + EPSILON)
    return tokens_in * inverse, inverse


def normalize_back(grad, normal, inverse, gain):
    scaled = grad * gain
    back = inverse * (scaled - normal * jnp.mean(scaled * normal, axis=-1, keepdims=True))
    axes = tuple(range(grad.ndim - 1))
    return back, jnp.sum(grad * normal, axis=axes)


def dot(a, b, left, right, kind=jnp.float32):
    return lax.dot_general(a, b, (((left,), (right,)), ((), ())), preferred_element_type=jnp.float32).astype(kind)


def swap(values, axis):
    return lax.ppermute(values, axis, [(0, 1), (1, 0)])


def ordered(mine, other, place, axis):
    first = place == 0
    return jnp.stack([jnp.where(first, mine, other), jnp.where(first, other, mine)], axis=axis)


def take(values, index, axis):
    return lax.dynamic_index_in_dim(values, index, axis, keepdims=False)


def shards(
    inputs, cotangent, lengths, buckets,
    query_weight, key_weight, value_weight, projection_weight, gate_weight, up_weight, down_weight,
    attention_gain, feedforward_gain, bias_table,
):
    low = jnp.bfloat16
    x, c = lax.axis_index("ctx"), lax.axis_index("tp")
    shard_size = lax.axis_size("shard")
    half, width = inputs.shape[1:]
    quarter = half // 2
    length = 2 * half
    blocks = length // BLOCK
    bucket_count, heads = bias_table.shape
    inner = query_weight.shape[1]
    hidden_width = gate_weight.shape[1]

    steps = hidden_steps(hidden_width)
    at_project = 128 + 3 * inner
    at_hidden = at_project + inner
    gains = jnp.pad(jnp.stack([attention_gain, feedforward_gain], axis=1), ((0, 0), (0, 126)))
    columns = [gains, query_weight, key_weight, value_weight, projection_weight]
    for j, n in enumerate(steps):
        at = HIDDEN_STEP * j
        columns += [w[:, at : at + n] for w in (gate_weight, up_weight, down_weight)]
    own = jnp.concatenate(columns, axis=1)
    pieces = split_columns(0, at_project, 4) + split_columns(at_project, at_hidden, 2)
    for j, n in enumerate(steps):
        at = at_hidden + 3 * HIDDEN_STEP * j
        pieces += split_columns(at, at + 3 * n, 2)
    pieces = [(a, b, ORDERS[i % len(ORDERS)]) for i, (a, b) in enumerate(pieces)]

    sequence_length = take(lengths[:, 0], x, 0)
    starts = [min(max(i - 1, 0), blocks - BAND) * BLOCK for i in range(blocks)]
    start_of = jnp.asarray(starts, jnp.int32)
    own_band = jnp.stack(
        [
            lax.dynamic_slice(buckets, (i * BLOCK, start_of[x * (blocks // 2) + i]), (BLOCK, BAND * BLOCK))
            for i in range(blocks // 2)
        ]
    ).astype(low)
    table = bias_table.astype(jnp.float32)
    table_rows = jnp.broadcast_to(
        jnp.pad(table.T, ((0, 0), (0, 128 - bucket_count)))[:, None, :], (heads, 8, 128)
    )
    block_at = jnp.arange(blocks) * BLOCK
    below = (block_at[None, :] < start_of[:, None])[None]
    above = (block_at[None, :] >= start_of[:, None] + BAND * BLOCK)[None]
    far_low, far_high = bucket_count // 2 - 1, bucket_count - 1
    constant = jnp.where(below, table[far_low][:, None, None], 0.0) + jnp.where(above, table[far_high][:, None, None], 0.0)
    qaux = jnp.concatenate(
        [constant, jnp.ones((heads, blocks, 1)), jnp.zeros((heads, blocks, 127 - blocks))], axis=-1
    )
    slots = jnp.arange(length, dtype=jnp.int32)
    kaux = jnp.concatenate(
        [
            (slots[:, None] // BLOCK == jnp.arange(blocks)[None, :]).astype(jnp.float32),
            jnp.where(slots < sequence_length, 0.0, -1e30)[:, None],
            jnp.zeros((length, 127 - blocks)),
        ],
        axis=1,
    ).astype(low)
    live = jnp.broadcast_to((slots < sequence_length).astype(jnp.float32)[:, None], (length, 128))

    (
        full, normed_one, qkv, attended, band, hidden_grads, grad_branch, tokens_own,
        lse, output, grad_middle, gain_two_rows,
    ) = front(
        shard_size, pieces, WINDOW, inner, hidden_width,
        own, inputs, cotangent, own_band, table_rows, qaux, kaux, live,
    )
    full = full.reshape(width, own.shape[1])
    project_full = full[:, at_project:at_hidden]
    gain_one = full[:, 0].astype(jnp.float32)
    attended = jnp.swapaxes(attended, 0, 1).reshape(length, inner)
    grid = (2, 2, quarter, width)

    def reduce_rows(partial):
        parts = partial.reshape(grid)
        return take(parts, c, 1) + swap(take(parts, 1 - c, 1).astype(low), "tp").astype(jnp.float32)

    gain_two_part = jnp.sum(gain_two_rows, axis=(0, 1))
    bandt = jnp.swapaxes(band, 1, 2).astype(jnp.int32)
    biast = bias_bands(bandt, table_rows)
    grad_project = dot(grad_branch, attended, 0, 0, low)
    grad_attended = dot(grad_branch, project_full, 1, 0, low)
    grad_q, grad_k, grad_v, band_grads, sums = attention_backward(qkv, kaux, qaux, biast, lse, grad_attended)
    table_grad = table_band(bandt, band_grads, bucket_count)
    sums = sums.reshape(heads, blocks, blocks, BLOCK).sum(-1)
    table_grad = table_grad.at[far_low].add(jnp.sum(jnp.where(jnp.swapaxes(below, 1, 2), sums, 0.0), axis=(1, 2)))
    table_grad = table_grad.at[far_high].add(jnp.sum(jnp.where(jnp.swapaxes(above, 1, 2), sums, 0.0), axis=(1, 2)))
    grad_query = dot(normed_one, grad_q, 0, 0, low)
    grad_key = dot(normed_one, grad_k, 0, 0, low)
    grad_value = dot(normed_one, grad_v, 0, 0, low)
    grad_one = reduce_rows(
        dot(grad_q, full[:, 128 : 128 + inner], 1, 1)
        + dot(grad_k, full[:, 128 + inner : 128 + 2 * inner], 1, 1)
        + dot(grad_v, full[:, 128 + 2 * inner : at_project], 1, 1)
    )
    normal_one, inverse_one = normalize(tokens_own.astype(jnp.float32))
    back_one, gain_one_part = normalize_back(grad_one, normal_one, inverse_one, gain_one)
    input_grad = (grad_middle + back_one).astype(low)

    def to_owners(mine):
        kept, leaving = take(mine, x, 0), take(mine, 1 - x, 0)
        pair = ordered(kept, swap(leaving, "ctx"), x, 0)
        return ordered(pair, swap(pair, "tp"), c, 1).reshape(2, half, width)

    output = to_owners(output)
    input_grad = to_owners(input_grad).astype(jnp.float32)

    rows = query_weight.shape[0]
    small = jnp.concatenate(
        [gain_one_part.reshape(-1, 128), gain_two_part.reshape(-1, 128), table_grad.reshape(-1, 128)], axis=0
    )
    used = small.shape[0]
    small = jnp.pad(small, ((0, -used % 8), (0, 0)))
    grads = [hidden_grads] + [
        g.reshape(shard_size // 2, 2, 2, rows, g.shape[1]) for g in (grad_project, grad_query, grad_key, grad_value)
    ]
    cuts = [(0, a, b) for a, b in split_columns(0, 3 * hidden_width, 6)]
    cuts += [(t, 0, inner) for t in range(1, 5)]
    cuts = [(t, a, b, i % 2) for i, (t, a, b) in enumerate(cuts)]
    *sums_out, small_out = scatter_gradients(shard_size, grads, small, cuts)
    hidden_sums, project, query, key, value_w = sums_out
    at = [3 * HIDDEN_STEP * j for j in range(len(steps))]
    gate_w, up_w, down = [
        jnp.concatenate([hidden_sums[:, a + k * n : a + (k + 1) * n] for a, n in zip(at, steps)], axis=1) for k in range(3)
    ]
    lines = width // 128
    me = lax.axis_index("shard") * 2 + x

    def own_gain(part):
        return lax.dynamic_slice_in_dim(small_out[1, part * lines : (part + 1) * lines].reshape(-1), me * rows, rows)

    table_total = small_out[0, 2 * lines : used].reshape(bucket_count, heads)
    return (
        output, input_grad, query, key, value_w, project, gate_w, up_w, down,
        own_gain(0), own_gain(1), table_total,
    )


def solution(mesh):
    rows = P(None, ("shard", "ctx"), None)
    weight = P(("shard", "ctx"), "tp")
    gain = P(("shard", "ctx"))
    table = P(None, "tp")
    return jax.shard_map(
        shards,
        mesh=mesh,
        in_specs=(rows, rows, P(None, "shard"), P("ctx", None)) + (weight,) * 7 + (gain, gain, table),
        out_specs=(rows, rows) + (weight,) * 7 + (gain, gain, table),
        check_vma=False,
    )
```

```python
import functools

import jax
import jax.numpy as jnp
from jax import lax
from jax.experimental import pallas as pl
from jax.experimental.pallas import tpu as pltpu
from jax.sharding import PartitionSpec as P

EPSILON = 1e-06
GELU_ROOT = 0.7978845608028654
GELU_CUBIC = 0.044715
MESH = pl.DeviceIdType.MESH
MIB = 1024 * 1024


BAND = 3
BLOCK = 128


def lane_head(rows, width, which):
    lanes = lax.broadcasted_iota(jnp.int32, (rows, width), 1)
    half = width // 2
    return (lanes < half) if which == 0 else (lanes >= half)


def band_start(row_block, blocks):
    return jnp.clip(row_block - 1, 0, blocks - BAND)


def split_columns(start, stop, pieces):
    tiles = (stop - start) // 128
    edges = [start + 128 * (tiles * i // pieces) for i in range(pieces + 1)]
    return [(a, b) for a, b in zip(edges, edges[1:]) if b > a]


class Place:
    def __init__(self, shard_size):
        self.deep = shard_size // 2
        shard = lax.axis_index("shard")
        self.z = shard // 2
        self.y = shard % 2
        self.x = lax.axis_index("ctx")
        self.c = lax.axis_index("tp")

    def device(self, z=None, y=None, x=None, c=None):
        z = self.z if z is None else z
        y = self.y if y is None else y
        x = self.x if x is None else x
        c = self.c if c is None else c
        return (z * 2 + y, x, c)

    def line(self, distance):
        return (self.z + distance) % self.deep

    def peers(self):
        others = [self.device(z=self.line(d)) for d in range(1, self.deep)]
        return others + [self.device(y=1 - self.y), self.device(x=1 - self.x), self.device(c=1 - self.c)]


def meet(place):
    barrier = pltpu.get_barrier_semaphore()
    peers = place.peers()
    for peer in peers:
        pl.semaphore_signal(barrier, inc=1, device_id=peer, device_id_type=MESH)
    pl.semaphore_wait(barrier, len(peers))


def send(source, target, send_sem, recv_sem, device):
    return pltpu.make_async_remote_copy(
        src_ref=source, dst_ref=target, send_sem=send_sem, recv_sem=recv_sem, device_id=device, device_id_type=MESH
    )


LAST = (((1,), (1,)), ((), ()))
FIRST = (((0,), (0,)), ((), ()))
HIDDEN_STEP = 256
HALF_BUCKETS = 16


def hidden_steps(hidden):
    return [min(HIDDEN_STEP, hidden - at) for at in range(0, hidden, HIDDEN_STEP)]


class Gather:
    def __init__(self, place, pieces, own_ref, full_ref, send_sem, recv_sem):
        self.place, self.pieces, self.own, self.full = place, pieces, own_ref, full_ref
        self.send_sem, self.recv_sem = send_sem, recv_sem
        self.queue = []

    def held(self, piece, hop):
        a, b, order = self.pieces[piece]
        place, done = self.place, order[:hop]
        at = [slice(None) if name in done else getattr(place, name) for name in "zyx"]
        return self.full.at[at[0], at[1], at[2], :, a:b]

    def copies(self, piece, hop):
        place = self.place
        a, b, order = self.pieces[piece]
        target = self.held(piece, hop)
        source = self.own.at[:, a:b] if hop == 0 else target
        name = order[hop]
        if name == "z":
            peers = [place.device(z=place.line(d)) for d in range(1, place.deep)]
        elif name == "y":
            peers = [place.device(y=1 - place.y)]
        else:
            peers = [place.device(x=1 - place.x)]
        return [
            send(source, target, self.send_sem.at[piece, hop, i], self.recv_sem.at[piece, hop, i], peer)
            for i, peer in enumerate(peers)
        ]

    def start(self, piece, hop):
        for copy in self.copies(piece, hop):
            copy.start()

    def arrive(self, piece, hop):
        for copy in self.copies(piece, hop):
            copy.wait_recv()

    def sent(self):
        for piece in range(len(self.pieces)):
            for hop in range(3):
                for copy in self.copies(piece, hop):
                    copy.wait_send()

    def plan(self, window):
        count = len(self.pieces)
        self.window = window

        def second(piece):
            def act():
                self.arrive(piece, 0)
                self.start(piece, 1)
                if piece + window < count:
                    self.start(piece + window, 0)
            return act

        def third(piece):
            def act():
                self.arrive(piece, 1)
                self.start(piece, 2)
            return act

        for piece in range(count + 1):
            if piece < count:
                self.queue.append((None, second(piece)))
            if piece > 0:
                self.queue.append((piece - 1, third(piece - 1)))
        for piece in range(min(window, count)):
            self.start(piece, 0)

    def run(self, steps):
        for _ in range(min(steps, len(self.queue))):
            self.queue.pop(0)[1]()

    def take(self, steps):
        taken, self.queue = self.queue[:steps], self.queue[steps:]
        return [act for _, act in taken]

    def need(self, pieces):
        for piece in pieces:
            while any(mark == piece for mark, _ in self.queue):
                self.run(1)
        for piece in pieces:
            self.arrive(piece, 2)


def query_aux(table, step, blocks):
    parts = []
    lanes = lax.broadcasted_iota(jnp.int32, (BLOCK, 128), 1)
    buckets = 2 * HALF_BUCKETS
    below = jnp.broadcast_to(table[0:1, HALF_BUCKETS - 1 : HALF_BUCKETS], (BLOCK, 128))
    above = jnp.broadcast_to(table[0:1, buckets - 1 : buckets], (BLOCK, 128))
    for sub in range(2):
        start = band_start(2 * step + sub, blocks)
        value = jnp.where(lanes < start, below, 0.0)
        value = jnp.where((lanes >= start + BAND) & (lanes < blocks), above, value)
        parts.append(jnp.where(lanes == blocks, 1.0, value))
    return jnp.concatenate(parts, axis=0).astype(jnp.bfloat16)


def gelu_all(gate):
    square = gate * gate
    tangent = jnp.tanh(GELU_ROOT * (gate + GELU_CUBIC * square * gate))
    value = 0.5 * gate * (1.0 + tangent)
    slope = 0.5 * (1.0 + tangent) + 0.5 * gate * (1.0 - tangent * tangent) * (
        GELU_ROOT + (3.0 * GELU_CUBIC * GELU_ROOT) * square
    )
    return value, slope


def front_kernel(
    shard_size, pieces, window, sizes,
    lengths_ref, gains_ref, query_ref, key_ref, value_ref, project_ref, gate_ref, up_ref, down_ref,
    inputs_ref, cots_ref, buckets_ref, table_ref,
    full_ref, normed_out, qkv_out, bandt_out, biast_out, grads_out, attended_out, tokens_own_ref,
    lse_ref, output_ref, middle_grad_ref, gain_ref,
    own_ref, tok, cot, band, bandt, bias, biast, kaux, gain_buf, qkv, normed, scores, attended, project_w,
    normal, away, arrived, two_t, low_t, acc_out, acc_two, w_buf, g_buf, hid, ggate, gup,
    send_sem, recv_sem, near_send, near_recv, local_sem, w_sem, g_sem, own_sem, bt_sem,
):
    inner, hidden = sizes
    length, width = tok.shape
    half, quarter = length // 2, length // 4
    heads, blocks = bias.shape[:2]
    pairs = heads // 2
    deep = shard_size // 2
    low = jnp.bfloat16
    place = Place(shard_size)
    x, c = place.x, place.c
    at_q = 128
    at_project = at_q + 3 * inner
    at_hidden = at_project + inner
    steps = hidden_steps(hidden)
    per_step = 2
    first_hidden_piece = len(pieces) - per_step * len(steps)
    project_pieces = [i for i, (a, b, _) in enumerate(pieces) if at_project <= a < at_hidden]
    qkv_pieces = [i for i, (a, b, _) in enumerate(pieces) if a < at_project]

    def own_load(i, source, target):
        return pltpu.make_async_copy(source, target, local_sem.at[i])

    parts, at = [], 0
    for ref in (gains_ref, query_ref, key_ref, value_ref, project_ref):
        parts.append((ref, at))
        at += ref.shape[1]
    own_loads = [
        pltpu.make_async_copy(ref, own_ref.at[:, at : at + ref.shape[1]], own_sem.at[i]) for i, (ref, at) in enumerate(parts)
    ]
    for j, n in enumerate(steps):
        for k, ref in enumerate((gate_ref, up_ref, down_ref)):
            at = at_hidden + 3 * HIDDEN_STEP * j + k * n
            own_loads.append(
                pltpu.make_async_copy(
                    ref.at[:, HIDDEN_STEP * j : HIDDEN_STEP * j + n], own_ref.at[:, at : at + n], own_sem.at[len(own_loads)]
                )
            )

    def band_source(block):
        start = pl.multiple_of(band_start(block, blocks) * BLOCK, BLOCK)
        first = block - x * (blocks // 2)
        return buckets_ref.at[pl.ds(pl.multiple_of(first * BLOCK, BLOCK), BLOCK), pl.ds(start, BAND * BLOCK)]

    own_tok = own_load(0, inputs_ref.at[x], tok.at[pl.ds(x * half, half)])
    own_cot = own_load(1, cots_ref.at[x], cot.at[pl.ds(x * half, half)])
    own_bands = [
        own_load(13 + i, band_source(x * (blocks // 2) + i), band.at[x * (blocks // 2) + i]) for i in range(blocks // 2)
    ]
    own_full = own_load(3, own_ref, full_ref.at[place.z, place.y, x])
    for copy in (*own_loads, *own_bands, own_tok, own_cot):
        copy.start()
    meet(place)
    for copy in own_loads:
        copy.wait()
    own_full.start()

    gather = Gather(place, pieces, own_ref, full_ref, send_sem, recv_sem)
    to_x, to_c = place.device(x=1 - x), place.device(c=1 - c)

    def x_rows(sender_x, sender_c):
        return pl.ds(sender_x * half + sender_c * quarter, quarter)

    def near(i, source, target, device):
        return send(source, target, near_send.at[i], near_recv.at[i], device)

    mine = [x * (blocks // 2) + c * (blocks // 4) + i for i in range(blocks // 4)]
    theirs = [(1 - x) * (blocks // 2) + c * (blocks // 4) + i for i in range(blocks // 4)]
    band_x = [near(16 + i, band_source(block), band.at[block], to_x) for i, block in enumerate(mine)]
    tok_x = near(1, inputs_ref.at[1 - x, pl.ds(c * quarter, quarter)], tok.at[x_rows(x, c)], to_x)
    cot_x = near(2, cots_ref.at[1 - x, pl.ds(c * quarter, quarter)], cot.at[x_rows(x, c)], to_x)
    band_c = [near(16 + len(mine) + i, band.at[block], band.at[block], to_c) for i, block in enumerate(theirs)]
    tok_c = near(4, tok.at[x_rows(1 - x, c)], tok.at[x_rows(1 - x, c)], to_c)
    cot_c = near(5, cot.at[x_rows(1 - x, c)], cot.at[x_rows(1 - x, c)], to_c)
    for copy in band_x:
        copy.start()
    tok_x.start()
    gather.plan(window)
    cot_x.start()
    own_full.wait()
    lanes_of = lax.broadcasted_iota(jnp.int32, (length, 128), 1)
    rows_of = lax.broadcasted_iota(jnp.int32, (length, 128), 0)
    valid = lengths_ref[x, 0]
    blocked = jnp.where(rows_of // BLOCK == lanes_of, 1.0, 0.0)
    kaux[...] = jnp.where((lanes_of == blocks) & (rows_of >= valid), -1e30, blocked).astype(low)
    for copy in band_x:
        copy.wait()
    for copy in band_c:
        copy.start()
    tok_x.wait()
    tok_c.start()
    for copy in (*own_bands, *band_c):
        copy.wait()
    gather.run(2)

    def bias_step(i, carry):
        block = i // (BLOCK // 16)
        at = pl.multiple_of((i % (BLOCK // 16)) * 16, 16)
        index = band[block, pl.ds(at, 16), :]
        for col in range(BAND):
            lanes = slice(col * BLOCK, (col + 1) * BLOCK)
            for head in range(heads):
                table = table_ref[head]
                got = [jnp.take_along_axis(table, index[8 * k : 8 * k + 8, lanes], axis=1) for k in range(2)]
                bias[head, block, pl.ds(at, 16), lanes] = jnp.concatenate(got, axis=0).astype(low)
        return carry

    lax.fori_loop(0, blocks * (BLOCK // 16) // 2, bias_step, 0)
    gather.run(4)
    lax.fori_loop(blocks * (BLOCK // 16) // 2, blocks * (BLOCK // 16), bias_step, 0)
    gather.run(2)

    def biast_store(block, slot):
        return pltpu.make_async_copy(biast.at[slot], biast_out.at[:, block], bt_sem.at[slot])

    def biast_block(block, carry):
        slot = block % 2

        @pl.when(block > 1)
        def _():
            biast_store(block - 2, slot).wait()

        bandt[block] = jnp.transpose(band[block].astype(jnp.float32)).astype(low)

        def inner_step(i, carry):
            at = pl.multiple_of(i * 16, 16)
            index = bandt[block, pl.ds(at, 16), :].astype(jnp.float32).astype(jnp.int32)
            for head in range(heads):
                got = [jnp.take_along_axis(table_ref[head], index[8 * k : 8 * k + 8], axis=1) for k in range(2)]
                biast[slot, head, pl.ds(at, 16), :] = jnp.concatenate(got, axis=0).astype(low)
            return carry

        lax.fori_loop(0, BAND * BLOCK // 16, inner_step, 0)
        biast_store(block, slot).start()
        return carry

    lax.fori_loop(0, blocks // 2, biast_block, 0)
    gather.run(4)
    lax.fori_loop(blocks // 2, blocks, biast_block, 0)
    gather.run(2)
    biast_store(blocks - 2, 0).wait()
    biast_store(blocks - 1, 1).wait()
    bandt_store = own_load(4, bandt, bandt_out)
    bandt_store.start()
    own_tok.wait()
    tok_c.wait()
    own_cot.wait()
    cot_x.wait()
    cot_c.start()
    cot_c.wait()

    def live_step(i, carry):
        rows = pl.ds(pl.multiple_of(i * BLOCK, BLOCK), BLOCK)
        here = lax.broadcasted_iota(jnp.int32, (BLOCK, width), 0) + i * BLOCK < valid
        masked = jnp.where(here, cot[rows, :].astype(jnp.float32), 0.0).astype(low)
        cot[rows, :] = masked
        low_t[:, rows] = jnp.transpose(masked)
        return carry

    lax.fori_loop(0, blocks, live_step, 0)

    gather.need(qkv_pieces)
    load_gains = own_load(5, full_ref.at[:, :, :, :, 0:at_q], gain_buf)
    third = 3 * inner // 2
    loads_wide = [
        pltpu.make_async_copy(
            full_ref.at[:, :, :, :, at_q + third * k : at_q + third * (k + 1)], w_buf.at[k, :, :, :, :, 0:third], w_sem.at[k]
        )
        for k in range(2)
    ]
    for copy in (load_gains, *loads_wide):
        copy.start()
    load_gains.wait()
    gains = jnp.transpose(gain_buf[...].reshape(width, 128).astype(jnp.float32))
    gain_one, gain_two = gains[0:1, :], gains[1:2, :]

    def norm_step(i, carry):
        rows = pl.ds(pl.multiple_of(i * BLOCK, BLOCK), BLOCK)
        present = tok[rows, :].astype(jnp.float32)
        inverse = lax.rsqrt(jnp.mean(present * present, axis=-1, keepdims=True) + EPSILON)
        got = (present * inverse * gain_one).astype(low)
        normed[rows, :] = got
        two_t[:, rows] = jnp.transpose(got)
        return carry

    lax.fori_loop(0, blocks, norm_step, 0)
    normed_store = own_load(6, two_t, normed_out)
    normed_store.start()
    for copy in loads_wide:
        copy.wait()
    gather.run(2)

    for col in range(3 * pairs // 2):
        slot, at = 256 * col // third, 256 * col % third
        lanes = slice(at, at + 256)

        def qkv_step(i, carry):
            rows = pl.ds(pl.multiple_of(i * 256, 256), 256)
            got = jnp.dot(
                normed[rows, :], w_buf[slot, :, :, :, :, lanes].reshape(width, 256), preferred_element_type=jnp.float32
            ).astype(low)
            qkv[2 * col, rows, :] = got[:, :128]
            qkv[2 * col + 1, rows, :] = got[:, 128:]
            return carry

        lax.fori_loop(0, length // 256, qkv_step, 0)
        if col % 2:
            gather.run(1)
    qkv_store = own_load(7, qkv, qkv_out)
    qkv_store.start()

    units = pairs * (length // 256)
    acts = gather.take(min(len(gather.queue), 10))

    def unit_step(unit, carry):
        for k, act in enumerate(acts):
            @pl.when(unit == (k * units) // len(acts))
            def _(act=act):
                act()
        pair = unit // (length // 256)
        step = unit % (length // 256)
        rows = pl.ds(pl.multiple_of(step * 256, 256), 256)
        queries = qkv[pair, rows, :]
        keys = jnp.concatenate([qkv[pairs + pair], kaux[...]], axis=1)
        outs = []
        for head in range(2):
            aux = query_aux(table_ref[2 * pair + head], step, blocks)
            masked = jnp.where(lane_head(256, 128, head), queries, jnp.zeros_like(queries))
            scores[...] = lax.dot_general(
                jnp.concatenate([masked, aux], axis=1), keys, LAST, preferred_element_type=jnp.float32
            )
            for sub in range(2):
                start = pl.multiple_of(band_start(step * 2 + sub, blocks) * BLOCK, BLOCK)
                scores[sub * BLOCK : (sub + 1) * BLOCK, pl.ds(start, BAND * BLOCK)] += bias[
                    2 * pair + head, 2 * step + sub
                ].astype(jnp.float32)
            got = scores[...]
            highest = jnp.max(got, axis=1, keepdims=True)
            exponent = jnp.exp(got - highest)
            total = jnp.sum(exponent, axis=1, keepdims=True)
            outs.append(
                jnp.dot(exponent.astype(low), qkv[2 * pairs + pair], preferred_element_type=jnp.float32) * (1.0 / total)
            )
            lse = jnp.broadcast_to(highest + jnp.log(total), (256, 128))
            lse_ref[pair, step, head : head + 1, :] = jnp.transpose(lse)[0:1, :]
        attended[pair, rows, :] = jnp.where(lane_head(256, 128, 0), outs[0], outs[1]).astype(low)
        return carry

    lax.fori_loop(0, units, unit_step, 0)
    normed_store.wait()
    two = normed
    gather.need(project_pieces)
    load_project = own_load(9, full_ref.at[:, :, :, :, at_project:at_hidden], project_w)
    load_project.start()
    load_project.wait()

    def branch(rows):
        left = jnp.concatenate([attended[pair, rows, :] for pair in range(pairs)], axis=1)
        return lax.dot_general(left, project_w[...].reshape(width, inner), LAST, preferred_element_type=jnp.float32)

    def part_rows(part, core):
        return pl.ds(pl.multiple_of(part * half + core * quarter, quarter), quarter)

    def swap_part(i, part, slot=0):
        return near(i + part, away.at[slot + part], arrived.at[slot + part], to_c)

    for part in range(2):
        away[part] = branch(part_rows(part, 1 - c)).astype(low)
        swap_part(6, part).start()
    for part in range(2):
        normal[part] = branch(part_rows(part, c)) + tok[part_rows(part, c), :].astype(jnp.float32)

    def share(i, part, buffer):
        return near(i + part, buffer.at[part_rows(part, c)], buffer.at[part_rows(part, c)], to_c)

    tokens_store = [own_load(11 + part, tok.at[part_rows(part, c)], tokens_own_ref.at[part]) for part in range(2)]
    for copy in tokens_store:
        copy.start()
    for part in range(2):
        swap_part(6, part).wait()
        middle = normal[part] + arrived[part].astype(jnp.float32)
        normal[part] = middle
        inverse = lax.rsqrt(jnp.mean(middle * middle, axis=-1, keepdims=True) + EPSILON)
        two[part_rows(part, c), :] = (middle * inverse * gain_two).astype(low)
        share(8, part, two).start()
    gather.run(2)
    for part in range(2):
        share(8, part, two).wait()

    def turn_step(i, carry):
        rows = pl.ds(pl.multiple_of(i * BLOCK, BLOCK), BLOCK)
        two_t[:, rows] = jnp.transpose(two[rows, :])
        return carry

    lax.fori_loop(0, blocks, turn_step, 0)
    gather.run(2)

    def bounds(j):
        at = at_hidden + 3 * HIDDEN_STEP * j
        return at, at + 3 * steps[j]

    def load_step(j):
        a, b = bounds(j)
        return pltpu.make_async_copy(
            full_ref.at[:, :, :, :, a:b], w_buf.at[j % 2, :, :, :, :, 0 : b - a], w_sem.at[j % 2]
        )

    def store_step(j):
        a, b = bounds(j)
        return pltpu.make_async_copy(
            g_buf.at[j % 2, :, :, :, :, 0 : b - a],
            grads_out.at[:, :, :, :, a - at_hidden : b - at_hidden],
            g_sem.at[j % 2],
        )

    gather.need(range(first_hidden_piece, first_hidden_piece + per_step))
    load_step(0).start()
    for j, units_here in enumerate(steps):
        n = units_here
        slot = j % 2
        load_step(j).wait()

        def weight(k, slot=slot, n=n):
            return w_buf[slot, :, :, :, :, k * n : (k + 1) * n].reshape(width, n)

        def rows_step(i, carry, j=j, n=n, weight=weight):
            rows = pl.ds(pl.multiple_of(i * 256, 256), 256)
            left, grad = two[rows, :], cot[rows, :]
            gate = jnp.dot(left, weight(0), preferred_element_type=jnp.float32)
            up = jnp.dot(left, weight(1), preferred_element_type=jnp.float32)
            grad_hidden = jnp.dot(grad, weight(2), preferred_element_type=jnp.float32)
            value, slope = gelu_all(gate)
            hid[rows, 0:n] = (value * up).astype(low)
            ggate[rows, 0:n] = (grad_hidden * up * slope).astype(low)
            gup[rows, 0:n] = (grad_hidden * value).astype(low)
            out = lax.dot_general(hid[rows, 0:n], weight(2), LAST, preferred_element_type=jnp.float32)
            back = lax.dot_general(ggate[rows, 0:n], weight(0), LAST, preferred_element_type=jnp.float32)
            back = back + lax.dot_general(gup[rows, 0:n], weight(1), LAST, preferred_element_type=jnp.float32)
            if j == 0:
                acc_out[rows, :] = out
                acc_two[rows, :] = back
            else:
                acc_out[rows, :] += out
                acc_two[rows, :] += back
            return carry

        lax.fori_loop(0, length // 256, rows_step, 0)
        gather.run(2)
        if j + 1 < len(steps):
            first = first_hidden_piece + per_step * (j + 1)
            gather.need(range(first, first + per_step))
            load_step(j + 1).start()
        if j > 1:
            store_step(j - 2).wait()

        tiles = width // 256

        def grads_step(i, carry, slot=slot, n=n):
            rows = pl.ds(pl.multiple_of(i * 256, 256), 256)
            for k, (left, right) in enumerate(((two_t, ggate), (two_t, gup), (low_t, hid))):
                got = jnp.dot(left[rows, :], right[:, 0:n], preferred_element_type=jnp.float32).astype(low)
                span = deep // tiles
                g_buf[slot, pl.ds(i * span, span), :, :, :, k * n : (k + 1) * n] = got.reshape(
                    (span,) + g_buf.shape[2:5] + (n,)
                )
            return carry

        lax.fori_loop(0, tiles, grads_step, 0)
        store_step(j).start()
    gather.run(len(gather.queue))

    def share_sum(i, acc, slot):
        for part in range(2):
            away[slot + part] = acc[part_rows(part, 1 - c), :].astype(low)
            swap_part(i, part, slot).start()

    share_sum(10, acc_two, 0)
    for part in range(2):
        swap_part(10, part).wait()
        grad_two = acc_two[part_rows(part, c), :] + arrived[part].astype(jnp.float32)
        middle = normal[part]
        inverse = lax.rsqrt(jnp.mean(middle * middle, axis=-1, keepdims=True) + EPSILON)
        unit = middle * inverse
        weighted = jnp.sum((grad_two * unit).reshape(quarter // 8, 8, width), axis=0)
        gain_ref[part] = weighted
        scaled = grad_two * gain_two
        grad_middle = cot[part_rows(part, c), :].astype(jnp.float32) + inverse * (
            scaled - unit * jnp.mean(scaled * unit, axis=-1, keepdims=True)
        )
        middle_grad_ref[part] = grad_middle
        two[part_rows(part, c), :] = grad_middle.astype(low)
        share(12, part, two).start()
    share_sum(14, acc_out, 2)
    for part in range(2):
        swap_part(14, part, 2).wait()
        output_ref[part] = (normal[part] + acc_out[part_rows(part, c), :] + arrived[2 + part].astype(jnp.float32)).astype(low)
    for part in range(2):
        share(12, part, two).wait()
    for j in range(max(0, len(steps) - 2), len(steps)):
        store_step(j).wait()

    lax.fori_loop(0, blocks, turn_step, 0)

    def project_step(i, carry):
        rows = pl.ds(pl.multiple_of(i * 256, 256), 256)
        right = jnp.concatenate([attended[pair] for pair in range(pairs)], axis=1)
        got = jnp.dot(two_t[rows, :], right, preferred_element_type=jnp.float32).astype(low)
        span = deep // (width // 256)
        g_buf[0, pl.ds(i * span, span), :, :, :, 0:inner] = got.reshape((span,) + g_buf.shape[2:5] + (inner,))
        return carry

    lax.fori_loop(0, width // 256, project_step, 0)
    project_store = own_load(8, g_buf.at[0, :, :, :, :, 0:inner], grads_out.at[:, :, :, :, 3 * hidden : 3 * hidden + inner])
    project_store.start()

    def attended_step(i, carry):
        rows = pl.ds(pl.multiple_of(i * 256, 256), 256)
        got = jnp.dot(two[rows, :], project_w[...].reshape(width, inner), preferred_element_type=jnp.float32).astype(low)
        for pair in range(pairs):
            attended[pair, rows, :] = got[:, pair * 128 : (pair + 1) * 128]
        return carry

    lax.fori_loop(0, length // 256, attended_step, 0)
    attended_store = own_load(10, attended, attended_out)
    attended_store.start()
    for copy in (bandt_store, qkv_store, attended_store, project_store, *tokens_store):
        copy.wait()
    gather.sent()


def front(shard_size, pieces, window, lengths, gains, weights, inputs, cots, buckets, table_rows):
    low, f32 = jnp.bfloat16, jnp.float32
    deep = shard_size // 2
    rows, inner = weights[0].shape
    hidden = weights[4].shape[1]
    wide = pieces[-1][1]
    half, width = inputs.shape[1:]
    length, quarter = 2 * half, half // 2
    heads = table_rows.shape[0]
    blocks = length // BLOCK
    pairs = heads // 2
    shape = jax.ShapeDtypeStruct
    vmem, hbm = pl.BlockSpec(memory_space=pltpu.VMEM), pl.BlockSpec(memory_space=pl.ANY)
    dma = pltpu.SemaphoreType.DMA
    count = len(pieces)
    step = HIDDEN_STEP
    out_shape = [
        shape((deep, 2, 2, rows, wide), low),
        shape((width, length), low),
        shape((3 * pairs, length, 128), low),
        shape((blocks, BAND * BLOCK, BLOCK), low),
        shape((heads, blocks, BAND * BLOCK, BLOCK), low),
        shape((deep, 2, 2, rows, 3 * hidden + inner), low),
        shape((pairs, length, 128), low),
        shape((2, quarter, width), low),
        shape((pairs, length // 256, 2, 256), f32),
        shape((2, quarter, width), low),
        shape((2, quarter, width), f32),
        shape((2, 8, width), f32),
    ]
    scratch = [
        pltpu.VMEM((rows, wide), low),
        pltpu.VMEM((length, width), low),
        pltpu.VMEM((length, width), low),
        pltpu.VMEM((blocks, BLOCK, BAND * BLOCK), jnp.int32),
        pltpu.VMEM((blocks, BAND * BLOCK, BLOCK), low),
        pltpu.VMEM((heads, blocks, BLOCK, BAND * BLOCK), low),
        pltpu.VMEM((2, heads, BAND * BLOCK, BLOCK), low),
        pltpu.VMEM((length, 128), low),
        pltpu.VMEM((deep, 2, 2, rows, 128), low),
        pltpu.VMEM((3 * pairs, length, 128), low),
        pltpu.VMEM((length, width), low),
        pltpu.VMEM((256, length), f32),
        pltpu.VMEM((pairs, length, 128), low),
        pltpu.VMEM((deep, 2, 2, rows, inner), low),
        pltpu.VMEM((2, quarter, width), f32),
        pltpu.VMEM((4, quarter, width), low),
        pltpu.VMEM((4, quarter, width), low),
        pltpu.VMEM((width, length), low),
        pltpu.VMEM((width, length), low),
        pltpu.VMEM((length, width), f32),
        pltpu.VMEM((length, width), f32),
        pltpu.VMEM((2, deep, 2, 2, rows, 3 * step), low),
        pltpu.VMEM((2, deep, 2, 2, rows, 3 * step), low),
        pltpu.VMEM((length, step), low),
        pltpu.VMEM((length, step), low),
        pltpu.VMEM((length, step), low),
        dma((count, 3, deep - 1)),
        dma((count, 3, deep - 1)),
        dma((16 + blocks // 2,)),
        dma((16 + blocks // 2,)),
        dma((13 + blocks // 2,)),
        dma((2,)),
        dma((2,)),
        dma((5 + 3 * len(hidden_steps(hidden)),)),
        dma((2,)),
    ]
    return pl.pallas_call(
        functools.partial(front_kernel, shard_size, pieces, window, (inner, hidden)),
        out_shape=out_shape,
        in_specs=[pl.BlockSpec(memory_space=pltpu.SMEM)] + [hbm] * 11 + [vmem],
        out_specs=[hbm] * 8 + [vmem] * 4,
        scratch_shapes=scratch,
        compiler_params=pltpu.CompilerParams(
            collective_id=1, has_side_effects=True, vmem_limit_bytes=60 * MIB
        ),
        name="front",
    )(lengths, gains, *weights, inputs, cots, buckets, table_rows)


GROUP = 16
TURNS = 4


class Scatter:
    def __init__(self, place, pieces, sources, outs, buffers, sems):
        self.place, self.pieces, self.sources, self.outs = place, pieces, sources, outs
        self.first, self.own, self.second, self.third = buffers
        self.own_sem, self.send_sem, self.recv_sem = sems
        self.queue = []

    def peer(self, name):
        place = self.place
        return place.device(y=1 - place.y) if name == "y" else place.device(x=1 - place.x)

    def rest(self, piece):
        order = self.pieces[piece][3]
        return [name for name in "zyx" if name != order[0]]

    def cut(self, piece, name, value):
        t, a, b, _ = self.pieces[piece]
        at = [value if name == other else slice(None) for other in "zyx"]
        return self.sources[t].at[at[0], at[1], at[2], :, a:b]

    def own_copy(self, piece):
        order = self.pieces[piece][3]
        return pltpu.make_async_copy(
            self.cut(piece, order[0], getattr(self.place, order[0])), self.own[piece], self.own_sem.at[piece]
        )

    def copies(self, piece, hop):
        place, order = self.place, self.pieces[piece][3]
        name, rest = order[hop], self.rest(piece)
        own, made = self.own[piece], []

        def at(**index):
            return tuple(index[n] if n in index else slice(None) for n in rest)

        def add(source, target, device):
            i = len(made)
            made.append(send(source, target, self.send_sem.at[piece, hop, i], self.recv_sem.at[piece, hop, i], device))

        if hop == 0:
            if name == "z":
                for d in range(1, place.deep):
                    z = place.line(d)
                    add(self.cut(piece, "z", z), self.first[piece].at[d - 1], place.device(z=z))
            else:
                add(self.cut(piece, name, 1 - getattr(place, name)), self.first[piece], self.peer(name))
            return made
        fixed = {} if hop == 1 else {order[1]: getattr(place, order[1])}
        buffer = self.second[piece] if hop == 1 else self.third[piece]
        if name == "z":
            for d in range(1, place.deep):
                z = place.line(d)
                add(own.at[at(z=z, **fixed)], buffer.at[d - 1], place.device(z=z))
        else:
            add(own.at[at(**{name: 1 - getattr(place, name)}, **fixed)], buffer, self.peer(name))
        return made

    def start(self, piece, hop):
        for copy in self.copies(piece, hop):
            copy.start()

    def arrive(self, piece, hop):
        for copy in self.copies(piece, hop):
            copy.wait_recv()

    def begin(self, pieces):
        for piece in pieces:
            self.start(piece, 0)
            self.own_copy(piece).start()

    def add_first(self, piece):
        order = self.pieces[piece][3]
        self.arrive(piece, 0)
        self.own_copy(piece).wait()
        own, came = self.own[piece], self.first[piece]
        inner = own.shape[1]

        def body(i, carry):
            for k in range(inner):
                if order[0] == "z":
                    total = own[i, k].astype(jnp.float32)
                    for d in range(came.shape[0]):
                        total = total + came[d, i, k].astype(jnp.float32)
                    own[i, k] = total.astype(jnp.bfloat16)
                else:
                    own[i, k] = own[i, k] + came[i, k]
            return carry

        lax.fori_loop(0, own.shape[0], body, 0)
        self.start(piece, 1)

    def add_second(self, piece):
        place, order = self.place, self.pieces[piece][3]
        name, rest = order[1], self.rest(piece)
        self.arrive(piece, 1)
        own, came = self.own[piece], self.second[piece]
        mine = getattr(place, name)
        spans = own.shape[1] if rest[0] == name else own.shape[0]

        def body(i, carry):
            if rest[0] == name:
                own[mine, i] = own[mine, i] + came[i]
            else:
                own[i, mine] = own[i, mine] + came[i]
            return carry

        lax.fori_loop(0, spans, body, 0)
        self.start(piece, 2)

    def add_third(self, piece):
        place, order = self.place, self.pieces[piece][3]
        t, a, b, _ = self.pieces[piece]
        rest = self.rest(piece)
        self.arrive(piece, 2)
        total = self.own[piece][getattr(place, rest[0]), getattr(place, rest[1])].astype(jnp.float32)
        if order[2] == "z":
            for d in range(1, place.deep):
                total = total + self.third[piece][d - 1].astype(jnp.float32)
        else:
            total = total + self.third[piece][...].astype(jnp.float32)
        self.outs[t][:, a:b] = total

    def plan(self, pieces):
        pieces = list(pieces)
        for i in range(len(pieces) + 2):
            if i < len(pieces):
                self.queue.append(functools.partial(self.add_first, pieces[i]))
            if 0 < i <= len(pieces):
                self.queue.append(functools.partial(self.add_second, pieces[i - 1]))
            if i > 1:
                self.queue.append(functools.partial(self.add_third, pieces[i - 2]))

    def run(self, steps):
        for _ in range(min(steps, len(self.queue))):
            self.queue.pop(0)()

    def take(self, steps):
        taken, self.queue = self.queue[:steps], self.queue[steps:]
        return taken

    def sent(self):
        for piece in range(len(self.pieces)):
            for hop in range(3):
                for copy in self.copies(piece, hop):
                    copy.wait_send()


def piece_buffers(piece, deep, rows):
    _, a, b, order = piece
    sizes = {"z": deep, "y": 2, "x": 2}
    rest = [name for name in "zyx" if name != order[0]]
    left = [sizes[name] for name in rest]
    last = [sizes[name] for name in rest if name != order[1]]
    tail = [rows, b - a]
    lead = [deep - 1]
    first = (lead if order[0] == "z" else []) + left + tail
    second = (lead if order[1] == "z" else []) + last + tail
    third = (lead if order[2] == "z" else []) + tail
    return [tuple(shape) for shape in (first, left + tail, second, third)]


def back_kernel(shard_size, pieces, early, sizes, *refs):
    inner, hidden, buckets = sizes
    count = len(pieces)
    (
        lengths_ref, full_ref, normed_in, qkv_in, bandt_in, biast_in, grads_in, do_in,
        lse_ref, output_ref, middle_ref, tokens_ref, gain_two_ref, table_ref,
    ) = refs[:14]
    refs = refs[14:]
    hidden_out, weight_sums, output_out, input_out, small_out = refs[:5]
    refs = refs[5:]
    first, own, second, third = [refs[k * count : (k + 1) * count] for k in range(4)]
    refs = refs[4 * count :]
    (
        qkv, normed_t, bandt, bias, wqkv, gain_buf, do, scores, grads, far, dk_acc, dv_acc, kaux, wgrad,
        mine_sum, away, arrived, result, table_acc, hot, found,
        small, small_x, small_y, hold_x, hold_y, hold_z, small_c,
        own_sem, send_sem, recv_sem, near_send, near_recv, local_sem,
    ) = refs
    length = qkv.shape[1]
    width = normed_t.shape[0]
    half, quarter = length // 2, length // 4
    heads, blocks = bias.shape[:2]
    pairs = heads // 2
    deep = shard_size // 2
    low, f32 = jnp.bfloat16, jnp.float32
    place = Place(shard_size)
    x, y, z, c = place.x, place.y, place.z, place.c
    to_x, to_y, to_c = place.device(x=1 - x), place.device(y=1 - y), place.device(c=1 - c)

    def local(i, source, target):
        return pltpu.make_async_copy(source, target, local_sem.at[i])

    loads = [
        local(0, qkv_in, qkv), local(1, biast_in, bias), local(2, do_in, do),
        local(3, full_ref.at[:, :, :, :, 128 : 128 + 3 * inner], wqkv), local(4, normed_in, normed_t),
        local(5, bandt_in, bandt), local(6, full_ref.at[:, :, :, :, 0:128], gain_buf),
    ]
    for copy in loads:
        copy.start()
    meet(place)
    scatter = Scatter(
        place, pieces, (grads_in, wgrad), (hidden_out, weight_sums), (first, own, second, third), (own_sem, send_sem, recv_sem),
    )
    scatter.begin(range(early))
    scatter.plan(range(early))

    def near(i, source, target, device):
        return send(source, target, near_send.at[i], near_recv.at[i], device)

    def to_owners(i, values, out):
        here = out.at[x, pl.ds(c * quarter, quarter)]
        there = out.at[1 - x, pl.ds(c * quarter, quarter)]
        return (
            local(7 + i, values.at[x], here),
            near(4 * i, values.at[x], here, to_c),
            near(4 * i + 1, values.at[1 - x], here, to_x),
            near(4 * i + 2, there, there, to_c),
        )

    output_moves = to_owners(0, output_ref, output_out)
    for copy in output_moves[:3]:
        copy.start()

    lanes_of = lax.broadcasted_iota(jnp.int32, (length, 128), 1)
    rows_of = lax.broadcasted_iota(jnp.int32, (length, 128), 0)
    valid = lengths_ref[x, 0]
    blocked = jnp.where(rows_of // BLOCK == lanes_of, 1.0, 0.0)
    kaux[...] = jnp.where((lanes_of == blocks) & (rows_of >= valid), -1e30, blocked).astype(low)
    far[...] = jnp.zeros_like(far)
    for copy in loads[:3]:
        copy.wait()

    per_pair = length // 256
    units = pairs * per_pair
    acts = scatter.take(ATTENTION_ACTS)

    def unit_step(unit, carry):
        for k, act in enumerate(acts):
            @pl.when(unit == (k * units) // len(acts))
            def _(act=act):
                act()
        pair = unit // per_pair
        step = unit % per_pair
        rows = pl.ds(pl.multiple_of(step * 256, 256), 256)

        @pl.when(step == 0)
        def _():
            dk_acc[...] = jnp.zeros_like(dk_acc)
            dv_acc[...] = jnp.zeros_like(dv_acc)

        queries = qkv[pair, rows, :]
        grad = do[pair, rows, :]
        key_pair = qkv[pairs + pair]
        keys = jnp.concatenate([key_pair, kaux[...]], axis=1)
        values = qkv[2 * pairs + pair]
        dq = None
        for head in range(2):
            here = lane_head(256, 128, head)
            aux = query_aux(table_ref[2 * pair + head], step, blocks)
            q_masked = jnp.where(here, queries, jnp.zeros_like(queries))
            do_masked = jnp.where(here, grad, jnp.zeros_like(grad))
            scores[...] = lax.dot_general(
                keys, jnp.concatenate([q_masked, aux], axis=1), LAST, preferred_element_type=f32
            )
            for sub in range(2):
                start = pl.multiple_of(band_start(step * 2 + sub, blocks) * BLOCK, BLOCK)
                scores[pl.ds(start, BAND * BLOCK), sub * BLOCK : (sub + 1) * BLOCK] += bias[
                    2 * pair + head, 2 * step + sub
                ].astype(f32)
            soft = jnp.exp(scores[...] - lse_ref[pair, step, head : head + 1, :])
            dv_acc[...] += jnp.dot(soft.astype(low), do_masked, preferred_element_type=f32)
            grad_probs = lax.dot_general(values, do_masked, LAST, preferred_element_type=f32)
            weighted = jnp.sum(soft * grad_probs, axis=0, keepdims=True)
            grad_scores = (soft * (grad_probs - weighted)).astype(low)
            grads[...] = grad_scores
            dk_acc[...] += jnp.dot(grad_scores, q_masked, preferred_element_type=f32)
            k_masked = jnp.where(lane_head(length, 128, head), key_pair, jnp.zeros_like(key_pair))
            part = lax.dot_general(grad_scores, k_masked, FIRST, preferred_element_type=f32)
            dq = part if dq is None else dq + part
            sums = jnp.concatenate(
                [
                    jnp.sum(grad_scores[block * BLOCK : (block + 1) * BLOCK, :].astype(f32), axis=0, keepdims=True)
                    for block in range(blocks)
                ],
                axis=0,
            )
            block_of = lax.broadcasted_iota(jnp.int32, (blocks, BLOCK), 0)
            for sub in range(2):
                start = band_start(step * 2 + sub, blocks)
                at = pl.multiple_of(start * BLOCK, BLOCK)
                bias[2 * pair + head, 2 * step + sub] = grads[pl.ds(at, BAND * BLOCK), sub * BLOCK : (sub + 1) * BLOCK]
                part = sums[:, sub * BLOCK : (sub + 1) * BLOCK]
                far[0, 2 * pair + head] += jnp.where(block_of < start, part, 0.0)
                far[1, 2 * pair + head] += jnp.where(block_of >= start + BAND, part, 0.0)
        qkv[pair, rows, :] = dq.astype(low)

        @pl.when(step == per_pair - 1)
        def _():
            qkv[pairs + pair] = dk_acc[...].astype(low)
            qkv[2 * pairs + pair] = dv_acc[...].astype(low)

        return carry

    lax.fori_loop(0, units, unit_step, 0)
    for copy in output_moves[:3]:
        copy.wait()
    output_moves[3].start()
    for copy in loads[3:]:
        copy.wait()

    for t in range(3):
        def weight_step(i, carry, t=t):
            rows = pl.ds(pl.multiple_of(i * 256, 256), 256)
            right = jnp.concatenate([qkv[t * pairs + pair] for pair in range(pairs)], axis=1)
            got = jnp.dot(normed_t[rows, :], right, preferred_element_type=f32).astype(low)
            span = deep // (width // 256)
            wgrad[pl.ds(i * span, span), :, :, :, t * inner : (t + 1) * inner] = got.reshape(
                (span,) + wgrad.shape[1:4] + (inner,)
            )
            return carry

        lax.fori_loop(0, width // 256, weight_step, 0)
        late = [i for i in range(early, count) if t * inner <= pieces[i][1] < (t + 1) * inner]
        scatter.begin(late)
        scatter.plan(late)
        scatter.run(2)

    def part_rows(part, core):
        return pl.ds(pl.multiple_of(part * half + core * quarter, quarter), quarter)

    def grad_one(rows):
        left = jnp.concatenate([qkv[k, rows, :] for k in range(3 * pairs)], axis=1)
        return lax.dot_general(left, wqkv[...].reshape(width, 3 * inner), LAST, preferred_element_type=f32)

    swaps = [near(8 + part, away.at[part], arrived.at[part], to_c) for part in range(2)]

    def away_step(part, carry):
        away[part] = grad_one(part_rows(part, 1 - c)).astype(low)
        return carry

    def mine_step(part, carry):
        mine_sum[part] = grad_one(part_rows(part, c))
        return carry

    lax.fori_loop(0, 2, away_step, 0)
    for copy in swaps:
        copy.start()
    lax.fori_loop(0, 2, mine_step, 0)
    gains = jnp.transpose(gain_buf[...].reshape(width, 128).astype(f32))
    gain_one = gains[0:1, :]
    gain_sum = jnp.zeros((1, width), f32)
    for part in range(2):
        swaps[part].wait()
        total = mine_sum[part] + arrived[part].astype(f32)
        present = tokens_ref[part].astype(f32)
        inverse = lax.rsqrt(jnp.mean(present * present, axis=-1, keepdims=True) + EPSILON)
        unit = present * inverse
        gain_sum = gain_sum + jnp.sum(total * unit, axis=0, keepdims=True)
        scaled = total * gain_one
        back = inverse * (scaled - unit * jnp.mean(scaled * unit, axis=-1, keepdims=True))
        result[part] = (middle_ref[part] + back).astype(low)
    input_moves = to_owners(1, result, input_out)
    for copy in input_moves[:3]:
        copy.start()
    scatter.run(2)

    table_acc[...] = jnp.zeros_like(table_acc)
    groups = BAND * BLOCK // GROUP
    table_units = blocks // 2 * groups // TURNS
    table_acts = scatter.take(len(scatter.queue))

    def table_step(i, carry):
        for k, act in enumerate(table_acts):
            @pl.when(i == (k * table_units) // max(1, len(table_acts)))
            def _(act=act):
                act()
        total = None
        for turn in range(TURNS):
            group = i * TURNS + turn
            block = 2 * (group // groups)
            start = pl.multiple_of((group % groups) * GROUP, GROUP)
            for two in range(2):
                lanes = slice(two * BLOCK, (two + 1) * BLOCK)
                index = bandt[block + two, pl.ds(start, GROUP), :]
                for head in range(heads):
                    found[turn, head * GROUP : (head + 1) * GROUP, lanes] = bias[head, block + two, pl.ds(start, GROUP), :]
                for b in range(buckets):
                    hot[turn, b * GROUP : (b + 1) * GROUP, lanes] = jnp.where(
                        index == jnp.asarray(b, low), jnp.asarray(1, low), jnp.asarray(0, low)
                    )
            part = lax.dot_general(hot[turn], found[turn], LAST, preferred_element_type=f32)
            total = part if total is None else total + part
        table_acc[...] += total
        return carry

    lax.fori_loop(0, table_units, table_step, 0)
    row = lax.broadcasted_iota(jnp.int32, table_acc.shape, 0) % GROUP
    col = lax.broadcasted_iota(jnp.int32, table_acc.shape, 1) % GROUP
    kept = jnp.where(row == col, table_acc[...], 0.0).reshape(buckets, GROUP, heads * GROUP).sum(axis=1)
    bucket = lax.broadcasted_iota(jnp.int32, (buckets, 128), 0)
    head_of = lax.broadcasted_iota(jnp.int32, (buckets, 128), 1)
    table = jnp.zeros((buckets, 128), f32)
    for head in range(heads):
        amount = jnp.sum(kept[:, head * GROUP : (head + 1) * GROUP], axis=1, keepdims=True)
        table = table + jnp.where(head_of == head, amount, 0.0)
    for side, name in enumerate((buckets // 2 - 1, buckets - 1)):
        for head in range(heads):
            amount = jnp.sum(jnp.sum(far[side, head], axis=0, keepdims=True), axis=1, keepdims=True)
            table = table + jnp.where((bucket == name) & (head_of == head), amount, 0.0)

    lines = width // 128
    for i in range(lines):
        small[i : i + 1, :] = gain_sum[:, i * 128 : (i + 1) * 128]
    small[lines : 2 * lines, :] = gain_two_ref[...]
    small[2 * lines : 2 * lines + buckets, :] = table
    small_base = 10

    def small_line(d):
        return near(small_base + 2 + d, hold_z.at[z], hold_z.at[z], place.device(z=place.line(d)))

    move = near(small_base, small, small_x, to_x)
    move.start()
    move.wait()
    hold_x[...] = small[...] + small_x[...]
    move = near(small_base + 1, hold_x, small_y, to_y)
    move.start()
    move.wait()
    hold_z[z] = hold_x[...] + small_y[...]
    for d in range(1, deep):
        small_line(d).start()
    for d in range(1, deep):
        small_line(d).wait()
    hold_y[...] = jnp.sum(hold_z[...], axis=0)
    move = near(small_base + 2, hold_y, small_c, to_c)
    move.start()
    move.wait()
    small_out[0] = hold_y[...]
    small_out[1] = hold_y[...] + small_c[...]

    for copy in input_moves[:3]:
        copy.wait()
    input_moves[3].start()
    input_moves[3].wait()
    output_moves[3].wait()
    scatter.run(len(scatter.queue))
    scatter.sent()


def back(shard_size, pieces, early, buckets, lengths, full, normed_t, qkv, bandt, biast, grads, do, lse, output, middle, tokens, gain_two, table_rows):
    low, f32 = jnp.bfloat16, jnp.float32
    deep = shard_size // 2
    rows = full.shape[3]
    width, length = normed_t.shape
    half, quarter = length // 2, length // 4
    heads, blocks = biast.shape[:2]
    pairs = heads // 2
    inner = pairs * 128
    hidden = (grads.shape[4] - inner) // 3
    count = len(pieces)
    shape = jax.ShapeDtypeStruct
    vmem, hbm = pl.BlockSpec(memory_space=pltpu.VMEM), pl.BlockSpec(memory_space=pl.ANY)
    dma = pltpu.SemaphoreType.DMA
    lines = 2 * (width // 128) + buckets
    buffers = [piece_buffers(piece, deep, rows) for piece in pieces]
    scratch = [pltpu.VMEM(buffer[k], low) for k in range(4) for buffer in buffers]
    small = pltpu.VMEM((lines, 128), f32)
    scratch += [
        pltpu.VMEM((3 * pairs, length, 128), low),
        pltpu.VMEM((width, length), low),
        pltpu.VMEM((blocks, BAND * BLOCK, BLOCK), low),
        pltpu.VMEM((heads, blocks, BAND * BLOCK, BLOCK), low),
        pltpu.VMEM((deep, 2, 2, rows, 3 * inner), low),
        pltpu.VMEM((deep, 2, 2, rows, 128), low),
        pltpu.VMEM((pairs, length, 128), low),
        pltpu.VMEM((length, 256), f32),
        pltpu.VMEM((length, 256), low),
        pltpu.VMEM((2, heads, blocks, BLOCK), f32),
        pltpu.VMEM((length, 128), f32),
        pltpu.VMEM((length, 128), f32),
        pltpu.VMEM((length, 128), low),
        pltpu.VMEM((deep, 2, 2, rows, 3 * inner), low),
        pltpu.VMEM((2, quarter, width), f32),
        pltpu.VMEM((2, quarter, width), low),
        pltpu.VMEM((2, quarter, width), low),
        pltpu.VMEM((2, quarter, width), low),
        pltpu.VMEM((buckets * GROUP, heads * GROUP), f32),
        pltpu.VMEM((TURNS, buckets * GROUP, 2 * BLOCK), low),
        pltpu.VMEM((TURNS, heads * GROUP, 2 * BLOCK), low),
        small, small, small, small, small, pltpu.VMEM((deep, lines, 128), f32), small,
        dma((count,)),
        dma((count, 3, deep - 1)),
        dma((count, 3, deep - 1)),
        dma((12 + deep,)),
        dma((12 + deep,)),
        dma((9,)),
    ]
    return pl.pallas_call(
        functools.partial(back_kernel, shard_size, pieces, early, (inner, hidden, buckets)),
        out_shape=[
            shape((rows, 3 * hidden + inner), f32),
            shape((rows, 3 * inner), f32),
            shape((2, half, width), low),
            shape((2, half, width), low),
            shape((2, lines, 128), f32),
        ],
        in_specs=[pl.BlockSpec(memory_space=pltpu.SMEM)] + [hbm] * 7 + [vmem] * 6,
        out_specs=[vmem, vmem, hbm, hbm, vmem],
        scratch_shapes=scratch,
        compiler_params=pltpu.CompilerParams(
            collective_id=2, has_side_effects=True, vmem_limit_bytes=60 * MIB
        ),
        name="back",
    )(lengths, full, normed_t, qkv, bandt, biast, grads, do, lse, output, middle, tokens, gain_two, table_rows)


ORDERS = ("zyx", "zxy")
SUM_ORDERS = ("xyz", "yxz")
WINDOW = 6
ATTENTION_ACTS = 24


def shards(
    inputs, cotangent, lengths, buckets,
    query_weight, key_weight, value_weight, projection_weight, gate_weight, up_weight, down_weight,
    attention_gain, feedforward_gain, bias_table,
):
    x = lax.axis_index("ctx")
    shard_size = lax.axis_size("shard")
    width = inputs.shape[2]
    bucket_count, heads = bias_table.shape
    rows, inner = query_weight.shape
    hidden = gate_weight.shape[1]
    steps = hidden_steps(hidden)
    at_project = 128 + 3 * inner
    at_hidden = at_project + inner
    pieces = split_columns(0, at_project, 4) + split_columns(at_project, at_hidden, 2)
    for j, n in enumerate(steps):
        at = at_hidden + 3 * HIDDEN_STEP * j
        pieces += split_columns(at, at + 3 * n, 2)
    pieces = [(a, b, ORDERS[i % len(ORDERS)]) for i, (a, b) in enumerate(pieces)]

    gains = jnp.pad(jnp.stack([attention_gain, feedforward_gain], axis=1), ((0, 0), (0, 126)))
    table_rows = jnp.broadcast_to(
        jnp.pad(bias_table.astype(jnp.float32).T, ((0, 0), (0, 128 - bucket_count)))[:, None, :], (heads, 8, 128)
    )
    weights = (query_weight, key_weight, value_weight, projection_weight, gate_weight, up_weight, down_weight)
    (
        full, normed_t, qkv, bandt, biast, grads, grad_attended, tokens,
        lse, output, grad_middle, gain_two,
    ) = front(shard_size, pieces, WINDOW, lengths, gains, weights, inputs, cotangent, buckets, table_rows)

    cuts = [(0, a, b) for a, b in split_columns(0, 3 * hidden + inner, 12)]
    early = len(cuts)
    cuts += [(1, a, b) for t in range(3) for a, b in split_columns(t * inner, (t + 1) * inner, 1)]
    cuts = [(t, a, b, SUM_ORDERS[i % len(SUM_ORDERS)]) for i, (t, a, b) in enumerate(cuts)]
    gain_two = jnp.sum(gain_two, axis=(0, 1)).reshape(-1, 128)
    hidden_sums, weight_sums, output, input_grad, small = back(
        shard_size, cuts, early, bucket_count,
        lengths, full, normed_t, qkv, bandt, biast, grads, grad_attended,
        lse, output, grad_middle, tokens, gain_two, table_rows,
    )
    at = [3 * HIDDEN_STEP * j for j in range(len(steps))]
    gate, up, down = [
        jnp.concatenate([hidden_sums[:, a + k * n : a + (k + 1) * n] for a, n in zip(at, steps)], axis=1) for k in range(3)
    ]
    lines = width // 128
    me = lax.axis_index("shard") * 2 + x

    def own_gain(part):
        return lax.dynamic_slice_in_dim(small[1, part * lines : (part + 1) * lines].reshape(-1), me * rows, rows)

    return (
        output, input_grad.astype(jnp.float32),
        weight_sums[:, :inner], weight_sums[:, inner : 2 * inner], weight_sums[:, 2 * inner :], hidden_sums[:, 3 * hidden :],
        gate, up, down, own_gain(0), own_gain(1), small[0, 2 * lines :, :heads],
    )


def solution(mesh):
    rows = P(None, ("shard", "ctx"), None)
    weight = P(("shard", "ctx"), "tp")
    gain = P(("shard", "ctx"))
    table = P(None, "tp")
    return jax.shard_map(
        shards,
        mesh=mesh,
        in_specs=(rows, rows, P(None, "shard"), P("ctx", None)) + (weight,) * 7 + (gain, gain, table),
        out_specs=(rows, rows) + (weight,) * 7 + (gain, gain, table),
        check_vma=False,
    )
```

```python
import functools

import jax
import jax.numpy as jnp
from jax import lax
from jax.experimental import pallas as pl
from jax.experimental.pallas import tpu as pltpu
from jax.sharding import PartitionSpec as P

EPSILON = 1e-06
GELU_ROOT = 0.7978845608028654
GELU_CUBIC = 0.044715
MESH = pl.DeviceIdType.MESH
MIB = 1024 * 1024


BAND = 3
BLOCK = 128


def lane_head(rows, width, which):
    lanes = lax.broadcasted_iota(jnp.int32, (rows, width), 1)
    half = width // 2
    return (lanes < half) if which == 0 else (lanes >= half)


def band_start(row_block, blocks):
    return jnp.clip(row_block - 1, 0, blocks - BAND)


def split_columns(start, stop, pieces):
    tiles = (stop - start) // 128
    edges = [start + 128 * (tiles * i // pieces) for i in range(pieces + 1)]
    return [(a, b) for a, b in zip(edges, edges[1:]) if b > a]


class Place:
    def __init__(self, shard_size):
        self.deep = shard_size // 2
        shard = lax.axis_index("shard")
        self.z = shard // 2
        self.y = shard % 2
        self.x = lax.axis_index("ctx")
        self.c = lax.axis_index("tp")

    def device(self, z=None, y=None, x=None, c=None):
        z = self.z if z is None else z
        y = self.y if y is None else y
        x = self.x if x is None else x
        c = self.c if c is None else c
        return (z * 2 + y, x, c)

    def line(self, distance):
        return (self.z + distance) % self.deep

    def peers(self):
        others = [self.device(z=self.line(d)) for d in range(1, self.deep)]
        return others + [self.device(y=1 - self.y), self.device(x=1 - self.x), self.device(c=1 - self.c)]


def meet(place):
    barrier = pltpu.get_barrier_semaphore()
    peers = place.peers()
    for peer in peers:
        pl.semaphore_signal(barrier, inc=1, device_id=peer, device_id_type=MESH)
    pl.semaphore_wait(barrier, len(peers))


def send(source, target, send_sem, recv_sem, device):
    return pltpu.make_async_remote_copy(
        src_ref=source, dst_ref=target, send_sem=send_sem, recv_sem=recv_sem, device_id=device, device_id_type=MESH
    )


LAST = (((1,), (1,)), ((), ()))
FIRST = (((0,), (0,)), ((), ()))
HIDDEN_STEP = 256
HALF_BUCKETS = 16


def hidden_steps(hidden):
    return [min(HIDDEN_STEP, hidden - at) for at in range(0, hidden, HIDDEN_STEP)]


class Gather:
    def __init__(self, place, pieces, own_ref, full_ref, send_sem, recv_sem):
        self.place, self.pieces, self.own, self.full = place, pieces, own_ref, full_ref
        self.send_sem, self.recv_sem = send_sem, recv_sem
        self.queue = []

    def held(self, piece, hop):
        a, b, order = self.pieces[piece]
        place, done = self.place, order[:hop]
        at = [slice(None) if name in done else getattr(place, name) for name in "zyx"]
        return self.full.at[at[0], at[1], at[2], :, a:b]

    def copies(self, piece, hop):
        place = self.place
        a, b, order = self.pieces[piece]
        target = self.held(piece, hop)
        source = self.own.at[:, a:b] if hop == 0 else target
        name = order[hop]
        if name == "z":
            peers = [place.device(z=place.line(d)) for d in range(1, place.deep)]
        elif name == "y":
            peers = [place.device(y=1 - place.y)]
        else:
            peers = [place.device(x=1 - place.x)]
        return [
            send(source, target, self.send_sem.at[piece, hop, i], self.recv_sem.at[piece, hop, i], peer)
            for i, peer in enumerate(peers)
        ]

    def start(self, piece, hop):
        for copy in self.copies(piece, hop):
            copy.start()

    def arrive(self, piece, hop):
        for copy in self.copies(piece, hop):
            copy.wait_recv()

    def sent(self):
        for piece in range(len(self.pieces)):
            for hop in range(3):
                for copy in self.copies(piece, hop):
                    copy.wait_send()

    def plan(self, window):
        count = len(self.pieces)
        self.window = window

        def second(piece):
            def act():
                self.arrive(piece, 0)
                self.start(piece, 1)
                if piece + window < count:
                    self.start(piece + window, 0)
            return act

        def third(piece):
            def act():
                self.arrive(piece, 1)
                self.start(piece, 2)
            return act

        turned = 0
        for piece in range(count + LAG):
            if piece < count:
                self.queue.append((None, second(piece)))
            while turned < count and turned <= piece - (1 if turned < QUICK else LAG):
                self.queue.append((turned, third(turned)))
                turned += 1
        for piece in range(min(window, count)):
            self.start(piece, 0)

    def run(self, steps):
        for _ in range(min(steps, len(self.queue))):
            self.queue.pop(0)[1]()

    def take(self, steps):
        taken, self.queue = self.queue[:steps], self.queue[steps:]
        return [act for _, act in taken]

    def need(self, pieces):
        for piece in pieces:
            while any(mark == piece for mark, _ in self.queue):
                self.run(1)
        self.run(AHEAD)
        for piece in pieces:
            self.arrive(piece, 2)


def query_aux(table, step, blocks):
    parts = []
    lanes = lax.broadcasted_iota(jnp.int32, (BLOCK, 128), 1)
    buckets = 2 * HALF_BUCKETS
    below = jnp.broadcast_to(table[0:1, HALF_BUCKETS - 1 : HALF_BUCKETS], (BLOCK, 128))
    above = jnp.broadcast_to(table[0:1, buckets - 1 : buckets], (BLOCK, 128))
    for sub in range(2):
        start = band_start(2 * step + sub, blocks)
        value = jnp.where(lanes < start, below, 0.0)
        value = jnp.where((lanes >= start + BAND) & (lanes < blocks), above, value)
        parts.append(jnp.where(lanes == blocks, 1.0, value))
    return jnp.concatenate(parts, axis=0).astype(jnp.bfloat16)


def between(acts, units, skip, unit, head):
    slots = 2 * units - skip
    for k, act in enumerate(acts):
        slot = skip + (k * slots) // len(acts)
        if slot % 2 == head:
            pl.when(unit == slot // 2)(act)


def gelu_all(gate):
    square = gate * gate
    tangent = jnp.tanh(GELU_ROOT * (gate + GELU_CUBIC * square * gate))
    value = 0.5 * gate * (1.0 + tangent)
    slope = 0.5 * (1.0 + tangent) + 0.5 * gate * (1.0 - tangent * tangent) * (
        GELU_ROOT + (3.0 * GELU_CUBIC * GELU_ROOT) * square
    )
    return value, slope


def front_kernel(
    shard_size, pieces, window, sizes,
    lengths_ref, gains_ref, query_ref, key_ref, value_ref, project_ref, gate_ref, up_ref, down_ref,
    inputs_ref, cots_ref, buckets_ref, table_ref,
    full_ref, normed_out, qkv_out, bandt_out, biast_out, grads_out, attended_out, tokens_own_ref,
    lse_ref, output_ref, middle_grad_ref, gain_ref,
    own_ref, tok, cot, band_raw, band, bandt, bias, biast, kaux, gain_buf, qkv, normed, scores, attended, project_w,
    normal, away, arrived, two_t, low_t, acc_out, acc_two, w_buf, g_buf, hid, ggate, gup,
    send_sem, recv_sem, near_send, near_recv, local_sem, w_sem, g_sem, own_sem, bt_sem,
):
    inner, hidden = sizes
    length, width = tok.shape
    half, quarter = length // 2, length // 4
    heads, blocks = bias.shape[:2]
    pairs = heads // 2
    deep = shard_size // 2
    low = jnp.bfloat16
    place = Place(shard_size)
    x, c = place.x, place.c
    at_q = 128
    at_project = at_q + 3 * inner
    at_hidden = at_project + inner
    steps = hidden_steps(hidden)
    per_step = 2
    first_hidden_piece = len(pieces) - per_step * len(steps)
    project_pieces = [i for i, (a, b, _) in enumerate(pieces) if at_project <= a < at_hidden]
    qkv_pieces = [i for i, (a, b, _) in enumerate(pieces) if a < at_project]

    def own_load(i, source, target):
        return pltpu.make_async_copy(source, target, local_sem.at[i])

    parts, at = [], 0
    for ref in (gains_ref, query_ref, key_ref, value_ref, project_ref):
        parts.append((ref, at))
        at += ref.shape[1]
    own_loads = [
        pltpu.make_async_copy(ref, own_ref.at[:, at : at + ref.shape[1]], own_sem.at[i]) for i, (ref, at) in enumerate(parts)
    ]
    for j, n in enumerate(steps):
        for k, ref in enumerate((gate_ref, up_ref, down_ref)):
            at = at_hidden + 3 * HIDDEN_STEP * j + k * n
            own_loads.append(
                pltpu.make_async_copy(
                    ref.at[:, HIDDEN_STEP * j : HIDDEN_STEP * j + n], own_ref.at[:, at : at + n], own_sem.at[len(own_loads)]
                )
            )

    def band_source(block):
        start = pl.multiple_of(band_start(block, blocks) * BLOCK, BLOCK)
        first = block - x * (blocks // 2)
        return buckets_ref.at[pl.ds(pl.multiple_of(first * BLOCK, BLOCK), BLOCK), pl.ds(start, BAND * BLOCK)]

    own_tok = own_load(0, inputs_ref.at[x], tok.at[pl.ds(x * half, half)])
    own_cot = own_load(1, cots_ref.at[x], cot.at[pl.ds(x * half, half)])
    own_bands = [
        own_load(13 + i, band_source(x * (blocks // 2) + i), band_raw.at[i]) for i in range(blocks // 2)
    ]
    own_full = own_load(3, own_ref, full_ref.at[place.z, place.y, x])
    for copy in (*own_loads, *own_bands, own_tok, own_cot):
        copy.start()
    meet(place)
    for copy in own_loads:
        copy.wait()
    own_full.start()

    gather = Gather(place, pieces, own_ref, full_ref, send_sem, recv_sem)
    to_x, to_c = place.device(x=1 - x), place.device(c=1 - c)

    def x_rows(sender_x, sender_c):
        return pl.ds(sender_x * half + sender_c * quarter, quarter)

    def near(i, source, target, device):
        return send(source, target, near_send.at[i], near_recv.at[i], device)

    mine = [x * (blocks // 2) + c * (blocks // 4) + i for i in range(blocks // 4)]
    theirs = [(1 - x) * (blocks // 2) + c * (blocks // 4) + i for i in range(blocks // 4)]
    band_x = [near(16 + i, band.at[block], band.at[block], to_x) for i, block in enumerate(mine)]
    tok_x = near(1, inputs_ref.at[1 - x, pl.ds(c * quarter, quarter)], tok.at[x_rows(x, c)], to_x)
    cot_x = near(2, cots_ref.at[1 - x, pl.ds(c * quarter, quarter)], cot.at[x_rows(x, c)], to_x)
    band_c = [near(16 + len(mine) + i, band.at[block], band.at[block], to_c) for i, block in enumerate(theirs)]
    tok_c = near(4, tok.at[x_rows(1 - x, c)], tok.at[x_rows(1 - x, c)], to_c)
    cot_c = near(5, cot.at[x_rows(1 - x, c)], cot.at[x_rows(1 - x, c)], to_c)
    gather.plan(window)
    for copy in own_bands:
        copy.wait()
    for i in range(blocks // 2):
        band[x * (blocks // 2) + i] = band_raw[i].astype(jnp.float32).astype(low)
    for copy in band_x:
        copy.start()
    tok_x.start()
    own_full.wait()
    lanes_of = lax.broadcasted_iota(jnp.int32, (length, 128), 1)
    rows_of = lax.broadcasted_iota(jnp.int32, (length, 128), 0)
    valid = lengths_ref[x, 0]
    blocked = jnp.where(rows_of // BLOCK == lanes_of, 1.0, 0.0)
    kaux[...] = jnp.where((lanes_of == blocks) & (rows_of >= valid), -1e30, blocked).astype(low)
    gather.run(1)
    for copy in band_x:
        copy.wait()
    for copy in band_c:
        copy.start()
    gather.run(1)
    for copy in band_c:
        copy.wait()

    def bias_step(i, carry):
        block = i // (BLOCK // 16)
        at = pl.multiple_of((i % (BLOCK // 16)) * 16, 16)
        index = band[block, pl.ds(at, 16), :].astype(jnp.float32).astype(jnp.int32)
        for col in range(BAND):
            lanes = slice(col * BLOCK, (col + 1) * BLOCK)
            for head in range(heads):
                table = table_ref[head]
                got = [jnp.take_along_axis(table, index[8 * k : 8 * k + 8, lanes], axis=1) for k in range(2)]
                bias[head, block, pl.ds(at, 16), lanes] = jnp.concatenate(got, axis=0).astype(low)
        return carry

    bias_steps = blocks * (BLOCK // 16)
    for k in range(4):
        lax.fori_loop(bias_steps * k // 4, bias_steps * (k + 1) // 4, bias_step, 0)
        gather.run(1)
    tok_x.wait()
    tok_c.start()
    cot_x.start()

    def biast_store(block, slot):
        return pltpu.make_async_copy(biast.at[slot], biast_out.at[:, block], bt_sem.at[slot])

    def biast_block(block, carry):
        slot = block % 2

        @pl.when(block > 1)
        def _():
            biast_store(block - 2, slot).wait()

        bandt[block] = jnp.transpose(band[block].astype(jnp.float32)).astype(low)

        def inner_step(i, carry):
            at = pl.multiple_of(i * 16, 16)
            index = bandt[block, pl.ds(at, 16), :].astype(jnp.float32).astype(jnp.int32)
            for head in range(heads):
                got = [jnp.take_along_axis(table_ref[head], index[8 * k : 8 * k + 8], axis=1) for k in range(2)]
                biast[slot, head, pl.ds(at, 16), :] = jnp.concatenate(got, axis=0).astype(low)
            return carry

        lax.fori_loop(0, BAND * BLOCK // 16, inner_step, 0)
        biast_store(block, slot).start()
        return carry

    for k in range(4):
        lax.fori_loop(blocks * k // 4, blocks * (k + 1) // 4, biast_block, 0)
        gather.run(1)
    biast_store(blocks - 2, 0).wait()
    biast_store(blocks - 1, 1).wait()
    bandt_store = own_load(4, bandt, bandt_out)
    bandt_store.start()
    own_tok.wait()
    tok_c.wait()

    def live_step(i, carry):
        rows = pl.ds(pl.multiple_of(i * BLOCK, BLOCK), BLOCK)
        here = lax.broadcasted_iota(jnp.int32, (BLOCK, width), 0) + i * BLOCK < valid
        masked = jnp.where(here, cot[rows, :].astype(jnp.float32), 0.0).astype(low)
        cot[rows, :] = masked
        low_t[:, rows] = jnp.transpose(masked)
        return carry

    gather.need(qkv_pieces)
    load_gains = own_load(5, full_ref.at[:, :, :, :, 0:at_q], gain_buf)
    third = 3 * inner // 2
    loads_wide = [
        pltpu.make_async_copy(
            full_ref.at[:, :, :, :, at_q + third * k : at_q + third * (k + 1)], w_buf.at[k, :, :, :, :, 0:third], w_sem.at[k]
        )
        for k in range(2)
    ]
    for copy in (load_gains, *loads_wide):
        copy.start()
    load_gains.wait()
    gains = jnp.transpose(gain_buf[...].reshape(width, 128).astype(jnp.float32))
    gain_one, gain_two = gains[0:1, :], gains[1:2, :]

    def norm_step(i, carry):
        rows = pl.ds(pl.multiple_of(i * BLOCK, BLOCK), BLOCK)
        present = tok[rows, :].astype(jnp.float32)
        inverse = lax.rsqrt(jnp.mean(present * present, axis=-1, keepdims=True) + EPSILON)
        got = (present * inverse * gain_one).astype(low)
        normed[rows, :] = got
        two_t[:, rows] = jnp.transpose(got)
        return carry

    lax.fori_loop(0, blocks, norm_step, 0)
    normed_store = own_load(6, two_t, normed_out)
    normed_store.start()
    for copy in loads_wide:
        copy.wait()
    gather.run(2)

    for col in range(3 * pairs // 2):
        slot, at = 256 * col // third, 256 * col % third
        lanes = slice(at, at + 256)

        def qkv_step(i, carry):
            rows = pl.ds(pl.multiple_of(i * 256, 256), 256)
            got = jnp.dot(
                normed[rows, :], w_buf[slot, :, :, :, :, lanes].reshape(width, 256), preferred_element_type=jnp.float32
            ).astype(low)
            qkv[2 * col, rows, :] = got[:, :128]
            qkv[2 * col + 1, rows, :] = got[:, 128:]
            return carry

        lax.fori_loop(0, length // 256, qkv_step, 0)
        if col % 2:
            gather.run(1)
    qkv_store = own_load(7, qkv, qkv_out)
    qkv_store.start()

    units = pairs * (length // 256)
    acts = gather.take(min(len(gather.queue), FORWARD_ACTS))

    def unit_step(unit, carry):
        pair = unit // (length // 256)
        step = unit % (length // 256)
        rows = pl.ds(pl.multiple_of(step * 256, 256), 256)
        queries = qkv[pair, rows, :]
        keys = jnp.concatenate([qkv[pairs + pair], kaux[...]], axis=1)
        outs = []
        for head in range(2):
            between(acts, units, 0, unit, head)
            aux = query_aux(table_ref[2 * pair + head], step, blocks)
            masked = jnp.where(lane_head(256, 128, head), queries, jnp.zeros_like(queries))
            scores[...] = lax.dot_general(
                jnp.concatenate([masked, aux], axis=1), keys, LAST, preferred_element_type=jnp.float32
            )
            for sub in range(2):
                start = pl.multiple_of(band_start(step * 2 + sub, blocks) * BLOCK, BLOCK)
                scores[sub * BLOCK : (sub + 1) * BLOCK, pl.ds(start, BAND * BLOCK)] += bias[
                    2 * pair + head, 2 * step + sub
                ].astype(jnp.float32)
            got = scores[...]
            highest = jnp.max(got, axis=1, keepdims=True)
            exponent = jnp.exp(got - highest)
            total = jnp.sum(exponent, axis=1, keepdims=True)
            outs.append(
                jnp.dot(exponent.astype(low), qkv[2 * pairs + pair], preferred_element_type=jnp.float32) * (1.0 / total)
            )
            lse = jnp.broadcast_to(highest + jnp.log(total), (256, 128))
            lse_ref[pair, step, head : head + 1, :] = jnp.transpose(lse)[0:1, :]
        attended[pair, rows, :] = jnp.where(lane_head(256, 128, 0), outs[0], outs[1]).astype(low)
        return carry

    lax.fori_loop(0, units, unit_step, 0)
    own_cot.wait()
    cot_x.wait()
    cot_c.start()

    normed_store.wait()
    two = normed
    gather.need(project_pieces)
    load_project = own_load(9, full_ref.at[:, :, :, :, at_project:at_hidden], project_w)
    load_project.start()
    load_project.wait()

    def branch(rows):
        left = jnp.concatenate([attended[pair, rows, :] for pair in range(pairs)], axis=1)
        return lax.dot_general(left, project_w[...].reshape(width, inner), LAST, preferred_element_type=jnp.float32)

    def part_rows(part, core):
        return pl.ds(pl.multiple_of(part * half + core * quarter, quarter), quarter)

    def swap_part(i, part, slot=0):
        return near(i + part, away.at[slot + part], arrived.at[slot + part], to_c)

    for part in range(2):
        away[part] = branch(part_rows(part, 1 - c)).astype(low)
        swap_part(6, part).start()
    for part in range(2):
        normal[part] = branch(part_rows(part, c)) + tok[part_rows(part, c), :].astype(jnp.float32)

    def share(i, part, buffer):
        return near(i + part, buffer.at[part_rows(part, c)], buffer.at[part_rows(part, c)], to_c)

    tokens_store = [own_load(11 + part, tok.at[part_rows(part, c)], tokens_own_ref.at[part]) for part in range(2)]
    for copy in tokens_store:
        copy.start()
    for part in range(2):
        swap_part(6, part).wait()
        middle = normal[part] + arrived[part].astype(jnp.float32)
        normal[part] = middle
        inverse = lax.rsqrt(jnp.mean(middle * middle, axis=-1, keepdims=True) + EPSILON)
        two[part_rows(part, c), :] = (middle * inverse * gain_two).astype(low)
        share(8, part, two).start()
    gather.run(1)
    for part in range(2):
        share(8, part, two).wait()

    def turn_step(i, carry):
        rows = pl.ds(pl.multiple_of(i * BLOCK, BLOCK), BLOCK)
        two_t[:, rows] = jnp.transpose(two[rows, :])
        return carry

    lax.fori_loop(0, blocks, turn_step, 0)
    gather.run(1)
    cot_c.wait()
    lax.fori_loop(0, blocks, live_step, 0)
    gather.run(1)

    def bounds(j):
        at = at_hidden + 3 * HIDDEN_STEP * j
        return at, at + 3 * steps[j]

    def load_step(j):
        a, b = bounds(j)
        return pltpu.make_async_copy(
            full_ref.at[:, :, :, :, a:b], w_buf.at[j % 2, :, :, :, :, 0 : b - a], w_sem.at[j % 2]
        )

    def store_step(j):
        a, b = bounds(j)
        return pltpu.make_async_copy(
            g_buf.at[j % 2, :, :, :, :, 0 : b - a],
            grads_out.at[:, :, :, :, a - at_hidden : b - at_hidden],
            g_sem.at[j % 2],
        )

    gather.need(range(first_hidden_piece, first_hidden_piece + per_step))
    load_step(0).start()
    for j, units_here in enumerate(steps):
        n = units_here
        slot = j % 2
        load_step(j).wait()

        def weight(k, slot=slot, n=n):
            return w_buf[slot, :, :, :, :, k * n : (k + 1) * n].reshape(width, n)

        def rows_step(i, carry, j=j, n=n, weight=weight):
            rows = pl.ds(pl.multiple_of(i * 256, 256), 256)
            left, grad = two[rows, :], cot[rows, :]
            gate = jnp.dot(left, weight(0), preferred_element_type=jnp.float32)
            up = jnp.dot(left, weight(1), preferred_element_type=jnp.float32)
            grad_hidden = jnp.dot(grad, weight(2), preferred_element_type=jnp.float32)
            value, slope = gelu_all(gate)
            hid[rows, 0:n] = (value * up).astype(low)
            ggate[rows, 0:n] = (grad_hidden * up * slope).astype(low)
            gup[rows, 0:n] = (grad_hidden * value).astype(low)
            out = lax.dot_general(hid[rows, 0:n], weight(2), LAST, preferred_element_type=jnp.float32)
            back = lax.dot_general(ggate[rows, 0:n], weight(0), LAST, preferred_element_type=jnp.float32)
            back = back + lax.dot_general(gup[rows, 0:n], weight(1), LAST, preferred_element_type=jnp.float32)
            if j == 0:
                acc_out[rows, :] = out
                acc_two[rows, :] = back
            else:
                acc_out[rows, :] += out
                acc_two[rows, :] += back
            return carry

        lax.fori_loop(0, length // 256, rows_step, 0)
        gather.run(1)
        if j + 1 < len(steps):
            first = first_hidden_piece + per_step * (j + 1)
            gather.need(range(first, first + per_step))
            load_step(j + 1).start()
        if j > 1:
            store_step(j - 2).wait()

        tiles = width // 256

        def grads_step(i, carry, slot=slot, n=n):
            rows = pl.ds(pl.multiple_of(i * 256, 256), 256)
            for k, (left, right) in enumerate(((two_t, ggate), (two_t, gup), (low_t, hid))):
                got = jnp.dot(left[rows, :], right[:, 0:n], preferred_element_type=jnp.float32).astype(low)
                span = deep // tiles
                g_buf[slot, pl.ds(i * span, span), :, :, :, k * n : (k + 1) * n] = got.reshape(
                    (span,) + g_buf.shape[2:5] + (n,)
                )
            return carry

        lax.fori_loop(0, tiles, grads_step, 0)
        store_step(j).start()
    gather.run(len(gather.queue))

    def share_sum(i, acc, slot):
        for part in range(2):
            away[slot + part] = acc[part_rows(part, 1 - c), :].astype(low)
            swap_part(i, part, slot).start()

    share_sum(10, acc_two, 0)
    for part in range(2):
        swap_part(10, part).wait()
        grad_two = acc_two[part_rows(part, c), :] + arrived[part].astype(jnp.float32)
        middle = normal[part]
        inverse = lax.rsqrt(jnp.mean(middle * middle, axis=-1, keepdims=True) + EPSILON)
        unit = middle * inverse
        weighted = jnp.sum((grad_two * unit).reshape(quarter // 8, 8, width), axis=0)
        gain_ref[part] = weighted
        scaled = grad_two * gain_two
        grad_middle = cot[part_rows(part, c), :].astype(jnp.float32) + inverse * (
            scaled - unit * jnp.mean(scaled * unit, axis=-1, keepdims=True)
        )
        middle_grad_ref[part] = grad_middle
        two[part_rows(part, c), :] = grad_middle.astype(low)
        share(12, part, two).start()
    share_sum(14, acc_out, 2)
    for part in range(2):
        swap_part(14, part, 2).wait()
        output_ref[part] = (normal[part] + acc_out[part_rows(part, c), :] + arrived[2 + part].astype(jnp.float32)).astype(low)
    for part in range(2):
        share(12, part, two).wait()
    for j in range(max(0, len(steps) - 2), len(steps)):
        store_step(j).wait()

    lax.fori_loop(0, blocks, turn_step, 0)

    def project_step(i, carry):
        rows = pl.ds(pl.multiple_of(i * 256, 256), 256)
        right = jnp.concatenate([attended[pair] for pair in range(pairs)], axis=1)
        got = jnp.dot(two_t[rows, :], right, preferred_element_type=jnp.float32).astype(low)
        span = deep // (width // 256)
        g_buf[0, pl.ds(i * span, span), :, :, :, 0:inner] = got.reshape((span,) + g_buf.shape[2:5] + (inner,))
        return carry

    lax.fori_loop(0, width // 256, project_step, 0)
    project_store = own_load(8, g_buf.at[0, :, :, :, :, 0:inner], grads_out.at[:, :, :, :, 3 * hidden : 3 * hidden + inner])
    project_store.start()

    def attended_step(i, carry):
        rows = pl.ds(pl.multiple_of(i * 256, 256), 256)
        got = jnp.dot(two[rows, :], project_w[...].reshape(width, inner), preferred_element_type=jnp.float32).astype(low)
        for pair in range(pairs):
            attended[pair, rows, :] = got[:, pair * 128 : (pair + 1) * 128]
        return carry

    lax.fori_loop(0, length // 256, attended_step, 0)
    attended_store = own_load(10, attended, attended_out)
    attended_store.start()
    for copy in (bandt_store, qkv_store, attended_store, project_store, *tokens_store):
        copy.wait()
    gather.sent()


def front(shard_size, pieces, window, lengths, gains, weights, inputs, cots, buckets, table_rows):
    low, f32 = jnp.bfloat16, jnp.float32
    deep = shard_size // 2
    rows, inner = weights[0].shape
    hidden = weights[4].shape[1]
    wide = pieces[-1][1]
    half, width = inputs.shape[1:]
    length, quarter = 2 * half, half // 2
    heads = table_rows.shape[0]
    blocks = length // BLOCK
    pairs = heads // 2
    shape = jax.ShapeDtypeStruct
    vmem, hbm = pl.BlockSpec(memory_space=pltpu.VMEM), pl.BlockSpec(memory_space=pl.ANY)
    dma = pltpu.SemaphoreType.DMA
    count = len(pieces)
    step = HIDDEN_STEP
    out_shape = [
        shape((deep, 2, 2, rows, wide), low),
        shape((width, length), low),
        shape((3 * pairs, length, 128), low),
        shape((blocks, BAND * BLOCK, BLOCK), low),
        shape((heads, blocks, BAND * BLOCK, BLOCK), low),
        shape((deep, 2, 2, rows, 3 * hidden + inner), low),
        shape((pairs, length, 128), low),
        shape((2, quarter, width), low),
        shape((pairs, length // 256, 2, 256), f32),
        shape((2, quarter, width), low),
        shape((2, quarter, width), f32),
        shape((2, 8, width), f32),
    ]
    scratch = [
        pltpu.VMEM((rows, wide), low),
        pltpu.VMEM((length, width), low),
        pltpu.VMEM((length, width), low),
        pltpu.VMEM((blocks // 2, BLOCK, BAND * BLOCK), jnp.int32),
        pltpu.VMEM((blocks, BLOCK, BAND * BLOCK), low),
        pltpu.VMEM((blocks, BAND * BLOCK, BLOCK), low),
        pltpu.VMEM((heads, blocks, BLOCK, BAND * BLOCK), low),
        pltpu.VMEM((2, heads, BAND * BLOCK, BLOCK), low),
        pltpu.VMEM((length, 128), low),
        pltpu.VMEM((deep, 2, 2, rows, 128), low),
        pltpu.VMEM((3 * pairs, length, 128), low),
        pltpu.VMEM((length, width), low),
        pltpu.VMEM((256, length), f32),
        pltpu.VMEM((pairs, length, 128), low),
        pltpu.VMEM((deep, 2, 2, rows, inner), low),
        pltpu.VMEM((2, quarter, width), f32),
        pltpu.VMEM((4, quarter, width), low),
        pltpu.VMEM((4, quarter, width), low),
        pltpu.VMEM((width, length), low),
        pltpu.VMEM((width, length), low),
        pltpu.VMEM((length, width), f32),
        pltpu.VMEM((length, width), f32),
        pltpu.VMEM((2, deep, 2, 2, rows, 3 * step), low),
        pltpu.VMEM((2, deep, 2, 2, rows, 3 * step), low),
        pltpu.VMEM((length, step), low),
        pltpu.VMEM((length, step), low),
        pltpu.VMEM((length, step), low),
        dma((count, 3, deep - 1)),
        dma((count, 3, deep - 1)),
        dma((16 + blocks // 2,)),
        dma((16 + blocks // 2,)),
        dma((13 + blocks // 2,)),
        dma((2,)),
        dma((2,)),
        dma((5 + 3 * len(hidden_steps(hidden)),)),
        dma((2,)),
    ]
    return pl.pallas_call(
        functools.partial(front_kernel, shard_size, pieces, window, (inner, hidden)),
        out_shape=out_shape,
        in_specs=[pl.BlockSpec(memory_space=pltpu.SMEM)] + [hbm] * 11 + [vmem],
        out_specs=[hbm] * 8 + [vmem] * 4,
        scratch_shapes=scratch,
        compiler_params=pltpu.CompilerParams(
            collective_id=1, has_side_effects=True, vmem_limit_bytes=60 * MIB
        ),
        name="front",
    )(lengths, gains, *weights, inputs, cots, buckets, table_rows)


GROUP = 16
TURNS = 4


class Scatter:
    def __init__(self, place, pieces, sources, outs, buffers, sems):
        self.place, self.pieces, self.sources, self.outs = place, pieces, sources, outs
        self.first, self.own, self.second, self.third = buffers
        self.own_sem, self.send_sem, self.recv_sem = sems
        self.queue = []

    def peer(self, name):
        place = self.place
        return place.device(y=1 - place.y) if name == "y" else place.device(x=1 - place.x)

    def rest(self, piece):
        order = self.pieces[piece][3]
        return [name for name in "zyx" if name != order[0]]

    def cut(self, piece, name, value):
        t, a, b = self.pieces[piece][:3]
        at = [value if name == other else slice(None) for other in "zyx"]
        if t:
            return self.sources[1].at[t - 1, at[0], at[1], at[2]]
        return self.sources[0].at[at[0], at[1], at[2], :, a:b]

    def own_copy(self, piece):
        order = self.pieces[piece][3]
        return pltpu.make_async_copy(
            self.cut(piece, order[0], getattr(self.place, order[0])), self.own[piece], self.own_sem.at[piece]
        )

    def copies(self, piece, hop):
        place, order = self.place, self.pieces[piece][3]
        name, rest = order[hop], self.rest(piece)
        own, made = self.own[piece], []

        def at(**index):
            return tuple(index[n] if n in index else slice(None) for n in rest)

        def add(source, target, device):
            i = len(made)
            made.append(send(source, target, self.send_sem.at[piece, hop, i], self.recv_sem.at[piece, hop, i], device))

        if hop == 0:
            if name == "z":
                for d in range(1, place.deep):
                    z = place.line(d)
                    add(self.cut(piece, "z", z), self.first[piece].at[d - 1], place.device(z=z))
            else:
                add(self.cut(piece, name, 1 - getattr(place, name)), self.first[piece], self.peer(name))
            return made
        fixed = {} if hop == 1 else {order[1]: getattr(place, order[1])}
        buffer = self.second[piece] if hop == 1 else self.third[piece]
        if name == "z":
            for d in range(1, place.deep):
                z = place.line(d)
                add(own.at[at(z=z, **fixed)], buffer.at[d - 1], place.device(z=z))
        else:
            add(own.at[at(**{name: 1 - getattr(place, name)}, **fixed)], buffer, self.peer(name))
        return made

    def start(self, piece, hop):
        for copy in self.copies(piece, hop):
            copy.start()

    def arrive(self, piece, hop):
        for copy in self.copies(piece, hop):
            copy.wait_recv()

    def begin(self, piece):
        self.start(piece, 0)
        self.own_copy(piece).start()

    def add_first(self, piece):
        order = self.pieces[piece][3]
        self.arrive(piece, 0)
        self.own_copy(piece).wait()
        if piece + self.window < self.early:
            self.begin(piece + self.window)
        own, came = self.own[piece], self.first[piece]
        inner = own.shape[1]

        def body(i, carry):
            for k in range(inner):
                if order[0] == "z":
                    total = own[i, k].astype(jnp.float32)
                    for d in range(came.shape[0]):
                        total = total + came[d, i, k].astype(jnp.float32)
                    own[i, k] = total.astype(jnp.bfloat16)
                else:
                    own[i, k] = own[i, k] + came[i, k]
            return carry

        lax.fori_loop(0, own.shape[0], body, 0)
        self.start(piece, 1)

    def add_second(self, piece):
        place, order = self.place, self.pieces[piece][3]
        name, rest = order[1], self.rest(piece)
        self.arrive(piece, 1)
        own, came = self.own[piece], self.second[piece]
        mine = getattr(place, name)
        spans = own.shape[1] if rest[0] == name else own.shape[0]

        def body(i, carry):
            if name == "z":
                total = own[mine, i].astype(jnp.float32)
                for d in range(came.shape[0]):
                    total = total + came[d, i].astype(jnp.float32)
                own[mine, i] = total.astype(jnp.bfloat16)
            elif rest[0] == name:
                own[mine, i] = own[mine, i] + came[i]
            else:
                own[i, mine] = own[i, mine] + came[i]
            return carry

        lax.fori_loop(0, spans, body, 0)
        self.start(piece, 2)

    def add_third(self, piece):
        place, order = self.place, self.pieces[piece][3]
        rest = self.rest(piece)
        self.arrive(piece, 2)
        total = self.own[piece][getattr(place, rest[0]), getattr(place, rest[1])].astype(jnp.float32)
        if order[2] == "z":
            for d in range(1, place.deep):
                total = total + self.third[piece][d - 1].astype(jnp.float32)
        else:
            total = total + self.third[piece][...].astype(jnp.float32)
        for out, start, at, n in self.pieces[piece][4]:
            self.outs[out][:, start : start + n] = total[:, at : at + n]

    def plan(self, window, early):
        self.window, self.early = window, early
        count = len(self.pieces)
        for i in range(count + SUM_LAGS[1]):
            if i < count:
                self.queue.append(functools.partial(self.add_first, i))
            if 0 <= i - SUM_LAGS[0] < count:
                self.queue.append(functools.partial(self.add_second, i - SUM_LAGS[0]))
            if 0 <= i - SUM_LAGS[1] < count:
                self.queue.append(functools.partial(self.add_third, i - SUM_LAGS[1]))
        for i in range(min(window, early)):
            self.begin(i)

    def run(self, steps):
        for _ in range(min(steps, len(self.queue))):
            self.queue.pop(0)()

    def take(self, steps):
        taken, self.queue = self.queue[:steps], self.queue[steps:]
        return taken

    def sent(self):
        for piece in range(len(self.pieces)):
            for hop in range(3):
                for copy in self.copies(piece, hop):
                    copy.wait_send()


def piece_buffers(piece, deep, rows):
    _, a, b, order, _ = piece
    sizes = {"z": deep, "y": 2, "x": 2}
    rest = [name for name in "zyx" if name != order[0]]
    left = [sizes[name] for name in rest]
    last = [sizes[name] for name in rest if name != order[1]]
    tail = [rows, b - a]
    lead = [deep - 1]
    first = (lead if order[0] == "z" else []) + left + tail
    second = (lead if order[1] == "z" else []) + last + tail
    third = (lead if order[2] == "z" else []) + tail
    return [tuple(shape) for shape in (first, left + tail, second, third)]


def back_kernel(shard_size, pieces, early, sizes, *refs):
    inner, hidden, buckets = sizes
    count = len(pieces)
    (
        lengths_ref, full_ref, normed_in, qkv_in, bandt_in, biast_in, grads_in, do_in,
        lse_ref, output_ref, middle_ref, tokens_ref, gain_two_ref, table_ref,
    ) = refs[:14]
    refs = refs[14:]
    weight_outs, (output_out, input_out, small_out) = refs[:7], refs[7:10]
    refs = refs[10:]
    first, own, second, third = [refs[k * count : (k + 1) * count] for k in range(4)]
    refs = refs[4 * count :]
    (
        qkv, normed_t, bandt, bias, wqkv, gain_buf, do, scores, grads, far, dk_acc, dv_acc, kaux, wgrad,
        mine_sum, away, arrived, result, table_acc, hot, found,
        small, small_x, small_y, hold_x, hold_y, hold_z, small_c,
        own_sem, send_sem, recv_sem, near_send, near_recv, local_sem,
    ) = refs
    length = qkv.shape[1]
    width = normed_t.shape[0]
    half, quarter = length // 2, length // 4
    heads, blocks = bias.shape[:2]
    pairs = heads // 2
    deep = shard_size // 2
    low, f32 = jnp.bfloat16, jnp.float32
    place = Place(shard_size)
    x, y, z, c = place.x, place.y, place.z, place.c
    to_x, to_y, to_c = place.device(x=1 - x), place.device(y=1 - y), place.device(c=1 - c)

    def local(i, source, target):
        return pltpu.make_async_copy(source, target, local_sem.at[i])

    loads = [
        local(0, qkv_in, qkv), local(1, biast_in, bias), local(2, do_in, do),
        local(3, full_ref.at[:, :, :, :, 128 : 128 + 3 * inner], wqkv), local(4, normed_in, normed_t),
        local(5, bandt_in, bandt), local(6, full_ref.at[:, :, :, :, 0:128], gain_buf),
    ]
    for copy in loads:
        copy.start()
    meet(place)
    scatter = Scatter(
        place, pieces, (grads_in, wgrad), weight_outs, (first, own, second, third), (own_sem, send_sem, recv_sem),
    )
    scatter.plan(SUM_WINDOW, early)

    def near(i, source, target, device):
        return send(source, target, near_send.at[i], near_recv.at[i], device)

    def to_owners(i, values, out):
        here = out.at[x, pl.ds(c * quarter, quarter)]
        there = out.at[1 - x, pl.ds(c * quarter, quarter)]
        return (
            local(7 + i, values.at[x], here),
            near(4 * i, values.at[x], here, to_c),
            near(4 * i + 1, values.at[1 - x], here, to_x),
            near(4 * i + 2, there, there, to_c),
        )

    output_moves = to_owners(0, output_ref, output_out)
    for copy in output_moves[:3]:
        copy.start()

    lanes_of = lax.broadcasted_iota(jnp.int32, (length, 128), 1)
    rows_of = lax.broadcasted_iota(jnp.int32, (length, 128), 0)
    valid = lengths_ref[x, 0]
    blocked = jnp.where(rows_of // BLOCK == lanes_of, 1.0, 0.0)
    kaux[...] = jnp.where((lanes_of == blocks) & (rows_of >= valid), -1e30, blocked).astype(low)
    far[...] = jnp.zeros_like(far)
    for copy in loads:
        copy.wait()

    per_pair = length // 256
    units = pairs * per_pair
    acts = scatter.take(ATTENTION_ACTS)

    def unit_step(unit, carry):
        pair = unit // per_pair
        step = unit % per_pair
        rows = pl.ds(pl.multiple_of(step * 256, 256), 256)

        @pl.when(step == 0)
        def _():
            dk_acc[...] = jnp.zeros_like(dk_acc)
            dv_acc[...] = jnp.zeros_like(dv_acc)

        queries = qkv[pair, rows, :]
        grad = do[pair, rows, :]
        key_pair = qkv[pairs + pair]
        keys = jnp.concatenate([key_pair, kaux[...]], axis=1)
        values = qkv[2 * pairs + pair]
        dq = None
        for head in range(2):
            between(acts, units, ACT_FIRST, unit, head)
            here = lane_head(256, 128, head)
            aux = query_aux(table_ref[2 * pair + head], step, blocks)
            q_masked = jnp.where(here, queries, jnp.zeros_like(queries))
            do_masked = jnp.where(here, grad, jnp.zeros_like(grad))
            scores[...] = lax.dot_general(
                keys, jnp.concatenate([q_masked, aux], axis=1), LAST, preferred_element_type=f32
            )
            for sub in range(2):
                start = pl.multiple_of(band_start(step * 2 + sub, blocks) * BLOCK, BLOCK)
                scores[pl.ds(start, BAND * BLOCK), sub * BLOCK : (sub + 1) * BLOCK] += bias[
                    2 * pair + head, 2 * step + sub
                ].astype(f32)
            soft = jnp.exp(scores[...] - lse_ref[pair, step, head : head + 1, :])
            dv_acc[...] += jnp.dot(soft.astype(low), do_masked, preferred_element_type=f32)
            grad_probs = lax.dot_general(values, do_masked, LAST, preferred_element_type=f32)
            weighted = jnp.sum(soft * grad_probs, axis=0, keepdims=True)
            grad_scores = (soft * (grad_probs - weighted)).astype(low)
            grads[...] = grad_scores
            dk_acc[...] += jnp.dot(grad_scores, q_masked, preferred_element_type=f32)
            k_masked = jnp.where(lane_head(length, 128, head), key_pair, jnp.zeros_like(key_pair))
            part = lax.dot_general(grad_scores, k_masked, FIRST, preferred_element_type=f32)
            dq = part if dq is None else dq + part
            sums = jnp.concatenate(
                [
                    jnp.sum(grad_scores[block * BLOCK : (block + 1) * BLOCK, :].astype(f32), axis=0, keepdims=True)
                    for block in range(blocks)
                ],
                axis=0,
            )
            block_of = lax.broadcasted_iota(jnp.int32, (blocks, BLOCK), 0)
            for sub in range(2):
                start = band_start(step * 2 + sub, blocks)
                at = pl.multiple_of(start * BLOCK, BLOCK)
                bias[2 * pair + head, 2 * step + sub] = grads[pl.ds(at, BAND * BLOCK), sub * BLOCK : (sub + 1) * BLOCK]
                part = sums[:, sub * BLOCK : (sub + 1) * BLOCK]
                far[0, 2 * pair + head] += jnp.where(block_of < start, part, 0.0)
                far[1, 2 * pair + head] += jnp.where(block_of >= start + BAND, part, 0.0)
        qkv[pair, rows, :] = dq.astype(low)

        @pl.when(step == per_pair - 1)
        def _():
            qkv[pairs + pair] = dk_acc[...].astype(low)
            qkv[2 * pairs + pair] = dv_acc[...].astype(low)
            right = jnp.concatenate([qkv[t * pairs + pair] for t in range(3)], axis=1)

            def weight_step(i, carry):
                rows = pl.ds(pl.multiple_of(i * 256, 256), 256)
                got = jnp.dot(normed_t[rows, :], right, preferred_element_type=f32).astype(low)
                span = deep // (width // 256)
                wgrad[pair, pl.ds(i * span, span)] = got.reshape((span,) + wgrad.shape[2:5] + (3 * 128,))
                return carry

            lax.fori_loop(0, width // 256, weight_step, 0)

        for late in range(early, count):
            @pl.when(unit == (late - early + 1) * per_pair - 1)
            def _(late=late):
                scatter.begin(late)

        return carry

    lax.fori_loop(0, units, unit_step, 0)
    for copy in output_moves[:3]:
        copy.wait()
    output_moves[3].start()
    def part_rows(part, core):
        return pl.ds(pl.multiple_of(part * half + core * quarter, quarter), quarter)

    def grad_one(rows):
        left = jnp.concatenate([qkv[k, rows, :] for k in range(3 * pairs)], axis=1)
        return lax.dot_general(left, wqkv[...].reshape(width, 3 * inner), LAST, preferred_element_type=f32)

    swaps = [near(8 + part, away.at[part], arrived.at[part], to_c) for part in range(2)]

    def away_step(part, carry):
        away[part] = grad_one(part_rows(part, 1 - c)).astype(low)
        return carry

    def mine_step(part, carry):
        mine_sum[part] = grad_one(part_rows(part, c))
        return carry

    lax.fori_loop(0, 2, away_step, 0)
    for copy in swaps:
        copy.start()
    scatter.run(1)
    lax.fori_loop(0, 2, mine_step, 0)
    scatter.run(1)
    gains = jnp.transpose(gain_buf[...].reshape(width, 128).astype(f32))
    gain_one = gains[0:1, :]
    gain_sum = jnp.zeros((1, width), f32)
    for part in range(2):
        swaps[part].wait()
        total = mine_sum[part] + arrived[part].astype(f32)
        present = tokens_ref[part].astype(f32)
        inverse = lax.rsqrt(jnp.mean(present * present, axis=-1, keepdims=True) + EPSILON)
        unit = present * inverse
        gain_sum = gain_sum + jnp.sum(total * unit, axis=0, keepdims=True)
        scaled = total * gain_one
        back = inverse * (scaled - unit * jnp.mean(scaled * unit, axis=-1, keepdims=True))
        result[part] = (middle_ref[part] + back).astype(low)
        scatter.run(1)
    input_moves = to_owners(1, result, input_out)
    for copy in input_moves[:3]:
        copy.start()
    table_acc[...] = jnp.zeros_like(table_acc)
    groups = BAND * BLOCK // GROUP
    table_units = blocks // 2 * groups // TURNS
    table_acts = scatter.take(TABLE_ACTS)

    def table_step(i, carry):
        for k, act in enumerate(table_acts):
            @pl.when(i == (k * table_units) // max(1, len(table_acts)))
            def _(act=act):
                act()
        total = None
        for turn in range(TURNS):
            group = i * TURNS + turn
            block = 2 * (group // groups)
            start = pl.multiple_of((group % groups) * GROUP, GROUP)
            for two in range(2):
                lanes = slice(two * BLOCK, (two + 1) * BLOCK)
                index = bandt[block + two, pl.ds(start, GROUP), :]
                for head in range(heads):
                    found[turn, head * GROUP : (head + 1) * GROUP, lanes] = bias[head, block + two, pl.ds(start, GROUP), :]
                for b in range(buckets):
                    hot[turn, b * GROUP : (b + 1) * GROUP, lanes] = jnp.where(
                        index == jnp.asarray(b, low), jnp.asarray(1, low), jnp.asarray(0, low)
                    )
            part = lax.dot_general(hot[turn], found[turn], LAST, preferred_element_type=f32)
            total = part if total is None else total + part
        table_acc[...] += total
        return carry

    lax.fori_loop(0, table_units, table_step, 0)
    row = lax.broadcasted_iota(jnp.int32, table_acc.shape, 0) % GROUP
    col = lax.broadcasted_iota(jnp.int32, table_acc.shape, 1) % GROUP
    kept = jnp.where(row == col, table_acc[...], 0.0).reshape(buckets, GROUP, heads * GROUP).sum(axis=1)
    bucket = lax.broadcasted_iota(jnp.int32, (buckets, 128), 0)
    head_of = lax.broadcasted_iota(jnp.int32, (buckets, 128), 1)
    table = jnp.zeros((buckets, 128), f32)
    for head in range(heads):
        amount = jnp.sum(kept[:, head * GROUP : (head + 1) * GROUP], axis=1, keepdims=True)
        table = table + jnp.where(head_of == head, amount, 0.0)
    for side, name in enumerate((buckets // 2 - 1, buckets - 1)):
        for head in range(heads):
            amount = jnp.sum(jnp.sum(far[side, head], axis=0, keepdims=True), axis=1, keepdims=True)
            table = table + jnp.where((bucket == name) & (head_of == head), amount, 0.0)

    lines = width // 128
    for i in range(lines):
        small[i : i + 1, :] = gain_sum[:, i * 128 : (i + 1) * 128]
    small[lines : 2 * lines, :] = gain_two_ref[...]
    small[2 * lines : 2 * lines + buckets, :] = table
    small_base = 10

    def small_line(d):
        return near(small_base + 2 + d, hold_z.at[z], hold_z.at[z], place.device(z=place.line(d)))

    move = near(small_base, small, small_x, to_x)
    move.start()
    scatter.run(1)
    move.wait()
    hold_x[...] = small[...] + small_x[...]
    move = near(small_base + 1, hold_x, small_y, to_y)
    move.start()
    scatter.run(1)
    move.wait()
    hold_z[z] = hold_x[...] + small_y[...]
    for d in range(1, deep):
        small_line(d).start()
    scatter.run(1)
    for d in range(1, deep):
        small_line(d).wait()
    hold_y[...] = jnp.sum(hold_z[...], axis=0)
    move = near(small_base + 2, hold_y, small_c, to_c)
    move.start()
    scatter.run(1)
    move.wait()
    small_out[0] = hold_y[...]
    small_out[1] = hold_y[...] + small_c[...]

    for copy in input_moves[:3]:
        copy.wait()
    input_moves[3].start()
    input_moves[3].wait()
    output_moves[3].wait()
    scatter.run(len(scatter.queue))
    scatter.sent()


def back(shard_size, pieces, early, buckets, lengths, full, normed_t, qkv, bandt, biast, grads, do, lse, output, middle, tokens, gain_two, table_rows):
    low, f32 = jnp.bfloat16, jnp.float32
    deep = shard_size // 2
    rows = full.shape[3]
    width, length = normed_t.shape
    half, quarter = length // 2, length // 4
    heads, blocks = biast.shape[:2]
    pairs = heads // 2
    inner = pairs * 128
    hidden = (grads.shape[4] - inner) // 3
    count = len(pieces)
    shape = jax.ShapeDtypeStruct
    vmem, hbm = pl.BlockSpec(memory_space=pltpu.VMEM), pl.BlockSpec(memory_space=pl.ANY)
    dma = pltpu.SemaphoreType.DMA
    lines = 2 * (width // 128) + buckets
    buffers = [piece_buffers(piece, deep, rows) for piece in pieces]
    scratch = [pltpu.VMEM(buffer[k], low) for k in range(4) for buffer in buffers]
    small = pltpu.VMEM((lines, 128), f32)
    scratch += [
        pltpu.VMEM((3 * pairs, length, 128), low),
        pltpu.VMEM((width, length), low),
        pltpu.VMEM((blocks, BAND * BLOCK, BLOCK), low),
        pltpu.VMEM((heads, blocks, BAND * BLOCK, BLOCK), low),
        pltpu.VMEM((deep, 2, 2, rows, 3 * inner), low),
        pltpu.VMEM((deep, 2, 2, rows, 128), low),
        pltpu.VMEM((pairs, length, 128), low),
        pltpu.VMEM((length, 256), f32),
        pltpu.VMEM((length, 256), low),
        pltpu.VMEM((2, heads, blocks, BLOCK), f32),
        pltpu.VMEM((length, 128), f32),
        pltpu.VMEM((length, 128), f32),
        pltpu.VMEM((length, 128), low),
        pltpu.VMEM((pairs, deep, 2, 2, rows, 3 * 128), low),
        pltpu.VMEM((2, quarter, width), f32),
        pltpu.VMEM((2, quarter, width), low),
        pltpu.VMEM((2, quarter, width), low),
        pltpu.VMEM((2, quarter, width), low),
        pltpu.VMEM((buckets * GROUP, heads * GROUP), f32),
        pltpu.VMEM((TURNS, buckets * GROUP, 2 * BLOCK), low),
        pltpu.VMEM((TURNS, heads * GROUP, 2 * BLOCK), low),
        small, small, small, small, small, pltpu.VMEM((deep, lines, 128), f32), small,
        dma((count,)),
        dma((count, 3, deep - 1)),
        dma((count, 3, deep - 1)),
        dma((12 + deep,)),
        dma((12 + deep,)),
        dma((9,)),
    ]
    return pl.pallas_call(
        functools.partial(back_kernel, shard_size, pieces, early, (inner, hidden, buckets)),
        out_shape=[
            *[shape((rows, n), f32) for n in (inner,) * 4 + (hidden,) * 3],
            shape((2, half, width), low),
            shape((2, half, width), low),
            shape((2, lines, 128), f32),
        ],
        in_specs=[pl.BlockSpec(memory_space=pltpu.SMEM)] + [hbm] * 7 + [vmem] * 6,
        out_specs=[vmem] * 7 + [hbm, hbm, vmem],
        scratch_shapes=scratch,
        compiler_params=pltpu.CompilerParams(
            collective_id=2, has_side_effects=True, vmem_limit_bytes=60 * MIB
        ),
        name="back",
    )(lengths, full, normed_t, qkv, bandt, biast, grads, do, lse, output, middle, tokens, gain_two, table_rows)


ORDERS = ("xyz", "zxy", "zyx", "zxy", "zxy", "zyx", "zxy", "zyx", "zxy")
SUM_ORDERS = ("yxz", "xyz", "yzx", "yxz", "xzy", "yxz")
WINDOW = 4
AHEAD = 4
LAG = 3
QUICK = 4
SUM_WINDOW = 3
SUM_LAGS = (2, 4)
FORWARD_ACTS = 8
ATTENTION_ACTS = 20
ACT_FIRST = 5
TABLE_ACTS = 7


def front_pieces(inner, hidden):
    at_project = 128 + 3 * inner
    at_hidden = at_project + inner
    pieces = split_columns(0, at_project, 4) + split_columns(at_project, at_hidden, 2)
    for j, n in enumerate(hidden_steps(hidden)):
        at = at_hidden + 3 * HIDDEN_STEP * j
        pieces += split_columns(at, at + 3 * n, 2)
    return [(a, b, ORDERS[i % len(ORDERS)]) for i, (a, b) in enumerate(pieces)]


def back_pieces(inner, hidden):
    where = []
    for j, n in enumerate(hidden_steps(hidden)):
        for k in range(3):
            where.append((3 * HIDDEN_STEP * j + k * n, n, 4 + k, HIDDEN_STEP * j))
    where.append((3 * hidden, inner, 3, 0))
    cuts = []
    for j, n in enumerate(hidden_steps(hidden)):
        at = 3 * HIDDEN_STEP * j
        cuts += split_columns(at, at + 3 * n, 2 if n > 128 else 1)
    cuts += split_columns(3 * hidden, 3 * hidden + inner, 2)
    pieces = []
    for a, b in cuts:
        segments = []
        for start, n, out, column in where:
            low, high = max(a, start), min(b, start + n)
            if low < high:
                segments.append((out, column + low - start, low - a, high - low))
        pieces.append((0, a, b, segments))
    early = len(pieces)
    for pair in range(inner // 128):
        pieces.append((1 + pair, 0, 3 * 128, [(t, pair * 128, t * 128, 128) for t in range(3)]))
    return [(t, a, b, SUM_ORDERS[i % len(SUM_ORDERS)], segments) for i, (t, a, b, segments) in enumerate(pieces)], early


def shards(
    inputs, cotangent, lengths, buckets,
    query_weight, key_weight, value_weight, projection_weight, gate_weight, up_weight, down_weight,
    attention_gain, feedforward_gain, bias_table,
):
    x = lax.axis_index("ctx")
    shard_size = lax.axis_size("shard")
    width = inputs.shape[2]
    bucket_count, heads = bias_table.shape
    rows, inner = query_weight.shape
    hidden = gate_weight.shape[1]
    gains = jnp.pad(jnp.stack([attention_gain, feedforward_gain], axis=1), ((0, 0), (0, 126)))
    table_rows = jnp.broadcast_to(
        jnp.pad(bias_table.astype(jnp.float32).T, ((0, 0), (0, 128 - bucket_count)))[:, None, :], (heads, 8, 128)
    )
    weights = (query_weight, key_weight, value_weight, projection_weight, gate_weight, up_weight, down_weight)
    (
        full, normed_t, qkv, bandt, biast, grads, grad_attended, tokens,
        lse, output, grad_middle, gain_two,
    ) = front(shard_size, front_pieces(inner, hidden), WINDOW, lengths, gains, weights, inputs, cotangent, buckets, table_rows)

    cuts, early = back_pieces(inner, hidden)
    gain_two = jnp.sum(gain_two, axis=(0, 1)).reshape(-1, 128)
    *weight_sums, output, input_grad, small = back(
        shard_size, cuts, early, bucket_count,
        lengths, full, normed_t, qkv, bandt, biast, grads, grad_attended,
        lse, output, grad_middle, tokens, gain_two, table_rows,
    )
    lines = width // 128
    me = lax.axis_index("shard") * 2 + x

    def own_gain(part):
        return lax.dynamic_slice_in_dim(small[1, part * lines : (part + 1) * lines].reshape(-1), me * rows, rows)

    return (
        output, input_grad.astype(jnp.float32),
        *weight_sums, own_gain(0), own_gain(1), small[0, 2 * lines :, :heads],
    )


def solution(mesh):
    rows = P(None, ("shard", "ctx"), None)
    weight = P(("shard", "ctx"), "tp")
    gain = P(("shard", "ctx"))
    table = P(None, "tp")
    return jax.shard_map(
        shards,
        mesh=mesh,
        in_specs=(rows, rows, P(None, "shard"), P("ctx", None)) + (weight,) * 7 + (gain, gain, table),
        out_specs=(rows, rows) + (weight,) * 7 + (gain, gain, table),
        check_vma=False,
    )
```

```python
import functools

import jax
import jax.numpy as jnp
from jax import lax
from jax.experimental import pallas as pl
from jax.experimental.pallas import tpu as pltpu
from jax.sharding import PartitionSpec as P

EPSILON = 1e-06
GELU_ROOT = 0.7978845608028654
GELU_CUBIC = 0.044715
MESH = pl.DeviceIdType.MESH
MIB = 1024 * 1024


BAND = 3
BLOCK = 128


def lane_head(rows, width, which):
    lanes = lax.broadcasted_iota(jnp.int32, (rows, width), 1)
    half = width // 2
    return (lanes < half) if which == 0 else (lanes >= half)


def band_start(row_block, blocks):
    return jnp.clip(row_block - 1, 0, blocks - BAND)


def split_columns(start, stop, pieces):
    tiles = (stop - start) // 128
    edges = [start + 128 * (tiles * i // pieces) for i in range(pieces + 1)]
    return [(a, b) for a, b in zip(edges, edges[1:]) if b > a]


class Place:
    def __init__(self, shard_size):
        self.deep = shard_size // 2
        shard = lax.axis_index("shard")
        self.z = shard // 2
        self.y = shard % 2
        self.x = lax.axis_index("ctx")
        self.c = lax.axis_index("tp")

    def device(self, z=None, y=None, x=None, c=None):
        z = self.z if z is None else z
        y = self.y if y is None else y
        x = self.x if x is None else x
        c = self.c if c is None else c
        return (z * 2 + y, x, c)

    def line(self, distance):
        return (self.z + distance) % self.deep

    def peers(self):
        others = [self.device(z=self.line(d)) for d in range(1, self.deep)]
        return others + [self.device(y=1 - self.y), self.device(x=1 - self.x), self.device(c=1 - self.c)]


def meet(place):
    barrier = pltpu.get_barrier_semaphore()
    peers = place.peers()
    for peer in peers:
        pl.semaphore_signal(barrier, inc=1, device_id=peer, device_id_type=MESH)
    pl.semaphore_wait(barrier, len(peers))


def send(source, target, send_sem, recv_sem, device):
    return pltpu.make_async_remote_copy(
        src_ref=source, dst_ref=target, send_sem=send_sem, recv_sem=recv_sem, device_id=device, device_id_type=MESH
    )


LAST = (((1,), (1,)), ((), ()))
FIRST = (((0,), (0,)), ((), ()))
HIDDEN_STEP = 256
HALF_BUCKETS = 16


def hidden_steps(hidden):
    return [min(HIDDEN_STEP, hidden - at) for at in range(0, hidden, HIDDEN_STEP)]


class Gather:
    def __init__(self, place, pieces, own_ref, full_ref, send_sem, recv_sem):
        self.place, self.pieces, self.own, self.full = place, pieces, own_ref, full_ref
        self.send_sem, self.recv_sem = send_sem, recv_sem
        self.queue = []

    def held(self, piece, hop):
        a, b, order = self.pieces[piece]
        place, done = self.place, order[:hop]
        at = [slice(None) if name in done else getattr(place, name) for name in "zyx"]
        return self.full.at[at[0], at[1], at[2], :, a:b]

    def copies(self, piece, hop):
        place = self.place
        a, b, order = self.pieces[piece]
        target = self.held(piece, hop)
        source = self.own.at[:, a:b] if hop == 0 else target
        name = order[hop]
        if name == "z":
            peers = [place.device(z=place.line(d)) for d in range(1, place.deep)]
        elif name == "y":
            peers = [place.device(y=1 - place.y)]
        else:
            peers = [place.device(x=1 - place.x)]
        return [
            send(source, target, self.send_sem.at[piece, hop, i], self.recv_sem.at[piece, hop, i], peer)
            for i, peer in enumerate(peers)
        ]

    def start(self, piece, hop):
        for copy in self.copies(piece, hop):
            copy.start()

    def arrive(self, piece, hop):
        for copy in self.copies(piece, hop):
            copy.wait_recv()

    def sent(self):
        for piece in range(len(self.pieces)):
            for hop in range(3):
                for copy in self.copies(piece, hop):
                    copy.wait_send()

    def plan(self, window):
        count = len(self.pieces)
        self.window = window

        def second(piece):
            def act():
                self.arrive(piece, 0)
                self.start(piece, 1)
                if piece + window < count:
                    self.start(piece + window, 0)
            return act

        def third(piece):
            def act():
                self.arrive(piece, 1)
                self.start(piece, 2)
            return act

        turned = 0
        for piece in range(count + LAG):
            if piece < count:
                self.queue.append((None, second(piece)))
            while turned < count and turned <= piece - (1 if turned < QUICK else LAG):
                self.queue.append((turned, third(turned)))
                turned += 1
        for piece in range(min(window, count)):
            self.start(piece, 0)

    def run(self, steps):
        for _ in range(min(steps, len(self.queue))):
            self.queue.pop(0)[1]()

    def take(self, steps):
        taken, self.queue = self.queue[:steps], self.queue[steps:]
        return [act for _, act in taken]

    def need(self, pieces):
        for piece in pieces:
            while any(mark == piece for mark, _ in self.queue):
                self.run(1)
        self.run(AHEAD)
        for piece in pieces:
            self.arrive(piece, 2)


def query_aux(table, step, blocks):
    parts = []
    lanes = lax.broadcasted_iota(jnp.int32, (BLOCK, 128), 1)
    buckets = 2 * HALF_BUCKETS
    below = jnp.broadcast_to(table[0:1, HALF_BUCKETS - 1 : HALF_BUCKETS], (BLOCK, 128))
    above = jnp.broadcast_to(table[0:1, buckets - 1 : buckets], (BLOCK, 128))
    for sub in range(2):
        start = band_start(2 * step + sub, blocks)
        value = jnp.where(lanes < start, below, 0.0)
        value = jnp.where((lanes >= start + BAND) & (lanes < blocks), above, value)
        parts.append(jnp.where(lanes == blocks, 1.0, value))
    return jnp.concatenate(parts, axis=0).astype(jnp.bfloat16)


def between(acts, units, skip, unit, head):
    slots = 2 * units - skip
    for k, act in enumerate(acts):
        slot = skip + (k * slots) // len(acts)
        if slot % 2 == head:
            pl.when(unit == slot // 2)(act)


def gelu_all(gate):
    square = gate * gate
    tangent = jnp.tanh(GELU_ROOT * (gate + GELU_CUBIC * square * gate))
    value = 0.5 * gate * (1.0 + tangent)
    slope = 0.5 * (1.0 + tangent) + 0.5 * gate * (1.0 - tangent * tangent) * (
        GELU_ROOT + (3.0 * GELU_CUBIC * GELU_ROOT) * square
    )
    return value, slope


def front_kernel(
    shard_size, pieces, window, sizes, given,
    lengths_ref, gains_ref, query_ref, key_ref, value_ref, project_ref, gate_ref, up_ref, down_ref,
    inputs_ref, cots_ref, buckets_ref, table_ref,
    full_ref, normed_out, qkv_out, bandt_out, biast_out, grads_out, attended_out, tokens_own_ref,
    lse_ref, output_ref, middle_grad_ref, gain_ref, *rest,
):
    came_outs, rest = rest[: len(given)], rest[len(given) :]
    (
    own_ref, tok, cot, band_raw, band, bandt, bias, biast, kaux, gain_buf, qkv, normed, scores, attended, project_w,
    normal, away, arrived, two_t, low_t, acc_out, acc_two, w_buf, g_buf, hid, ggate, gup,
    send_sem, recv_sem, near_send, near_recv, local_sem, w_sem, g_sem, own_sem, bt_sem, early_send, early_recv,
    ) = rest
    inner, hidden = sizes
    length, width = tok.shape
    half, quarter = length // 2, length // 4
    heads, blocks = bias.shape[:2]
    pairs = heads // 2
    deep = shard_size // 2
    low = jnp.bfloat16
    place = Place(shard_size)
    x, c = place.x, place.c
    at_q = 128
    at_project = at_q + 3 * inner
    at_hidden = at_project + inner
    steps = hidden_steps(hidden)
    per_step = 2
    first_hidden_piece = len(pieces) - per_step * len(steps)
    project_pieces = [i for i, (a, b, _) in enumerate(pieces) if at_project <= a < at_hidden]
    qkv_pieces = [i for i, (a, b, _) in enumerate(pieces) if a < at_project]

    def own_load(i, source, target):
        return pltpu.make_async_copy(source, target, local_sem.at[i])

    parts, at = [], 0
    for ref in (gains_ref, query_ref, key_ref, value_ref, project_ref):
        parts.append((ref, at))
        at += ref.shape[1]
    own_loads = [
        pltpu.make_async_copy(ref, own_ref.at[:, at : at + ref.shape[1]], own_sem.at[i]) for i, (ref, at) in enumerate(parts)
    ]
    for j, n in enumerate(steps):
        for k, ref in enumerate((gate_ref, up_ref, down_ref)):
            at = at_hidden + 3 * HIDDEN_STEP * j + k * n
            own_loads.append(
                pltpu.make_async_copy(
                    ref.at[:, HIDDEN_STEP * j : HIDDEN_STEP * j + n], own_ref.at[:, at : at + n], own_sem.at[len(own_loads)]
                )
            )

    def band_source(block):
        start = pl.multiple_of(band_start(block, blocks) * BLOCK, BLOCK)
        first = block - x * (blocks // 2)
        return buckets_ref.at[pl.ds(pl.multiple_of(first * BLOCK, BLOCK), BLOCK), pl.ds(start, BAND * BLOCK)]

    own_tok = own_load(0, inputs_ref.at[x], tok.at[pl.ds(x * half, half)])
    own_cot = own_load(1, cots_ref.at[x], cot.at[pl.ds(x * half, half)])
    own_bands = [
        own_load(13 + i, band_source(x * (blocks // 2) + i), band_raw.at[i]) for i in range(blocks // 2)
    ]
    own_full = own_load(3, own_ref, full_ref.at[place.z, place.y, x])
    for copy in (*own_loads, *own_bands, own_tok, own_cot):
        copy.start()
    meet(place)
    for copy in own_loads:
        copy.wait()
    own_full.start()

    gather = Gather(place, pieces, own_ref, full_ref, send_sem, recv_sem)
    to_x, to_c = place.device(x=1 - x), place.device(c=1 - c)

    def x_rows(sender_x, sender_c):
        return pl.ds(sender_x * half + sender_c * quarter, quarter)

    def near(i, source, target, device):
        return send(source, target, near_send.at[i], near_recv.at[i], device)

    mine = [x * (blocks // 2) + c * (blocks // 4) + i for i in range(blocks // 4)]
    theirs = [(1 - x) * (blocks // 2) + c * (blocks // 4) + i for i in range(blocks // 4)]
    band_x = [near(16 + i, band.at[block], band.at[block], to_x) for i, block in enumerate(mine)]
    tok_x = near(1, inputs_ref.at[1 - x, pl.ds(c * quarter, quarter)], tok.at[x_rows(x, c)], to_x)
    cot_x = near(2, cots_ref.at[1 - x, pl.ds(c * quarter, quarter)], cot.at[x_rows(x, c)], to_x)
    band_c = [near(16 + len(mine) + i, band.at[block], band.at[block], to_c) for i, block in enumerate(theirs)]
    tok_c = near(4, tok.at[x_rows(1 - x, c)], tok.at[x_rows(1 - x, c)], to_c)
    cot_c = near(5, cot.at[x_rows(1 - x, c)], cot.at[x_rows(1 - x, c)], to_c)
    gather.plan(window)
    for copy in own_bands:
        copy.wait()
    for i in range(blocks // 2):
        band[x * (blocks // 2) + i] = band_raw[i].astype(jnp.float32).astype(low)
    for copy in band_x:
        copy.start()
    tok_x.start()
    own_full.wait()
    lanes_of = lax.broadcasted_iota(jnp.int32, (length, 128), 1)
    rows_of = lax.broadcasted_iota(jnp.int32, (length, 128), 0)
    valid = lengths_ref[x, 0]
    blocked = jnp.where(rows_of // BLOCK == lanes_of, 1.0, 0.0)
    kaux[...] = jnp.where((lanes_of == blocks) & (rows_of >= valid), -1e30, blocked).astype(low)
    gather.run(1)
    for copy in band_x:
        copy.wait()
    for copy in band_c:
        copy.start()
    gather.run(1)
    for copy in band_c:
        copy.wait()

    def bias_step(i, carry):
        block = i // (BLOCK // 16)
        at = pl.multiple_of((i % (BLOCK // 16)) * 16, 16)
        index = band[block, pl.ds(at, 16), :].astype(jnp.float32).astype(jnp.int32)
        for col in range(BAND):
            lanes = slice(col * BLOCK, (col + 1) * BLOCK)
            for head in range(heads):
                table = table_ref[head]
                got = [jnp.take_along_axis(table, index[8 * k : 8 * k + 8, lanes], axis=1) for k in range(2)]
                bias[head, block, pl.ds(at, 16), lanes] = jnp.concatenate(got, axis=0).astype(low)
        return carry

    bias_steps = blocks * (BLOCK // 16)
    for k in range(4):
        lax.fori_loop(bias_steps * k // 4, bias_steps * (k + 1) // 4, bias_step, 0)
        gather.run(1)
    tok_x.wait()
    tok_c.start()
    cot_x.start()

    def biast_store(block, slot):
        return pltpu.make_async_copy(biast.at[slot], biast_out.at[:, block], bt_sem.at[slot])

    def biast_block(block, carry):
        slot = block % 2

        @pl.when(block > 1)
        def _():
            biast_store(block - 2, slot).wait()

        bandt[block] = jnp.transpose(band[block].astype(jnp.float32)).astype(low)

        def inner_step(i, carry):
            at = pl.multiple_of(i * 16, 16)
            index = bandt[block, pl.ds(at, 16), :].astype(jnp.float32).astype(jnp.int32)
            for head in range(heads):
                got = [jnp.take_along_axis(table_ref[head], index[8 * k : 8 * k + 8], axis=1) for k in range(2)]
                biast[slot, head, pl.ds(at, 16), :] = jnp.concatenate(got, axis=0).astype(low)
            return carry

        lax.fori_loop(0, BAND * BLOCK // 16, inner_step, 0)
        biast_store(block, slot).start()
        return carry

    for k in range(4):
        lax.fori_loop(blocks * k // 4, blocks * (k + 1) // 4, biast_block, 0)
        gather.run(1)
    biast_store(blocks - 2, 0).wait()
    biast_store(blocks - 1, 1).wait()
    bandt_store = own_load(4, bandt, bandt_out)
    bandt_store.start()
    own_tok.wait()
    tok_c.wait()

    def live_step(i, carry):
        rows = pl.ds(pl.multiple_of(i * BLOCK, BLOCK), BLOCK)
        here = lax.broadcasted_iota(jnp.int32, (BLOCK, width), 0) + i * BLOCK < valid
        masked = jnp.where(here, cot[rows, :].astype(jnp.float32), 0.0).astype(low)
        cot[rows, :] = masked
        low_t[:, rows] = jnp.transpose(masked)
        return carry

    gather.need(qkv_pieces)
    load_gains = own_load(5, full_ref.at[:, :, :, :, 0:at_q], gain_buf)
    third = 3 * inner // 2
    loads_wide = [
        pltpu.make_async_copy(
            full_ref.at[:, :, :, :, at_q + third * k : at_q + third * (k + 1)], w_buf.at[k, :, :, :, :, 0:third], w_sem.at[k]
        )
        for k in range(2)
    ]
    for copy in (load_gains, *loads_wide):
        copy.start()
    load_gains.wait()
    gains = jnp.transpose(gain_buf[...].reshape(width, 128).astype(jnp.float32))
    gain_one, gain_two = gains[0:1, :], gains[1:2, :]

    def norm_step(i, carry):
        rows = pl.ds(pl.multiple_of(i * BLOCK, BLOCK), BLOCK)
        present = tok[rows, :].astype(jnp.float32)
        inverse = lax.rsqrt(jnp.mean(present * present, axis=-1, keepdims=True) + EPSILON)
        got = (present * inverse * gain_one).astype(low)
        normed[rows, :] = got
        two_t[:, rows] = jnp.transpose(got)
        return carry

    lax.fori_loop(0, blocks, norm_step, 0)
    normed_store = own_load(6, two_t, normed_out)
    normed_store.start()
    for copy in loads_wide:
        copy.wait()
    gather.run(2)

    for col in range(3 * pairs // 2):
        slot, at = 256 * col // third, 256 * col % third
        lanes = slice(at, at + 256)

        def qkv_step(i, carry):
            rows = pl.ds(pl.multiple_of(i * 256, 256), 256)
            got = jnp.dot(
                normed[rows, :], w_buf[slot, :, :, :, :, lanes].reshape(width, 256), preferred_element_type=jnp.float32
            ).astype(low)
            qkv[2 * col, rows, :] = got[:, :128]
            qkv[2 * col + 1, rows, :] = got[:, 128:]
            return carry

        lax.fori_loop(0, length // 256, qkv_step, 0)
        if col % 2:
            gather.run(1)
    qkv_store = own_load(7, qkv, qkv_out)
    qkv_store.start()

    units = pairs * (length // 256)
    acts = gather.take(min(len(gather.queue), FORWARD_ACTS))

    def unit_step(unit, carry):
        pair = unit // (length // 256)
        step = unit % (length // 256)
        rows = pl.ds(pl.multiple_of(step * 256, 256), 256)
        queries = qkv[pair, rows, :]
        keys = jnp.concatenate([qkv[pairs + pair], kaux[...]], axis=1)
        outs = []
        for head in range(2):
            between(acts, units, 0, unit, head)
            aux = query_aux(table_ref[2 * pair + head], step, blocks)
            masked = jnp.where(lane_head(256, 128, head), queries, jnp.zeros_like(queries))
            scores[...] = lax.dot_general(
                jnp.concatenate([masked, aux], axis=1), keys, LAST, preferred_element_type=jnp.float32
            )
            for sub in range(2):
                start = pl.multiple_of(band_start(step * 2 + sub, blocks) * BLOCK, BLOCK)
                scores[sub * BLOCK : (sub + 1) * BLOCK, pl.ds(start, BAND * BLOCK)] += bias[
                    2 * pair + head, 2 * step + sub
                ].astype(jnp.float32)
            got = scores[...]
            highest = jnp.max(got, axis=1, keepdims=True)
            exponent = jnp.exp(got - highest)
            total = jnp.sum(exponent, axis=1, keepdims=True)
            outs.append(
                jnp.dot(exponent.astype(low), qkv[2 * pairs + pair], preferred_element_type=jnp.float32) * (1.0 / total)
            )
            lse = jnp.broadcast_to(highest + jnp.log(total), (256, 128))
            lse_ref[pair, step, head : head + 1, :] = jnp.transpose(lse)[0:1, :]
        attended[pair, rows, :] = jnp.where(lane_head(256, 128, 0), outs[0], outs[1]).astype(low)
        return carry

    lax.fori_loop(0, units, unit_step, 0)
    own_cot.wait()
    cot_x.wait()
    cot_c.start()

    normed_store.wait()
    two = normed
    gather.need(project_pieces)
    load_project = own_load(9, full_ref.at[:, :, :, :, at_project:at_hidden], project_w)
    load_project.start()
    load_project.wait()

    def branch(rows):
        left = jnp.concatenate([attended[pair, rows, :] for pair in range(pairs)], axis=1)
        return lax.dot_general(left, project_w[...].reshape(width, inner), LAST, preferred_element_type=jnp.float32)

    def part_rows(part, core):
        return pl.ds(pl.multiple_of(part * half + core * quarter, quarter), quarter)

    def swap_part(i, part, slot=0):
        return near(i + part, away.at[slot + part], arrived.at[slot + part], to_c)

    for part in range(2):
        away[part] = branch(part_rows(part, 1 - c)).astype(low)
        swap_part(6, part).start()
    for part in range(2):
        normal[part] = branch(part_rows(part, c)) + tok[part_rows(part, c), :].astype(jnp.float32)

    def share(i, part, buffer):
        return near(i + part, buffer.at[part_rows(part, c)], buffer.at[part_rows(part, c)], to_c)

    tokens_store = [own_load(11 + part, tok.at[part_rows(part, c)], tokens_own_ref.at[part]) for part in range(2)]
    for copy in tokens_store:
        copy.start()
    for part in range(2):
        swap_part(6, part).wait()
        middle = normal[part] + arrived[part].astype(jnp.float32)
        normal[part] = middle
        inverse = lax.rsqrt(jnp.mean(middle * middle, axis=-1, keepdims=True) + EPSILON)
        two[part_rows(part, c), :] = (middle * inverse * gain_two).astype(low)
        share(8, part, two).start()
    gather.run(1)
    for part in range(2):
        share(8, part, two).wait()

    def turn_step(i, carry):
        rows = pl.ds(pl.multiple_of(i * BLOCK, BLOCK), BLOCK)
        two_t[:, rows] = jnp.transpose(two[rows, :])
        return carry

    lax.fori_loop(0, blocks, turn_step, 0)
    gather.run(1)
    cot_c.wait()
    lax.fori_loop(0, blocks, live_step, 0)
    gather.run(1)

    def bounds(j):
        at = at_hidden + 3 * HIDDEN_STEP * j
        return at, at + 3 * steps[j]

    def load_step(j):
        a, b = bounds(j)
        return pltpu.make_async_copy(
            full_ref.at[:, :, :, :, a:b], w_buf.at[j % 2, :, :, :, :, 0 : b - a], w_sem.at[j % 2]
        )

    def store_step(j):
        a, b = bounds(j)
        return pltpu.make_async_copy(
            g_buf.at[j % 2, :, :, :, :, 0 : b - a],
            grads_out.at[:, :, :, :, a - at_hidden : b - at_hidden],
            g_sem.at[j % 2],
        )

    early_sums = []
    for k, (a, b, name) in enumerate(given):
        source = grads_out.at[:, :, 1 - x, :, a:b] if name == "x" else grads_out.at[:, 1 - place.y, :, :, a:b]
        device = to_x if name == "x" else place.device(y=1 - place.y)
        early_sums.append(send(source, came_outs[k], early_send.at[k], early_recv.at[k], device))
    gather.need(range(first_hidden_piece, first_hidden_piece + per_step))
    load_step(0).start()
    for j, units_here in enumerate(steps):
        n = units_here
        slot = j % 2
        load_step(j).wait()

        def weight(k, slot=slot, n=n):
            return w_buf[slot, :, :, :, :, k * n : (k + 1) * n].reshape(width, n)

        inside = gather.take(ROW_ACTS)

        def rows_step(i, carry, j=j, n=n, weight=weight, inside=inside):
            for k, act in enumerate(inside):
                pl.when(i == (2 * k + 1) * (length // 256) // (2 * len(inside)))(act)
            rows = pl.ds(pl.multiple_of(i * 256, 256), 256)
            left, grad = two[rows, :], cot[rows, :]
            gate = jnp.dot(left, weight(0), preferred_element_type=jnp.float32)
            up = jnp.dot(left, weight(1), preferred_element_type=jnp.float32)
            grad_hidden = jnp.dot(grad, weight(2), preferred_element_type=jnp.float32)
            value, slope = gelu_all(gate)
            hid[rows, 0:n] = (value * up).astype(low)
            ggate[rows, 0:n] = (grad_hidden * up * slope).astype(low)
            gup[rows, 0:n] = (grad_hidden * value).astype(low)
            out = lax.dot_general(hid[rows, 0:n], weight(2), LAST, preferred_element_type=jnp.float32)
            back = lax.dot_general(ggate[rows, 0:n], weight(0), LAST, preferred_element_type=jnp.float32)
            back = back + lax.dot_general(gup[rows, 0:n], weight(1), LAST, preferred_element_type=jnp.float32)
            if j == 0:
                acc_out[rows, :] = out
                acc_two[rows, :] = back
            else:
                acc_out[rows, :] += out
                acc_two[rows, :] += back
            return carry

        lax.fori_loop(0, length // 256, rows_step, 0)
        if j + 1 < len(steps):
            first = first_hidden_piece + per_step * (j + 1)
            gather.need(range(first, first + per_step))
            load_step(j + 1).start()
            if j + 2 == len(steps):
                for copy in early_sums:
                    copy.start()
        if j > 1:
            store_step(j - 2).wait()

        tiles = width // 256

        def grads_step(i, carry, slot=slot, n=n):
            rows = pl.ds(pl.multiple_of(i * 256, 256), 256)
            for k, (left, right) in enumerate(((two_t, ggate), (two_t, gup), (low_t, hid))):
                got = jnp.dot(left[rows, :], right[:, 0:n], preferred_element_type=jnp.float32).astype(low)
                span = deep // tiles
                g_buf[slot, pl.ds(i * span, span), :, :, :, k * n : (k + 1) * n] = got.reshape(
                    (span,) + g_buf.shape[2:5] + (n,)
                )
            return carry

        lax.fori_loop(0, tiles, grads_step, 0)
        store_step(j).start()
    gather.run(len(gather.queue))

    def share_sum(i, acc, slot):
        for part in range(2):
            away[slot + part] = acc[part_rows(part, 1 - c), :].astype(low)
            swap_part(i, part, slot).start()

    share_sum(10, acc_two, 0)
    for part in range(2):
        swap_part(10, part).wait()
        grad_two = acc_two[part_rows(part, c), :] + arrived[part].astype(jnp.float32)
        middle = normal[part]
        inverse = lax.rsqrt(jnp.mean(middle * middle, axis=-1, keepdims=True) + EPSILON)
        unit = middle * inverse
        weighted = jnp.sum((grad_two * unit).reshape(quarter // 8, 8, width), axis=0)
        gain_ref[part] = weighted
        scaled = grad_two * gain_two
        grad_middle = cot[part_rows(part, c), :].astype(jnp.float32) + inverse * (
            scaled - unit * jnp.mean(scaled * unit, axis=-1, keepdims=True)
        )
        middle_grad_ref[part] = grad_middle
        two[part_rows(part, c), :] = grad_middle.astype(low)
        share(12, part, two).start()
    share_sum(14, acc_out, 2)
    for part in range(2):
        swap_part(14, part, 2).wait()
        output_ref[part] = (normal[part] + acc_out[part_rows(part, c), :] + arrived[2 + part].astype(jnp.float32)).astype(low)
    for part in range(2):
        share(12, part, two).wait()
    for j in range(max(0, len(steps) - 2), len(steps)):
        store_step(j).wait()

    lax.fori_loop(0, blocks, turn_step, 0)

    def project_step(i, carry):
        rows = pl.ds(pl.multiple_of(i * 256, 256), 256)
        right = jnp.concatenate([attended[pair] for pair in range(pairs)], axis=1)
        got = jnp.dot(two_t[rows, :], right, preferred_element_type=jnp.float32).astype(low)
        span = deep // (width // 256)
        g_buf[0, pl.ds(i * span, span), :, :, :, 0:inner] = got.reshape((span,) + g_buf.shape[2:5] + (inner,))
        return carry

    lax.fori_loop(0, width // 256, project_step, 0)
    project_store = own_load(8, g_buf.at[0, :, :, :, :, 0:inner], grads_out.at[:, :, :, :, 3 * hidden : 3 * hidden + inner])
    project_store.start()

    def attended_step(i, carry):
        rows = pl.ds(pl.multiple_of(i * 256, 256), 256)
        got = jnp.dot(two[rows, :], project_w[...].reshape(width, inner), preferred_element_type=jnp.float32).astype(low)
        for pair in range(pairs):
            attended[pair, rows, :] = got[:, pair * 128 : (pair + 1) * 128]
        return carry

    lax.fori_loop(0, length // 256, attended_step, 0)
    attended_store = own_load(10, attended, attended_out)
    attended_store.start()
    for copy in (bandt_store, qkv_store, attended_store, project_store, *tokens_store, *early_sums):
        copy.wait()
    gather.sent()


def front(shard_size, pieces, window, given, lengths, gains, weights, inputs, cots, buckets, table_rows):
    low, f32 = jnp.bfloat16, jnp.float32
    deep = shard_size // 2
    rows, inner = weights[0].shape
    hidden = weights[4].shape[1]
    wide = pieces[-1][1]
    half, width = inputs.shape[1:]
    length, quarter = 2 * half, half // 2
    heads = table_rows.shape[0]
    blocks = length // BLOCK
    pairs = heads // 2
    shape = jax.ShapeDtypeStruct
    vmem, hbm = pl.BlockSpec(memory_space=pltpu.VMEM), pl.BlockSpec(memory_space=pl.ANY)
    dma = pltpu.SemaphoreType.DMA
    count = len(pieces)
    step = HIDDEN_STEP
    out_shape = [
        shape((deep, 2, 2, rows, wide), low),
        shape((width, length), low),
        shape((3 * pairs, length, 128), low),
        shape((blocks, BAND * BLOCK, BLOCK), low),
        shape((heads, blocks, BAND * BLOCK, BLOCK), low),
        shape((deep, 2, 2, rows, 3 * hidden + inner), low),
        shape((pairs, length, 128), low),
        shape((2, quarter, width), low),
        shape((pairs, length // 256, 2, 256), f32),
        shape((2, quarter, width), low),
        shape((2, quarter, width), f32),
        shape((2, 8, width), f32),
    ] + [shape((deep, 2, rows, b - a), low) for a, b, _ in given]
    scratch = [
        pltpu.VMEM((rows, wide), low),
        pltpu.VMEM((length, width), low),
        pltpu.VMEM((length, width), low),
        pltpu.VMEM((blocks // 2, BLOCK, BAND * BLOCK), jnp.int32),
        pltpu.VMEM((blocks, BLOCK, BAND * BLOCK), low),
        pltpu.VMEM((blocks, BAND * BLOCK, BLOCK), low),
        pltpu.VMEM((heads, blocks, BLOCK, BAND * BLOCK), low),
        pltpu.VMEM((2, heads, BAND * BLOCK, BLOCK), low),
        pltpu.VMEM((length, 128), low),
        pltpu.VMEM((deep, 2, 2, rows, 128), low),
        pltpu.VMEM((3 * pairs, length, 128), low),
        pltpu.VMEM((length, width), low),
        pltpu.VMEM((256, length), f32),
        pltpu.VMEM((pairs, length, 128), low),
        pltpu.VMEM((deep, 2, 2, rows, inner), low),
        pltpu.VMEM((2, quarter, width), f32),
        pltpu.VMEM((4, quarter, width), low),
        pltpu.VMEM((4, quarter, width), low),
        pltpu.VMEM((width, length), low),
        pltpu.VMEM((width, length), low),
        pltpu.VMEM((length, width), f32),
        pltpu.VMEM((length, width), f32),
        pltpu.VMEM((2, deep, 2, 2, rows, 3 * step), low),
        pltpu.VMEM((2, deep, 2, 2, rows, 3 * step), low),
        pltpu.VMEM((length, step), low),
        pltpu.VMEM((length, step), low),
        pltpu.VMEM((length, step), low),
        dma((count, 3, deep - 1)),
        dma((count, 3, deep - 1)),
        dma((16 + blocks // 2,)),
        dma((16 + blocks // 2,)),
        dma((13 + blocks // 2,)),
        dma((2,)),
        dma((2,)),
        dma((5 + 3 * len(hidden_steps(hidden)),)),
        dma((2,)),
        dma((len(given),)),
        dma((len(given),)),
    ]
    return pl.pallas_call(
        functools.partial(front_kernel, shard_size, pieces, window, (inner, hidden), given),
        out_shape=out_shape,
        in_specs=[pl.BlockSpec(memory_space=pltpu.SMEM)] + [hbm] * 11 + [vmem],
        out_specs=[hbm] * 8 + [vmem] * 4 + [hbm] * len(given),
        scratch_shapes=scratch,
        compiler_params=pltpu.CompilerParams(
            collective_id=1, has_side_effects=True, vmem_limit_bytes=60 * MIB
        ),
        name="front",
    )(lengths, gains, *weights, inputs, cots, buckets, table_rows)


GROUP = 16
TURNS = 4


class Scatter:
    def __init__(self, place, pieces, sources, outs, buffers, sems, came):
        self.came = came
        self.place, self.pieces, self.sources, self.outs = place, pieces, sources, outs
        self.first, self.own, self.second, self.third = buffers
        self.own_sem, self.send_sem, self.recv_sem = sems
        self.queue = []

    def peer(self, name):
        place = self.place
        return place.device(y=1 - place.y) if name == "y" else place.device(x=1 - place.x)

    def rest(self, piece):
        order = self.pieces[piece][3]
        return [name for name in "zyx" if name != order[0]]

    def cut(self, piece, name, value):
        t, a, b = self.pieces[piece][:3]
        at = [value if name == other else slice(None) for other in "zyx"]
        if t:
            return self.sources[1].at[t - 1, at[0], at[1], at[2]]
        return self.sources[0].at[at[0], at[1], at[2], :, a:b]

    def own_copy(self, piece):
        order = self.pieces[piece][3]
        return pltpu.make_async_copy(
            self.cut(piece, order[0], getattr(self.place, order[0])), self.own[piece], self.own_sem.at[piece]
        )

    def copies(self, piece, hop):
        place, order = self.place, self.pieces[piece][3]
        name, rest = order[hop], self.rest(piece)
        own, made = self.own[piece], []

        def at(**index):
            return tuple(index[n] if n in index else slice(None) for n in rest)

        def add(source, target, device):
            i = len(made)
            made.append(send(source, target, self.send_sem.at[piece, hop, i], self.recv_sem.at[piece, hop, i], device))

        if hop == 0:
            if name == "z":
                for d in range(1, place.deep):
                    z = place.line(d)
                    add(self.cut(piece, "z", z), self.first[piece].at[d - 1], place.device(z=z))
            else:
                add(self.cut(piece, name, 1 - getattr(place, name)), self.first[piece], self.peer(name))
            return made
        fixed = {} if hop == 1 else {order[1]: getattr(place, order[1])}
        buffer = self.second[piece] if hop == 1 else self.third[piece]
        if name == "z":
            for d in range(1, place.deep):
                z = place.line(d)
                add(own.at[at(z=z, **fixed)], buffer.at[d - 1], place.device(z=z))
        else:
            add(own.at[at(**{name: 1 - getattr(place, name)}, **fixed)], buffer, self.peer(name))
        return made

    def start(self, piece, hop):
        for copy in self.copies(piece, hop):
            copy.start()

    def arrive(self, piece, hop):
        for copy in self.copies(piece, hop):
            copy.wait_recv()

    def came_copy(self, piece):
        return pltpu.make_async_copy(self.came[piece], self.first[piece], self.recv_sem.at[piece, 0, 0])

    def begin(self, piece):
        if piece < len(self.came):
            self.came_copy(piece).start()
        else:
            self.start(piece, 0)
        self.own_copy(piece).start()

    def add_first(self, piece):
        order = self.pieces[piece][3]
        if piece < len(self.came):
            self.came_copy(piece).wait()
        else:
            self.arrive(piece, 0)
        self.own_copy(piece).wait()
        if piece >= len(self.came) and self.waiting:
            self.begin(self.waiting.pop(0))
        own, came = self.own[piece], self.first[piece]
        inner = own.shape[1]

        def body(i, carry):
            for k in range(inner):
                if order[0] == "z":
                    total = own[i, k].astype(jnp.float32)
                    for d in range(came.shape[0]):
                        total = total + came[d, i, k].astype(jnp.float32)
                    own[i, k] = total.astype(jnp.bfloat16)
                else:
                    own[i, k] = own[i, k] + came[i, k]
            return carry

        lax.fori_loop(0, own.shape[0], body, 0)
        self.start(piece, 1)

    def add_second(self, piece):
        place, order = self.place, self.pieces[piece][3]
        name, rest = order[1], self.rest(piece)
        self.arrive(piece, 1)
        own, came = self.own[piece], self.second[piece]
        mine = getattr(place, name)
        spans = own.shape[1] if rest[0] == name else own.shape[0]

        def body(i, carry):
            if name == "z":
                total = own[mine, i].astype(jnp.float32)
                for d in range(came.shape[0]):
                    total = total + came[d, i].astype(jnp.float32)
                own[mine, i] = total.astype(jnp.bfloat16)
            elif rest[0] == name:
                own[mine, i] = own[mine, i] + came[i]
            else:
                own[i, mine] = own[i, mine] + came[i]
            return carry

        lax.fori_loop(0, spans, body, 0)
        self.start(piece, 2)

    def add_third(self, piece):
        place, order = self.place, self.pieces[piece][3]
        rest = self.rest(piece)
        self.arrive(piece, 2)
        total = self.own[piece][getattr(place, rest[0]), getattr(place, rest[1])].astype(jnp.float32)
        if order[2] == "z":
            for d in range(1, place.deep):
                total = total + self.third[piece][d - 1].astype(jnp.float32)
        else:
            total = total + self.third[piece][...].astype(jnp.float32)
        for out, start, at, n in self.pieces[piece][4]:
            self.outs[out][:, start : start + n] = total[:, at : at + n]

    def plan(self, window):
        self.waiting = [i for i, piece in enumerate(self.pieces) if piece[0] == 0]
        count = len(self.pieces)
        for i in range(count + SUM_LAGS[1]):
            if i < count:
                self.queue.append(functools.partial(self.add_first, i))
            if 0 <= i - SUM_LAGS[0] < count:
                self.queue.append(functools.partial(self.add_second, i - SUM_LAGS[0]))
            if 0 <= i - SUM_LAGS[1] < count:
                self.queue.append(functools.partial(self.add_third, i - SUM_LAGS[1]))
        for _ in range(min(len(self.came) + window, len(self.waiting))):
            self.begin(self.waiting.pop(0))

    def run(self, steps):
        for _ in range(min(steps, len(self.queue))):
            self.queue.pop(0)()

    def take(self, steps):
        taken, self.queue = self.queue[:steps], self.queue[steps:]
        return taken

    def sent(self):
        for piece in range(len(self.pieces)):
            for hop in range(0 if piece >= len(self.came) else 1, 3):
                for copy in self.copies(piece, hop):
                    copy.wait_send()


def piece_buffers(piece, deep, rows):
    _, a, b, order, _ = piece
    sizes = {"z": deep, "y": 2, "x": 2}
    rest = [name for name in "zyx" if name != order[0]]
    left = [sizes[name] for name in rest]
    last = [sizes[name] for name in rest if name != order[1]]
    tail = [rows, b - a]
    lead = [deep - 1]
    first = (lead if order[0] == "z" else []) + left + tail
    second = (lead if order[1] == "z" else []) + last + tail
    third = (lead if order[2] == "z" else []) + tail
    return [tuple(shape) for shape in (first, left + tail, second, third)]


def back_kernel(shard_size, pieces, sizes, given, *refs):
    inner, hidden, buckets = sizes
    count = len(pieces)
    (
        lengths_ref, full_ref, normed_in, qkv_in, bandt_in, biast_in, grads_in, do_in,
        lse_ref, output_ref, middle_ref, tokens_ref, gain_two_ref, table_ref,
    ) = refs[:14]
    came, refs = refs[14 : 14 + given], refs[14 + given :]
    weight_outs, (output_out, input_out, small_out) = refs[:7], refs[7:10]
    refs = refs[10:]
    first, own, second, third = [refs[k * count : (k + 1) * count] for k in range(4)]
    refs = refs[4 * count :]
    (
        qkv, normed_t, bandt, bias, wqkv, gain_buf, do, scores, grads, far, dk_acc, dv_acc, kaux, wgrad,
        mine_sum, away, arrived, result, table_acc, hot, found,
        small, small_x, small_y, hold_x, hold_y, hold_z, small_c,
        own_sem, send_sem, recv_sem, near_send, near_recv, local_sem,
    ) = refs
    length = qkv.shape[1]
    width = normed_t.shape[0]
    half, quarter = length // 2, length // 4
    heads, blocks = bias.shape[:2]
    pairs = heads // 2
    deep = shard_size // 2
    low, f32 = jnp.bfloat16, jnp.float32
    place = Place(shard_size)
    x, y, z, c = place.x, place.y, place.z, place.c
    to_x, to_y, to_c = place.device(x=1 - x), place.device(y=1 - y), place.device(c=1 - c)

    def local(i, source, target):
        return pltpu.make_async_copy(source, target, local_sem.at[i])

    loads = [
        local(0, qkv_in, qkv), local(1, biast_in, bias), local(2, do_in, do),
        local(3, full_ref.at[:, :, :, :, 128 : 128 + 3 * inner], wqkv), local(4, normed_in, normed_t),
        local(5, bandt_in, bandt), local(6, full_ref.at[:, :, :, :, 0:128], gain_buf),
    ]
    for copy in loads:
        copy.start()
    meet(place)
    scatter = Scatter(
        place, pieces, (grads_in, wgrad), weight_outs, (first, own, second, third), (own_sem, send_sem, recv_sem), came,
    )
    scatter.plan(SUM_WINDOW)

    def near(i, source, target, device):
        return send(source, target, near_send.at[i], near_recv.at[i], device)

    def to_owners(i, values, out):
        here = out.at[x, pl.ds(c * quarter, quarter)]
        there = out.at[1 - x, pl.ds(c * quarter, quarter)]
        return (
            local(7 + i, values.at[x], here),
            near(4 * i, values.at[x], here, to_c),
            near(4 * i + 1, values.at[1 - x], here, to_x),
            near(4 * i + 2, there, there, to_c),
        )

    output_moves = to_owners(0, output_ref, output_out)
    for copy in output_moves[:3]:
        copy.start()

    lanes_of = lax.broadcasted_iota(jnp.int32, (length, 128), 1)
    rows_of = lax.broadcasted_iota(jnp.int32, (length, 128), 0)
    valid = lengths_ref[x, 0]
    blocked = jnp.where(rows_of // BLOCK == lanes_of, 1.0, 0.0)
    kaux[...] = jnp.where((lanes_of == blocks) & (rows_of >= valid), -1e30, blocked).astype(low)
    far[...] = jnp.zeros_like(far)
    for copy in loads:
        copy.wait()

    per_pair = length // 256
    units = pairs * per_pair
    acts = scatter.take(ATTENTION_ACTS)

    def unit_step(unit, carry):
        pair = unit // per_pair
        step = unit % per_pair
        rows = pl.ds(pl.multiple_of(step * 256, 256), 256)

        @pl.when(step == 0)
        def _():
            dk_acc[...] = jnp.zeros_like(dk_acc)
            dv_acc[...] = jnp.zeros_like(dv_acc)

        queries = qkv[pair, rows, :]
        grad = do[pair, rows, :]
        key_pair = qkv[pairs + pair]
        keys = jnp.concatenate([key_pair, kaux[...]], axis=1)
        values = qkv[2 * pairs + pair]
        dq = None
        for head in range(2):
            between(acts, units, ACT_FIRST, unit, head)
            here = lane_head(256, 128, head)
            aux = query_aux(table_ref[2 * pair + head], step, blocks)
            q_masked = jnp.where(here, queries, jnp.zeros_like(queries))
            do_masked = jnp.where(here, grad, jnp.zeros_like(grad))
            scores[...] = lax.dot_general(
                keys, jnp.concatenate([q_masked, aux], axis=1), LAST, preferred_element_type=f32
            )
            for sub in range(2):
                start = pl.multiple_of(band_start(step * 2 + sub, blocks) * BLOCK, BLOCK)
                scores[pl.ds(start, BAND * BLOCK), sub * BLOCK : (sub + 1) * BLOCK] += bias[
                    2 * pair + head, 2 * step + sub
                ].astype(f32)
            soft = jnp.exp(scores[...] - lse_ref[pair, step, head : head + 1, :])
            dv_acc[...] += jnp.dot(soft.astype(low), do_masked, preferred_element_type=f32)
            grad_probs = lax.dot_general(values, do_masked, LAST, preferred_element_type=f32)
            weighted = jnp.sum(soft * grad_probs, axis=0, keepdims=True)
            grad_scores = (soft * (grad_probs - weighted)).astype(low)
            grads[...] = grad_scores
            dk_acc[...] += jnp.dot(grad_scores, q_masked, preferred_element_type=f32)
            k_masked = jnp.where(lane_head(length, 128, head), key_pair, jnp.zeros_like(key_pair))
            part = lax.dot_general(grad_scores, k_masked, FIRST, preferred_element_type=f32)
            dq = part if dq is None else dq + part
            sums = jnp.concatenate(
                [
                    jnp.sum(grad_scores[block * BLOCK : (block + 1) * BLOCK, :].astype(f32), axis=0, keepdims=True)
                    for block in range(blocks)
                ],
                axis=0,
            )
            block_of = lax.broadcasted_iota(jnp.int32, (blocks, BLOCK), 0)
            for sub in range(2):
                start = band_start(step * 2 + sub, blocks)
                at = pl.multiple_of(start * BLOCK, BLOCK)
                bias[2 * pair + head, 2 * step + sub] = grads[pl.ds(at, BAND * BLOCK), sub * BLOCK : (sub + 1) * BLOCK]
                part = sums[:, sub * BLOCK : (sub + 1) * BLOCK]
                far[0, 2 * pair + head] += jnp.where(block_of < start, part, 0.0)
                far[1, 2 * pair + head] += jnp.where(block_of >= start + BAND, part, 0.0)
        qkv[pair, rows, :] = dq.astype(low)

        @pl.when(step == per_pair - 1)
        def _():
            qkv[pairs + pair] = dk_acc[...].astype(low)
            qkv[2 * pairs + pair] = dv_acc[...].astype(low)
            right = jnp.concatenate([qkv[t * pairs + pair] for t in range(3)], axis=1)

            def weight_step(i, carry):
                rows = pl.ds(pl.multiple_of(i * 256, 256), 256)
                got = jnp.dot(normed_t[rows, :], right, preferred_element_type=f32).astype(low)
                span = deep // (width // 256)
                wgrad[pair, pl.ds(i * span, span)] = got.reshape((span,) + wgrad.shape[2:5] + (3 * 128,))
                return carry

            lax.fori_loop(0, width // 256, weight_step, 0)

        for late, piece in enumerate(pieces):
            if piece[0]:
                @pl.when(unit == piece[0] * per_pair - 1)
                def _(late=late):
                    scatter.begin(late)

        return carry

    lax.fori_loop(0, units, unit_step, 0)
    for copy in output_moves[:3]:
        copy.wait()
    output_moves[3].start()
    def part_rows(part, core):
        return pl.ds(pl.multiple_of(part * half + core * quarter, quarter), quarter)

    def grad_one(rows):
        left = jnp.concatenate([qkv[k, rows, :] for k in range(3 * pairs)], axis=1)
        return lax.dot_general(left, wqkv[...].reshape(width, 3 * inner), LAST, preferred_element_type=f32)

    swaps = [near(8 + part, away.at[part], arrived.at[part], to_c) for part in range(2)]

    def away_step(part, carry):
        away[part] = grad_one(part_rows(part, 1 - c)).astype(low)
        return carry

    def mine_step(part, carry):
        mine_sum[part] = grad_one(part_rows(part, c))
        return carry

    lax.fori_loop(0, 2, away_step, 0)
    for copy in swaps:
        copy.start()
    scatter.run(1)
    lax.fori_loop(0, 2, mine_step, 0)
    scatter.run(1)
    gains = jnp.transpose(gain_buf[...].reshape(width, 128).astype(f32))
    gain_one = gains[0:1, :]
    gain_sum = jnp.zeros((1, width), f32)
    for part in range(2):
        swaps[part].wait()
        total = mine_sum[part] + arrived[part].astype(f32)
        present = tokens_ref[part].astype(f32)
        inverse = lax.rsqrt(jnp.mean(present * present, axis=-1, keepdims=True) + EPSILON)
        unit = present * inverse
        gain_sum = gain_sum + jnp.sum(total * unit, axis=0, keepdims=True)
        scaled = total * gain_one
        back = inverse * (scaled - unit * jnp.mean(scaled * unit, axis=-1, keepdims=True))
        result[part] = (middle_ref[part] + back).astype(low)
        scatter.run(1)
    input_moves = to_owners(1, result, input_out)
    for copy in input_moves[:3]:
        copy.start()
    table_acc[...] = jnp.zeros_like(table_acc)
    groups = BAND * BLOCK // GROUP
    table_units = blocks // 2 * groups // TURNS
    table_acts = scatter.take(TABLE_ACTS)

    def table_step(i, carry):
        for k, act in enumerate(table_acts):
            @pl.when(i == (k * table_units) // max(1, len(table_acts)))
            def _(act=act):
                act()
        total = None
        for turn in range(TURNS):
            group = i * TURNS + turn
            block = 2 * (group // groups)
            start = pl.multiple_of((group % groups) * GROUP, GROUP)
            for two in range(2):
                lanes = slice(two * BLOCK, (two + 1) * BLOCK)
                index = bandt[block + two, pl.ds(start, GROUP), :]
                for head in range(heads):
                    found[turn, head * GROUP : (head + 1) * GROUP, lanes] = bias[head, block + two, pl.ds(start, GROUP), :]
                for b in range(buckets):
                    hot[turn, b * GROUP : (b + 1) * GROUP, lanes] = jnp.where(
                        index == jnp.asarray(b, low), jnp.asarray(1, low), jnp.asarray(0, low)
                    )
            part = lax.dot_general(hot[turn], found[turn], LAST, preferred_element_type=f32)
            total = part if total is None else total + part
        table_acc[...] += total
        return carry

    lax.fori_loop(0, table_units, table_step, 0)
    row = lax.broadcasted_iota(jnp.int32, table_acc.shape, 0) % GROUP
    col = lax.broadcasted_iota(jnp.int32, table_acc.shape, 1) % GROUP
    kept = jnp.where(row == col, table_acc[...], 0.0).reshape(buckets, GROUP, heads * GROUP).sum(axis=1)
    bucket = lax.broadcasted_iota(jnp.int32, (buckets, 128), 0)
    head_of = lax.broadcasted_iota(jnp.int32, (buckets, 128), 1)
    table = jnp.zeros((buckets, 128), f32)
    for head in range(heads):
        amount = jnp.sum(kept[:, head * GROUP : (head + 1) * GROUP], axis=1, keepdims=True)
        table = table + jnp.where(head_of == head, amount, 0.0)
    for side, name in enumerate((buckets // 2 - 1, buckets - 1)):
        for head in range(heads):
            amount = jnp.sum(jnp.sum(far[side, head], axis=0, keepdims=True), axis=1, keepdims=True)
            table = table + jnp.where((bucket == name) & (head_of == head), amount, 0.0)

    lines = width // 128
    for i in range(lines):
        small[i : i + 1, :] = gain_sum[:, i * 128 : (i + 1) * 128]
    small[lines : 2 * lines, :] = gain_two_ref[...]
    small[2 * lines : 2 * lines + buckets, :] = table
    small_base = 10

    def small_line(d):
        return near(small_base + 2 + d, hold_z.at[z], hold_z.at[z], place.device(z=place.line(d)))

    move = near(small_base, small, small_x, to_x)
    move.start()
    scatter.run(1)
    move.wait()
    hold_x[...] = small[...] + small_x[...]
    move = near(small_base + 1, hold_x, small_y, to_y)
    move.start()
    scatter.run(1)
    move.wait()
    hold_z[z] = hold_x[...] + small_y[...]
    for d in range(1, deep):
        small_line(d).start()
    scatter.run(1)
    for d in range(1, deep):
        small_line(d).wait()
    hold_y[...] = jnp.sum(hold_z[...], axis=0)
    move = near(small_base + 2, hold_y, small_c, to_c)
    move.start()
    scatter.run(1)
    move.wait()
    small_out[0] = hold_y[...]
    small_out[1] = hold_y[...] + small_c[...]

    for copy in input_moves[:3]:
        copy.wait()
    input_moves[3].start()
    input_moves[3].wait()
    output_moves[3].wait()
    scatter.run(len(scatter.queue))
    scatter.sent()


def back(shard_size, pieces, buckets, lengths, full, normed_t, qkv, bandt, biast, grads, do, lse, output, middle, tokens, gain_two, table_rows, came):
    low, f32 = jnp.bfloat16, jnp.float32
    deep = shard_size // 2
    rows = full.shape[3]
    width, length = normed_t.shape
    half, quarter = length // 2, length // 4
    heads, blocks = biast.shape[:2]
    pairs = heads // 2
    inner = pairs * 128
    hidden = (grads.shape[4] - inner) // 3
    count = len(pieces)
    shape = jax.ShapeDtypeStruct
    vmem, hbm = pl.BlockSpec(memory_space=pltpu.VMEM), pl.BlockSpec(memory_space=pl.ANY)
    dma = pltpu.SemaphoreType.DMA
    lines = 2 * (width // 128) + buckets
    buffers = [piece_buffers(piece, deep, rows) for piece in pieces]
    scratch = [pltpu.VMEM(buffer[k], low) for k in range(4) for buffer in buffers]
    small = pltpu.VMEM((lines, 128), f32)
    scratch += [
        pltpu.VMEM((3 * pairs, length, 128), low),
        pltpu.VMEM((width, length), low),
        pltpu.VMEM((blocks, BAND * BLOCK, BLOCK), low),
        pltpu.VMEM((heads, blocks, BAND * BLOCK, BLOCK), low),
        pltpu.VMEM((deep, 2, 2, rows, 3 * inner), low),
        pltpu.VMEM((deep, 2, 2, rows, 128), low),
        pltpu.VMEM((pairs, length, 128), low),
        pltpu.VMEM((length, 256), f32),
        pltpu.VMEM((length, 256), low),
        pltpu.VMEM((2, heads, blocks, BLOCK), f32),
        pltpu.VMEM((length, 128), f32),
        pltpu.VMEM((length, 128), f32),
        pltpu.VMEM((length, 128), low),
        pltpu.VMEM((pairs, deep, 2, 2, rows, 3 * 128), low),
        pltpu.VMEM((2, quarter, width), f32),
        pltpu.VMEM((2, quarter, width), low),
        pltpu.VMEM((2, quarter, width), low),
        pltpu.VMEM((2, quarter, width), low),
        pltpu.VMEM((buckets * GROUP, heads * GROUP), f32),
        pltpu.VMEM((TURNS, buckets * GROUP, 2 * BLOCK), low),
        pltpu.VMEM((TURNS, heads * GROUP, 2 * BLOCK), low),
        small, small, small, small, small, pltpu.VMEM((deep, lines, 128), f32), small,
        dma((count,)),
        dma((count, 3, deep - 1)),
        dma((count, 3, deep - 1)),
        dma((12 + deep,)),
        dma((12 + deep,)),
        dma((9,)),
    ]
    return pl.pallas_call(
        functools.partial(back_kernel, shard_size, pieces, (inner, hidden, buckets), len(came)),
        out_shape=[
            *[shape((rows, n), f32) for n in (inner,) * 4 + (hidden,) * 3],
            shape((2, half, width), low),
            shape((2, half, width), low),
            shape((2, lines, 128), f32),
        ],
        in_specs=[pl.BlockSpec(memory_space=pltpu.SMEM)] + [hbm] * 7 + [vmem] * 6 + [hbm] * len(came),
        out_specs=[vmem] * 7 + [hbm, hbm, vmem],
        scratch_shapes=scratch,
        compiler_params=pltpu.CompilerParams(
            collective_id=2, has_side_effects=True, vmem_limit_bytes=60 * MIB
        ),
        name="back",
    )(lengths, full, normed_t, qkv, bandt, biast, grads, do, lse, output, middle, tokens, gain_two, table_rows, *came)


def finish_kernel(*refs):
    count = len(refs) // 2
    for source, target in zip(refs[:count], refs[count:]):
        target[...] = source[...].astype(target.dtype)


def finish(weight_sums, output, input_grad):
    steps = 4 if weight_sums[0].shape[0] % 32 == 0 else 2
    values = [*weight_sums, output, input_grad]
    kinds = [jnp.float32] * len(weight_sums) + [output.dtype, jnp.float32]
    specs = [pl.BlockSpec((w.shape[0] // steps, w.shape[1]), lambda i: (i, 0)) for w in weight_sums]
    specs += [pl.BlockSpec((2, v.shape[1] // steps, v.shape[2]), lambda i: (0, i, 0)) for v in (output, input_grad)]
    return pl.pallas_call(
        finish_kernel,
        grid=(steps,),
        in_specs=specs,
        out_specs=specs,
        out_shape=[jax.ShapeDtypeStruct(v.shape, kind) for v, kind in zip(values, kinds)],
        compiler_params=pltpu.CompilerParams(vmem_limit_bytes=60 * MIB),
        name="finish",
    )(*values)


ORDERS = ("xyz", "zxy", "zyx", "zxy", "zxy", "zyx", "zxy", "zyx", "zxy")
SUM_ORDERS = ("yxz", "xyz", "yzx", "xzy", "yxz", "yxz")
GIVEN = 4
LATE_FIRST = 6
LATE_STEP = 3
ROW_ACTS = 2
WINDOW = 4
AHEAD = 2
LAG = 3
QUICK = 4
SUM_WINDOW = 3
SUM_LAGS = (2, 4)
FORWARD_ACTS = 8
ATTENTION_ACTS = 20
ACT_FIRST = 5
TABLE_ACTS = 7


def front_pieces(inner, hidden):
    at_project = 128 + 3 * inner
    at_hidden = at_project + inner
    pieces = split_columns(0, at_project, 4) + split_columns(at_project, at_hidden, 2)
    for j, n in enumerate(hidden_steps(hidden)):
        at = at_hidden + 3 * HIDDEN_STEP * j
        pieces += split_columns(at, at + 3 * n, 2)
    return [(a, b, ORDERS[i % len(ORDERS)]) for i, (a, b) in enumerate(pieces)]


def back_pieces(inner, hidden):
    where = []
    for j, n in enumerate(hidden_steps(hidden)):
        for k in range(3):
            where.append((3 * HIDDEN_STEP * j + k * n, n, 4 + k, HIDDEN_STEP * j))
    where.append((3 * hidden, inner, 3, 0))
    cuts = []
    for j, n in enumerate(hidden_steps(hidden)):
        at = 3 * HIDDEN_STEP * j
        cuts += split_columns(at, at + 3 * n, 2 if n > 128 else 1)
    cuts += split_columns(3 * hidden, 3 * hidden + inner, 2)
    pieces = []
    for a, b in cuts:
        segments = []
        for start, n, out, column in where:
            low, high = max(a, start), min(b, start + n)
            if low < high:
                segments.append((out, column + low - start, low - a, high - low))
        pieces.append((0, a, b, segments))
    for pair in range(inner // 128):
        piece = (1 + pair, 0, 3 * 128, [(t, pair * 128, t * 128, 128) for t in range(3)])
        pieces.insert(min(len(pieces), LATE_FIRST + LATE_STEP * pair), piece)
    return [(t, a, b, SUM_ORDERS[i % len(SUM_ORDERS)], segments) for i, (t, a, b, segments) in enumerate(pieces)]


def shards(
    inputs, cotangent, lengths, buckets,
    query_weight, key_weight, value_weight, projection_weight, gate_weight, up_weight, down_weight,
    attention_gain, feedforward_gain, bias_table,
):
    x = lax.axis_index("ctx")
    shard_size = lax.axis_size("shard")
    width = inputs.shape[2]
    bucket_count, heads = bias_table.shape
    rows, inner = query_weight.shape
    hidden = gate_weight.shape[1]
    cuts = back_pieces(inner, hidden)
    gains = jnp.pad(jnp.stack([attention_gain, feedforward_gain], axis=1), ((0, 0), (0, 126)))
    table_rows = jnp.broadcast_to(
        jnp.pad(bias_table.astype(jnp.float32).T, ((0, 0), (0, 128 - bucket_count)))[:, None, :], (heads, 8, 128)
    )
    weights = (query_weight, key_weight, value_weight, projection_weight, gate_weight, up_weight, down_weight)
    (
        full, normed_t, qkv, bandt, biast, grads, grad_attended, tokens,
        lse, output, grad_middle, gain_two, *came,
    ) = front(shard_size, front_pieces(inner, hidden), WINDOW, [(a, b, order[0]) for _, a, b, order, _ in cuts[:GIVEN]], lengths, gains, weights, inputs, cotangent, buckets, table_rows)

    gain_two = jnp.sum(gain_two, axis=(0, 1)).reshape(-1, 128)
    *weight_sums, output, input_grad, small = back(
        shard_size, cuts, bucket_count,
        lengths, full, normed_t, qkv, bandt, biast, grads, grad_attended,
        lse, output, grad_middle, tokens, gain_two, table_rows, came,
    )
    *weight_sums, output, input_grad = finish(weight_sums, output, input_grad)
    lines = width // 128
    me = lax.axis_index("shard") * 2 + x

    def own_gain(part):
        return lax.dynamic_slice_in_dim(small[1, part * lines : (part + 1) * lines].reshape(-1), me * rows, rows)

    return (
        output, input_grad,
        *weight_sums, own_gain(0), own_gain(1), small[0, 2 * lines :, :heads],
    )


def solution(mesh):
    rows = P(None, ("shard", "ctx"), None)
    weight = P(("shard", "ctx"), "tp")
    gain = P(("shard", "ctx"))
    table = P(None, "tp")
    return jax.shard_map(
        shards,
        mesh=mesh,
        in_specs=(rows, rows, P(None, "shard"), P("ctx", None)) + (weight,) * 7 + (gain, gain, table),
        out_specs=(rows, rows) + (weight,) * 7 + (gain, gain, table),
        check_vma=False,
    )
```

```python
import functools

import jax
import jax.numpy as jnp
from jax import lax
from jax.experimental import pallas as pl
from jax.experimental.pallas import tpu as pltpu
from jax.sharding import PartitionSpec as P

EPSILON = 1e-06
GELU_ROOT = 0.7978845608028654
GELU_CUBIC = 0.044715
MESH = pl.DeviceIdType.MESH
MIB = 1024 * 1024


BAND = 3
BLOCK = 128


def lane_head(rows, width, which):
    lanes = lax.broadcasted_iota(jnp.int32, (rows, width), 1)
    half = width // 2
    return (lanes < half) if which == 0 else (lanes >= half)


def band_start(row_block, blocks):
    return jnp.clip(row_block - 1, 0, blocks - BAND)


def split_columns(start, stop, pieces):
    tiles = (stop - start) // 128
    edges = [start + 128 * (tiles * i // pieces) for i in range(pieces + 1)]
    return [(a, b) for a, b in zip(edges, edges[1:]) if b > a]


class Place:
    def __init__(self, shard_size):
        self.deep = shard_size // 2
        shard = lax.axis_index("shard")
        self.z = shard // 2
        self.y = shard % 2
        self.x = lax.axis_index("ctx")
        self.c = lax.axis_index("tp")

    def device(self, z=None, y=None, x=None, c=None):
        z = self.z if z is None else z
        y = self.y if y is None else y
        x = self.x if x is None else x
        c = self.c if c is None else c
        return (z * 2 + y, x, c)

    def line(self, distance):
        return (self.z + distance) % self.deep

    def peers(self):
        others = [self.device(z=self.line(d)) for d in range(1, self.deep)]
        return others + [self.device(y=1 - self.y), self.device(x=1 - self.x), self.device(c=1 - self.c)]


def meet(place):
    barrier = pltpu.get_barrier_semaphore()
    peers = place.peers()
    for peer in peers:
        pl.semaphore_signal(barrier, inc=1, device_id=peer, device_id_type=MESH)
    pl.semaphore_wait(barrier, len(peers))


def send(source, target, send_sem, recv_sem, device):
    return pltpu.make_async_remote_copy(
        src_ref=source, dst_ref=target, send_sem=send_sem, recv_sem=recv_sem, device_id=device, device_id_type=MESH
    )


LAST = (((1,), (1,)), ((), ()))
FIRST = (((0,), (0,)), ((), ()))
HIDDEN_STEP = 256
HALF_BUCKETS = 16


def hidden_steps(hidden):
    return [min(HIDDEN_STEP, hidden - at) for at in range(0, hidden, HIDDEN_STEP)]


class Gather:
    def __init__(self, place, pieces, own_ref, full_ref, send_sem, recv_sem):
        self.place, self.pieces, self.own, self.full = place, pieces, own_ref, full_ref
        self.send_sem, self.recv_sem = send_sem, recv_sem
        self.queue = []

    def held(self, piece, hop):
        a, b, order = self.pieces[piece]
        place, done = self.place, order[:hop]
        at = [slice(None) if name in done else getattr(place, name) for name in "zyx"]
        return self.full.at[at[0], at[1], at[2], :, a:b]

    def copies(self, piece, hop):
        place = self.place
        a, b, order = self.pieces[piece]
        target = self.held(piece, hop)
        source = self.own.at[:, a:b] if hop == 0 else target
        name = order[hop]
        if name == "z":
            peers = [place.device(z=place.line(d)) for d in range(1, place.deep)]
        elif name == "y":
            peers = [place.device(y=1 - place.y)]
        else:
            peers = [place.device(x=1 - place.x)]
        return [
            send(source, target, self.send_sem.at[piece, hop, i], self.recv_sem.at[piece, hop, i], peer)
            for i, peer in enumerate(peers)
        ]

    def start(self, piece, hop):
        for copy in self.copies(piece, hop):
            copy.start()

    def arrive(self, piece, hop):
        for copy in self.copies(piece, hop):
            copy.wait_recv()

    def sent(self):
        for piece in range(len(self.pieces)):
            for hop in range(3):
                for copy in self.copies(piece, hop):
                    copy.wait_send()

    def plan(self, window):
        count = len(self.pieces)
        self.window = window

        def second(piece):
            def act():
                self.arrive(piece, 0)
                self.start(piece, 1)
                if piece + window < count:
                    self.start(piece + window, 0)
            return act

        def third(piece):
            def act():
                self.arrive(piece, 1)
                self.start(piece, 2)
            return act

        turned = 0
        for piece in range(count + LAG):
            if piece < count:
                self.queue.append((None, second(piece)))
            while turned < count and turned <= piece - (1 if turned < QUICK else LAG):
                self.queue.append((turned, third(turned)))
                turned += 1
        for piece in range(min(window, count)):
            self.start(piece, 0)

    def run(self, steps):
        for _ in range(min(steps, len(self.queue))):
            self.queue.pop(0)[1]()

    def take(self, steps):
        taken, self.queue = self.queue[:steps], self.queue[steps:]
        return [act for _, act in taken]

    def need(self, pieces):
        for piece in pieces:
            while any(mark == piece for mark, _ in self.queue):
                self.run(1)
        self.run(AHEAD)
        for piece in pieces:
            self.arrive(piece, 2)


def query_aux(table, step, blocks):
    parts = []
    lanes = lax.broadcasted_iota(jnp.int32, (BLOCK, 128), 1)
    buckets = 2 * HALF_BUCKETS
    below = jnp.broadcast_to(table[0:1, HALF_BUCKETS - 1 : HALF_BUCKETS], (BLOCK, 128))
    above = jnp.broadcast_to(table[0:1, buckets - 1 : buckets], (BLOCK, 128))
    for sub in range(2):
        start = band_start(2 * step + sub, blocks)
        value = jnp.where(lanes < start, below, 0.0)
        value = jnp.where((lanes >= start + BAND) & (lanes < blocks), above, value)
        parts.append(jnp.where(lanes == blocks, 1.0, value))
    return jnp.concatenate(parts, axis=0).astype(jnp.bfloat16)


def between(acts, units, skip, unit, head):
    slots = 2 * units - skip
    for k, act in enumerate(acts):
        slot = skip + (k * slots) // len(acts)
        if slot % 2 == head:
            pl.when(unit == slot // 2)(act)


def gelu_all(gate):
    square = gate * gate
    tangent = jnp.tanh(GELU_ROOT * (gate + GELU_CUBIC * square * gate))
    value = 0.5 * gate * (1.0 + tangent)
    slope = 0.5 * (1.0 + tangent) + 0.5 * gate * (1.0 - tangent * tangent) * (
        GELU_ROOT + (3.0 * GELU_CUBIC * GELU_ROOT) * square
    )
    return value, slope


def front_kernel(
    shard_size, pieces, window, sizes, given,
    lengths_ref, gains_ref, query_ref, key_ref, value_ref, project_ref, gate_ref, up_ref, down_ref,
    inputs_ref, cots_ref, buckets_ref, table_ref,
    full_ref, normed_out, qkv_out, bandt_out, biast_out, grads_out, attended_out, tokens_own_ref,
    lse_ref, output_ref, middle_grad_ref, gain_ref, *rest,
):
    came_outs, rest = rest[: len(given)], rest[len(given) :]
    (
    own_ref, tok, cot, band_raw, band, bandt, bias, biast, kaux, gain_buf, qkv, normed, scores, attended, project_w,
    normal, away, arrived, two_t, low_t, acc_out, acc_two, w_buf, g_buf, hid, ggate, gup,
    send_sem, recv_sem, near_send, near_recv, local_sem, w_sem, g_sem, own_sem, bt_sem, early_send, early_recv,
    ) = rest
    inner, hidden = sizes
    length, width = tok.shape
    half, quarter = length // 2, length // 4
    heads, blocks = bias.shape[:2]
    pairs = heads // 2
    deep = shard_size // 2
    low = jnp.bfloat16
    place = Place(shard_size)
    x, c = place.x, place.c
    at_q = 128
    at_project = at_q + 3 * inner
    at_hidden = at_project + inner
    steps = hidden_steps(hidden)
    per_step = 2
    first_hidden_piece = len(pieces) - per_step * len(steps)
    project_pieces = [i for i, (a, b, _) in enumerate(pieces) if at_project <= a < at_hidden]
    qkv_pieces = [i for i, (a, b, _) in enumerate(pieces) if a < at_project]

    def own_load(i, source, target):
        return pltpu.make_async_copy(source, target, local_sem.at[i])

    parts, at = [], 0
    for ref in (gains_ref, query_ref, key_ref, value_ref, project_ref):
        parts.append((ref, at))
        at += ref.shape[1]
    own_loads = [
        pltpu.make_async_copy(ref, own_ref.at[:, at : at + ref.shape[1]], own_sem.at[i]) for i, (ref, at) in enumerate(parts)
    ]
    for j, n in enumerate(steps):
        for k, ref in enumerate((gate_ref, up_ref, down_ref)):
            at = at_hidden + 3 * HIDDEN_STEP * j + k * n
            own_loads.append(
                pltpu.make_async_copy(
                    ref.at[:, HIDDEN_STEP * j : HIDDEN_STEP * j + n], own_ref.at[:, at : at + n], own_sem.at[len(own_loads)]
                )
            )

    def band_source(block):
        start = pl.multiple_of(band_start(block, blocks) * BLOCK, BLOCK)
        first = block - x * (blocks // 2)
        return buckets_ref.at[pl.ds(pl.multiple_of(first * BLOCK, BLOCK), BLOCK), pl.ds(start, BAND * BLOCK)]

    own_tok = own_load(0, inputs_ref.at[x], tok.at[pl.ds(x * half, half)])
    own_cot = own_load(1, cots_ref.at[x], cot.at[pl.ds(x * half, half)])
    own_bands = [
        own_load(13 + i, band_source(x * (blocks // 2) + i), band_raw.at[i]) for i in range(blocks // 2)
    ]
    own_full = own_load(3, own_ref, full_ref.at[place.z, place.y, x])
    for copy in (*own_loads, *own_bands, own_tok, own_cot):
        copy.start()
    meet(place)
    for copy in own_loads:
        copy.wait()
    own_full.start()

    gather = Gather(place, pieces, own_ref, full_ref, send_sem, recv_sem)
    to_x, to_c = place.device(x=1 - x), place.device(c=1 - c)

    def x_rows(sender_x, sender_c):
        return pl.ds(sender_x * half + sender_c * quarter, quarter)

    def near(i, source, target, device):
        return send(source, target, near_send.at[i], near_recv.at[i], device)

    mine = [x * (blocks // 2) + c * (blocks // 4) + i for i in range(blocks // 4)]
    theirs = [(1 - x) * (blocks // 2) + c * (blocks // 4) + i for i in range(blocks // 4)]
    band_x = [near(16 + i, band.at[block], band.at[block], to_x) for i, block in enumerate(mine)]
    tok_x = near(1, inputs_ref.at[1 - x, pl.ds(c * quarter, quarter)], tok.at[x_rows(x, c)], to_x)
    cot_x = near(2, cots_ref.at[1 - x, pl.ds(c * quarter, quarter)], cot.at[x_rows(x, c)], to_x)
    band_c = [near(16 + len(mine) + i, band.at[block], band.at[block], to_c) for i, block in enumerate(theirs)]
    tok_c = near(4, tok.at[x_rows(1 - x, c)], tok.at[x_rows(1 - x, c)], to_c)
    cot_c = near(5, cot.at[x_rows(1 - x, c)], cot.at[x_rows(1 - x, c)], to_c)
    gather.plan(window)
    for copy in own_bands:
        copy.wait()
    for i in range(blocks // 2):
        band[x * (blocks // 2) + i] = band_raw[i].astype(jnp.float32).astype(low)
    for copy in band_x:
        copy.start()
    tok_x.start()
    own_full.wait()
    lanes_of = lax.broadcasted_iota(jnp.int32, (length, 128), 1)
    rows_of = lax.broadcasted_iota(jnp.int32, (length, 128), 0)
    valid = lengths_ref[x, 0]
    blocked = jnp.where(rows_of // BLOCK == lanes_of, 1.0, 0.0)
    kaux[...] = jnp.where((lanes_of == blocks) & (rows_of >= valid), -1e30, blocked).astype(low)
    gather.run(1)
    for copy in band_x:
        copy.wait()
    for copy in band_c:
        copy.start()
    gather.run(1)
    for copy in band_c:
        copy.wait()

    def bias_step(i, carry):
        block = i // (BLOCK // 16)
        at = pl.multiple_of((i % (BLOCK // 16)) * 16, 16)
        index = band[block, pl.ds(at, 16), :].astype(jnp.float32).astype(jnp.int32)
        for col in range(BAND):
            lanes = slice(col * BLOCK, (col + 1) * BLOCK)
            for head in range(heads):
                table = table_ref[head]
                got = [jnp.take_along_axis(table, index[8 * k : 8 * k + 8, lanes], axis=1) for k in range(2)]
                bias[head, block, pl.ds(at, 16), lanes] = jnp.concatenate(got, axis=0).astype(low)
        return carry

    bias_steps = blocks * (BLOCK // 16)
    for k in range(4):
        lax.fori_loop(bias_steps * k // 4, bias_steps * (k + 1) // 4, bias_step, 0)
        gather.run(1)
    tok_x.wait()
    tok_c.start()
    cot_x.start()

    def biast_store(block, slot):
        return pltpu.make_async_copy(biast.at[slot], biast_out.at[:, block], bt_sem.at[slot])

    def biast_block(block, carry):
        slot = block % 2

        @pl.when(block > 1)
        def _():
            biast_store(block - 2, slot).wait()

        bandt[block] = jnp.transpose(band[block].astype(jnp.float32)).astype(low)

        def inner_step(i, carry):
            at = pl.multiple_of(i * 16, 16)
            index = bandt[block, pl.ds(at, 16), :].astype(jnp.float32).astype(jnp.int32)
            for head in range(heads):
                got = [jnp.take_along_axis(table_ref[head], index[8 * k : 8 * k + 8], axis=1) for k in range(2)]
                biast[slot, head, pl.ds(at, 16), :] = jnp.concatenate(got, axis=0).astype(low)
            return carry

        lax.fori_loop(0, BAND * BLOCK // 16, inner_step, 0)
        biast_store(block, slot).start()
        return carry

    for k in range(4):
        lax.fori_loop(blocks * k // 4, blocks * (k + 1) // 4, biast_block, 0)
        gather.run(1)
    biast_store(blocks - 2, 0).wait()
    biast_store(blocks - 1, 1).wait()
    bandt_store = own_load(4, bandt, bandt_out)
    bandt_store.start()
    own_tok.wait()
    tok_c.wait()

    def live_step(i, carry):
        rows = pl.ds(pl.multiple_of(i * BLOCK, BLOCK), BLOCK)
        here = lax.broadcasted_iota(jnp.int32, (BLOCK, width), 0) + i * BLOCK < valid
        masked = jnp.where(here, cot[rows, :].astype(jnp.float32), 0.0).astype(low)
        cot[rows, :] = masked
        low_t[:, rows] = jnp.transpose(masked)
        return carry

    gather.need(qkv_pieces)
    load_gains = own_load(5, full_ref.at[:, :, :, :, 0:at_q], gain_buf)
    third = 3 * inner // 2
    loads_wide = [
        pltpu.make_async_copy(
            full_ref.at[:, :, :, :, at_q + third * k : at_q + third * (k + 1)], w_buf.at[k, :, :, :, :, 0:third], w_sem.at[k]
        )
        for k in range(2)
    ]
    for copy in (load_gains, *loads_wide):
        copy.start()
    load_gains.wait()
    gains = jnp.transpose(gain_buf[...].reshape(width, 128).astype(jnp.float32))
    gain_one, gain_two = gains[0:1, :], gains[1:2, :]

    def norm_step(i, carry):
        rows = pl.ds(pl.multiple_of(i * BLOCK, BLOCK), BLOCK)
        present = tok[rows, :].astype(jnp.float32)
        inverse = lax.rsqrt(jnp.mean(present * present, axis=-1, keepdims=True) + EPSILON)
        got = (present * inverse * gain_one).astype(low)
        normed[rows, :] = got
        two_t[:, rows] = jnp.transpose(got)
        return carry

    lax.fori_loop(0, blocks, norm_step, 0)
    normed_store = own_load(6, two_t, normed_out)
    normed_store.start()
    for copy in loads_wide:
        copy.wait()
    gather.run(2)

    for col in range(3 * pairs // 2):
        slot, at = 256 * col // third, 256 * col % third
        lanes = slice(at, at + 256)

        def qkv_step(i, carry):
            rows = pl.ds(pl.multiple_of(i * 256, 256), 256)
            got = jnp.dot(
                normed[rows, :], w_buf[slot, :, :, :, :, lanes].reshape(width, 256), preferred_element_type=jnp.float32
            ).astype(low)
            qkv[2 * col, rows, :] = got[:, :128]
            qkv[2 * col + 1, rows, :] = got[:, 128:]
            return carry

        lax.fori_loop(0, length // 256, qkv_step, 0)
        if col % 2:
            gather.run(1)
    qkv_store = own_load(7, qkv, qkv_out)
    qkv_store.start()

    units = pairs * (length // 256)
    acts = gather.take(min(len(gather.queue), FORWARD_ACTS))

    def unit_step(unit, carry):
        pair = unit // (length // 256)
        step = unit % (length // 256)
        rows = pl.ds(pl.multiple_of(step * 256, 256), 256)
        queries = qkv[pair, rows, :]
        keys = jnp.concatenate([qkv[pairs + pair], kaux[...]], axis=1)
        outs = []
        for head in range(2):
            between(acts, units, 0, unit, head)
            aux = query_aux(table_ref[2 * pair + head], step, blocks)
            masked = jnp.where(lane_head(256, 128, head), queries, jnp.zeros_like(queries))
            scores[...] = lax.dot_general(
                jnp.concatenate([masked, aux], axis=1), keys, LAST, preferred_element_type=jnp.float32
            )
            for sub in range(2):
                start = pl.multiple_of(band_start(step * 2 + sub, blocks) * BLOCK, BLOCK)
                scores[sub * BLOCK : (sub + 1) * BLOCK, pl.ds(start, BAND * BLOCK)] += bias[
                    2 * pair + head, 2 * step + sub
                ].astype(jnp.float32)
            got = scores[...]
            highest = jnp.max(got, axis=1, keepdims=True)
            exponent = jnp.exp(got - highest)
            total = jnp.sum(exponent, axis=1, keepdims=True)
            outs.append(
                jnp.dot(exponent.astype(low), qkv[2 * pairs + pair], preferred_element_type=jnp.float32) * (1.0 / total)
            )
            lse = jnp.broadcast_to(highest + jnp.log(total), (256, 128))
            lse_ref[pair, step, head : head + 1, :] = jnp.transpose(lse)[0:1, :]
        attended[pair, rows, :] = jnp.where(lane_head(256, 128, 0), outs[0], outs[1]).astype(low)
        return carry

    lax.fori_loop(0, units, unit_step, 0)
    own_cot.wait()
    cot_x.wait()
    cot_c.start()

    normed_store.wait()
    two = normed
    gather.need(project_pieces)
    load_project = own_load(9, full_ref.at[:, :, :, :, at_project:at_hidden], project_w)
    load_project.start()
    load_project.wait()

    def branch(rows):
        left = jnp.concatenate([attended[pair, rows, :] for pair in range(pairs)], axis=1)
        return lax.dot_general(left, project_w[...].reshape(width, inner), LAST, preferred_element_type=jnp.float32)

    def part_rows(part, core):
        return pl.ds(pl.multiple_of(part * half + core * quarter, quarter), quarter)

    def swap_part(i, part, slot=0):
        return near(i + part, away.at[slot + part], arrived.at[slot + part], to_c)

    for part in range(2):
        away[part] = branch(part_rows(part, 1 - c)).astype(low)
        swap_part(6, part).start()
    for part in range(2):
        normal[part] = branch(part_rows(part, c)) + tok[part_rows(part, c), :].astype(jnp.float32)

    def share(i, part, buffer):
        return near(i + part, buffer.at[part_rows(part, c)], buffer.at[part_rows(part, c)], to_c)

    tokens_store = [own_load(11 + part, tok.at[part_rows(part, c)], tokens_own_ref.at[part]) for part in range(2)]
    for copy in tokens_store:
        copy.start()
    for part in range(2):
        swap_part(6, part).wait()
        middle = normal[part] + arrived[part].astype(jnp.float32)
        normal[part] = middle
        inverse = lax.rsqrt(jnp.mean(middle * middle, axis=-1, keepdims=True) + EPSILON)
        two[part_rows(part, c), :] = (middle * inverse * gain_two).astype(low)
        share(8, part, two).start()
    gather.run(1)
    for part in range(2):
        share(8, part, two).wait()

    def turn_step(i, carry):
        rows = pl.ds(pl.multiple_of(i * BLOCK, BLOCK), BLOCK)
        two_t[:, rows] = jnp.transpose(two[rows, :])
        return carry

    lax.fori_loop(0, blocks, turn_step, 0)
    gather.run(1)
    cot_c.wait()
    lax.fori_loop(0, blocks, live_step, 0)
    gather.run(1)

    def bounds(j):
        at = at_hidden + 3 * HIDDEN_STEP * j
        return at, at + 3 * steps[j]

    def load_step(j):
        a, b = bounds(j)
        return pltpu.make_async_copy(
            full_ref.at[:, :, :, :, a:b], w_buf.at[j % 2, :, :, :, :, 0 : b - a], w_sem.at[j % 2]
        )

    def store_step(j):
        a, b = bounds(j)
        return pltpu.make_async_copy(
            g_buf.at[j % 2, :, :, :, :, 0 : b - a],
            grads_out.at[:, :, :, :, a - at_hidden : b - at_hidden],
            g_sem.at[j % 2],
        )

    early_sums = []
    for k, (a, b, name) in enumerate(given):
        source = grads_out.at[:, :, 1 - x, :, a:b] if name == "x" else grads_out.at[:, 1 - place.y, :, :, a:b]
        device = to_x if name == "x" else place.device(y=1 - place.y)
        early_sums.append(send(source, came_outs[k], early_send.at[k], early_recv.at[k], device))
    gather.need(range(first_hidden_piece, first_hidden_piece + per_step))
    load_step(0).start()
    for j, units_here in enumerate(steps):
        n = units_here
        slot = j % 2
        load_step(j).wait()

        def weight(k, slot=slot, n=n):
            return w_buf[slot, :, :, :, :, k * n : (k + 1) * n].reshape(width, n)

        inside = gather.take(ROW_ACTS)

        def rows_step(i, carry, j=j, n=n, weight=weight, inside=inside):
            for k, act in enumerate(inside):
                pl.when(i == (2 * k + 1) * (length // 256) // (2 * len(inside)))(act)
            rows = pl.ds(pl.multiple_of(i * 256, 256), 256)
            left, grad = two[rows, :], cot[rows, :]
            gate = jnp.dot(left, weight(0), preferred_element_type=jnp.float32)
            up = jnp.dot(left, weight(1), preferred_element_type=jnp.float32)
            grad_hidden = jnp.dot(grad, weight(2), preferred_element_type=jnp.float32)
            value, slope = gelu_all(gate)
            hid[rows, 0:n] = (value * up).astype(low)
            ggate[rows, 0:n] = (grad_hidden * up * slope).astype(low)
            gup[rows, 0:n] = (grad_hidden * value).astype(low)
            out = lax.dot_general(hid[rows, 0:n], weight(2), LAST, preferred_element_type=jnp.float32)
            back = lax.dot_general(ggate[rows, 0:n], weight(0), LAST, preferred_element_type=jnp.float32)
            back = back + lax.dot_general(gup[rows, 0:n], weight(1), LAST, preferred_element_type=jnp.float32)
            if j == 0:
                acc_out[rows, :] = out
                acc_two[rows, :] = back
            else:
                acc_out[rows, :] += out
                acc_two[rows, :] += back
            return carry

        lax.fori_loop(0, length // 256, rows_step, 0)
        if j + 1 < len(steps):
            first = first_hidden_piece + per_step * (j + 1)
            gather.need(range(first, first + per_step))
            load_step(j + 1).start()
        if j > 1:
            store_step(j - 2).wait()
        if j + 2 >= len(steps):
            for copy, (_, b, _) in zip(early_sums, given):
                ready = max(0, -(-b // (3 * HIDDEN_STEP)) - 1)
                if ready == j - 2 or (ready < j - 2 and j + 2 == len(steps)):
                    copy.start()

        tiles = width // 256

        def grads_step(i, carry, slot=slot, n=n):
            rows = pl.ds(pl.multiple_of(i * 256, 256), 256)
            for k, (left, right) in enumerate(((two_t, ggate), (two_t, gup), (low_t, hid))):
                got = jnp.dot(left[rows, :], right[:, 0:n], preferred_element_type=jnp.float32).astype(low)
                span = deep // tiles
                g_buf[slot, pl.ds(i * span, span), :, :, :, k * n : (k + 1) * n] = got.reshape(
                    (span,) + g_buf.shape[2:5] + (n,)
                )
            return carry

        lax.fori_loop(0, tiles, grads_step, 0)
        store_step(j).start()
    gather.run(len(gather.queue))

    def share_sum(i, acc, slot):
        for part in range(2):
            away[slot + part] = acc[part_rows(part, 1 - c), :].astype(low)
            swap_part(i, part, slot).start()

    share_sum(10, acc_two, 0)
    for part in range(2):
        swap_part(10, part).wait()
        grad_two = acc_two[part_rows(part, c), :] + arrived[part].astype(jnp.float32)
        middle = normal[part]
        inverse = lax.rsqrt(jnp.mean(middle * middle, axis=-1, keepdims=True) + EPSILON)
        unit = middle * inverse
        weighted = jnp.sum((grad_two * unit).reshape(quarter // 8, 8, width), axis=0)
        gain_ref[part] = weighted
        scaled = grad_two * gain_two
        grad_middle = cot[part_rows(part, c), :].astype(jnp.float32) + inverse * (
            scaled - unit * jnp.mean(scaled * unit, axis=-1, keepdims=True)
        )
        middle_grad_ref[part] = grad_middle
        two[part_rows(part, c), :] = grad_middle.astype(low)
        share(12, part, two).start()
    share_sum(14, acc_out, 2)
    for part in range(2):
        swap_part(14, part, 2).wait()
        output_ref[part] = (normal[part] + acc_out[part_rows(part, c), :] + arrived[2 + part].astype(jnp.float32)).astype(low)
    for part in range(2):
        share(12, part, two).wait()
    for j in range(max(0, len(steps) - 2), len(steps)):
        store_step(j).wait()

    lax.fori_loop(0, blocks, turn_step, 0)

    def project_step(i, carry):
        rows = pl.ds(pl.multiple_of(i * 256, 256), 256)
        right = jnp.concatenate([attended[pair] for pair in range(pairs)], axis=1)
        got = jnp.dot(two_t[rows, :], right, preferred_element_type=jnp.float32).astype(low)
        span = deep // (width // 256)
        g_buf[0, pl.ds(i * span, span), :, :, :, 0:inner] = got.reshape((span,) + g_buf.shape[2:5] + (inner,))
        return carry

    lax.fori_loop(0, width // 256, project_step, 0)
    project_store = own_load(8, g_buf.at[0, :, :, :, :, 0:inner], grads_out.at[:, :, :, :, 3 * hidden : 3 * hidden + inner])
    project_store.start()

    def attended_step(i, carry):
        rows = pl.ds(pl.multiple_of(i * 256, 256), 256)
        got = jnp.dot(two[rows, :], project_w[...].reshape(width, inner), preferred_element_type=jnp.float32).astype(low)
        for pair in range(pairs):
            attended[pair, rows, :] = got[:, pair * 128 : (pair + 1) * 128]
        return carry

    lax.fori_loop(0, length // 256, attended_step, 0)
    attended_store = own_load(10, attended, attended_out)
    attended_store.start()
    for copy in (bandt_store, qkv_store, attended_store, project_store, *tokens_store, *early_sums):
        copy.wait()
    gather.sent()


def front(shard_size, pieces, window, given, lengths, gains, weights, inputs, cots, buckets, table_rows):
    low, f32 = jnp.bfloat16, jnp.float32
    deep = shard_size // 2
    rows, inner = weights[0].shape
    hidden = weights[4].shape[1]
    wide = pieces[-1][1]
    half, width = inputs.shape[1:]
    length, quarter = 2 * half, half // 2
    heads = table_rows.shape[0]
    blocks = length // BLOCK
    pairs = heads // 2
    shape = jax.ShapeDtypeStruct
    vmem, hbm = pl.BlockSpec(memory_space=pltpu.VMEM), pl.BlockSpec(memory_space=pl.ANY)
    dma = pltpu.SemaphoreType.DMA
    count = len(pieces)
    step = HIDDEN_STEP
    out_shape = [
        shape((deep, 2, 2, rows, wide), low),
        shape((width, length), low),
        shape((3 * pairs, length, 128), low),
        shape((blocks, BAND * BLOCK, BLOCK), low),
        shape((heads, blocks, BAND * BLOCK, BLOCK), low),
        shape((deep, 2, 2, rows, 3 * hidden + inner), low),
        shape((pairs, length, 128), low),
        shape((2, quarter, width), low),
        shape((pairs, length // 256, 2, 256), f32),
        shape((2, quarter, width), low),
        shape((2, quarter, width), f32),
        shape((2, 8, width), f32),
    ] + [shape((deep, 2, rows, b - a), low) for a, b, _ in given]
    scratch = [
        pltpu.VMEM((rows, wide), low),
        pltpu.VMEM((length, width), low),
        pltpu.VMEM((length, width), low),
        pltpu.VMEM((blocks // 2, BLOCK, BAND * BLOCK), jnp.int32),
        pltpu.VMEM((blocks, BLOCK, BAND * BLOCK), low),
        pltpu.VMEM((blocks, BAND * BLOCK, BLOCK), low),
        pltpu.VMEM((heads, blocks, BLOCK, BAND * BLOCK), low),
        pltpu.VMEM((2, heads, BAND * BLOCK, BLOCK), low),
        pltpu.VMEM((length, 128), low),
        pltpu.VMEM((deep, 2, 2, rows, 128), low),
        pltpu.VMEM((3 * pairs, length, 128), low),
        pltpu.VMEM((length, width), low),
        pltpu.VMEM((256, length), f32),
        pltpu.VMEM((pairs, length, 128), low),
        pltpu.VMEM((deep, 2, 2, rows, inner), low),
        pltpu.VMEM((2, quarter, width), f32),
        pltpu.VMEM((4, quarter, width), low),
        pltpu.VMEM((4, quarter, width), low),
        pltpu.VMEM((width, length), low),
        pltpu.VMEM((width, length), low),
        pltpu.VMEM((length, width), f32),
        pltpu.VMEM((length, width), f32),
        pltpu.VMEM((2, deep, 2, 2, rows, 3 * step), low),
        pltpu.VMEM((2, deep, 2, 2, rows, 3 * step), low),
        pltpu.VMEM((length, step), low),
        pltpu.VMEM((length, step), low),
        pltpu.VMEM((length, step), low),
        dma((count, 3, deep - 1)),
        dma((count, 3, deep - 1)),
        dma((16 + blocks // 2,)),
        dma((16 + blocks // 2,)),
        dma((13 + blocks // 2,)),
        dma((2,)),
        dma((2,)),
        dma((5 + 3 * len(hidden_steps(hidden)),)),
        dma((2,)),
        dma((len(given),)),
        dma((len(given),)),
    ]
    return pl.pallas_call(
        functools.partial(front_kernel, shard_size, pieces, window, (inner, hidden), given),
        out_shape=out_shape,
        in_specs=[pl.BlockSpec(memory_space=pltpu.SMEM)] + [hbm] * 11 + [vmem],
        out_specs=[hbm] * 8 + [vmem] * 4 + [hbm] * len(given),
        scratch_shapes=scratch,
        compiler_params=pltpu.CompilerParams(
            collective_id=1, has_side_effects=True, vmem_limit_bytes=60 * MIB
        ),
        name="front",
    )(lengths, gains, *weights, inputs, cots, buckets, table_rows)


GROUP = 16
TURNS = 4


class Scatter:
    def __init__(self, place, pieces, sources, outs, buffers, sems, came):
        self.came = came
        self.place, self.pieces, self.sources, self.outs = place, pieces, sources, outs
        self.first, self.own, self.second, self.third = buffers
        self.own_sem, self.send_sem, self.recv_sem = sems
        self.queue = []

    def peer(self, name):
        place = self.place
        return place.device(y=1 - place.y) if name == "y" else place.device(x=1 - place.x)

    def rest(self, piece):
        order = self.pieces[piece][3]
        return [name for name in "zyx" if name != order[0]]

    def cut(self, piece, name, value):
        t, a, b = self.pieces[piece][:3]
        at = [value if name == other else slice(None) for other in "zyx"]
        if t:
            return self.sources[1].at[t - 1, at[0], at[1], at[2]]
        return self.sources[0].at[at[0], at[1], at[2], :, a:b]

    def own_copy(self, piece):
        order = self.pieces[piece][3]
        return pltpu.make_async_copy(
            self.cut(piece, order[0], getattr(self.place, order[0])), self.own[piece], self.own_sem.at[piece]
        )

    def copies(self, piece, hop):
        place, order = self.place, self.pieces[piece][3]
        name, rest = order[hop], self.rest(piece)
        own, made = self.own[piece], []

        def at(**index):
            return tuple(index[n] if n in index else slice(None) for n in rest)

        def add(source, target, device):
            i = len(made)
            made.append(send(source, target, self.send_sem.at[piece, hop, i], self.recv_sem.at[piece, hop, i], device))

        if hop == 0:
            if name == "z":
                for d in range(1, place.deep):
                    z = place.line(d)
                    add(self.cut(piece, "z", z), self.first[piece].at[d - 1], place.device(z=z))
            else:
                add(self.cut(piece, name, 1 - getattr(place, name)), self.first[piece], self.peer(name))
            return made
        fixed = {} if hop == 1 else {order[1]: getattr(place, order[1])}
        buffer = self.second[piece] if hop == 1 else self.third[piece]
        if name == "z":
            for d in range(1, place.deep):
                z = place.line(d)
                add(own.at[at(z=z, **fixed)], buffer.at[d - 1], place.device(z=z))
        else:
            add(own.at[at(**{name: 1 - getattr(place, name)}, **fixed)], buffer, self.peer(name))
        return made

    def start(self, piece, hop):
        for copy in self.copies(piece, hop):
            copy.start()

    def arrive(self, piece, hop):
        for copy in self.copies(piece, hop):
            copy.wait_recv()

    def came_copy(self, piece):
        return pltpu.make_async_copy(self.came[piece], self.first[piece], self.recv_sem.at[piece, 0, 0])

    def begin(self, piece):
        if piece < len(self.came):
            self.came_copy(piece).start()
        else:
            self.start(piece, 0)
        self.own_copy(piece).start()

    def add_first(self, piece):
        order = self.pieces[piece][3]
        if piece < len(self.came):
            self.came_copy(piece).wait()
        else:
            self.arrive(piece, 0)
        self.own_copy(piece).wait()
        if piece >= len(self.came) and self.waiting:
            self.begin(self.waiting.pop(0))
        own, came = self.own[piece], self.first[piece]
        inner = own.shape[1]

        def body(i, carry):
            for k in range(inner):
                if order[0] == "z":
                    total = own[i, k].astype(jnp.float32)
                    for d in range(came.shape[0]):
                        total = total + came[d, i, k].astype(jnp.float32)
                    own[i, k] = total.astype(jnp.bfloat16)
                else:
                    own[i, k] = own[i, k] + came[i, k]
            return carry

        lax.fori_loop(0, own.shape[0], body, 0)
        self.start(piece, 1)

    def add_second(self, piece):
        place, order = self.place, self.pieces[piece][3]
        name, rest = order[1], self.rest(piece)
        self.arrive(piece, 1)
        own, came = self.own[piece], self.second[piece]
        mine = getattr(place, name)
        spans = own.shape[1] if rest[0] == name else own.shape[0]

        def body(i, carry):
            if name == "z":
                total = own[mine, i].astype(jnp.float32)
                for d in range(came.shape[0]):
                    total = total + came[d, i].astype(jnp.float32)
                own[mine, i] = total.astype(jnp.bfloat16)
            elif rest[0] == name:
                own[mine, i] = own[mine, i] + came[i]
            else:
                own[i, mine] = own[i, mine] + came[i]
            return carry

        lax.fori_loop(0, spans, body, 0)
        self.start(piece, 2)

    def add_third(self, piece):
        place, order = self.place, self.pieces[piece][3]
        rest = self.rest(piece)
        self.arrive(piece, 2)
        total = self.own[piece][getattr(place, rest[0]), getattr(place, rest[1])].astype(jnp.float32)
        if order[2] == "z":
            for d in range(1, place.deep):
                total = total + self.third[piece][d - 1].astype(jnp.float32)
        else:
            total = total + self.third[piece][...].astype(jnp.float32)
        for out, start, at, n in self.pieces[piece][4]:
            self.outs[out][:, start : start + n] = total[:, at : at + n]

    def plan(self, window):
        self.waiting = [i for i, piece in enumerate(self.pieces) if piece[0] == 0]
        count = len(self.pieces)
        for i in range(count + SUM_LAGS[1]):
            if i < count:
                self.queue.append(functools.partial(self.add_first, i))
            if 0 <= i - SUM_LAGS[0] < count:
                self.queue.append(functools.partial(self.add_second, i - SUM_LAGS[0]))
            if 0 <= i - SUM_LAGS[1] < count:
                self.queue.append(functools.partial(self.add_third, i - SUM_LAGS[1]))
        for _ in range(min(len(self.came) + window, len(self.waiting))):
            self.begin(self.waiting.pop(0))

    def run(self, steps):
        for _ in range(min(steps, len(self.queue))):
            self.queue.pop(0)()

    def take(self, steps):
        taken, self.queue = self.queue[:steps], self.queue[steps:]
        return taken

    def sent(self):
        for piece in range(len(self.pieces)):
            for hop in range(0 if piece >= len(self.came) else 1, 3):
                for copy in self.copies(piece, hop):
                    copy.wait_send()


def piece_buffers(piece, deep, rows):
    _, a, b, order, _ = piece
    sizes = {"z": deep, "y": 2, "x": 2}
    rest = [name for name in "zyx" if name != order[0]]
    left = [sizes[name] for name in rest]
    last = [sizes[name] for name in rest if name != order[1]]
    tail = [rows, b - a]
    lead = [deep - 1]
    first = (lead if order[0] == "z" else []) + left + tail
    second = (lead if order[1] == "z" else []) + last + tail
    third = (lead if order[2] == "z" else []) + tail
    return [tuple(shape) for shape in (first, left + tail, second, third)]


def back_kernel(shard_size, pieces, sizes, given, *refs):
    inner, hidden, buckets = sizes
    count = len(pieces)
    (
        lengths_ref, full_ref, normed_in, qkv_in, bandt_in, biast_in, grads_in, do_in,
        lse_ref, output_ref, middle_ref, tokens_ref, gain_two_ref, table_ref,
    ) = refs[:14]
    came, refs = refs[14 : 14 + given], refs[14 + given :]
    weight_outs, (output_out, input_out, small_out) = refs[:7], refs[7:10]
    refs = refs[10:]
    first, own, second, third = [refs[k * count : (k + 1) * count] for k in range(4)]
    refs = refs[4 * count :]
    (
        qkv, normed_t, bandt, bias, wqkv, gain_buf, do, scores, grads, far, dk_acc, dv_acc, kaux, wgrad,
        mine_sum, away, arrived, result, table_acc, hot, found,
        small, small_x, small_y, hold_x, hold_y, hold_z, small_c,
        own_sem, send_sem, recv_sem, near_send, near_recv, local_sem,
    ) = refs
    length = qkv.shape[1]
    width = normed_t.shape[0]
    half, quarter = length // 2, length // 4
    heads, blocks = bias.shape[:2]
    pairs = heads // 2
    deep = shard_size // 2
    low, f32 = jnp.bfloat16, jnp.float32
    place = Place(shard_size)
    x, y, z, c = place.x, place.y, place.z, place.c
    to_x, to_y, to_c = place.device(x=1 - x), place.device(y=1 - y), place.device(c=1 - c)

    def local(i, source, target):
        return pltpu.make_async_copy(source, target, local_sem.at[i])

    loads = [
        local(0, qkv_in, qkv), local(1, biast_in, bias), local(2, do_in, do),
        local(3, full_ref.at[:, :, :, :, 128 : 128 + 3 * inner], wqkv), local(4, normed_in, normed_t),
        local(5, bandt_in, bandt), local(6, full_ref.at[:, :, :, :, 0:128], gain_buf),
    ]
    for copy in loads:
        copy.start()
    meet(place)
    scatter = Scatter(
        place, pieces, (grads_in, wgrad), weight_outs, (first, own, second, third), (own_sem, send_sem, recv_sem), came,
    )
    scatter.plan(SUM_WINDOW)

    def near(i, source, target, device):
        return send(source, target, near_send.at[i], near_recv.at[i], device)

    def to_owners(i, values, out):
        here = out.at[x, pl.ds(c * quarter, quarter)]
        there = out.at[1 - x, pl.ds(c * quarter, quarter)]
        return (
            local(7 + i, values.at[x], here),
            near(4 * i, values.at[x], here, to_c),
            near(4 * i + 1, values.at[1 - x], here, to_x),
            near(4 * i + 2, there, there, to_c),
        )

    output_moves = to_owners(0, output_ref, output_out)
    for copy in output_moves[:3]:
        copy.start()

    lanes_of = lax.broadcasted_iota(jnp.int32, (length, 128), 1)
    rows_of = lax.broadcasted_iota(jnp.int32, (length, 128), 0)
    valid = lengths_ref[x, 0]
    blocked = jnp.where(rows_of // BLOCK == lanes_of, 1.0, 0.0)
    kaux[...] = jnp.where((lanes_of == blocks) & (rows_of >= valid), -1e30, blocked).astype(low)
    far[...] = jnp.zeros_like(far)
    for copy in loads:
        copy.wait()

    per_pair = length // 256
    units = pairs * per_pair
    acts = scatter.take(ATTENTION_ACTS)

    def unit_step(unit, carry):
        pair = unit // per_pair
        step = unit % per_pair
        rows = pl.ds(pl.multiple_of(step * 256, 256), 256)

        @pl.when(step == 0)
        def _():
            dk_acc[...] = jnp.zeros_like(dk_acc)
            dv_acc[...] = jnp.zeros_like(dv_acc)

        queries = qkv[pair, rows, :]
        grad = do[pair, rows, :]
        key_pair = qkv[pairs + pair]
        keys = jnp.concatenate([key_pair, kaux[...]], axis=1)
        values = qkv[2 * pairs + pair]
        dq = None
        for head in range(2):
            between(acts, units, ACT_FIRST, unit, head)
            here = lane_head(256, 128, head)
            aux = query_aux(table_ref[2 * pair + head], step, blocks)
            q_masked = jnp.where(here, queries, jnp.zeros_like(queries))
            do_masked = jnp.where(here, grad, jnp.zeros_like(grad))
            scores[...] = lax.dot_general(
                keys, jnp.concatenate([q_masked, aux], axis=1), LAST, preferred_element_type=f32
            )
            for sub in range(2):
                start = pl.multiple_of(band_start(step * 2 + sub, blocks) * BLOCK, BLOCK)
                scores[pl.ds(start, BAND * BLOCK), sub * BLOCK : (sub + 1) * BLOCK] += bias[
                    2 * pair + head, 2 * step + sub
                ].astype(f32)
            soft = jnp.exp(scores[...] - lse_ref[pair, step, head : head + 1, :])
            dv_acc[...] += jnp.dot(soft.astype(low), do_masked, preferred_element_type=f32)
            grad_probs = lax.dot_general(values, do_masked, LAST, preferred_element_type=f32)
            weighted = jnp.sum(soft * grad_probs, axis=0, keepdims=True)
            grad_scores = (soft * (grad_probs - weighted)).astype(low)
            grads[...] = grad_scores
            dk_acc[...] += jnp.dot(grad_scores, q_masked, preferred_element_type=f32)
            k_masked = jnp.where(lane_head(length, 128, head), key_pair, jnp.zeros_like(key_pair))
            part = lax.dot_general(grad_scores, k_masked, FIRST, preferred_element_type=f32)
            dq = part if dq is None else dq + part
            sums = jnp.concatenate(
                [
                    jnp.sum(grad_scores[block * BLOCK : (block + 1) * BLOCK, :].astype(f32), axis=0, keepdims=True)
                    for block in range(blocks)
                ],
                axis=0,
            )
            block_of = lax.broadcasted_iota(jnp.int32, (blocks, BLOCK), 0)
            for sub in range(2):
                start = band_start(step * 2 + sub, blocks)
                at = pl.multiple_of(start * BLOCK, BLOCK)
                bias[2 * pair + head, 2 * step + sub] = grads[pl.ds(at, BAND * BLOCK), sub * BLOCK : (sub + 1) * BLOCK]
                part = sums[:, sub * BLOCK : (sub + 1) * BLOCK]
                far[0, 2 * pair + head] += jnp.where(block_of < start, part, 0.0)
                far[1, 2 * pair + head] += jnp.where(block_of >= start + BAND, part, 0.0)
        qkv[pair, rows, :] = dq.astype(low)

        @pl.when(step == per_pair - 1)
        def _():
            qkv[pairs + pair] = dk_acc[...].astype(low)
            qkv[2 * pairs + pair] = dv_acc[...].astype(low)
            right = jnp.concatenate([qkv[t * pairs + pair] for t in range(3)], axis=1)

            def weight_step(i, carry):
                rows = pl.ds(pl.multiple_of(i * 256, 256), 256)
                got = jnp.dot(normed_t[rows, :], right, preferred_element_type=f32).astype(low)
                span = deep // (width // 256)
                wgrad[pair, pl.ds(i * span, span)] = got.reshape((span,) + wgrad.shape[2:5] + (3 * 128,))
                return carry

            lax.fori_loop(0, width // 256, weight_step, 0)

        for late, piece in enumerate(pieces):
            if piece[0]:
                @pl.when(unit == piece[0] * per_pair - 1)
                def _(late=late):
                    scatter.begin(late)

        return carry

    lax.fori_loop(0, units, unit_step, 0)
    for copy in output_moves[:3]:
        copy.wait()
    output_moves[3].start()
    def part_rows(part, core):
        return pl.ds(pl.multiple_of(part * half + core * quarter, quarter), quarter)

    def grad_one(rows):
        left = jnp.concatenate([qkv[k, rows, :] for k in range(3 * pairs)], axis=1)
        return lax.dot_general(left, wqkv[...].reshape(width, 3 * inner), LAST, preferred_element_type=f32)

    swaps = [near(8 + part, away.at[part], arrived.at[part], to_c) for part in range(2)]

    def away_step(part, carry):
        away[part] = grad_one(part_rows(part, 1 - c)).astype(low)
        return carry

    def mine_step(part, carry):
        mine_sum[part] = grad_one(part_rows(part, c))
        return carry

    lax.fori_loop(0, 2, away_step, 0)
    for copy in swaps:
        copy.start()
    scatter.run(1)
    lax.fori_loop(0, 2, mine_step, 0)
    scatter.run(1)
    gains = jnp.transpose(gain_buf[...].reshape(width, 128).astype(f32))
    gain_one = gains[0:1, :]
    gain_sum = jnp.zeros((1, width), f32)
    for part in range(2):
        swaps[part].wait()
        total = mine_sum[part] + arrived[part].astype(f32)
        present = tokens_ref[part].astype(f32)
        inverse = lax.rsqrt(jnp.mean(present * present, axis=-1, keepdims=True) + EPSILON)
        unit = present * inverse
        gain_sum = gain_sum + jnp.sum(total * unit, axis=0, keepdims=True)
        scaled = total * gain_one
        back = inverse * (scaled - unit * jnp.mean(scaled * unit, axis=-1, keepdims=True))
        result[part] = (middle_ref[part] + back).astype(low)
        scatter.run(1)
    input_moves = to_owners(1, result, input_out)
    for copy in input_moves[:3]:
        copy.start()
    table_acc[...] = jnp.zeros_like(table_acc)
    groups = BAND * BLOCK // GROUP
    table_units = blocks // 2 * groups // TURNS
    table_acts = scatter.take(TABLE_ACTS)

    def table_step(i, carry):
        for k, act in enumerate(table_acts):
            @pl.when(i == (k * table_units) // max(1, len(table_acts)))
            def _(act=act):
                act()
        total = None
        for turn in range(TURNS):
            group = i * TURNS + turn
            block = 2 * (group // groups)
            start = pl.multiple_of((group % groups) * GROUP, GROUP)
            for two in range(2):
                lanes = slice(two * BLOCK, (two + 1) * BLOCK)
                index = bandt[block + two, pl.ds(start, GROUP), :]
                for head in range(heads):
                    found[turn, head * GROUP : (head + 1) * GROUP, lanes] = bias[head, block + two, pl.ds(start, GROUP), :]
                for b in range(buckets):
                    hot[turn, b * GROUP : (b + 1) * GROUP, lanes] = jnp.where(
                        index == jnp.asarray(b, low), jnp.asarray(1, low), jnp.asarray(0, low)
                    )
            part = lax.dot_general(hot[turn], found[turn], LAST, preferred_element_type=f32)
            total = part if total is None else total + part
        table_acc[...] += total
        return carry

    lax.fori_loop(0, table_units, table_step, 0)
    row = lax.broadcasted_iota(jnp.int32, table_acc.shape, 0) % GROUP
    col = lax.broadcasted_iota(jnp.int32, table_acc.shape, 1) % GROUP
    kept = jnp.where(row == col, table_acc[...], 0.0).reshape(buckets, GROUP, heads * GROUP).sum(axis=1)
    bucket = lax.broadcasted_iota(jnp.int32, (buckets, 128), 0)
    head_of = lax.broadcasted_iota(jnp.int32, (buckets, 128), 1)
    table = jnp.zeros((buckets, 128), f32)
    for head in range(heads):
        amount = jnp.sum(kept[:, head * GROUP : (head + 1) * GROUP], axis=1, keepdims=True)
        table = table + jnp.where(head_of == head, amount, 0.0)
    for side, name in enumerate((buckets // 2 - 1, buckets - 1)):
        for head in range(heads):
            amount = jnp.sum(jnp.sum(far[side, head], axis=0, keepdims=True), axis=1, keepdims=True)
            table = table + jnp.where((bucket == name) & (head_of == head), amount, 0.0)

    lines = width // 128
    for i in range(lines):
        small[i : i + 1, :] = gain_sum[:, i * 128 : (i + 1) * 128]
    gain_two_sum = jnp.sum(gain_two_ref[0] + gain_two_ref[1], axis=0, keepdims=True)
    for i in range(lines):
        small[lines + i : lines + i + 1, :] = gain_two_sum[:, i * 128 : (i + 1) * 128]
    small[2 * lines : 2 * lines + buckets, :] = table
    small_base = 10

    def small_line(d):
        return near(small_base + 2 + d, hold_z.at[z], hold_z.at[z], place.device(z=place.line(d)))

    move = near(small_base, small, small_x, to_x)
    move.start()
    scatter.run(1)
    move.wait()
    hold_x[...] = small[...] + small_x[...]
    move = near(small_base + 1, hold_x, small_y, to_y)
    move.start()
    scatter.run(1)
    move.wait()
    hold_z[z] = hold_x[...] + small_y[...]
    for d in range(1, deep):
        small_line(d).start()
    scatter.run(1)
    for d in range(1, deep):
        small_line(d).wait()
    hold_y[...] = jnp.sum(hold_z[...], axis=0)
    move = near(small_base + 2, hold_y, small_c, to_c)
    move.start()
    scatter.run(1)
    move.wait()
    small_out[0] = hold_y[...]
    small_out[1] = hold_y[...] + small_c[...]

    for copy in input_moves[:3]:
        copy.wait()
    input_moves[3].start()
    input_moves[3].wait()
    output_moves[3].wait()
    scatter.run(len(scatter.queue))
    scatter.sent()


def back(shard_size, pieces, buckets, lengths, full, normed_t, qkv, bandt, biast, grads, do, lse, output, middle, tokens, gain_two, table_rows, came):
    low, f32 = jnp.bfloat16, jnp.float32
    deep = shard_size // 2
    rows = full.shape[3]
    width, length = normed_t.shape
    half, quarter = length // 2, length // 4
    heads, blocks = biast.shape[:2]
    pairs = heads // 2
    inner = pairs * 128
    hidden = (grads.shape[4] - inner) // 3
    count = len(pieces)
    shape = jax.ShapeDtypeStruct
    vmem, hbm = pl.BlockSpec(memory_space=pltpu.VMEM), pl.BlockSpec(memory_space=pl.ANY)
    dma = pltpu.SemaphoreType.DMA
    lines = 2 * (width // 128) + buckets
    buffers = [piece_buffers(piece, deep, rows) for piece in pieces]
    scratch = [pltpu.VMEM(buffer[k], low) for k in range(4) for buffer in buffers]
    small = pltpu.VMEM((lines, 128), f32)
    scratch += [
        pltpu.VMEM((3 * pairs, length, 128), low),
        pltpu.VMEM((width, length), low),
        pltpu.VMEM((blocks, BAND * BLOCK, BLOCK), low),
        pltpu.VMEM((heads, blocks, BAND * BLOCK, BLOCK), low),
        pltpu.VMEM((deep, 2, 2, rows, 3 * inner), low),
        pltpu.VMEM((deep, 2, 2, rows, 128), low),
        pltpu.VMEM((pairs, length, 128), low),
        pltpu.VMEM((length, 256), f32),
        pltpu.VMEM((length, 256), low),
        pltpu.VMEM((2, heads, blocks, BLOCK), f32),
        pltpu.VMEM((length, 128), f32),
        pltpu.VMEM((length, 128), f32),
        pltpu.VMEM((length, 128), low),
        pltpu.VMEM((pairs, deep, 2, 2, rows, 3 * 128), low),
        pltpu.VMEM((2, quarter, width), f32),
        pltpu.VMEM((2, quarter, width), low),
        pltpu.VMEM((2, quarter, width), low),
        pltpu.VMEM((2, quarter, width), low),
        pltpu.VMEM((buckets * GROUP, heads * GROUP), f32),
        pltpu.VMEM((TURNS, buckets * GROUP, 2 * BLOCK), low),
        pltpu.VMEM((TURNS, heads * GROUP, 2 * BLOCK), low),
        small, small, small, small, small, pltpu.VMEM((deep, lines, 128), f32), small,
        dma((count,)),
        dma((count, 3, deep - 1)),
        dma((count, 3, deep - 1)),
        dma((12 + deep,)),
        dma((12 + deep,)),
        dma((9,)),
    ]
    return pl.pallas_call(
        functools.partial(back_kernel, shard_size, pieces, (inner, hidden, buckets), len(came)),
        out_shape=[
            *[shape((rows, n), f32) for n in (inner,) * 4 + (hidden,) * 3],
            shape((2, half, width), low),
            shape((2, half, width), low),
            shape((2, lines, 128), f32),
        ],
        in_specs=[pl.BlockSpec(memory_space=pltpu.SMEM)] + [hbm] * 7 + [vmem] * 6 + [hbm] * len(came),
        out_specs=[vmem] * 7 + [hbm, hbm, vmem],
        scratch_shapes=scratch,
        compiler_params=pltpu.CompilerParams(
            collective_id=2, has_side_effects=True, vmem_limit_bytes=60 * MIB
        ),
        name="back",
    )(lengths, full, normed_t, qkv, bandt, biast, grads, do, lse, output, middle, tokens, gain_two, table_rows, *came)


def finish_kernel(*refs):
    count = len(refs) // 2
    for source, target in zip(refs[:count], refs[count:]):
        target[...] = source[...].astype(target.dtype)


def finish(weight_sums, output, input_grad):
    steps = 4 if weight_sums[0].shape[0] % 32 == 0 else 2
    values = [*weight_sums, output, input_grad]
    kinds = [jnp.float32] * len(weight_sums) + [output.dtype, jnp.float32]
    specs = [pl.BlockSpec((w.shape[0] // steps, w.shape[1]), lambda i: (i, 0)) for w in weight_sums]
    specs += [pl.BlockSpec((2, v.shape[1] // steps, v.shape[2]), lambda i: (0, i, 0)) for v in (output, input_grad)]
    return pl.pallas_call(
        finish_kernel,
        grid=(steps,),
        in_specs=specs,
        out_specs=specs,
        out_shape=[jax.ShapeDtypeStruct(v.shape, kind) for v, kind in zip(values, kinds)],
        compiler_params=pltpu.CompilerParams(vmem_limit_bytes=60 * MIB),
        name="finish",
    )(*values)


ORDERS = ("xyz", "zxy", "zyx", "zxy", "zxy", "zyx", "zxy", "zyx", "zxy")
SUM_ORDERS = ("yxz", "xyz")
GIVEN = 6
LATE_FIRST = 6
LATE_STEP = 3
ROW_ACTS = 2
WINDOW = 4
AHEAD = 2
LAG = 3
QUICK = 4
SUM_WINDOW = 3
SUM_LAGS = (2, 4)
FORWARD_ACTS = 8
ATTENTION_ACTS = 28
ACT_FIRST = 2
TABLE_ACTS = 14


def front_pieces(inner, hidden):
    at_project = 128 + 3 * inner
    at_hidden = at_project + inner
    pieces = split_columns(0, at_project, 4) + split_columns(at_project, at_hidden, 2)
    for j, n in enumerate(hidden_steps(hidden)):
        at = at_hidden + 3 * HIDDEN_STEP * j
        pieces += split_columns(at, at + 3 * n, 2)
    return [(a, b, ORDERS[i % len(ORDERS)]) for i, (a, b) in enumerate(pieces)]


def back_pieces(inner, hidden):
    where = []
    for j, n in enumerate(hidden_steps(hidden)):
        for k in range(3):
            where.append((3 * HIDDEN_STEP * j + k * n, n, 4 + k, HIDDEN_STEP * j))
    where.append((3 * hidden, inner, 3, 0))
    cuts = []
    for j, n in enumerate(hidden_steps(hidden)):
        at = 3 * HIDDEN_STEP * j
        cuts += split_columns(at, at + 3 * n, 2 if n > 128 else 1)
    cuts += split_columns(3 * hidden, 3 * hidden + inner, 2)
    pieces = []
    for a, b in cuts:
        segments = []
        for start, n, out, column in where:
            low, high = max(a, start), min(b, start + n)
            if low < high:
                segments.append((out, column + low - start, low - a, high - low))
        pieces.append((0, a, b, segments))
    for pair in range(inner // 128):
        piece = (1 + pair, 0, 3 * 128, [(t, pair * 128, t * 128, 128) for t in range(3)])
        pieces.insert(min(len(pieces), LATE_FIRST + LATE_STEP * pair), piece)
    return [(t, a, b, SUM_ORDERS[i % len(SUM_ORDERS)], segments) for i, (t, a, b, segments) in enumerate(pieces)]


def shards(
    inputs, cotangent, lengths, buckets,
    query_weight, key_weight, value_weight, projection_weight, gate_weight, up_weight, down_weight,
    attention_gain, feedforward_gain, bias_table,
):
    x = lax.axis_index("ctx")
    shard_size = lax.axis_size("shard")
    width = inputs.shape[2]
    bucket_count, heads = bias_table.shape
    rows, inner = query_weight.shape
    hidden = gate_weight.shape[1]
    cuts = back_pieces(inner, hidden)
    gains = jnp.pad(jnp.stack([attention_gain, feedforward_gain], axis=1), ((0, 0), (0, 126)))
    table_rows = jnp.broadcast_to(
        jnp.pad(bias_table.astype(jnp.float32).T, ((0, 0), (0, 128 - bucket_count)))[:, None, :], (heads, 8, 128)
    )
    weights = (query_weight, key_weight, value_weight, projection_weight, gate_weight, up_weight, down_weight)
    (
        full, normed_t, qkv, bandt, biast, grads, grad_attended, tokens,
        lse, output, grad_middle, gain_two, *came,
    ) = front(shard_size, front_pieces(inner, hidden), WINDOW, [(a, b, order[0]) for _, a, b, order, _ in cuts[:GIVEN]], lengths, gains, weights, inputs, cotangent, buckets, table_rows)

    *weight_sums, output, input_grad, small = back(
        shard_size, cuts, bucket_count,
        lengths, full, normed_t, qkv, bandt, biast, grads, grad_attended,
        lse, output, grad_middle, tokens, gain_two, table_rows, came,
    )
    *weight_sums, output, input_grad = finish(weight_sums, output, input_grad)
    lines = width // 128
    me = lax.axis_index("shard") * 2 + x

    def own_gain(part):
        return lax.dynamic_slice_in_dim(small[1, part * lines : (part + 1) * lines].reshape(-1), me * rows, rows)

    return (
        output, input_grad,
        *weight_sums, own_gain(0), own_gain(1), small[0, 2 * lines :, :heads],
    )


def solution(mesh):
    rows = P(None, ("shard", "ctx"), None)
    weight = P(("shard", "ctx"), "tp")
    gain = P(("shard", "ctx"))
    table = P(None, "tp")
    return jax.shard_map(
        shards,
        mesh=mesh,
        in_specs=(rows, rows, P(None, "shard"), P("ctx", None)) + (weight,) * 7 + (gain, gain, table),
        out_specs=(rows, rows) + (weight,) * 7 + (gain, gain, table),
        check_vma=False,
    )
```

```python
import functools

import jax
import jax.numpy as jnp
from jax import lax
from jax.experimental import pallas as pl
from jax.experimental.pallas import tpu as pltpu
from jax.sharding import PartitionSpec as P

EPSILON = 1e-06
GELU_ROOT = 0.7978845608028654
GELU_CUBIC = 0.044715
MESH = pl.DeviceIdType.MESH
MIB = 1024 * 1024


BAND = 3
BLOCK = 128


def lane_head(rows, width, which):
    lanes = lax.broadcasted_iota(jnp.int32, (rows, width), 1)
    half = width // 2
    return (lanes < half) if which == 0 else (lanes >= half)


def band_start(row_block, blocks):
    return jnp.clip(row_block - 1, 0, blocks - BAND)


def split_columns(start, stop, pieces):
    tiles = (stop - start) // 128
    edges = [start + 128 * (tiles * i // pieces) for i in range(pieces + 1)]
    return [(a, b) for a, b in zip(edges, edges[1:]) if b > a]


class Place:
    def __init__(self, shard_size):
        self.deep = shard_size // 2
        shard = lax.axis_index("shard")
        self.z = shard // 2
        self.y = shard % 2
        self.x = lax.axis_index("ctx")
        self.c = lax.axis_index("tp")

    def device(self, z=None, y=None, x=None, c=None):
        z = self.z if z is None else z
        y = self.y if y is None else y
        x = self.x if x is None else x
        c = self.c if c is None else c
        return (z * 2 + y, x, c)

    def line(self, distance):
        return (self.z + distance) % self.deep

    def peers(self):
        others = [self.device(z=self.line(d)) for d in range(1, self.deep)]
        return others + [self.device(y=1 - self.y), self.device(x=1 - self.x), self.device(c=1 - self.c)]


def meet(place):
    barrier = pltpu.get_barrier_semaphore()
    peers = place.peers()
    for peer in peers:
        pl.semaphore_signal(barrier, inc=1, device_id=peer, device_id_type=MESH)
    pl.semaphore_wait(barrier, len(peers))


def send(source, target, send_sem, recv_sem, device):
    return pltpu.make_async_remote_copy(
        src_ref=source, dst_ref=target, send_sem=send_sem, recv_sem=recv_sem, device_id=device, device_id_type=MESH
    )


LAST = (((1,), (1,)), ((), ()))
FIRST = (((0,), (0,)), ((), ()))
HIDDEN_STEP = 256
HALF_BUCKETS = 16


def hidden_steps(hidden):
    return [min(HIDDEN_STEP, hidden - at) for at in range(0, hidden, HIDDEN_STEP)]


class Gather:
    def __init__(self, place, pieces, own_ref, full_ref, send_sem, recv_sem):
        self.place, self.pieces, self.own, self.full = place, pieces, own_ref, full_ref
        self.send_sem, self.recv_sem = send_sem, recv_sem
        self.queue = []

    def held(self, piece, hop):
        a, b, order = self.pieces[piece]
        place, done = self.place, order[:hop]
        at = [slice(None) if name in done else getattr(place, name) for name in "zyx"]
        return self.full.at[at[0], at[1], at[2], :, a:b]

    def copies(self, piece, hop):
        place = self.place
        a, b, order = self.pieces[piece]
        target = self.held(piece, hop)
        source = self.own.at[:, a:b] if hop == 0 else target
        name = order[hop]
        if name == "z":
            peers = [place.device(z=place.line(d)) for d in range(1, place.deep)]
        elif name == "y":
            peers = [place.device(y=1 - place.y)]
        else:
            peers = [place.device(x=1 - place.x)]
        return [
            send(source, target, self.send_sem.at[piece, hop, i], self.recv_sem.at[piece, hop, i], peer)
            for i, peer in enumerate(peers)
        ]

    def start(self, piece, hop):
        for copy in self.copies(piece, hop):
            copy.start()

    def arrive(self, piece, hop):
        for copy in self.copies(piece, hop):
            copy.wait_recv()

    def sent(self):
        for piece in range(len(self.pieces)):
            for hop in range(3):
                for copy in self.copies(piece, hop):
                    copy.wait_send()

    def plan(self, window):
        count = len(self.pieces)
        self.window = window

        def second(piece):
            def act():
                self.arrive(piece, 0)
                self.start(piece, 1)
                if piece + window < count:
                    self.start(piece + window, 0)
            return act

        def third(piece):
            def act():
                self.arrive(piece, 1)
                self.start(piece, 2)
            return act

        turned = 0
        for piece in range(count + LAG):
            if piece < count:
                self.queue.append((None, second(piece)))
            while turned < count and turned <= piece - (1 if turned < QUICK else LAG):
                self.queue.append((turned, third(turned)))
                turned += 1
        for piece in range(min(window, count)):
            self.start(piece, 0)

    def run(self, steps):
        for _ in range(min(steps, len(self.queue))):
            self.queue.pop(0)[1]()

    def take(self, steps):
        taken, self.queue = self.queue[:steps], self.queue[steps:]
        return [act for _, act in taken]

    def need(self, pieces):
        for piece in pieces:
            while any(mark == piece for mark, _ in self.queue):
                self.run(1)
        self.run(AHEAD)
        for piece in pieces:
            self.arrive(piece, 2)


def query_aux(table, step, blocks):
    parts = []
    lanes = lax.broadcasted_iota(jnp.int32, (BLOCK, 128), 1)
    buckets = 2 * HALF_BUCKETS
    below = jnp.broadcast_to(table[0:1, HALF_BUCKETS - 1 : HALF_BUCKETS], (BLOCK, 128))
    above = jnp.broadcast_to(table[0:1, buckets - 1 : buckets], (BLOCK, 128))
    for sub in range(2):
        start = band_start(2 * step + sub, blocks)
        value = jnp.where(lanes < start, below, 0.0)
        value = jnp.where((lanes >= start + BAND) & (lanes < blocks), above, value)
        parts.append(jnp.where(lanes == blocks, 1.0, value))
    return jnp.concatenate(parts, axis=0).astype(jnp.bfloat16)


def between(acts, units, skip, unit, head):
    slots = 2 * units - skip
    for k, act in enumerate(acts):
        slot = skip + (k * slots) // len(acts)
        if slot % 2 == head:
            pl.when(unit == slot // 2)(act)


def gelu_all(gate):
    square = gate * gate
    tangent = jnp.tanh(GELU_ROOT * (gate + GELU_CUBIC * square * gate))
    value = 0.5 * gate * (1.0 + tangent)
    slope = 0.5 * (1.0 + tangent) + 0.5 * gate * (1.0 - tangent * tangent) * (
        GELU_ROOT + (3.0 * GELU_CUBIC * GELU_ROOT) * square
    )
    return value, slope


def front_kernel(
    shard_size, pieces, window, sizes, given,
    lengths_ref, gains_ref, query_ref, key_ref, value_ref, project_ref, gate_ref, up_ref, down_ref,
    inputs_ref, cots_ref, buckets_ref, table_ref,
    full_ref, normed_out, qkv_out, bandt_out, biast_out, grads_out, attended_out, tokens_own_ref,
    lse_ref, output_ref, middle_grad_ref, gain_ref, *rest,
):
    came_outs, rest = rest[: len(given)], rest[len(given) :]
    (
    own_ref, tok, cot, band_raw, band, bandt, bias, biast, kaux, gain_buf, qkv, normed, scores, attended, project_w,
    normal, away, arrived, two_t, low_t, acc_out, acc_two, w_buf, g_buf, hid, ggate, gup,
    send_sem, recv_sem, near_send, near_recv, local_sem, w_sem, g_sem, own_sem, bt_sem, early_send, early_recv,
    ) = rest
    inner, hidden = sizes
    length, width = tok.shape
    half, quarter = length // 2, length // 4
    heads, blocks = bias.shape[:2]
    pairs = heads // 2
    deep = shard_size // 2
    low = jnp.bfloat16
    place = Place(shard_size)
    x, c = place.x, place.c
    at_q = 128
    at_project = at_q + 3 * inner
    at_hidden = at_project + inner
    steps = hidden_steps(hidden)
    per_step = 2
    first_hidden_piece = len(pieces) - per_step * len(steps)
    project_pieces = [i for i, (a, b, _) in enumerate(pieces) if at_project <= a < at_hidden]
    qkv_pieces = [i for i, (a, b, _) in enumerate(pieces) if a < at_project]

    def own_load(i, source, target):
        return pltpu.make_async_copy(source, target, local_sem.at[i])

    parts, at = [], 0
    for ref in (gains_ref, query_ref, key_ref, value_ref, project_ref):
        parts.append((ref, at))
        at += ref.shape[1]
    own_loads = [
        pltpu.make_async_copy(ref, own_ref.at[:, at : at + ref.shape[1]], own_sem.at[i]) for i, (ref, at) in enumerate(parts)
    ]
    for j, n in enumerate(steps):
        for k, ref in enumerate((gate_ref, up_ref, down_ref)):
            at = at_hidden + 3 * HIDDEN_STEP * j + k * n
            own_loads.append(
                pltpu.make_async_copy(
                    ref.at[:, HIDDEN_STEP * j : HIDDEN_STEP * j + n], own_ref.at[:, at : at + n], own_sem.at[len(own_loads)]
                )
            )

    def band_source(block):
        start = pl.multiple_of(band_start(block, blocks) * BLOCK, BLOCK)
        first = block - x * (blocks // 2)
        return buckets_ref.at[pl.ds(pl.multiple_of(first * BLOCK, BLOCK), BLOCK), pl.ds(start, BAND * BLOCK)]

    own_tok = own_load(0, inputs_ref.at[x], tok.at[pl.ds(x * half, half)])
    own_cot = own_load(1, cots_ref.at[x], cot.at[pl.ds(x * half, half)])
    own_bands = [
        own_load(13 + i, band_source(x * (blocks // 2) + i), band_raw.at[i]) for i in range(blocks // 2)
    ]
    own_full = own_load(3, own_ref, full_ref.at[place.z, place.y, x])
    for copy in (*own_loads, *own_bands, own_tok, own_cot):
        copy.start()
    meet(place)
    for copy in own_loads:
        copy.wait()
    own_full.start()

    gather = Gather(place, pieces, own_ref, full_ref, send_sem, recv_sem)
    to_x, to_c = place.device(x=1 - x), place.device(c=1 - c)

    def x_rows(sender_x, sender_c):
        return pl.ds(sender_x * half + sender_c * quarter, quarter)

    def near(i, source, target, device):
        return send(source, target, near_send.at[i], near_recv.at[i], device)

    mine = [x * (blocks // 2) + c * (blocks // 4) + i for i in range(blocks // 4)]
    theirs = [(1 - x) * (blocks // 2) + c * (blocks // 4) + i for i in range(blocks // 4)]
    band_x = [near(16 + i, band.at[block], band.at[block], to_x) for i, block in enumerate(mine)]
    tok_x = near(1, inputs_ref.at[1 - x, pl.ds(c * quarter, quarter)], tok.at[x_rows(x, c)], to_x)
    cot_x = near(2, cots_ref.at[1 - x, pl.ds(c * quarter, quarter)], cot.at[x_rows(x, c)], to_x)
    band_c = [near(16 + len(mine) + i, band.at[block], band.at[block], to_c) for i, block in enumerate(theirs)]
    tok_c = near(4, tok.at[x_rows(1 - x, c)], tok.at[x_rows(1 - x, c)], to_c)
    cot_c = near(5, cot.at[x_rows(1 - x, c)], cot.at[x_rows(1 - x, c)], to_c)
    gather.plan(window)
    for copy in own_bands:
        copy.wait()
    for i in range(blocks // 2):
        band[x * (blocks // 2) + i] = band_raw[i].astype(jnp.float32).astype(low)
    for copy in band_x:
        copy.start()
    tok_x.start()
    own_full.wait()
    lanes_of = lax.broadcasted_iota(jnp.int32, (length, 128), 1)
    rows_of = lax.broadcasted_iota(jnp.int32, (length, 128), 0)
    valid = lengths_ref[x, 0]
    blocked = jnp.where(rows_of // BLOCK == lanes_of, 1.0, 0.0)
    kaux[...] = jnp.where((lanes_of == blocks) & (rows_of >= valid), -1e30, blocked).astype(low)
    gather.run(1)
    for copy in band_x:
        copy.wait()
    for copy in band_c:
        copy.start()
    gather.run(1)
    for copy in band_c:
        copy.wait()

    def bias_step(i, carry):
        block = i // (BLOCK // 16)
        at = pl.multiple_of((i % (BLOCK // 16)) * 16, 16)
        index = band[block, pl.ds(at, 16), :].astype(jnp.float32).astype(jnp.int32)
        for col in range(BAND):
            lanes = slice(col * BLOCK, (col + 1) * BLOCK)
            for head in range(heads):
                table = table_ref[head]
                got = [jnp.take_along_axis(table, index[8 * k : 8 * k + 8, lanes], axis=1) for k in range(2)]
                bias[head, block, pl.ds(at, 16), lanes] = jnp.concatenate(got, axis=0).astype(low)
        return carry

    bias_steps = blocks * (BLOCK // 16)
    for k in range(4):
        lax.fori_loop(bias_steps * k // 4, bias_steps * (k + 1) // 4, bias_step, 0)
        gather.run(1)
    tok_x.wait()
    tok_c.start()
    cot_x.start()

    def biast_store(block, slot):
        return pltpu.make_async_copy(biast.at[slot], biast_out.at[:, block], bt_sem.at[slot])

    def biast_block(block, carry):
        slot = block % 2

        @pl.when(block > 1)
        def _():
            biast_store(block - 2, slot).wait()

        bandt[block] = jnp.transpose(band[block].astype(jnp.float32)).astype(low)

        def inner_step(i, carry):
            at = pl.multiple_of(i * 16, 16)
            index = bandt[block, pl.ds(at, 16), :].astype(jnp.float32).astype(jnp.int32)
            for head in range(heads):
                got = [jnp.take_along_axis(table_ref[head], index[8 * k : 8 * k + 8], axis=1) for k in range(2)]
                biast[slot, head, pl.ds(at, 16), :] = jnp.concatenate(got, axis=0).astype(low)
            return carry

        lax.fori_loop(0, BAND * BLOCK // 16, inner_step, 0)
        biast_store(block, slot).start()
        return carry

    for k in range(4):
        lax.fori_loop(blocks * k // 4, blocks * (k + 1) // 4, biast_block, 0)
        gather.run(1)
    biast_store(blocks - 2, 0).wait()
    biast_store(blocks - 1, 1).wait()
    bandt_store = own_load(4, bandt, bandt_out)
    bandt_store.start()
    own_tok.wait()
    tok_c.wait()

    def live_step(i, carry):
        rows = pl.ds(pl.multiple_of(i * BLOCK, BLOCK), BLOCK)
        here = lax.broadcasted_iota(jnp.int32, (BLOCK, width), 0) + i * BLOCK < valid
        masked = jnp.where(here, cot[rows, :].astype(jnp.float32), 0.0).astype(low)
        cot[rows, :] = masked
        low_t[:, rows] = jnp.transpose(masked)
        return carry

    gather.need(qkv_pieces)
    load_gains = own_load(5, full_ref.at[:, :, :, :, 0:at_q], gain_buf)
    third = 3 * inner // 2
    loads_wide = [
        pltpu.make_async_copy(
            full_ref.at[:, :, :, :, at_q + third * k : at_q + third * (k + 1)], w_buf.at[k, :, :, :, :, 0:third], w_sem.at[k]
        )
        for k in range(2)
    ]
    for copy in (load_gains, *loads_wide):
        copy.start()
    load_gains.wait()
    gains = jnp.transpose(gain_buf[...].reshape(width, 128).astype(jnp.float32))
    gain_one, gain_two = gains[0:1, :], gains[1:2, :]

    def norm_step(i, carry):
        rows = pl.ds(pl.multiple_of(i * BLOCK, BLOCK), BLOCK)
        present = tok[rows, :].astype(jnp.float32)
        inverse = lax.rsqrt(jnp.mean(present * present, axis=-1, keepdims=True) + EPSILON)
        got = (present * inverse * gain_one).astype(low)
        normed[rows, :] = got
        two_t[:, rows] = jnp.transpose(got)
        return carry

    lax.fori_loop(0, blocks, norm_step, 0)
    normed_store = own_load(6, two_t, normed_out)
    normed_store.start()
    for copy in loads_wide:
        copy.wait()
    gather.run(2)

    for col in range(3 * pairs // 2):
        slot, at = 256 * col // third, 256 * col % third
        lanes = slice(at, at + 256)

        def qkv_step(i, carry):
            rows = pl.ds(pl.multiple_of(i * 256, 256), 256)
            got = jnp.dot(
                normed[rows, :], w_buf[slot, :, :, :, :, lanes].reshape(width, 256), preferred_element_type=jnp.float32
            ).astype(low)
            qkv[2 * col, rows, :] = got[:, :128]
            qkv[2 * col + 1, rows, :] = got[:, 128:]
            return carry

        lax.fori_loop(0, length // 256, qkv_step, 0)
        if col % 2:
            gather.run(1)
    qkv_store = own_load(7, qkv, qkv_out)
    qkv_store.start()

    units = pairs * (length // 256)
    acts = gather.take(min(len(gather.queue), FORWARD_ACTS))

    def unit_step(unit, carry):
        pair = unit // (length // 256)
        step = unit % (length // 256)
        rows = pl.ds(pl.multiple_of(step * 256, 256), 256)
        queries = qkv[pair, rows, :]
        keys = jnp.concatenate([qkv[pairs + pair], kaux[...]], axis=1)
        outs = []
        for head in range(2):
            between(acts, units, 0, unit, head)
            aux = query_aux(table_ref[2 * pair + head], step, blocks)
            masked = jnp.where(lane_head(256, 128, head), queries, jnp.zeros_like(queries))
            scores[...] = lax.dot_general(
                jnp.concatenate([masked, aux], axis=1), keys, LAST, preferred_element_type=jnp.float32
            )
            for sub in range(2):
                start = pl.multiple_of(band_start(step * 2 + sub, blocks) * BLOCK, BLOCK)
                scores[sub * BLOCK : (sub + 1) * BLOCK, pl.ds(start, BAND * BLOCK)] += bias[
                    2 * pair + head, 2 * step + sub
                ].astype(jnp.float32)
            got = scores[...]
            highest = jnp.max(got, axis=1, keepdims=True)
            exponent = jnp.exp(got - highest)
            total = jnp.sum(exponent, axis=1, keepdims=True)
            outs.append(
                jnp.dot(exponent.astype(low), qkv[2 * pairs + pair], preferred_element_type=jnp.float32) * (1.0 / total)
            )
            lse = jnp.broadcast_to(highest + jnp.log(total), (256, 128))
            lse_ref[pair, step, head : head + 1, :] = jnp.transpose(lse)[0:1, :]
        attended[pair, rows, :] = jnp.where(lane_head(256, 128, 0), outs[0], outs[1]).astype(low)
        return carry

    lax.fori_loop(0, units, unit_step, 0)
    own_cot.wait()
    cot_x.wait()
    cot_c.start()

    normed_store.wait()
    two = normed
    gather.need(project_pieces)
    load_project = own_load(9, full_ref.at[:, :, :, :, at_project:at_hidden], project_w)
    load_project.start()
    load_project.wait()

    def branch(rows):
        left = jnp.concatenate([attended[pair, rows, :] for pair in range(pairs)], axis=1)
        return lax.dot_general(left, project_w[...].reshape(width, inner), LAST, preferred_element_type=jnp.float32)

    def part_rows(part, core):
        return pl.ds(pl.multiple_of(part * half + core * quarter, quarter), quarter)

    def swap_part(i, part, slot=0):
        return near(i + part, away.at[slot + part], arrived.at[slot + part], to_c)

    for part in range(2):
        away[part] = branch(part_rows(part, 1 - c)).astype(low)
        swap_part(6, part).start()
    for part in range(2):
        normal[part] = branch(part_rows(part, c)) + tok[part_rows(part, c), :].astype(jnp.float32)

    def share(i, part, buffer):
        return near(i + part, buffer.at[part_rows(part, c)], buffer.at[part_rows(part, c)], to_c)

    tokens_store = [own_load(11 + part, tok.at[part_rows(part, c)], tokens_own_ref.at[part]) for part in range(2)]
    for copy in tokens_store:
        copy.start()
    for part in range(2):
        swap_part(6, part).wait()
        middle = normal[part] + arrived[part].astype(jnp.float32)
        normal[part] = middle
        inverse = lax.rsqrt(jnp.mean(middle * middle, axis=-1, keepdims=True) + EPSILON)
        two[part_rows(part, c), :] = (middle * inverse * gain_two).astype(low)
        share(8, part, two).start()
    gather.run(1)
    for part in range(2):
        share(8, part, two).wait()

    def turn_step(i, carry):
        rows = pl.ds(pl.multiple_of(i * BLOCK, BLOCK), BLOCK)
        two_t[:, rows] = jnp.transpose(two[rows, :])
        return carry

    lax.fori_loop(0, blocks, turn_step, 0)
    gather.run(1)
    cot_c.wait()
    lax.fori_loop(0, blocks, live_step, 0)
    gather.run(1)

    def bounds(j):
        at = at_hidden + 3 * HIDDEN_STEP * j
        return at, at + 3 * steps[j]

    def load_step(j):
        a, b = bounds(j)
        return pltpu.make_async_copy(
            full_ref.at[:, :, :, :, a:b], w_buf.at[j % 2, :, :, :, :, 0 : b - a], w_sem.at[j % 2]
        )

    def store_step(j):
        a, b = bounds(j)
        return pltpu.make_async_copy(
            g_buf.at[j % 2, :, :, :, :, 0 : b - a],
            grads_out.at[:, :, :, :, a - at_hidden : b - at_hidden],
            g_sem.at[j % 2],
        )

    early_sums = []
    for k, (a, b, name) in enumerate(given):
        source = grads_out.at[:, :, 1 - x, :, a:b] if name == "x" else grads_out.at[:, 1 - place.y, :, :, a:b]
        device = to_x if name == "x" else place.device(y=1 - place.y)
        early_sums.append(send(source, came_outs[k], early_send.at[k], early_recv.at[k], device))
    gather.need(range(first_hidden_piece, first_hidden_piece + per_step))
    load_step(0).start()
    for j, units_here in enumerate(steps):
        n = units_here
        slot = j % 2
        load_step(j).wait()

        def weight(k, slot=slot, n=n):
            return w_buf[slot, :, :, :, :, k * n : (k + 1) * n].reshape(width, n)

        inside = gather.take(ROW_ACTS)

        def rows_step(i, carry, j=j, n=n, weight=weight, inside=inside):
            for k, act in enumerate(inside):
                pl.when(i == (2 * k + 1) * (length // 256) // (2 * len(inside)))(act)
            rows = pl.ds(pl.multiple_of(i * 256, 256), 256)
            left, grad = two[rows, :], cot[rows, :]
            gate = jnp.dot(left, weight(0), preferred_element_type=jnp.float32)
            up = jnp.dot(left, weight(1), preferred_element_type=jnp.float32)
            grad_hidden = jnp.dot(grad, weight(2), preferred_element_type=jnp.float32)
            value, slope = gelu_all(gate)
            hid[rows, 0:n] = (value * up).astype(low)
            ggate[rows, 0:n] = (grad_hidden * up * slope).astype(low)
            gup[rows, 0:n] = (grad_hidden * value).astype(low)
            out = lax.dot_general(hid[rows, 0:n], weight(2), LAST, preferred_element_type=jnp.float32)
            back = lax.dot_general(ggate[rows, 0:n], weight(0), LAST, preferred_element_type=jnp.float32)
            back = back + lax.dot_general(gup[rows, 0:n], weight(1), LAST, preferred_element_type=jnp.float32)
            if j == 0:
                acc_out[rows, :] = out
                acc_two[rows, :] = back
            else:
                acc_out[rows, :] += out
                acc_two[rows, :] += back
            return carry

        lax.fori_loop(0, length // 256, rows_step, 0)
        if j + 1 < len(steps):
            first = first_hidden_piece + per_step * (j + 1)
            gather.need(range(first, first + per_step))
            load_step(j + 1).start()
        if j > 1:
            store_step(j - 2).wait()
        if j + 2 >= len(steps):
            for copy, (_, b, _) in zip(early_sums, given):
                ready = max(0, -(-b // (3 * HIDDEN_STEP)) - 1)
                if ready == j - 2 or (ready < j - 2 and j + 2 == len(steps)):
                    copy.start()

        tiles = width // 256

        def grads_step(i, carry, slot=slot, n=n):
            rows = pl.ds(pl.multiple_of(i * 256, 256), 256)
            for k, (left, right) in enumerate(((two_t, ggate), (two_t, gup), (low_t, hid))):
                got = jnp.dot(left[rows, :], right[:, 0:n], preferred_element_type=jnp.float32).astype(low)
                span = deep // tiles
                g_buf[slot, pl.ds(i * span, span), :, :, :, k * n : (k + 1) * n] = got.reshape(
                    (span,) + g_buf.shape[2:5] + (n,)
                )
            return carry

        lax.fori_loop(0, tiles, grads_step, 0)
        store_step(j).start()
    gather.run(len(gather.queue))

    def share_sum(i, acc, slot):
        for part in range(2):
            away[slot + part] = acc[part_rows(part, 1 - c), :].astype(low)
            swap_part(i, part, slot).start()

    share_sum(10, acc_two, 0)
    for part in range(2):
        swap_part(10, part).wait()
        grad_two = acc_two[part_rows(part, c), :] + arrived[part].astype(jnp.float32)
        middle = normal[part]
        inverse = lax.rsqrt(jnp.mean(middle * middle, axis=-1, keepdims=True) + EPSILON)
        unit = middle * inverse
        weighted = jnp.sum((grad_two * unit).reshape(quarter // 8, 8, width), axis=0)
        gain_ref[part] = weighted
        scaled = grad_two * gain_two
        grad_middle = cot[part_rows(part, c), :].astype(jnp.float32) + inverse * (
            scaled - unit * jnp.mean(scaled * unit, axis=-1, keepdims=True)
        )
        middle_grad_ref[part] = grad_middle
        two[part_rows(part, c), :] = grad_middle.astype(low)
        share(12, part, two).start()
    share_sum(14, acc_out, 2)
    for part in range(2):
        swap_part(14, part, 2).wait()
        output_ref[part] = (normal[part] + acc_out[part_rows(part, c), :] + arrived[2 + part].astype(jnp.float32)).astype(low)
    for part in range(2):
        share(12, part, two).wait()
    for j in range(max(0, len(steps) - 2), len(steps)):
        store_step(j).wait()

    lax.fori_loop(0, blocks, turn_step, 0)

    def project_step(i, carry):
        rows = pl.ds(pl.multiple_of(i * 256, 256), 256)
        right = jnp.concatenate([attended[pair] for pair in range(pairs)], axis=1)
        got = jnp.dot(two_t[rows, :], right, preferred_element_type=jnp.float32).astype(low)
        span = deep // (width // 256)
        g_buf[0, pl.ds(i * span, span), :, :, :, 0:inner] = got.reshape((span,) + g_buf.shape[2:5] + (inner,))
        return carry

    lax.fori_loop(0, width // 256, project_step, 0)
    project_store = own_load(8, g_buf.at[0, :, :, :, :, 0:inner], grads_out.at[:, :, :, :, 3 * hidden : 3 * hidden + inner])
    project_store.start()

    def attended_step(i, carry):
        rows = pl.ds(pl.multiple_of(i * 256, 256), 256)
        got = jnp.dot(two[rows, :], project_w[...].reshape(width, inner), preferred_element_type=jnp.float32).astype(low)
        for pair in range(pairs):
            attended[pair, rows, :] = got[:, pair * 128 : (pair + 1) * 128]
        return carry

    lax.fori_loop(0, length // 256, attended_step, 0)
    attended_store = own_load(10, attended, attended_out)
    attended_store.start()
    for copy in (bandt_store, qkv_store, attended_store, project_store, *tokens_store, *early_sums):
        copy.wait()
    gather.sent()


def front(shard_size, pieces, window, given, lengths, gains, weights, inputs, cots, buckets, table_rows):
    low, f32 = jnp.bfloat16, jnp.float32
    deep = shard_size // 2
    rows, inner = weights[0].shape
    hidden = weights[4].shape[1]
    wide = pieces[-1][1]
    half, width = inputs.shape[1:]
    length, quarter = 2 * half, half // 2
    heads = table_rows.shape[0]
    blocks = length // BLOCK
    pairs = heads // 2
    shape = jax.ShapeDtypeStruct
    vmem, hbm = pl.BlockSpec(memory_space=pltpu.VMEM), pl.BlockSpec(memory_space=pl.ANY)
    dma = pltpu.SemaphoreType.DMA
    count = len(pieces)
    step = HIDDEN_STEP
    out_shape = [
        shape((deep, 2, 2, rows, wide), low),
        shape((width, length), low),
        shape((3 * pairs, length, 128), low),
        shape((blocks, BAND * BLOCK, BLOCK), low),
        shape((heads, blocks, BAND * BLOCK, BLOCK), low),
        shape((deep, 2, 2, rows, 3 * hidden + inner), low),
        shape((pairs, length, 128), low),
        shape((2, quarter, width), low),
        shape((pairs, length // 256, 2, 256), f32),
        shape((2, quarter, width), low),
        shape((2, quarter, width), f32),
        shape((2, 8, width), f32),
    ] + [shape((deep, 2, rows, b - a), low) for a, b, _ in given]
    scratch = [
        pltpu.VMEM((rows, wide), low),
        pltpu.VMEM((length, width), low),
        pltpu.VMEM((length, width), low),
        pltpu.VMEM((blocks // 2, BLOCK, BAND * BLOCK), jnp.int32),
        pltpu.VMEM((blocks, BLOCK, BAND * BLOCK), low),
        pltpu.VMEM((blocks, BAND * BLOCK, BLOCK), low),
        pltpu.VMEM((heads, blocks, BLOCK, BAND * BLOCK), low),
        pltpu.VMEM((2, heads, BAND * BLOCK, BLOCK), low),
        pltpu.VMEM((length, 128), low),
        pltpu.VMEM((deep, 2, 2, rows, 128), low),
        pltpu.VMEM((3 * pairs, length, 128), low),
        pltpu.VMEM((length, width), low),
        pltpu.VMEM((256, length), f32),
        pltpu.VMEM((pairs, length, 128), low),
        pltpu.VMEM((deep, 2, 2, rows, inner), low),
        pltpu.VMEM((2, quarter, width), f32),
        pltpu.VMEM((4, quarter, width), low),
        pltpu.VMEM((4, quarter, width), low),
        pltpu.VMEM((width, length), low),
        pltpu.VMEM((width, length), low),
        pltpu.VMEM((length, width), f32),
        pltpu.VMEM((length, width), f32),
        pltpu.VMEM((2, deep, 2, 2, rows, 3 * step), low),
        pltpu.VMEM((2, deep, 2, 2, rows, 3 * step), low),
        pltpu.VMEM((length, step), low),
        pltpu.VMEM((length, step), low),
        pltpu.VMEM((length, step), low),
        dma((count, 3, deep - 1)),
        dma((count, 3, deep - 1)),
        dma((16 + blocks // 2,)),
        dma((16 + blocks // 2,)),
        dma((13 + blocks // 2,)),
        dma((2,)),
        dma((2,)),
        dma((5 + 3 * len(hidden_steps(hidden)),)),
        dma((2,)),
        dma((len(given),)),
        dma((len(given),)),
    ]
    return pl.pallas_call(
        functools.partial(front_kernel, shard_size, pieces, window, (inner, hidden), given),
        out_shape=out_shape,
        in_specs=[pl.BlockSpec(memory_space=pltpu.SMEM)] + [hbm] * 11 + [vmem],
        out_specs=[hbm] * 8 + [vmem] * 4 + [hbm] * len(given),
        scratch_shapes=scratch,
        compiler_params=pltpu.CompilerParams(
            collective_id=1, has_side_effects=True, vmem_limit_bytes=60 * MIB
        ),
        name="front",
    )(lengths, gains, *weights, inputs, cots, buckets, table_rows)


GROUP = 16
TURNS = 4


class Scatter:
    def __init__(self, place, pieces, sources, outs, buffers, sems, came):
        self.came = came
        self.place, self.pieces, self.sources, self.outs = place, pieces, sources, outs
        self.first, self.own, self.second, self.third = buffers
        self.own_sem, self.send_sem, self.recv_sem = sems
        self.queue = []

    def peer(self, name):
        place = self.place
        return place.device(y=1 - place.y) if name == "y" else place.device(x=1 - place.x)

    def rest(self, piece):
        order = self.pieces[piece][3]
        return [name for name in "zyx" if name != order[0]]

    def cut(self, piece, name, value):
        t, a, b = self.pieces[piece][:3]
        at = [value if name == other else slice(None) for other in "zyx"]
        if t:
            return self.sources[1].at[t - 1, at[0], at[1], at[2]]
        return self.sources[0].at[at[0], at[1], at[2], :, a:b]

    def own_copy(self, piece):
        order = self.pieces[piece][3]
        return pltpu.make_async_copy(
            self.cut(piece, order[0], getattr(self.place, order[0])), self.own[piece], self.own_sem.at[piece]
        )

    def copies(self, piece, hop):
        place, order = self.place, self.pieces[piece][3]
        name, rest = order[hop], self.rest(piece)
        own, made = self.own[piece], []

        def at(**index):
            return tuple(index[n] if n in index else slice(None) for n in rest)

        def add(source, target, device):
            i = len(made)
            made.append(send(source, target, self.send_sem.at[piece, hop, i], self.recv_sem.at[piece, hop, i], device))

        if hop == 0:
            if name == "z":
                for d in range(1, place.deep):
                    z = place.line(d)
                    add(self.cut(piece, "z", z), self.first[piece].at[d - 1], place.device(z=z))
            else:
                add(self.cut(piece, name, 1 - getattr(place, name)), self.first[piece], self.peer(name))
            return made
        fixed = {} if hop == 1 else {order[1]: getattr(place, order[1])}
        buffer = self.second[piece] if hop == 1 else self.third[piece]
        if name == "z":
            for d in range(1, place.deep):
                z = place.line(d)
                add(own.at[at(z=z, **fixed)], buffer.at[d - 1], place.device(z=z))
        else:
            add(own.at[at(**{name: 1 - getattr(place, name)}, **fixed)], buffer, self.peer(name))
        return made

    def start(self, piece, hop):
        for copy in self.copies(piece, hop):
            copy.start()

    def arrive(self, piece, hop):
        for copy in self.copies(piece, hop):
            copy.wait_recv()

    def came_copy(self, piece):
        return pltpu.make_async_copy(self.came[piece], self.first[piece], self.recv_sem.at[piece, 0, 0])

    def begin(self, piece):
        if piece < len(self.came):
            self.came_copy(piece).start()
        else:
            self.start(piece, 0)
        self.own_copy(piece).start()

    def add_first(self, piece):
        order = self.pieces[piece][3]
        if piece < len(self.came):
            self.came_copy(piece).wait()
        else:
            self.arrive(piece, 0)
        self.own_copy(piece).wait()
        if piece >= len(self.came) and self.waiting:
            self.begin(self.waiting.pop(0))
        own, came = self.own[piece], self.first[piece]
        inner = own.shape[1]

        def body(i, carry):
            for k in range(inner):
                if order[0] == "z":
                    total = own[i, k].astype(jnp.float32)
                    for d in range(came.shape[0]):
                        total = total + came[d, i, k].astype(jnp.float32)
                    own[i, k] = total.astype(jnp.bfloat16)
                else:
                    own[i, k] = own[i, k] + came[i, k]
            return carry

        lax.fori_loop(0, own.shape[0], body, 0)
        self.start(piece, 1)

    def add_second(self, piece):
        place, order = self.place, self.pieces[piece][3]
        name, rest = order[1], self.rest(piece)
        self.arrive(piece, 1)
        own, came = self.own[piece], self.second[piece]
        mine = getattr(place, name)
        spans = own.shape[1] if rest[0] == name else own.shape[0]

        def body(i, carry):
            if name == "z":
                total = own[mine, i].astype(jnp.float32)
                for d in range(came.shape[0]):
                    total = total + came[d, i].astype(jnp.float32)
                own[mine, i] = total.astype(jnp.bfloat16)
            elif rest[0] == name:
                own[mine, i] = own[mine, i] + came[i]
            else:
                own[i, mine] = own[i, mine] + came[i]
            return carry

        lax.fori_loop(0, spans, body, 0)
        self.start(piece, 2)

    def add_third(self, piece):
        place, order = self.place, self.pieces[piece][3]
        rest = self.rest(piece)
        self.arrive(piece, 2)
        total = self.own[piece][getattr(place, rest[0]), getattr(place, rest[1])].astype(jnp.float32)
        if order[2] == "z":
            for d in range(1, place.deep):
                total = total + self.third[piece][d - 1].astype(jnp.float32)
        else:
            total = total + self.third[piece][...].astype(jnp.float32)
        for out, start, at, n in self.pieces[piece][4]:
            self.outs[out][:, start : start + n] = total[:, at : at + n]

    def plan(self, window):
        self.waiting = [i for i, piece in enumerate(self.pieces) if piece[0] == 0]
        count = len(self.pieces)
        for i in range(count + SUM_LAGS[1]):
            if i < count:
                self.queue.append(functools.partial(self.add_first, i))
            if 0 <= i - SUM_LAGS[0] < count:
                self.queue.append(functools.partial(self.add_second, i - SUM_LAGS[0]))
            if 0 <= i - SUM_LAGS[1] < count:
                self.queue.append(functools.partial(self.add_third, i - SUM_LAGS[1]))
        for _ in range(min(len(self.came) + window, len(self.waiting))):
            self.begin(self.waiting.pop(0))

    def run(self, steps):
        for _ in range(min(steps, len(self.queue))):
            self.queue.pop(0)()

    def take(self, steps):
        taken, self.queue = self.queue[:steps], self.queue[steps:]
        return taken

    def sent(self):
        for piece in range(len(self.pieces)):
            for hop in range(0 if piece >= len(self.came) else 1, 3):
                for copy in self.copies(piece, hop):
                    copy.wait_send()


def piece_buffers(piece, deep, rows):
    _, a, b, order, _ = piece
    sizes = {"z": deep, "y": 2, "x": 2}
    rest = [name for name in "zyx" if name != order[0]]
    left = [sizes[name] for name in rest]
    last = [sizes[name] for name in rest if name != order[1]]
    tail = [rows, b - a]
    lead = [deep - 1]
    first = (lead if order[0] == "z" else []) + left + tail
    second = (lead if order[1] == "z" else []) + last + tail
    third = (lead if order[2] == "z" else []) + tail
    return [tuple(shape) for shape in (first, left + tail, second, third)]


def back_kernel(shard_size, pieces, sizes, given, *refs):
    inner, hidden, buckets = sizes
    count = len(pieces)
    (
        lengths_ref, full_ref, normed_in, qkv_in, bandt_in, biast_in, grads_in, do_in,
        lse_ref, output_ref, middle_ref, tokens_ref, gain_two_ref, table_ref,
    ) = refs[:14]
    came, refs = refs[14 : 14 + given], refs[14 + given :]
    weight_outs, (output_out, input_out, small_out) = refs[:7], refs[7:10]
    refs = refs[10:]
    first, own, second, third = [refs[k * count : (k + 1) * count] for k in range(4)]
    refs = refs[4 * count :]
    (
        qkv, normed_t, bandt, bias, wqkv, gain_buf, do, scores, grads, far, dk_acc, dv_acc, kaux, wgrad,
        mine_sum, away, arrived, result, table_acc, hot, found,
        small, small_x, small_y, hold_x, hold_y, hold_z, small_c,
        own_sem, send_sem, recv_sem, near_send, near_recv, local_sem,
    ) = refs
    length = qkv.shape[1]
    width = normed_t.shape[0]
    half, quarter = length // 2, length // 4
    heads, blocks = bias.shape[:2]
    pairs = heads // 2
    deep = shard_size // 2
    low, f32 = jnp.bfloat16, jnp.float32
    place = Place(shard_size)
    x, y, z, c = place.x, place.y, place.z, place.c
    to_x, to_y, to_c = place.device(x=1 - x), place.device(y=1 - y), place.device(c=1 - c)

    def local(i, source, target):
        return pltpu.make_async_copy(source, target, local_sem.at[i])

    loads = [
        local(0, qkv_in, qkv), local(1, biast_in, bias), local(2, do_in, do),
        local(3, full_ref.at[:, :, :, :, 128 : 128 + 3 * inner], wqkv), local(4, normed_in, normed_t),
        local(5, bandt_in, bandt), local(6, full_ref.at[:, :, :, :, 0:128], gain_buf),
    ]
    for copy in loads:
        copy.start()
    meet(place)
    scatter = Scatter(
        place, pieces, (grads_in, wgrad), weight_outs, (first, own, second, third), (own_sem, send_sem, recv_sem), came,
    )
    scatter.plan(SUM_WINDOW)

    def near(i, source, target, device):
        return send(source, target, near_send.at[i], near_recv.at[i], device)

    def to_owners(i, values, out):
        here = out.at[x, pl.ds(c * quarter, quarter)]
        there = out.at[1 - x, pl.ds(c * quarter, quarter)]
        return (
            local(7 + i, values.at[x], here),
            near(4 * i, values.at[x], here, to_c),
            near(4 * i + 1, values.at[1 - x], here, to_x),
            near(4 * i + 2, there, there, to_c),
        )

    output_moves = to_owners(0, output_ref, output_out)
    for copy in output_moves[:3]:
        copy.start()

    lanes_of = lax.broadcasted_iota(jnp.int32, (length, 128), 1)
    rows_of = lax.broadcasted_iota(jnp.int32, (length, 128), 0)
    valid = lengths_ref[x, 0]
    blocked = jnp.where(rows_of // BLOCK == lanes_of, 1.0, 0.0)
    kaux[...] = jnp.where((lanes_of == blocks) & (rows_of >= valid), -1e30, blocked).astype(low)
    far[...] = jnp.zeros_like(far)
    for copy in loads:
        copy.wait()

    per_pair = length // 256
    units = pairs * per_pair
    acts = scatter.take(ATTENTION_ACTS)

    def unit_step(unit, carry):
        pair = unit // per_pair
        step = unit % per_pair
        rows = pl.ds(pl.multiple_of(step * 256, 256), 256)

        @pl.when(step == 0)
        def _():
            dk_acc[...] = jnp.zeros_like(dk_acc)
            dv_acc[...] = jnp.zeros_like(dv_acc)

        queries = qkv[pair, rows, :]
        grad = do[pair, rows, :]
        key_pair = qkv[pairs + pair]
        keys = jnp.concatenate([key_pair, kaux[...]], axis=1)
        values = qkv[2 * pairs + pair]
        dq = None
        for head in range(2):
            between(acts, units, ACT_FIRST, unit, head)
            here = lane_head(256, 128, head)
            aux = query_aux(table_ref[2 * pair + head], step, blocks)
            q_masked = jnp.where(here, queries, jnp.zeros_like(queries))
            do_masked = jnp.where(here, grad, jnp.zeros_like(grad))
            scores[...] = lax.dot_general(
                keys, jnp.concatenate([q_masked, aux], axis=1), LAST, preferred_element_type=f32
            )
            for sub in range(2):
                start = pl.multiple_of(band_start(step * 2 + sub, blocks) * BLOCK, BLOCK)
                scores[pl.ds(start, BAND * BLOCK), sub * BLOCK : (sub + 1) * BLOCK] += bias[
                    2 * pair + head, 2 * step + sub
                ].astype(f32)
            soft = jnp.exp(scores[...] - lse_ref[pair, step, head : head + 1, :])
            dv_acc[...] += jnp.dot(soft.astype(low), do_masked, preferred_element_type=f32)
            grad_probs = lax.dot_general(values, do_masked, LAST, preferred_element_type=f32)
            weighted = jnp.sum(soft * grad_probs, axis=0, keepdims=True)
            grad_scores = (soft * (grad_probs - weighted)).astype(low)
            grads[...] = grad_scores
            dk_acc[...] += jnp.dot(grad_scores, q_masked, preferred_element_type=f32)
            k_masked = jnp.where(lane_head(length, 128, head), key_pair, jnp.zeros_like(key_pair))
            part = lax.dot_general(grad_scores, k_masked, FIRST, preferred_element_type=f32)
            dq = part if dq is None else dq + part
            sums = jnp.concatenate(
                [
                    jnp.sum(grad_scores[block * BLOCK : (block + 1) * BLOCK, :].astype(f32), axis=0, keepdims=True)
                    for block in range(blocks)
                ],
                axis=0,
            )
            block_of = lax.broadcasted_iota(jnp.int32, (blocks, BLOCK), 0)
            for sub in range(2):
                start = band_start(step * 2 + sub, blocks)
                at = pl.multiple_of(start * BLOCK, BLOCK)
                bias[2 * pair + head, 2 * step + sub] = grads[pl.ds(at, BAND * BLOCK), sub * BLOCK : (sub + 1) * BLOCK]
                part = sums[:, sub * BLOCK : (sub + 1) * BLOCK]
                far[0, 2 * pair + head] += jnp.where(block_of < start, part, 0.0)
                far[1, 2 * pair + head] += jnp.where(block_of >= start + BAND, part, 0.0)
        qkv[pair, rows, :] = dq.astype(low)

        @pl.when(step == per_pair - 1)
        def _():
            qkv[pairs + pair] = dk_acc[...].astype(low)
            qkv[2 * pairs + pair] = dv_acc[...].astype(low)
            right = jnp.concatenate([qkv[t * pairs + pair] for t in range(3)], axis=1)

            def weight_step(i, carry):
                rows = pl.ds(pl.multiple_of(i * 256, 256), 256)
                got = jnp.dot(normed_t[rows, :], right, preferred_element_type=f32).astype(low)
                span = deep // (width // 256)
                wgrad[pair, pl.ds(i * span, span)] = got.reshape((span,) + wgrad.shape[2:5] + (3 * 128,))
                return carry

            lax.fori_loop(0, width // 256, weight_step, 0)

        for late, piece in enumerate(pieces):
            if piece[0]:
                @pl.when(unit == piece[0] * per_pair - 1)
                def _(late=late):
                    scatter.begin(late)

        return carry

    lax.fori_loop(0, units, unit_step, 0)
    for copy in output_moves[:3]:
        copy.wait()
    output_moves[3].start()
    def part_rows(part, core):
        return pl.ds(pl.multiple_of(part * half + core * quarter, quarter), quarter)

    def grad_one(rows):
        left = jnp.concatenate([qkv[k, rows, :] for k in range(3 * pairs)], axis=1)
        return lax.dot_general(left, wqkv[...].reshape(width, 3 * inner), LAST, preferred_element_type=f32)

    swaps = [near(8 + part, away.at[part], arrived.at[part], to_c) for part in range(2)]

    def away_step(part, carry):
        away[part] = grad_one(part_rows(part, 1 - c)).astype(low)
        return carry

    def mine_step(part, carry):
        mine_sum[part] = grad_one(part_rows(part, c))
        return carry

    lax.fori_loop(0, 2, away_step, 0)
    for copy in swaps:
        copy.start()
    scatter.run(1)
    lax.fori_loop(0, 2, mine_step, 0)
    scatter.run(1)
    gains = jnp.transpose(gain_buf[...].reshape(width, 128).astype(f32))
    gain_one = gains[0:1, :]
    gain_sum = jnp.zeros((1, width), f32)
    for part in range(2):
        swaps[part].wait()
        total = mine_sum[part] + arrived[part].astype(f32)
        present = tokens_ref[part].astype(f32)
        inverse = lax.rsqrt(jnp.mean(present * present, axis=-1, keepdims=True) + EPSILON)
        unit = present * inverse
        gain_sum = gain_sum + jnp.sum(total * unit, axis=0, keepdims=True)
        scaled = total * gain_one
        back = inverse * (scaled - unit * jnp.mean(scaled * unit, axis=-1, keepdims=True))
        result[part] = (middle_ref[part] + back).astype(low)
        scatter.run(1)
    input_moves = to_owners(1, result, input_out)
    for copy in input_moves[:3]:
        copy.start()
    table_acc[...] = jnp.zeros_like(table_acc)
    groups = BAND * BLOCK // GROUP
    table_units = blocks // 2 * groups // TURNS
    table_acts = scatter.take(TABLE_ACTS)

    def table_step(i, carry):
        for k, act in enumerate(table_acts):
            @pl.when(i == (k * table_units) // max(1, len(table_acts)))
            def _(act=act):
                act()
        total = None
        for turn in range(TURNS):
            group = i * TURNS + turn
            block = 2 * (group // groups)
            start = pl.multiple_of((group % groups) * GROUP, GROUP)
            for two in range(2):
                lanes = slice(two * BLOCK, (two + 1) * BLOCK)
                index = bandt[block + two, pl.ds(start, GROUP), :]
                for head in range(heads):
                    found[turn, head * GROUP : (head + 1) * GROUP, lanes] = bias[head, block + two, pl.ds(start, GROUP), :]
                for b in range(buckets):
                    hot[turn, b * GROUP : (b + 1) * GROUP, lanes] = jnp.where(
                        index == jnp.asarray(b, low), jnp.asarray(1, low), jnp.asarray(0, low)
                    )
            part = lax.dot_general(hot[turn], found[turn], LAST, preferred_element_type=f32)
            total = part if total is None else total + part
        table_acc[...] += total
        return carry

    lax.fori_loop(0, table_units, table_step, 0)
    row = lax.broadcasted_iota(jnp.int32, table_acc.shape, 0) % GROUP
    col = lax.broadcasted_iota(jnp.int32, table_acc.shape, 1) % GROUP
    kept = jnp.where(row == col, table_acc[...], 0.0).reshape(buckets, GROUP, heads * GROUP).sum(axis=1)
    bucket = lax.broadcasted_iota(jnp.int32, (buckets, 128), 0)
    head_of = lax.broadcasted_iota(jnp.int32, (buckets, 128), 1)
    table = jnp.zeros((buckets, 128), f32)
    for head in range(heads):
        amount = jnp.sum(kept[:, head * GROUP : (head + 1) * GROUP], axis=1, keepdims=True)
        table = table + jnp.where(head_of == head, amount, 0.0)
    for side, name in enumerate((buckets // 2 - 1, buckets - 1)):
        for head in range(heads):
            amount = jnp.sum(jnp.sum(far[side, head], axis=0, keepdims=True), axis=1, keepdims=True)
            table = table + jnp.where((bucket == name) & (head_of == head), amount, 0.0)

    lines = width // 128
    for i in range(lines):
        small[i : i + 1, :] = gain_sum[:, i * 128 : (i + 1) * 128]
    gain_two_sum = jnp.sum(gain_two_ref[0] + gain_two_ref[1], axis=0, keepdims=True)
    for i in range(lines):
        small[lines + i : lines + i + 1, :] = gain_two_sum[:, i * 128 : (i + 1) * 128]
    small[2 * lines : 2 * lines + buckets, :] = table
    small_base = 10

    def small_line(d):
        return near(small_base + 2 + d, hold_z.at[z], hold_z.at[z], place.device(z=place.line(d)))

    move = near(small_base, small, small_x, to_x)
    move.start()
    scatter.run(1)
    move.wait()
    hold_x[...] = small[...] + small_x[...]
    move = near(small_base + 1, hold_x, small_y, to_y)
    move.start()
    scatter.run(1)
    move.wait()
    hold_z[z] = hold_x[...] + small_y[...]
    for d in range(1, deep):
        small_line(d).start()
    scatter.run(1)
    for d in range(1, deep):
        small_line(d).wait()
    hold_y[...] = jnp.sum(hold_z[...], axis=0)
    move = near(small_base + 2, hold_y, small_c, to_c)
    move.start()
    scatter.run(1)
    move.wait()
    small_out[0] = hold_y[...]
    small_out[1] = hold_y[...] + small_c[...]

    for copy in input_moves[:3]:
        copy.wait()
    input_moves[3].start()
    input_moves[3].wait()
    output_moves[3].wait()
    scatter.run(len(scatter.queue))
    scatter.sent()


def back(shard_size, pieces, buckets, lengths, full, normed_t, qkv, bandt, biast, grads, do, lse, output, middle, tokens, gain_two, table_rows, came):
    low, f32 = jnp.bfloat16, jnp.float32
    deep = shard_size // 2
    rows = full.shape[3]
    width, length = normed_t.shape
    half, quarter = length // 2, length // 4
    heads, blocks = biast.shape[:2]
    pairs = heads // 2
    inner = pairs * 128
    hidden = (grads.shape[4] - inner) // 3
    count = len(pieces)
    shape = jax.ShapeDtypeStruct
    vmem, hbm = pl.BlockSpec(memory_space=pltpu.VMEM), pl.BlockSpec(memory_space=pl.ANY)
    dma = pltpu.SemaphoreType.DMA
    lines = 2 * (width // 128) + buckets
    buffers = [piece_buffers(piece, deep, rows) for piece in pieces]
    scratch = [pltpu.VMEM(buffer[k], low) for k in range(4) for buffer in buffers]
    small = pltpu.VMEM((lines, 128), f32)
    scratch += [
        pltpu.VMEM((3 * pairs, length, 128), low),
        pltpu.VMEM((width, length), low),
        pltpu.VMEM((blocks, BAND * BLOCK, BLOCK), low),
        pltpu.VMEM((heads, blocks, BAND * BLOCK, BLOCK), low),
        pltpu.VMEM((deep, 2, 2, rows, 3 * inner), low),
        pltpu.VMEM((deep, 2, 2, rows, 128), low),
        pltpu.VMEM((pairs, length, 128), low),
        pltpu.VMEM((length, 256), f32),
        pltpu.VMEM((length, 256), low),
        pltpu.VMEM((2, heads, blocks, BLOCK), f32),
        pltpu.VMEM((length, 128), f32),
        pltpu.VMEM((length, 128), f32),
        pltpu.VMEM((length, 128), low),
        pltpu.VMEM((pairs, deep, 2, 2, rows, 3 * 128), low),
        pltpu.VMEM((2, quarter, width), f32),
        pltpu.VMEM((2, quarter, width), low),
        pltpu.VMEM((2, quarter, width), low),
        pltpu.VMEM((2, quarter, width), low),
        pltpu.VMEM((buckets * GROUP, heads * GROUP), f32),
        pltpu.VMEM((TURNS, buckets * GROUP, 2 * BLOCK), low),
        pltpu.VMEM((TURNS, heads * GROUP, 2 * BLOCK), low),
        small, small, small, small, small, pltpu.VMEM((deep, lines, 128), f32), small,
        dma((count,)),
        dma((count, 3, deep - 1)),
        dma((count, 3, deep - 1)),
        dma((12 + deep,)),
        dma((12 + deep,)),
        dma((9,)),
    ]
    return pl.pallas_call(
        functools.partial(back_kernel, shard_size, pieces, (inner, hidden, buckets), len(came)),
        out_shape=[
            *[shape((rows, n), f32) for n in (inner,) * 4 + (hidden,) * 3],
            shape((2, half, width), low),
            shape((2, half, width), low),
            shape((2, lines, 128), f32),
        ],
        in_specs=[pl.BlockSpec(memory_space=pltpu.SMEM)] + [hbm] * 7 + [vmem] * 6 + [hbm] * len(came),
        out_specs=[vmem] * 7 + [hbm, hbm, vmem],
        scratch_shapes=scratch,
        compiler_params=pltpu.CompilerParams(
            collective_id=2, has_side_effects=True, vmem_limit_bytes=60 * MIB
        ),
        name="back",
    )(lengths, full, normed_t, qkv, bandt, biast, grads, do, lse, output, middle, tokens, gain_two, table_rows, *came)


def finish_kernel(*refs):
    count = len(refs) // 2
    for source, target in zip(refs[:count], refs[count:]):
        target[...] = source[...].astype(target.dtype)


def finish(weight_sums, output, input_grad):
    steps = 4 if weight_sums[0].shape[0] % 32 == 0 else 2
    values = [*weight_sums, output, input_grad]
    kinds = [jnp.float32] * len(weight_sums) + [output.dtype, jnp.float32]
    specs = [pl.BlockSpec((w.shape[0] // steps, w.shape[1]), lambda i: (i, 0)) for w in weight_sums]
    specs += [pl.BlockSpec((2, v.shape[1] // steps, v.shape[2]), lambda i: (0, i, 0)) for v in (output, input_grad)]
    return pl.pallas_call(
        finish_kernel,
        grid=(steps,),
        in_specs=specs,
        out_specs=specs,
        out_shape=[jax.ShapeDtypeStruct(v.shape, kind) for v, kind in zip(values, kinds)],
        compiler_params=pltpu.CompilerParams(vmem_limit_bytes=60 * MIB),
        name="finish",
    )(*values)


ORDERS = ("xyz", "zxy", "zyx", "zxy", "zxy", "zyx", "zxy", "zyx", "zxy")
SUM_ORDERS = ("yxz", "xyz")
GIVEN = 6
LATE_FIRST = 6
LATE_STEP = 3
ROW_ACTS = 2
WINDOW = 4
AHEAD = 2
LAG = 4
QUICK = 4
SUM_WINDOW = 3
SUM_LAGS = (2, 4)
FORWARD_ACTS = 9
ATTENTION_ACTS = 28
ACT_FIRST = 2
TABLE_ACTS = 14


def front_pieces(inner, hidden):
    at_project = 128 + 3 * inner
    at_hidden = at_project + inner
    pieces = split_columns(0, at_project, 4) + split_columns(at_project, at_hidden, 2)
    for j, n in enumerate(hidden_steps(hidden)):
        at = at_hidden + 3 * HIDDEN_STEP * j
        pieces += split_columns(at, at + 3 * n, 2)
    return [(a, b, ORDERS[i % len(ORDERS)]) for i, (a, b) in enumerate(pieces)]


def back_pieces(inner, hidden):
    where = []
    for j, n in enumerate(hidden_steps(hidden)):
        for k in range(3):
            where.append((3 * HIDDEN_STEP * j + k * n, n, 4 + k, HIDDEN_STEP * j))
    where.append((3 * hidden, inner, 3, 0))
    cuts = []
    for j, n in enumerate(hidden_steps(hidden)):
        at = 3 * HIDDEN_STEP * j
        cuts += split_columns(at, at + 3 * n, 2 if n > 128 else 1)
    cuts += split_columns(3 * hidden, 3 * hidden + inner, 2)
    pieces = []
    for a, b in cuts:
        segments = []
        for start, n, out, column in where:
            low, high = max(a, start), min(b, start + n)
            if low < high:
                segments.append((out, column + low - start, low - a, high - low))
        pieces.append((0, a, b, segments))
    for pair in range(inner // 128):
        piece = (1 + pair, 0, 3 * 128, [(t, pair * 128, t * 128, 128) for t in range(3)])
        pieces.insert(min(len(pieces), LATE_FIRST + LATE_STEP * pair), piece)
    return [(t, a, b, SUM_ORDERS[i % len(SUM_ORDERS)], segments) for i, (t, a, b, segments) in enumerate(pieces)]


def shards(
    inputs, cotangent, lengths, buckets,
    query_weight, key_weight, value_weight, projection_weight, gate_weight, up_weight, down_weight,
    attention_gain, feedforward_gain, bias_table,
):
    x = lax.axis_index("ctx")
    shard_size = lax.axis_size("shard")
    width = inputs.shape[2]
    bucket_count, heads = bias_table.shape
    rows, inner = query_weight.shape
    hidden = gate_weight.shape[1]
    cuts = back_pieces(inner, hidden)
    gains = jnp.pad(jnp.stack([attention_gain, feedforward_gain], axis=1), ((0, 0), (0, 126)))
    table_rows = jnp.broadcast_to(
        jnp.pad(bias_table.astype(jnp.float32).T, ((0, 0), (0, 128 - bucket_count)))[:, None, :], (heads, 8, 128)
    )
    weights = (query_weight, key_weight, value_weight, projection_weight, gate_weight, up_weight, down_weight)
    (
        full, normed_t, qkv, bandt, biast, grads, grad_attended, tokens,
        lse, output, grad_middle, gain_two, *came,
    ) = front(shard_size, front_pieces(inner, hidden), WINDOW, [(a, b, order[0]) for _, a, b, order, _ in cuts[:GIVEN]], lengths, gains, weights, inputs, cotangent, buckets, table_rows)

    *weight_sums, output, input_grad, small = back(
        shard_size, cuts, bucket_count,
        lengths, full, normed_t, qkv, bandt, biast, grads, grad_attended,
        lse, output, grad_middle, tokens, gain_two, table_rows, came,
    )
    *weight_sums, output, input_grad = finish(weight_sums, output, input_grad)
    lines = width // 128
    me = lax.axis_index("shard") * 2 + x

    def own_gain(part):
        return lax.dynamic_slice_in_dim(small[1, part * lines : (part + 1) * lines].reshape(-1), me * rows, rows)

    return (
        output, input_grad,
        *weight_sums, own_gain(0), own_gain(1), small[0, 2 * lines :, :heads],
    )


def solution(mesh):
    rows = P(None, ("shard", "ctx"), None)
    weight = P(("shard", "ctx"), "tp")
    gain = P(("shard", "ctx"))
    table = P(None, "tp")
    return jax.shard_map(
        shards,
        mesh=mesh,
        in_specs=(rows, rows, P(None, "shard"), P("ctx", None)) + (weight,) * 7 + (gain, gain, table),
        out_specs=(rows, rows) + (weight,) * 7 + (gain, gain, table),
        check_vma=False,
    )
```

```python
import functools

import jax
import jax.numpy as jnp
from jax import lax
from jax.experimental import pallas as pl
from jax.experimental.pallas import tpu as pltpu
from jax.sharding import PartitionSpec as P

EPSILON = 1e-06
GELU_ROOT = 0.7978845608028654
GELU_CUBIC = 0.044715
MESH = pl.DeviceIdType.MESH
MIB = 1024 * 1024


BAND = 3
BLOCK = 128


def lane_head(rows, width, which):
    lanes = lax.broadcasted_iota(jnp.int32, (rows, width), 1)
    half = width // 2
    return (lanes < half) if which == 0 else (lanes >= half)


def band_start(row_block, blocks):
    return jnp.clip(row_block - 1, 0, blocks - BAND)


def split_columns(start, stop, pieces):
    tiles = (stop - start) // 128
    edges = [start + 128 * (tiles * i // pieces) for i in range(pieces + 1)]
    return [(a, b) for a, b in zip(edges, edges[1:]) if b > a]


class Place:
    def __init__(self, shard_size):
        self.deep = shard_size // 2
        shard = lax.axis_index("shard")
        self.z = shard // 2
        self.y = shard % 2
        self.x = lax.axis_index("ctx")
        self.c = lax.axis_index("tp")

    def device(self, z=None, y=None, x=None, c=None):
        z = self.z if z is None else z
        y = self.y if y is None else y
        x = self.x if x is None else x
        c = self.c if c is None else c
        return (z * 2 + y, x, c)

    def line(self, distance):
        return (self.z + distance) % self.deep

    def peers(self):
        others = [self.device(z=self.line(d)) for d in range(1, self.deep)]
        return others + [self.device(y=1 - self.y), self.device(x=1 - self.x), self.device(c=1 - self.c)]


def meet(place):
    barrier = pltpu.get_barrier_semaphore()
    peers = place.peers()
    for peer in peers:
        pl.semaphore_signal(barrier, inc=1, device_id=peer, device_id_type=MESH)
    pl.semaphore_wait(barrier, len(peers))


def send(source, target, send_sem, recv_sem, device):
    return pltpu.make_async_remote_copy(
        src_ref=source, dst_ref=target, send_sem=send_sem, recv_sem=recv_sem, device_id=device, device_id_type=MESH
    )


LAST = (((1,), (1,)), ((), ()))
FIRST = (((0,), (0,)), ((), ()))
HIDDEN_STEP = 256
HALF_BUCKETS = 16


def hidden_steps(hidden):
    return [min(HIDDEN_STEP, hidden - at) for at in range(0, hidden, HIDDEN_STEP)]


class Gather:
    def __init__(self, place, pieces, own_ref, full_ref, send_sem, recv_sem):
        self.place, self.pieces, self.own, self.full = place, pieces, own_ref, full_ref
        self.send_sem, self.recv_sem = send_sem, recv_sem
        self.queue = []

    def held(self, piece, hop):
        a, b, order = self.pieces[piece]
        place, done = self.place, order[:hop]
        at = [slice(None) if name in done else getattr(place, name) for name in "zyx"]
        return self.full.at[at[0], at[1], at[2], :, a:b]

    def copies(self, piece, hop):
        place = self.place
        a, b, order = self.pieces[piece]
        target = self.held(piece, hop)
        source = self.own.at[:, a:b] if hop == 0 else target
        name = order[hop]
        if name == "z":
            peers = [place.device(z=place.line(d)) for d in range(1, place.deep)]
        elif name == "y":
            peers = [place.device(y=1 - place.y)]
        else:
            peers = [place.device(x=1 - place.x)]
        return [
            send(source, target, self.send_sem.at[piece, hop, i], self.recv_sem.at[piece, hop, i], peer)
            for i, peer in enumerate(peers)
        ]

    def start(self, piece, hop):
        for copy in self.copies(piece, hop):
            copy.start()

    def arrive(self, piece, hop):
        for copy in self.copies(piece, hop):
            copy.wait_recv()

    def sent(self):
        for piece in range(len(self.pieces)):
            for hop in range(3):
                for copy in self.copies(piece, hop):
                    copy.wait_send()

    def plan(self, window):
        count = len(self.pieces)
        self.window = window

        def second(piece):
            def act():
                self.arrive(piece, 0)
                self.start(piece, 1)
                if piece + window < count:
                    self.start(piece + window, 0)
            return act

        def third(piece):
            def act():
                self.arrive(piece, 1)
                self.start(piece, 2)
            return act

        turned = 0
        for piece in range(count + LAG):
            if piece < count:
                self.queue.append((None, second(piece)))
            while turned < count and turned <= piece - (1 if turned < QUICK else LAG):
                self.queue.append((turned, third(turned)))
                turned += 1
        for piece in range(min(window, count)):
            self.start(piece, 0)

    def run(self, steps):
        for _ in range(min(steps, len(self.queue))):
            self.queue.pop(0)[1]()

    def take(self, steps):
        taken, self.queue = self.queue[:steps], self.queue[steps:]
        return [act for _, act in taken]

    def need(self, pieces):
        for piece in pieces:
            while any(mark == piece for mark, _ in self.queue):
                self.run(1)
        self.run(AHEAD)
        for piece in pieces:
            self.arrive(piece, 2)


def query_aux(table, step, blocks):
    parts = []
    lanes = lax.broadcasted_iota(jnp.int32, (BLOCK, 128), 1)
    buckets = 2 * HALF_BUCKETS
    below = jnp.broadcast_to(table[0:1, HALF_BUCKETS - 1 : HALF_BUCKETS], (BLOCK, 128))
    above = jnp.broadcast_to(table[0:1, buckets - 1 : buckets], (BLOCK, 128))
    for sub in range(2):
        start = band_start(2 * step + sub, blocks)
        value = jnp.where(lanes < start, below, 0.0)
        value = jnp.where((lanes >= start + BAND) & (lanes < blocks), above, value)
        parts.append(jnp.where(lanes == blocks, 1.0, value))
    return jnp.concatenate(parts, axis=0).astype(jnp.bfloat16)


def between(acts, units, skip, unit, head):
    slots = 2 * units - skip
    for k, act in enumerate(acts):
        slot = skip + (k * slots) // len(acts)
        if slot % 2 == head:
            pl.when(unit == slot // 2)(act)


def gelu_all(gate):
    square = gate * gate
    tangent = jnp.tanh(GELU_ROOT * (gate + GELU_CUBIC * square * gate))
    value = 0.5 * gate * (1.0 + tangent)
    slope = 0.5 * (1.0 + tangent) + 0.5 * gate * (1.0 - tangent * tangent) * (
        GELU_ROOT + (3.0 * GELU_CUBIC * GELU_ROOT) * square
    )
    return value, slope


def front_kernel(
    shard_size, pieces, window, sizes, given,
    lengths_ref, gains_ref, query_ref, key_ref, value_ref, project_ref, gate_ref, up_ref, down_ref,
    inputs_ref, cots_ref, buckets_ref, table_ref,
    full_ref, normed_out, qkv_out, bandt_out, biast_out, grads_out, attended_out, tokens_own_ref,
    lse_ref, output_ref, middle_grad_ref, gain_ref, *rest,
):
    came_outs, rest = rest[: len(given)], rest[len(given) :]
    (
    own_ref, tok, cot, band_raw, band, bandt, bias, biast, kaux, gain_buf, qkv, normed, scores, attended, project_w,
    normal, away, arrived, two_t, low_t, acc_out, acc_two, w_buf, g_buf, hid, ggate, gup,
    send_sem, recv_sem, near_send, near_recv, local_sem, w_sem, g_sem, own_sem, bt_sem, early_send, early_recv,
    ) = rest
    inner, hidden = sizes
    length, width = tok.shape
    half, quarter = length // 2, length // 4
    heads, blocks = bias.shape[:2]
    pairs = heads // 2
    deep = shard_size // 2
    low = jnp.bfloat16
    place = Place(shard_size)
    x, c = place.x, place.c
    at_q = 128
    at_project = at_q + 3 * inner
    at_hidden = at_project + inner
    steps = hidden_steps(hidden)
    per_step = 2
    first_hidden_piece = len(pieces) - per_step * len(steps)
    project_pieces = [i for i, (a, b, _) in enumerate(pieces) if at_project <= a < at_hidden]
    qkv_pieces = [i for i, (a, b, _) in enumerate(pieces) if a < at_project]

    def own_load(i, source, target):
        return pltpu.make_async_copy(source, target, local_sem.at[i])

    parts, at = [], 0
    for ref in (gains_ref, query_ref, key_ref, value_ref, project_ref):
        parts.append((ref, at))
        at += ref.shape[1]
    own_loads = [
        pltpu.make_async_copy(ref, own_ref.at[:, at : at + ref.shape[1]], own_sem.at[i]) for i, (ref, at) in enumerate(parts)
    ]
    for j, n in enumerate(steps):
        for k, ref in enumerate((gate_ref, up_ref, down_ref)):
            at = at_hidden + 3 * HIDDEN_STEP * j + k * n
            own_loads.append(
                pltpu.make_async_copy(
                    ref.at[:, HIDDEN_STEP * j : HIDDEN_STEP * j + n], own_ref.at[:, at : at + n], own_sem.at[len(own_loads)]
                )
            )

    def band_source(block):
        start = pl.multiple_of(band_start(block, blocks) * BLOCK, BLOCK)
        first = block - x * (blocks // 2)
        return buckets_ref.at[pl.ds(pl.multiple_of(first * BLOCK, BLOCK), BLOCK), pl.ds(start, BAND * BLOCK)]

    own_tok = own_load(0, inputs_ref.at[x], tok.at[pl.ds(x * half, half)])
    own_cot = own_load(1, cots_ref.at[x], cot.at[pl.ds(x * half, half)])
    own_bands = [
        own_load(13 + i, band_source(x * (blocks // 2) + i), band_raw.at[i]) for i in range(blocks // 2)
    ]
    own_full = own_load(3, own_ref, full_ref.at[place.z, place.y, x])
    for copy in (*own_loads, *own_bands, own_tok, own_cot):
        copy.start()
    meet(place)
    for copy in own_loads[:4]:
        copy.wait()

    gather = Gather(place, pieces, own_ref, full_ref, send_sem, recv_sem)
    to_x, to_c = place.device(x=1 - x), place.device(c=1 - c)

    def x_rows(sender_x, sender_c):
        return pl.ds(sender_x * half + sender_c * quarter, quarter)

    def near(i, source, target, device):
        return send(source, target, near_send.at[i], near_recv.at[i], device)

    mine = [x * (blocks // 2) + c * (blocks // 4) + i for i in range(blocks // 4)]
    theirs = [(1 - x) * (blocks // 2) + c * (blocks // 4) + i for i in range(blocks // 4)]
    band_x = [near(16 + i, band.at[block], band.at[block], to_x) for i, block in enumerate(mine)]
    tok_x = near(1, inputs_ref.at[1 - x, pl.ds(c * quarter, quarter)], tok.at[x_rows(x, c)], to_x)
    cot_x = near(2, cots_ref.at[1 - x, pl.ds(c * quarter, quarter)], cot.at[x_rows(x, c)], to_x)
    band_c = [near(16 + len(mine) + i, band.at[block], band.at[block], to_c) for i, block in enumerate(theirs)]
    tok_c = near(4, tok.at[x_rows(1 - x, c)], tok.at[x_rows(1 - x, c)], to_c)
    cot_c = near(5, cot.at[x_rows(1 - x, c)], cot.at[x_rows(1 - x, c)], to_c)
    gather.plan(min(window, len(qkv_pieces)))
    for copy in own_loads[4:]:
        copy.wait()
    own_full.start()
    for copy in own_bands:
        copy.wait()
    for i in range(blocks // 2):
        band[x * (blocks // 2) + i] = band_raw[i].astype(jnp.float32).astype(low)
    for copy in band_x:
        copy.start()
    tok_x.start()
    own_full.wait()
    lanes_of = lax.broadcasted_iota(jnp.int32, (length, 128), 1)
    rows_of = lax.broadcasted_iota(jnp.int32, (length, 128), 0)
    valid = lengths_ref[x, 0]
    blocked = jnp.where(rows_of // BLOCK == lanes_of, 1.0, 0.0)
    kaux[...] = jnp.where((lanes_of == blocks) & (rows_of >= valid), -1e30, blocked).astype(low)
    gather.run(1)
    for copy in band_x:
        copy.wait()
    for copy in band_c:
        copy.start()
    gather.run(1)
    for copy in band_c:
        copy.wait()

    def bias_step(i, carry):
        block = i // (BLOCK // 16)
        at = pl.multiple_of((i % (BLOCK // 16)) * 16, 16)
        index = band[block, pl.ds(at, 16), :].astype(jnp.float32).astype(jnp.int32)
        for col in range(BAND):
            lanes = slice(col * BLOCK, (col + 1) * BLOCK)
            for head in range(heads):
                table = table_ref[head]
                got = [jnp.take_along_axis(table, index[8 * k : 8 * k + 8, lanes], axis=1) for k in range(2)]
                bias[head, block, pl.ds(at, 16), lanes] = jnp.concatenate(got, axis=0).astype(low)
        return carry

    bias_steps = blocks * (BLOCK // 16)
    for k in range(4):
        lax.fori_loop(bias_steps * k // 4, bias_steps * (k + 1) // 4, bias_step, 0)
        gather.run(1)
    tok_x.wait()
    tok_c.start()
    cot_x.start()

    def biast_store(block, slot):
        return pltpu.make_async_copy(biast.at[slot], biast_out.at[:, block], bt_sem.at[slot])

    def biast_block(block, carry):
        slot = block % 2

        @pl.when(block > 1)
        def _():
            biast_store(block - 2, slot).wait()

        bandt[block] = jnp.transpose(band[block].astype(jnp.float32)).astype(low)

        def inner_step(i, carry):
            at = pl.multiple_of(i * 16, 16)
            index = bandt[block, pl.ds(at, 16), :].astype(jnp.float32).astype(jnp.int32)
            for head in range(heads):
                got = [jnp.take_along_axis(table_ref[head], index[8 * k : 8 * k + 8], axis=1) for k in range(2)]
                biast[slot, head, pl.ds(at, 16), :] = jnp.concatenate(got, axis=0).astype(low)
            return carry

        lax.fori_loop(0, BAND * BLOCK // 16, inner_step, 0)
        biast_store(block, slot).start()
        return carry

    for k in range(4):
        lax.fori_loop(blocks * k // 4, blocks * (k + 1) // 4, biast_block, 0)
        gather.run(1)
    biast_store(blocks - 2, 0).wait()
    biast_store(blocks - 1, 1).wait()
    bandt_store = own_load(4, bandt, bandt_out)
    bandt_store.start()
    own_tok.wait()
    tok_c.wait()

    def live_step(i, carry):
        rows = pl.ds(pl.multiple_of(i * BLOCK, BLOCK), BLOCK)
        here = lax.broadcasted_iota(jnp.int32, (BLOCK, width), 0) + i * BLOCK < valid
        masked = jnp.where(here, cot[rows, :].astype(jnp.float32), 0.0).astype(low)
        cot[rows, :] = masked
        low_t[:, rows] = jnp.transpose(masked)
        return carry

    gather.need(qkv_pieces)
    load_gains = own_load(5, full_ref.at[:, :, :, :, 0:at_q], gain_buf)
    third = 3 * inner // 2
    loads_wide = [
        pltpu.make_async_copy(
            full_ref.at[:, :, :, :, at_q + third * k : at_q + third * (k + 1)], w_buf.at[k, :, :, :, :, 0:third], w_sem.at[k]
        )
        for k in range(2)
    ]
    for copy in (load_gains, *loads_wide):
        copy.start()
    load_gains.wait()
    gains = jnp.transpose(gain_buf[...].reshape(width, 128).astype(jnp.float32))
    gain_one, gain_two = gains[0:1, :], gains[1:2, :]

    def norm_step(i, carry):
        rows = pl.ds(pl.multiple_of(i * BLOCK, BLOCK), BLOCK)
        present = tok[rows, :].astype(jnp.float32)
        inverse = lax.rsqrt(jnp.mean(present * present, axis=-1, keepdims=True) + EPSILON)
        got = (present * inverse * gain_one).astype(low)
        normed[rows, :] = got
        two_t[:, rows] = jnp.transpose(got)
        return carry

    lax.fori_loop(0, blocks, norm_step, 0)
    normed_store = own_load(6, two_t, normed_out)
    normed_store.start()
    for copy in loads_wide:
        copy.wait()
    gather.run(2)

    for col in range(3 * pairs // 2):
        slot, at = 256 * col // third, 256 * col % third
        lanes = slice(at, at + 256)

        def qkv_step(i, carry):
            rows = pl.ds(pl.multiple_of(i * 256, 256), 256)
            got = jnp.dot(
                normed[rows, :], w_buf[slot, :, :, :, :, lanes].reshape(width, 256), preferred_element_type=jnp.float32
            ).astype(low)
            qkv[2 * col, rows, :] = got[:, :128]
            qkv[2 * col + 1, rows, :] = got[:, 128:]
            return carry

        lax.fori_loop(0, length // 256, qkv_step, 0)
        if col % 2:
            gather.run(1)
    qkv_store = own_load(7, qkv, qkv_out)
    qkv_store.start()

    units = pairs * (length // 256)
    acts = gather.take(min(len(gather.queue), FORWARD_ACTS))

    def unit_step(unit, carry):
        pair = unit // (length // 256)
        step = unit % (length // 256)
        rows = pl.ds(pl.multiple_of(step * 256, 256), 256)
        queries = qkv[pair, rows, :]
        keys = jnp.concatenate([qkv[pairs + pair], kaux[...]], axis=1)
        outs = []
        for head in range(2):
            between(acts, units, 0, unit, head)
            aux = query_aux(table_ref[2 * pair + head], step, blocks)
            masked = jnp.where(lane_head(256, 128, head), queries, jnp.zeros_like(queries))
            scores[...] = lax.dot_general(
                jnp.concatenate([masked, aux], axis=1), keys, LAST, preferred_element_type=jnp.float32
            )
            for sub in range(2):
                start = pl.multiple_of(band_start(step * 2 + sub, blocks) * BLOCK, BLOCK)
                scores[sub * BLOCK : (sub + 1) * BLOCK, pl.ds(start, BAND * BLOCK)] += bias[
                    2 * pair + head, 2 * step + sub
                ].astype(jnp.float32)
            got = scores[...]
            highest = jnp.max(got, axis=1, keepdims=True)
            exponent = jnp.exp(got - highest)
            total = jnp.sum(exponent, axis=1, keepdims=True)
            outs.append(
                jnp.dot(exponent.astype(low), qkv[2 * pairs + pair], preferred_element_type=jnp.float32) * (1.0 / total)
            )
            lse = jnp.broadcast_to(highest + jnp.log(total), (256, 128))
            lse_ref[pair, step, head : head + 1, :] = jnp.transpose(lse)[0:1, :]
        attended[pair, rows, :] = jnp.where(lane_head(256, 128, 0), outs[0], outs[1]).astype(low)
        return carry

    lax.fori_loop(0, units, unit_step, 0)
    own_cot.wait()
    cot_x.wait()
    cot_c.start()

    normed_store.wait()
    two = normed
    gather.need(project_pieces)
    load_project = own_load(9, full_ref.at[:, :, :, :, at_project:at_hidden], project_w)
    load_project.start()
    load_project.wait()

    def branch(rows):
        left = jnp.concatenate([attended[pair, rows, :] for pair in range(pairs)], axis=1)
        return lax.dot_general(left, project_w[...].reshape(width, inner), LAST, preferred_element_type=jnp.float32)

    def part_rows(part, core):
        return pl.ds(pl.multiple_of(part * half + core * quarter, quarter), quarter)

    def swap_part(i, part, slot=0):
        return near(i + part, away.at[slot + part], arrived.at[slot + part], to_c)

    for part in range(2):
        away[part] = branch(part_rows(part, 1 - c)).astype(low)
        swap_part(6, part).start()
    for part in range(2):
        normal[part] = branch(part_rows(part, c)) + tok[part_rows(part, c), :].astype(jnp.float32)

    def share(i, part, buffer):
        return near(i + part, buffer.at[part_rows(part, c)], buffer.at[part_rows(part, c)], to_c)

    tokens_store = [own_load(11 + part, tok.at[part_rows(part, c)], tokens_own_ref.at[part]) for part in range(2)]
    for copy in tokens_store:
        copy.start()
    for part in range(2):
        swap_part(6, part).wait()
        middle = normal[part] + arrived[part].astype(jnp.float32)
        normal[part] = middle
        inverse = lax.rsqrt(jnp.mean(middle * middle, axis=-1, keepdims=True) + EPSILON)
        two[part_rows(part, c), :] = (middle * inverse * gain_two).astype(low)
        share(8, part, two).start()
    gather.run(1)
    for part in range(2):
        share(8, part, two).wait()

    def turn_step(i, carry):
        rows = pl.ds(pl.multiple_of(i * BLOCK, BLOCK), BLOCK)
        two_t[:, rows] = jnp.transpose(two[rows, :])
        return carry

    lax.fori_loop(0, blocks, turn_step, 0)
    gather.run(1)
    cot_c.wait()
    lax.fori_loop(0, blocks, live_step, 0)
    gather.run(1)

    def bounds(j):
        at = at_hidden + 3 * HIDDEN_STEP * j
        return at, at + 3 * steps[j]

    def load_step(j):
        a, b = bounds(j)
        return pltpu.make_async_copy(
            full_ref.at[:, :, :, :, a:b], w_buf.at[j % 2, :, :, :, :, 0 : b - a], w_sem.at[j % 2]
        )

    def store_step(j):
        a, b = bounds(j)
        return pltpu.make_async_copy(
            g_buf.at[j % 2, :, :, :, :, 0 : b - a],
            grads_out.at[:, :, :, :, a - at_hidden : b - at_hidden],
            g_sem.at[j % 2],
        )

    early_sums = []
    for k, (a, b, name) in enumerate(given):
        source = grads_out.at[:, :, 1 - x, :, a:b] if name == "x" else grads_out.at[:, 1 - place.y, :, :, a:b]
        device = to_x if name == "x" else place.device(y=1 - place.y)
        early_sums.append(send(source, came_outs[k], early_send.at[k], early_recv.at[k], device))
    gather.need(range(first_hidden_piece, first_hidden_piece + per_step))
    load_step(0).start()
    for j, units_here in enumerate(steps):
        n = units_here
        slot = j % 2
        load_step(j).wait()

        def weight(k, slot=slot, n=n):
            return w_buf[slot, :, :, :, :, k * n : (k + 1) * n].reshape(width, n)

        inside = gather.take(ROW_ACTS)

        def rows_step(i, carry, j=j, n=n, weight=weight, inside=inside):
            for k, act in enumerate(inside):
                pl.when(i == (2 * k + 1) * (length // 256) // (2 * len(inside)))(act)
            rows = pl.ds(pl.multiple_of(i * 256, 256), 256)
            left, grad = two[rows, :], cot[rows, :]
            gate = jnp.dot(left, weight(0), preferred_element_type=jnp.float32)
            up = jnp.dot(left, weight(1), preferred_element_type=jnp.float32)
            grad_hidden = jnp.dot(grad, weight(2), preferred_element_type=jnp.float32)
            value, slope = gelu_all(gate)
            hid[rows, 0:n] = (value * up).astype(low)
            ggate[rows, 0:n] = (grad_hidden * up * slope).astype(low)
            gup[rows, 0:n] = (grad_hidden * value).astype(low)
            out = lax.dot_general(hid[rows, 0:n], weight(2), LAST, preferred_element_type=jnp.float32)
            back = lax.dot_general(ggate[rows, 0:n], weight(0), LAST, preferred_element_type=jnp.float32)
            back = back + lax.dot_general(gup[rows, 0:n], weight(1), LAST, preferred_element_type=jnp.float32)
            if j == 0:
                acc_out[rows, :] = out
                acc_two[rows, :] = back
            else:
                acc_out[rows, :] += out
                acc_two[rows, :] += back
            return carry

        lax.fori_loop(0, length // 256, rows_step, 0)
        if j + 1 < len(steps):
            first = first_hidden_piece + per_step * (j + 1)
            gather.need(range(first, first + per_step))
            load_step(j + 1).start()
        if j > 1:
            store_step(j - 2).wait()
        if j + 2 >= len(steps):
            for copy, (_, b, _) in zip(early_sums, given):
                ready = max(0, -(-b // (3 * HIDDEN_STEP)) - 1)
                if ready == j - 2 or (ready < j - 2 and j + 2 == len(steps)):
                    copy.start()

        tiles = width // 256

        def grads_step(i, carry, slot=slot, n=n):
            rows = pl.ds(pl.multiple_of(i * 256, 256), 256)
            for k, (left, right) in enumerate(((two_t, ggate), (two_t, gup), (low_t, hid))):
                got = jnp.dot(left[rows, :], right[:, 0:n], preferred_element_type=jnp.float32).astype(low)
                span = deep // tiles
                g_buf[slot, pl.ds(i * span, span), :, :, :, k * n : (k + 1) * n] = got.reshape(
                    (span,) + g_buf.shape[2:5] + (n,)
                )
            return carry

        lax.fori_loop(0, tiles, grads_step, 0)
        store_step(j).start()
    gather.run(len(gather.queue))

    def share_sum(i, acc, slot):
        for part in range(2):
            away[slot + part] = acc[part_rows(part, 1 - c), :].astype(low)
            swap_part(i, part, slot).start()

    share_sum(10, acc_two, 0)
    for part in range(2):
        swap_part(10, part).wait()
        grad_two = acc_two[part_rows(part, c), :] + arrived[part].astype(jnp.float32)
        middle = normal[part]
        inverse = lax.rsqrt(jnp.mean(middle * middle, axis=-1, keepdims=True) + EPSILON)
        unit = middle * inverse
        weighted = jnp.sum((grad_two * unit).reshape(quarter // 8, 8, width), axis=0)
        gain_ref[part] = weighted
        scaled = grad_two * gain_two
        grad_middle = cot[part_rows(part, c), :].astype(jnp.float32) + inverse * (
            scaled - unit * jnp.mean(scaled * unit, axis=-1, keepdims=True)
        )
        middle_grad_ref[part] = grad_middle
        two[part_rows(part, c), :] = grad_middle.astype(low)
        share(12, part, two).start()
    share_sum(14, acc_out, 2)
    for part in range(2):
        swap_part(14, part, 2).wait()
        output_ref[part] = (normal[part] + acc_out[part_rows(part, c), :] + arrived[2 + part].astype(jnp.float32)).astype(low)
    for part in range(2):
        share(12, part, two).wait()
    for j in range(max(0, len(steps) - 2), len(steps)):
        store_step(j).wait()

    lax.fori_loop(0, blocks, turn_step, 0)

    def project_step(i, carry):
        rows = pl.ds(pl.multiple_of(i * 256, 256), 256)
        right = jnp.concatenate([attended[pair] for pair in range(pairs)], axis=1)
        got = jnp.dot(two_t[rows, :], right, preferred_element_type=jnp.float32).astype(low)
        span = deep // (width // 256)
        g_buf[0, pl.ds(i * span, span), :, :, :, 0:inner] = got.reshape((span,) + g_buf.shape[2:5] + (inner,))
        return carry

    lax.fori_loop(0, width // 256, project_step, 0)
    project_store = own_load(8, g_buf.at[0, :, :, :, :, 0:inner], grads_out.at[:, :, :, :, 3 * hidden : 3 * hidden + inner])
    project_store.start()

    def attended_step(i, carry):
        rows = pl.ds(pl.multiple_of(i * 256, 256), 256)
        got = jnp.dot(two[rows, :], project_w[...].reshape(width, inner), preferred_element_type=jnp.float32).astype(low)
        for pair in range(pairs):
            attended[pair, rows, :] = got[:, pair * 128 : (pair + 1) * 128]
        return carry

    lax.fori_loop(0, length // 256, attended_step, 0)
    attended_store = own_load(10, attended, attended_out)
    attended_store.start()
    for copy in (bandt_store, qkv_store, attended_store, project_store, *tokens_store, *early_sums):
        copy.wait()
    gather.sent()


def front(shard_size, pieces, window, given, lengths, gains, weights, inputs, cots, buckets, table_rows):
    low, f32 = jnp.bfloat16, jnp.float32
    deep = shard_size // 2
    rows, inner = weights[0].shape
    hidden = weights[4].shape[1]
    wide = pieces[-1][1]
    half, width = inputs.shape[1:]
    length, quarter = 2 * half, half // 2
    heads = table_rows.shape[0]
    blocks = length // BLOCK
    pairs = heads // 2
    shape = jax.ShapeDtypeStruct
    vmem, hbm = pl.BlockSpec(memory_space=pltpu.VMEM), pl.BlockSpec(memory_space=pl.ANY)
    dma = pltpu.SemaphoreType.DMA
    count = len(pieces)
    step = HIDDEN_STEP
    out_shape = [
        shape((deep, 2, 2, rows, wide), low),
        shape((width, length), low),
        shape((3 * pairs, length, 128), low),
        shape((blocks, BAND * BLOCK, BLOCK), low),
        shape((heads, blocks, BAND * BLOCK, BLOCK), low),
        shape((deep, 2, 2, rows, 3 * hidden + inner), low),
        shape((pairs, length, 128), low),
        shape((2, quarter, width), low),
        shape((pairs, length // 256, 2, 256), f32),
        shape((2, quarter, width), low),
        shape((2, quarter, width), f32),
        shape((2, 8, width), f32),
    ] + [shape((deep, 2, rows, b - a), low) for a, b, _ in given]
    scratch = [
        pltpu.VMEM((rows, wide), low),
        pltpu.VMEM((length, width), low),
        pltpu.VMEM((length, width), low),
        pltpu.VMEM((blocks // 2, BLOCK, BAND * BLOCK), jnp.int32),
        pltpu.VMEM((blocks, BLOCK, BAND * BLOCK), low),
        pltpu.VMEM((blocks, BAND * BLOCK, BLOCK), low),
        pltpu.VMEM((heads, blocks, BLOCK, BAND * BLOCK), low),
        pltpu.VMEM((2, heads, BAND * BLOCK, BLOCK), low),
        pltpu.VMEM((length, 128), low),
        pltpu.VMEM((deep, 2, 2, rows, 128), low),
        pltpu.VMEM((3 * pairs, length, 128), low),
        pltpu.VMEM((length, width), low),
        pltpu.VMEM((256, length), f32),
        pltpu.VMEM((pairs, length, 128), low),
        pltpu.VMEM((deep, 2, 2, rows, inner), low),
        pltpu.VMEM((2, quarter, width), f32),
        pltpu.VMEM((4, quarter, width), low),
        pltpu.VMEM((4, quarter, width), low),
        pltpu.VMEM((width, length), low),
        pltpu.VMEM((width, length), low),
        pltpu.VMEM((length, width), f32),
        pltpu.VMEM((length, width), f32),
        pltpu.VMEM((2, deep, 2, 2, rows, 3 * step), low),
        pltpu.VMEM((2, deep, 2, 2, rows, 3 * step), low),
        pltpu.VMEM((length, step), low),
        pltpu.VMEM((length, step), low),
        pltpu.VMEM((length, step), low),
        dma((count, 3, deep - 1)),
        dma((count, 3, deep - 1)),
        dma((16 + blocks // 2,)),
        dma((16 + blocks // 2,)),
        dma((13 + blocks // 2,)),
        dma((2,)),
        dma((2,)),
        dma((5 + 3 * len(hidden_steps(hidden)),)),
        dma((2,)),
        dma((len(given),)),
        dma((len(given),)),
    ]
    return pl.pallas_call(
        functools.partial(front_kernel, shard_size, pieces, window, (inner, hidden), given),
        out_shape=out_shape,
        in_specs=[pl.BlockSpec(memory_space=pltpu.SMEM)] + [hbm] * 11 + [vmem],
        out_specs=[hbm] * 8 + [vmem] * 4 + [hbm] * len(given),
        scratch_shapes=scratch,
        compiler_params=pltpu.CompilerParams(
            collective_id=1, has_side_effects=True, vmem_limit_bytes=60 * MIB
        ),
        name="front",
    )(lengths, gains, *weights, inputs, cots, buckets, table_rows)


GROUP = 16
TURNS = 4


class Scatter:
    def __init__(self, place, pieces, sources, outs, buffers, sems, came):
        self.came = came
        self.place, self.pieces, self.sources, self.outs = place, pieces, sources, outs
        self.first, self.own, self.second, self.third = buffers
        self.own_sem, self.send_sem, self.recv_sem = sems
        self.queue = []

    def peer(self, name):
        place = self.place
        return place.device(y=1 - place.y) if name == "y" else place.device(x=1 - place.x)

    def rest(self, piece):
        order = self.pieces[piece][3]
        return [name for name in "zyx" if name != order[0]]

    def cut(self, piece, name, value):
        t, a, b = self.pieces[piece][:3]
        at = [value if name == other else slice(None) for other in "zyx"]
        if t:
            return self.sources[1].at[t - 1, at[0], at[1], at[2]]
        return self.sources[0].at[at[0], at[1], at[2], :, a:b]

    def own_copy(self, piece):
        order = self.pieces[piece][3]
        return pltpu.make_async_copy(
            self.cut(piece, order[0], getattr(self.place, order[0])), self.own[piece], self.own_sem.at[piece]
        )

    def copies(self, piece, hop):
        place, order = self.place, self.pieces[piece][3]
        name, rest = order[hop], self.rest(piece)
        own, made = self.own[piece], []

        def at(**index):
            return tuple(index[n] if n in index else slice(None) for n in rest)

        def add(source, target, device):
            i = len(made)
            made.append(send(source, target, self.send_sem.at[piece, hop, i], self.recv_sem.at[piece, hop, i], device))

        if hop == 0:
            if name == "z":
                for d in range(1, place.deep):
                    z = place.line(d)
                    add(self.cut(piece, "z", z), self.first[piece].at[d - 1], place.device(z=z))
            else:
                add(self.cut(piece, name, 1 - getattr(place, name)), self.first[piece], self.peer(name))
            return made
        fixed = {} if hop == 1 else {order[1]: getattr(place, order[1])}
        buffer = self.second[piece] if hop == 1 else self.third[piece]
        if name == "z":
            for d in range(1, place.deep):
                z = place.line(d)
                add(own.at[at(z=z, **fixed)], buffer.at[d - 1], place.device(z=z))
        else:
            add(own.at[at(**{name: 1 - getattr(place, name)}, **fixed)], buffer, self.peer(name))
        return made

    def start(self, piece, hop):
        for copy in self.copies(piece, hop):
            copy.start()

    def arrive(self, piece, hop):
        for copy in self.copies(piece, hop):
            copy.wait_recv()

    def came_copy(self, piece):
        return pltpu.make_async_copy(self.came[piece], self.first[piece], self.recv_sem.at[piece, 0, 0])

    def begin(self, piece):
        if piece < len(self.came):
            self.came_copy(piece).start()
        else:
            self.start(piece, 0)
        self.own_copy(piece).start()

    def add_first(self, piece):
        order = self.pieces[piece][3]
        if piece < len(self.came):
            self.came_copy(piece).wait()
        else:
            self.arrive(piece, 0)
        self.own_copy(piece).wait()
        if piece >= len(self.came) and self.waiting:
            self.begin(self.waiting.pop(0))
        own, came = self.own[piece], self.first[piece]
        inner = own.shape[1]

        def body(i, carry):
            for k in range(inner):
                if order[0] == "z":
                    total = own[i, k].astype(jnp.float32)
                    for d in range(came.shape[0]):
                        total = total + came[d, i, k].astype(jnp.float32)
                    own[i, k] = total.astype(jnp.bfloat16)
                else:
                    own[i, k] = own[i, k] + came[i, k]
            return carry

        lax.fori_loop(0, own.shape[0], body, 0)
        self.start(piece, 1)

    def add_second(self, piece):
        place, order = self.place, self.pieces[piece][3]
        name, rest = order[1], self.rest(piece)
        self.arrive(piece, 1)
        own, came = self.own[piece], self.second[piece]
        mine = getattr(place, name)
        spans = own.shape[1] if rest[0] == name else own.shape[0]

        def body(i, carry):
            if name == "z":
                total = own[mine, i].astype(jnp.float32)
                for d in range(came.shape[0]):
                    total = total + came[d, i].astype(jnp.float32)
                own[mine, i] = total.astype(jnp.bfloat16)
            elif rest[0] == name:
                own[mine, i] = own[mine, i] + came[i]
            else:
                own[i, mine] = own[i, mine] + came[i]
            return carry

        lax.fori_loop(0, spans, body, 0)
        self.start(piece, 2)

    def add_third(self, piece):
        place, order = self.place, self.pieces[piece][3]
        rest = self.rest(piece)
        self.arrive(piece, 2)
        total = self.own[piece][getattr(place, rest[0]), getattr(place, rest[1])].astype(jnp.float32)
        if order[2] == "z":
            for d in range(1, place.deep):
                total = total + self.third[piece][d - 1].astype(jnp.float32)
        else:
            total = total + self.third[piece][...].astype(jnp.float32)
        for out, start, at, n in self.pieces[piece][4]:
            self.outs[out][:, start : start + n] = total[:, at : at + n]

    def plan(self, window):
        self.waiting = [i for i, piece in enumerate(self.pieces) if piece[0] == 0]
        count = len(self.pieces)
        for i in range(count + SUM_LAGS[1]):
            if i < count:
                self.queue.append(functools.partial(self.add_first, i))
            if 0 <= i - SUM_LAGS[0] < count:
                self.queue.append(functools.partial(self.add_second, i - SUM_LAGS[0]))
            if 0 <= i - SUM_LAGS[1] < count:
                self.queue.append(functools.partial(self.add_third, i - SUM_LAGS[1]))
        for _ in range(min(len(self.came) + window, len(self.waiting))):
            self.begin(self.waiting.pop(0))

    def run(self, steps):
        for _ in range(min(steps, len(self.queue))):
            self.queue.pop(0)()

    def take(self, steps):
        taken, self.queue = self.queue[:steps], self.queue[steps:]
        return taken

    def sent(self):
        for piece in range(len(self.pieces)):
            for hop in range(0 if piece >= len(self.came) else 1, 3):
                for copy in self.copies(piece, hop):
                    copy.wait_send()


def piece_buffers(piece, deep, rows):
    _, a, b, order, _ = piece
    sizes = {"z": deep, "y": 2, "x": 2}
    rest = [name for name in "zyx" if name != order[0]]
    left = [sizes[name] for name in rest]
    last = [sizes[name] for name in rest if name != order[1]]
    tail = [rows, b - a]
    lead = [deep - 1]
    first = (lead if order[0] == "z" else []) + left + tail
    second = (lead if order[1] == "z" else []) + last + tail
    third = (lead if order[2] == "z" else []) + tail
    return [tuple(shape) for shape in (first, left + tail, second, third)]


def back_kernel(shard_size, pieces, sizes, given, *refs):
    inner, hidden, buckets = sizes
    count = len(pieces)
    (
        lengths_ref, full_ref, normed_in, qkv_in, bandt_in, biast_in, grads_in, do_in,
        lse_ref, output_ref, middle_ref, tokens_ref, gain_two_ref, table_ref,
    ) = refs[:14]
    came, refs = refs[14 : 14 + given], refs[14 + given :]
    weight_outs, (output_out, input_out, small_out) = refs[:7], refs[7:10]
    refs = refs[10:]
    first, own, second, third = [refs[k * count : (k + 1) * count] for k in range(4)]
    refs = refs[4 * count :]
    (
        qkv, normed_t, bandt, bias, wqkv, gain_buf, do, scores, grads, far, dk_acc, dv_acc, kaux, wgrad,
        mine_sum, away, arrived, result, table_acc, hot, found,
        small, small_x, small_y, hold_x, hold_y, hold_z, small_c,
        own_sem, send_sem, recv_sem, near_send, near_recv, local_sem,
    ) = refs
    length = qkv.shape[1]
    width = normed_t.shape[0]
    half, quarter = length // 2, length // 4
    heads, blocks = bias.shape[:2]
    pairs = heads // 2
    deep = shard_size // 2
    low, f32 = jnp.bfloat16, jnp.float32
    place = Place(shard_size)
    x, y, z, c = place.x, place.y, place.z, place.c
    to_x, to_y, to_c = place.device(x=1 - x), place.device(y=1 - y), place.device(c=1 - c)

    def local(i, source, target):
        return pltpu.make_async_copy(source, target, local_sem.at[i])

    loads = [
        local(0, qkv_in, qkv), local(1, biast_in, bias), local(2, do_in, do),
        local(3, full_ref.at[:, :, :, :, 128 : 128 + 3 * inner], wqkv), local(4, normed_in, normed_t),
        local(5, bandt_in, bandt), local(6, full_ref.at[:, :, :, :, 0:128], gain_buf),
    ]
    for copy in loads:
        copy.start()
    meet(place)
    scatter = Scatter(
        place, pieces, (grads_in, wgrad), weight_outs, (first, own, second, third), (own_sem, send_sem, recv_sem), came,
    )
    scatter.plan(SUM_WINDOW)

    def near(i, source, target, device):
        return send(source, target, near_send.at[i], near_recv.at[i], device)

    def to_owners(i, values, out):
        here = out.at[x, pl.ds(c * quarter, quarter)]
        there = out.at[1 - x, pl.ds(c * quarter, quarter)]
        return (
            local(7 + i, values.at[x], here),
            near(4 * i, values.at[x], here, to_c),
            near(4 * i + 1, values.at[1 - x], here, to_x),
            near(4 * i + 2, there, there, to_c),
        )

    output_moves = to_owners(0, output_ref, output_out)
    for copy in output_moves[:3]:
        copy.start()

    lanes_of = lax.broadcasted_iota(jnp.int32, (length, 128), 1)
    rows_of = lax.broadcasted_iota(jnp.int32, (length, 128), 0)
    valid = lengths_ref[x, 0]
    blocked = jnp.where(rows_of // BLOCK == lanes_of, 1.0, 0.0)
    kaux[...] = jnp.where((lanes_of == blocks) & (rows_of >= valid), -1e30, blocked).astype(low)
    far[...] = jnp.zeros_like(far)
    for copy in loads:
        copy.wait()

    per_pair = length // 256
    units = pairs * per_pair
    acts = scatter.take(ATTENTION_ACTS)

    def unit_step(unit, carry):
        pair = unit // per_pair
        step = unit % per_pair
        rows = pl.ds(pl.multiple_of(step * 256, 256), 256)

        @pl.when(step == 0)
        def _():
            dk_acc[...] = jnp.zeros_like(dk_acc)
            dv_acc[...] = jnp.zeros_like(dv_acc)

        queries = qkv[pair, rows, :]
        grad = do[pair, rows, :]
        key_pair = qkv[pairs + pair]
        keys = jnp.concatenate([key_pair, kaux[...]], axis=1)
        values = qkv[2 * pairs + pair]
        dq = None
        for head in range(2):
            between(acts, units, ACT_FIRST, unit, head)
            here = lane_head(256, 128, head)
            aux = query_aux(table_ref[2 * pair + head], step, blocks)
            q_masked = jnp.where(here, queries, jnp.zeros_like(queries))
            do_masked = jnp.where(here, grad, jnp.zeros_like(grad))
            scores[...] = lax.dot_general(
                keys, jnp.concatenate([q_masked, aux], axis=1), LAST, preferred_element_type=f32
            )
            for sub in range(2):
                start = pl.multiple_of(band_start(step * 2 + sub, blocks) * BLOCK, BLOCK)
                scores[pl.ds(start, BAND * BLOCK), sub * BLOCK : (sub + 1) * BLOCK] += bias[
                    2 * pair + head, 2 * step + sub
                ].astype(f32)
            soft = jnp.exp(scores[...] - lse_ref[pair, step, head : head + 1, :])
            dv_acc[...] += jnp.dot(soft.astype(low), do_masked, preferred_element_type=f32)
            grad_probs = lax.dot_general(values, do_masked, LAST, preferred_element_type=f32)
            weighted = jnp.sum(soft * grad_probs, axis=0, keepdims=True)
            grad_scores = (soft * (grad_probs - weighted)).astype(low)
            grads[...] = grad_scores
            dk_acc[...] += jnp.dot(grad_scores, q_masked, preferred_element_type=f32)
            k_masked = jnp.where(lane_head(length, 128, head), key_pair, jnp.zeros_like(key_pair))
            part = lax.dot_general(grad_scores, k_masked, FIRST, preferred_element_type=f32)
            dq = part if dq is None else dq + part
            sums = jnp.concatenate(
                [
                    jnp.sum(grad_scores[block * BLOCK : (block + 1) * BLOCK, :].astype(f32), axis=0, keepdims=True)
                    for block in range(blocks)
                ],
                axis=0,
            )
            block_of = lax.broadcasted_iota(jnp.int32, (blocks, BLOCK), 0)
            for sub in range(2):
                start = band_start(step * 2 + sub, blocks)
                at = pl.multiple_of(start * BLOCK, BLOCK)
                bias[2 * pair + head, 2 * step + sub] = grads[pl.ds(at, BAND * BLOCK), sub * BLOCK : (sub + 1) * BLOCK]
                part = sums[:, sub * BLOCK : (sub + 1) * BLOCK]
                far[0, 2 * pair + head] += jnp.where(block_of < start, part, 0.0)
                far[1, 2 * pair + head] += jnp.where(block_of >= start + BAND, part, 0.0)
        qkv[pair, rows, :] = dq.astype(low)

        @pl.when(step == per_pair - 1)
        def _():
            qkv[pairs + pair] = dk_acc[...].astype(low)
            qkv[2 * pairs + pair] = dv_acc[...].astype(low)
            right = jnp.concatenate([qkv[t * pairs + pair] for t in range(3)], axis=1)

            def weight_step(i, carry):
                rows = pl.ds(pl.multiple_of(i * 256, 256), 256)
                got = jnp.dot(normed_t[rows, :], right, preferred_element_type=f32).astype(low)
                span = deep // (width // 256)
                wgrad[pair, pl.ds(i * span, span)] = got.reshape((span,) + wgrad.shape[2:5] + (3 * 128,))
                return carry

            lax.fori_loop(0, width // 256, weight_step, 0)

        for late, piece in enumerate(pieces):
            if piece[0]:
                @pl.when(unit == piece[0] * per_pair - 1)
                def _(late=late):
                    scatter.begin(late)

        return carry

    lax.fori_loop(0, units, unit_step, 0)
    for copy in output_moves[:3]:
        copy.wait()
    output_moves[3].start()
    def part_rows(part, core):
        return pl.ds(pl.multiple_of(part * half + core * quarter, quarter), quarter)

    def grad_one(rows):
        left = jnp.concatenate([qkv[k, rows, :] for k in range(3 * pairs)], axis=1)
        return lax.dot_general(left, wqkv[...].reshape(width, 3 * inner), LAST, preferred_element_type=f32)

    swaps = [near(8 + part, away.at[part], arrived.at[part], to_c) for part in range(2)]

    def away_step(part, carry):
        away[part] = grad_one(part_rows(part, 1 - c)).astype(low)
        return carry

    def mine_step(part, carry):
        mine_sum[part] = grad_one(part_rows(part, c))
        return carry

    lax.fori_loop(0, 2, away_step, 0)
    for copy in swaps:
        copy.start()
    scatter.run(1)
    lax.fori_loop(0, 2, mine_step, 0)
    scatter.run(1)
    gains = jnp.transpose(gain_buf[...].reshape(width, 128).astype(f32))
    gain_one = gains[0:1, :]
    gain_sum = jnp.zeros((1, width), f32)
    for part in range(2):
        swaps[part].wait()
        total = mine_sum[part] + arrived[part].astype(f32)
        present = tokens_ref[part].astype(f32)
        inverse = lax.rsqrt(jnp.mean(present * present, axis=-1, keepdims=True) + EPSILON)
        unit = present * inverse
        gain_sum = gain_sum + jnp.sum(total * unit, axis=0, keepdims=True)
        scaled = total * gain_one
        back = inverse * (scaled - unit * jnp.mean(scaled * unit, axis=-1, keepdims=True))
        result[part] = (middle_ref[part] + back).astype(low)
        scatter.run(1)
    input_moves = to_owners(1, result, input_out)
    for copy in input_moves[:3]:
        copy.start()
    table_acc[...] = jnp.zeros_like(table_acc)
    groups = BAND * BLOCK // GROUP
    table_units = blocks // 2 * groups // TURNS
    table_acts = scatter.take(TABLE_ACTS)

    def table_step(i, carry):
        for k, act in enumerate(table_acts):
            @pl.when(i == (k * table_units) // max(1, len(table_acts)))
            def _(act=act):
                act()
        total = None
        for turn in range(TURNS):
            group = i * TURNS + turn
            block = 2 * (group // groups)
            start = pl.multiple_of((group % groups) * GROUP, GROUP)
            for two in range(2):
                lanes = slice(two * BLOCK, (two + 1) * BLOCK)
                index = bandt[block + two, pl.ds(start, GROUP), :]
                for head in range(heads):
                    found[turn, head * GROUP : (head + 1) * GROUP, lanes] = bias[head, block + two, pl.ds(start, GROUP), :]
                for b in range(buckets):
                    hot[turn, b * GROUP : (b + 1) * GROUP, lanes] = jnp.where(
                        index == jnp.asarray(b, low), jnp.asarray(1, low), jnp.asarray(0, low)
                    )
            part = lax.dot_general(hot[turn], found[turn], LAST, preferred_element_type=f32)
            total = part if total is None else total + part
        table_acc[...] += total
        return carry

    lax.fori_loop(0, table_units, table_step, 0)
    row = lax.broadcasted_iota(jnp.int32, table_acc.shape, 0) % GROUP
    col = lax.broadcasted_iota(jnp.int32, table_acc.shape, 1) % GROUP
    kept = jnp.where(row == col, table_acc[...], 0.0).reshape(buckets, GROUP, heads * GROUP).sum(axis=1)
    bucket = lax.broadcasted_iota(jnp.int32, (buckets, 128), 0)
    head_of = lax.broadcasted_iota(jnp.int32, (buckets, 128), 1)
    table = jnp.zeros((buckets, 128), f32)
    for head in range(heads):
        amount = jnp.sum(kept[:, head * GROUP : (head + 1) * GROUP], axis=1, keepdims=True)
        table = table + jnp.where(head_of == head, amount, 0.0)
    for side, name in enumerate((buckets // 2 - 1, buckets - 1)):
        for head in range(heads):
            amount = jnp.sum(jnp.sum(far[side, head], axis=0, keepdims=True), axis=1, keepdims=True)
            table = table + jnp.where((bucket == name) & (head_of == head), amount, 0.0)

    lines = width // 128
    for i in range(lines):
        small[i : i + 1, :] = gain_sum[:, i * 128 : (i + 1) * 128]
    gain_two_sum = jnp.sum(gain_two_ref[0] + gain_two_ref[1], axis=0, keepdims=True)
    for i in range(lines):
        small[lines + i : lines + i + 1, :] = gain_two_sum[:, i * 128 : (i + 1) * 128]
    small[2 * lines : 2 * lines + buckets, :] = table
    small_base = 10

    def small_line(d):
        return near(small_base + 2 + d, hold_z.at[z], hold_z.at[z], place.device(z=place.line(d)))

    move = near(small_base, small, small_x, to_x)
    move.start()
    scatter.run(1)
    move.wait()
    hold_x[...] = small[...] + small_x[...]
    move = near(small_base + 1, hold_x, small_y, to_y)
    move.start()
    scatter.run(1)
    move.wait()
    hold_z[z] = hold_x[...] + small_y[...]
    for d in range(1, deep):
        small_line(d).start()
    scatter.run(1)
    for d in range(1, deep):
        small_line(d).wait()
    hold_y[...] = jnp.sum(hold_z[...], axis=0)
    move = near(small_base + 2, hold_y, small_c, to_c)
    move.start()
    scatter.run(1)
    move.wait()
    small_out[0] = hold_y[...]
    small_out[1] = hold_y[...] + small_c[...]

    for copy in input_moves[:3]:
        copy.wait()
    input_moves[3].start()
    input_moves[3].wait()
    output_moves[3].wait()
    scatter.run(len(scatter.queue))
    scatter.sent()


def back(shard_size, pieces, buckets, lengths, full, normed_t, qkv, bandt, biast, grads, do, lse, output, middle, tokens, gain_two, table_rows, came):
    low, f32 = jnp.bfloat16, jnp.float32
    deep = shard_size // 2
    rows = full.shape[3]
    width, length = normed_t.shape
    half, quarter = length // 2, length // 4
    heads, blocks = biast.shape[:2]
    pairs = heads // 2
    inner = pairs * 128
    hidden = (grads.shape[4] - inner) // 3
    count = len(pieces)
    shape = jax.ShapeDtypeStruct
    vmem, hbm = pl.BlockSpec(memory_space=pltpu.VMEM), pl.BlockSpec(memory_space=pl.ANY)
    dma = pltpu.SemaphoreType.DMA
    lines = 2 * (width // 128) + buckets
    buffers = [piece_buffers(piece, deep, rows) for piece in pieces]
    scratch = [pltpu.VMEM(buffer[k], low) for k in range(4) for buffer in buffers]
    small = pltpu.VMEM((lines, 128), f32)
    scratch += [
        pltpu.VMEM((3 * pairs, length, 128), low),
        pltpu.VMEM((width, length), low),
        pltpu.VMEM((blocks, BAND * BLOCK, BLOCK), low),
        pltpu.VMEM((heads, blocks, BAND * BLOCK, BLOCK), low),
        pltpu.VMEM((deep, 2, 2, rows, 3 * inner), low),
        pltpu.VMEM((deep, 2, 2, rows, 128), low),
        pltpu.VMEM((pairs, length, 128), low),
        pltpu.VMEM((length, 256), f32),
        pltpu.VMEM((length, 256), low),
        pltpu.VMEM((2, heads, blocks, BLOCK), f32),
        pltpu.VMEM((length, 128), f32),
        pltpu.VMEM((length, 128), f32),
        pltpu.VMEM((length, 128), low),
        pltpu.VMEM((pairs, deep, 2, 2, rows, 3 * 128), low),
        pltpu.VMEM((2, quarter, width), f32),
        pltpu.VMEM((2, quarter, width), low),
        pltpu.VMEM((2, quarter, width), low),
        pltpu.VMEM((2, quarter, width), low),
        pltpu.VMEM((buckets * GROUP, heads * GROUP), f32),
        pltpu.VMEM((TURNS, buckets * GROUP, 2 * BLOCK), low),
        pltpu.VMEM((TURNS, heads * GROUP, 2 * BLOCK), low),
        small, small, small, small, small, pltpu.VMEM((deep, lines, 128), f32), small,
        dma((count,)),
        dma((count, 3, deep - 1)),
        dma((count, 3, deep - 1)),
        dma((12 + deep,)),
        dma((12 + deep,)),
        dma((9,)),
    ]
    return pl.pallas_call(
        functools.partial(back_kernel, shard_size, pieces, (inner, hidden, buckets), len(came)),
        out_shape=[
            *[shape((rows, n), f32) for n in (inner,) * 4 + (hidden,) * 3],
            shape((2, half, width), low),
            shape((2, half, width), low),
            shape((2, lines, 128), f32),
        ],
        in_specs=[pl.BlockSpec(memory_space=pltpu.SMEM)] + [hbm] * 7 + [vmem] * 6 + [hbm] * len(came),
        out_specs=[vmem] * 7 + [hbm, hbm, vmem],
        scratch_shapes=scratch,
        compiler_params=pltpu.CompilerParams(
            collective_id=2, has_side_effects=True, vmem_limit_bytes=60 * MIB
        ),
        name="back",
    )(lengths, full, normed_t, qkv, bandt, biast, grads, do, lse, output, middle, tokens, gain_two, table_rows, *came)


def finish_kernel(*refs):
    count = len(refs) // 2
    for source, target in zip(refs[:count], refs[count:]):
        target[...] = source[...].astype(target.dtype)


def finish(weight_sums, output, input_grad):
    steps = 4 if weight_sums[0].shape[0] % 32 == 0 else 2
    values = [*weight_sums, output, input_grad]
    kinds = [jnp.float32] * len(weight_sums) + [output.dtype, jnp.float32]
    specs = [pl.BlockSpec((w.shape[0] // steps, w.shape[1]), lambda i: (i, 0)) for w in weight_sums]
    specs += [pl.BlockSpec((2, v.shape[1] // steps, v.shape[2]), lambda i: (0, i, 0)) for v in (output, input_grad)]
    return pl.pallas_call(
        finish_kernel,
        grid=(steps,),
        in_specs=specs,
        out_specs=specs,
        out_shape=[jax.ShapeDtypeStruct(v.shape, kind) for v, kind in zip(values, kinds)],
        compiler_params=pltpu.CompilerParams(vmem_limit_bytes=60 * MIB),
        name="finish",
    )(*values)


ORDERS = ("xyz", "zxy", "zyx", "zxy", "zxy", "zyx", "zxy", "zyx", "zxy")
SUM_ORDERS = ("yxz", "xyz")
GIVEN = 6
LATE_FIRST = 6
LATE_STEP = 3
ROW_ACTS = 2
WINDOW = 4
AHEAD = 2
LAG = 4
QUICK = 4
SUM_WINDOW = 3
SUM_LAGS = (2, 4)
FORWARD_ACTS = 9
ATTENTION_ACTS = 28
ACT_FIRST = 2
TABLE_ACTS = 14


def front_pieces(inner, hidden):
    at_project = 128 + 3 * inner
    at_hidden = at_project + inner
    pieces = split_columns(0, at_project, 4) + split_columns(at_project, at_hidden, 2)
    for j, n in enumerate(hidden_steps(hidden)):
        at = at_hidden + 3 * HIDDEN_STEP * j
        pieces += split_columns(at, at + 3 * n, 2)
    return [(a, b, ORDERS[i % len(ORDERS)]) for i, (a, b) in enumerate(pieces)]


def back_pieces(inner, hidden):
    where = []
    for j, n in enumerate(hidden_steps(hidden)):
        for k in range(3):
            where.append((3 * HIDDEN_STEP * j + k * n, n, 4 + k, HIDDEN_STEP * j))
    where.append((3 * hidden, inner, 3, 0))
    cuts = []
    for j, n in enumerate(hidden_steps(hidden)):
        at = 3 * HIDDEN_STEP * j
        cuts += split_columns(at, at + 3 * n, 2 if n > 128 else 1)
    cuts += split_columns(3 * hidden, 3 * hidden + inner, 2)
    pieces = []
    for a, b in cuts:
        segments = []
        for start, n, out, column in where:
            low, high = max(a, start), min(b, start + n)
            if low < high:
                segments.append((out, column + low - start, low - a, high - low))
        pieces.append((0, a, b, segments))
    for pair in range(inner // 128):
        piece = (1 + pair, 0, 3 * 128, [(t, pair * 128, t * 128, 128) for t in range(3)])
        pieces.insert(min(len(pieces), LATE_FIRST + LATE_STEP * pair), piece)
    return [(t, a, b, SUM_ORDERS[i % len(SUM_ORDERS)], segments) for i, (t, a, b, segments) in enumerate(pieces)]


def shards(
    inputs, cotangent, lengths, buckets,
    query_weight, key_weight, value_weight, projection_weight, gate_weight, up_weight, down_weight,
    attention_gain, feedforward_gain, bias_table,
):
    x = lax.axis_index("ctx")
    shard_size = lax.axis_size("shard")
    width = inputs.shape[2]
    bucket_count, heads = bias_table.shape
    rows, inner = query_weight.shape
    hidden = gate_weight.shape[1]
    cuts = back_pieces(inner, hidden)
    gains = jnp.pad(jnp.stack([attention_gain, feedforward_gain], axis=1), ((0, 0), (0, 126)))
    table_rows = jnp.broadcast_to(
        jnp.pad(bias_table.astype(jnp.float32).T, ((0, 0), (0, 128 - bucket_count)))[:, None, :], (heads, 8, 128)
    )
    weights = (query_weight, key_weight, value_weight, projection_weight, gate_weight, up_weight, down_weight)
    (
        full, normed_t, qkv, bandt, biast, grads, grad_attended, tokens,
        lse, output, grad_middle, gain_two, *came,
    ) = front(shard_size, front_pieces(inner, hidden), WINDOW, [(a, b, order[0]) for _, a, b, order, _ in cuts[:GIVEN]], lengths, gains, weights, inputs, cotangent, buckets, table_rows)

    *weight_sums, output, input_grad, small = back(
        shard_size, cuts, bucket_count,
        lengths, full, normed_t, qkv, bandt, biast, grads, grad_attended,
        lse, output, grad_middle, tokens, gain_two, table_rows, came,
    )
    *weight_sums, output, input_grad = finish(weight_sums, output, input_grad)
    lines = width // 128
    me = lax.axis_index("shard") * 2 + x

    def own_gain(part):
        return lax.dynamic_slice_in_dim(small[1, part * lines : (part + 1) * lines].reshape(-1), me * rows, rows)

    return (
        output, input_grad,
        *weight_sums, own_gain(0), own_gain(1), small[0, 2 * lines :, :heads],
    )


def solution(mesh):
    rows = P(None, ("shard", "ctx"), None)
    weight = P(("shard", "ctx"), "tp")
    gain = P(("shard", "ctx"))
    table = P(None, "tp")
    return jax.shard_map(
        shards,
        mesh=mesh,
        in_specs=(rows, rows, P(None, "shard"), P("ctx", None)) + (weight,) * 7 + (gain, gain, table),
        out_specs=(rows, rows) + (weight,) * 7 + (gain, gain, table),
        check_vma=False,
    )
```
